32 devices in a mesh: ax: 16 (over z, y, x), rad: 2 (over core).
Axes of the slice: x: 2, y: 2, z: 4, core: 2. Of those that a mesh axis runs over, the one named last changes fastest.
Arguments:
- parcel_motion: float32 [6, 65536], P(None, ('ax', 'rad')), may hold values from -6 to 6
- parcel_size: float32 [65536], P(('ax', 'rad')), may hold values from 0.5 to 2
- parcel_block: int32 [1024], P(('ax', 'rad')), may hold values from 0 to 127, as said below
- parcel_offset: int32 [65536], P(('ax', 'rad')), may hold values from 0 to 127
- gas_velocity: float32 [3, 256, 1024], P(None, 'ax', 'rad'), may hold values from -6 to 6
- pressure: float32 [256, 1024], P('ax', 'rad'), may hold values from -6 to 6
- block_cols: int32 [16, 128, 4], P('ax', 'rad'), may hold values from 0 to 127
- block_kinds: int32 [16, 128, 4], P('ax', 'rad'), may hold values from 0 to 7
- block_table: float32 [8, 128, 128], replicated, may hold values from -0.5 to 0.5
- send_axial: int32 [16, 2, 2, 64], P('ax', 'rad'), may hold values from 0 to 2047, as said below
- send_radial: int32 [16, 2, 2, 32], P('ax', 'rad'), may hold values from 0 to 2047, as said below
- send_counts: int32 [16, 2, 4], P('ax', 'rad'), may hold values from 0 to 64, as said below
Outputs:
- motion_out: float32 [6, 65536], P(None, ('ax', 'rad'))
- arrivals_axial: float32 [16, 2, 2, 7, 64], P('ax', 'rad')
- arrivals_radial: float32 [16, 2, 2, 7, 32], P('ax', 'rad')
- gas_out: float32 [3, 256, 1024], P(None, 'ax', 'rad')
- liquid_load: float32 [256, 1024], P('ax', 'rad')
- pressure_image: float32 [256, 1024], P('ax', 'rad')
The draws below stay inside these ranges and needn't reach their ends.
Inputs may be any that keep to these rules, and one draw needn't show every extreme that they name: `parcel_block`: most of a device's parcel blocks lie in cell blocks of its own radial group; the others lie in other radial groups of the slab. `send_axial`: each device's lists (both axial and both radial together) hold distinct indices of that device's parcels; entries past the counts are unused. `send_radial`: disjoint from the device's axial lists, see send_axial. `send_counts`: axial counts are at most 64, radial ones at most 32; devices of radial group 0 send full lists in all four directions.
All inputs are finite; a program needn't handle non-finite values.
Results may differ from the reference program's by a relative error of at most 0.000084.
Values sent between devices are 32-bit elements; how exact they have to be, the bound alone decides.
No kernel may reach another device: no remote copies, remote signals or barrier semaphores. Data moves between devices by JAX's collectives and lax.ppermute only.
A program may use at most 64 MiB of HBM per device.

```python
import math
import jax
import jax.numpy as jnp
from jax import lax

BLOCK = 128
PARCEL_GROUP = 64
RC = 512
AZ = 16
NPB = 32
K = 4
NT = 8
NB = 64
P_DEV = 2048
CAP_AX = 64
CAP_RAD = 32
ZLEN = 256
RLEN = 1024
PARCELS = 65536
PBLOCKS = 1024
N_AX = 16
N_RAD = 2


def parcel_order(key):
    keys = jax.random.split(jax.random.fold_in(key, 11), N_AX * N_RAD)
    return jax.vmap(lambda single: jax.random.permutation(single, P_DEV))(keys).astype(jnp.int32)


def draw_parcel_block(key, part):
    index = jnp.arange(PBLOCKS, dtype=jnp.int32)
    radial = index // NPB % N_RAD
    within = index % NPB
    local = jax.random.randint(jax.random.fold_in(key, 31), (PBLOCKS,), 0, NB).astype(jnp.int32)
    local = jnp.where(within == 0, NB - 1, local)
    local = jnp.where(within == 1, 0, local)
    away = jax.random.randint(jax.random.fold_in(key, 37), (PBLOCKS,), 0, 8).astype(jnp.int32) == 0
    away = jnp.logical_or(away, within == NPB - 1)
    away = jnp.logical_and(away, within >= 2)
    step = jax.random.randint(jax.random.fold_in(key, 41), (PBLOCKS,), 1, N_RAD).astype(jnp.int32)
    group = jnp.where(away, (radial + step) % N_RAD, radial)
    return (group * NB + local).astype(jnp.int32)


def draw_send_axial(key, part):
    order = parcel_order(key)
    return order[:, :2 * CAP_AX].reshape(N_AX, N_RAD, 2, CAP_AX)


def draw_send_radial(key, part):
    order = parcel_order(key)
    return order[:, 2 * CAP_AX:2 * CAP_AX + 2 * CAP_RAD].reshape(N_AX, N_RAD, 2, CAP_RAD)


def draw_send_counts(key, part):
    limits = jnp.array([CAP_AX, CAP_AX, CAP_RAD, CAP_RAD], jnp.int32)
    drawn = jax.random.randint(jax.random.fold_in(key, 23), (N_AX, N_RAD, 4), 0, limits + 1)
    core = (jnp.arange(N_RAD, dtype=jnp.int32) == 0)[None, :, None]
    return jnp.where(core, limits[None, None, :], drawn).astype(jnp.int32)


def set_ends(result, key, least, largest):
    place = [jax.random.randint(jax.random.fold_in(key, axis), (), 0, length) for axis, length in enumerate(result.shape)]
    widest = result.shape.index(max(result.shape))
    neighbour = place[:widest] + [(place[widest] + 1) % result.shape[widest]] + place[widest + 1:]
    return result.at[tuple(place)].set(least).at[tuple(neighbour)].set(largest)


def shard_levels(stream_key, dims, cuts, least, high):
    def one(axis_at, parts):
        steps = jax.random.uniform(jax.random.fold_in(jax.random.fold_in(stream_key, 6), axis_at), (parts,), jnp.float32, least / len(cuts), high / len(cuts))
        return jnp.repeat(jnp.exp(steps), dims[axis_at] // parts).reshape((-1,) + (1,) * (len(dims) - axis_at - 1))

    gain = one(*cuts[0])
    for cut in cuts[1:]:
        gain = gain * one(*cut)
    return gain


def bell_draw(key, dims, scale, bound, pieces=(), kind=jnp.bfloat16):
    values = scale * jax.random.normal(key, dims, jnp.float32)
    if pieces:
        values = values * shard_levels(key, dims, pieces, -0.22, 0.18)
    return jnp.clip(values, -bound, bound).astype(kind)


def setup_inputs(seed: int = 0) -> dict:
    streams_of = jax.random.split(jax.random.key(seed), 13)
    return {
        "parcel_motion": bell_draw(streams_of[0], (6, PARCELS), 1.0, 6.0, ((1, 32),), jnp.float32),
        "parcel_size": jnp.clip(jnp.exp(math.log(2.0) - 1.3862944 * jax.random.uniform(streams_of[1], (PARCELS,), jnp.float32) ** shard_levels(streams_of[1], (PARCELS,), ((0, 32),), -0.2, 0.2)), 0.5, 2.0),
        "parcel_block": draw_parcel_block(jax.random.fold_in(streams_of[12], 71), 0),
        "parcel_offset": set_ends(jax.random.randint(streams_of[3], (PARCELS,), 0, BLOCK), jax.random.fold_in(streams_of[3], 1), 0, BLOCK - 1).astype(jnp.int32),
        "gas_velocity": bell_draw(streams_of[4], (3, ZLEN, RLEN), 1.0, 6.0, ((1, 16), (2, 2)), jnp.float32),
        "pressure": bell_draw(streams_of[5], (ZLEN, RLEN), 1.0, 6.0, ((0, 16), (1, 2)), jnp.float32),
        "block_cols": set_ends(jax.random.randint(streams_of[6], (N_AX, NB * N_RAD, K), 0, NB * N_RAD), jax.random.fold_in(streams_of[6], 1), 0, (NB * N_RAD) - 1).astype(jnp.int32),
        "block_kinds": set_ends(jax.random.randint(streams_of[7], (N_AX, NB * N_RAD, K), 0, NT), jax.random.fold_in(streams_of[7], 1), 0, NT - 1).astype(jnp.int32),
        "block_table": bell_draw(streams_of[8], (NT, BLOCK, BLOCK), BLOCK ** -0.5, 0.5, (), jnp.float32),
        "send_axial": draw_send_axial(jax.random.fold_in(streams_of[12], 71), 0),
        "send_radial": draw_send_radial(jax.random.fold_in(streams_of[12], 71), 0),
        "send_counts": draw_send_counts(jax.random.fold_in(streams_of[12], 71), 0),
    }


TOP_PRECISION = lax.Precision.HIGHEST
DRAG = 0.5
STEP = 0.5
DIAG = 6.0


def slab_blocks(field):
    lead = field.shape[:-2]
    shaped = field.reshape(lead + (N_AX, AZ, N_RAD, RC))
    shaped = jnp.moveaxis(shaped, -2, -3)
    return shaped.reshape(lead + (N_AX, N_RAD * NB, BLOCK))


def unslab(block_list):
    lead = block_list.shape[:-3]
    shaped = block_list.reshape(lead + (N_AX, N_RAD, AZ, RC))
    shaped = jnp.moveaxis(shaped, -3, -2)
    return shaped.reshape(lead + (ZLEN, RLEN))


def reference(parcel_motion, parcel_size, parcel_block, parcel_offset, gas_velocity, pressure, block_cols, block_kinds, block_table, send_axial, send_radial, send_counts):
    gas_slab = slab_blocks(gas_velocity)
    device = jnp.arange(PARCELS, dtype=jnp.int32) // P_DEV
    axial = device // N_RAD
    owner_block = jnp.repeat(parcel_block, PARCEL_GROUP)
    visited_flags = gas_slab[:, axial, owner_block, parcel_offset]
    velocity = parcel_motion[3:6]
    factor = jnp.exp(-DRAG / (parcel_size * parcel_size))
    new_vel = visited_flags + (velocity - visited_flags) * factor
    new_pos = parcel_motion[0:3] + STEP * new_vel
    motion_out = jnp.concatenate([new_pos, new_vel], axis=0)
    mass = parcel_size * parcel_size * parcel_size
    deposit = jnp.concatenate([-mass * (new_vel - velocity), mass[None]], axis=0)
    sources = jnp.zeros((4, N_AX, N_RAD * NB, BLOCK), jnp.float32)
    sources = sources.at[:, axial, owner_block, parcel_offset].add(deposit)
    sources = unslab(sources)
    gas_out = gas_velocity + sources[:3]
    liquid_load = sources[3]

    state = jnp.concatenate([motion_out, parcel_size[None]], axis=0)
    state = state.reshape(7, N_AX, N_RAD, P_DEV).transpose(1, 2, 0, 3)

    def pick(lists, counts):
        width = lists.shape[-1]
        full_state = jnp.broadcast_to(state[:, :, None, :, :], (N_AX, N_RAD, 2, 7, P_DEV))
        full_lists = jnp.broadcast_to(lists[:, :, :, None, :], (N_AX, N_RAD, 2, 7, width))
        taken = jnp.take_along_axis(full_state, full_lists, axis=4)
        live = jnp.arange(width, dtype=jnp.int32)[None, None, None, :] < counts[..., None]
        return jnp.where(live[:, :, :, None, :], taken, jnp.float32(0.0))

    out_ax = pick(send_axial, send_counts[:, :, 0:2])
    zero_ax = jnp.zeros_like(out_ax[:1, :, 0])
    from_lower = jnp.concatenate([zero_ax, out_ax[:-1, :, 0]], axis=0)
    from_upper = jnp.concatenate([out_ax[1:, :, 1], zero_ax], axis=0)
    arrivals_axial = jnp.stack([from_lower, from_upper], axis=2)

    out_rad = pick(send_radial, send_counts[:, :, 2:4])
    zero_rad = jnp.zeros_like(out_rad[:, :1, 0])
    from_inner = jnp.concatenate([zero_rad, out_rad[:, :-1, 0]], axis=1)
    from_outer = jnp.concatenate([out_rad[:, 1:, 1], zero_rad], axis=1)
    arrivals_radial = jnp.stack([from_inner, from_outer], axis=2)

    padded = jnp.pad(pressure, ((1, 1), (0, 0)))
    image = DIAG * pressure - padded[2:] - padded[:-2]
    pres_slab = slab_blocks(pressure)
    picked = pres_slab[jnp.arange(N_AX, dtype=jnp.int32)[:, None, None], block_cols]
    kinds = (block_kinds[..., None] == jnp.arange(NT, dtype=jnp.int32)).astype(jnp.float32)
    grouped = jnp.einsum('abkt,abkn->abtn', kinds, picked, precision=TOP_PRECISION)
    coupled = jnp.einsum('abtn,tmn->abm', grouped, block_table, precision=TOP_PRECISION)
    pressure_image = image + unslab(coupled)
    return motion_out, arrivals_axial, arrivals_radial, gas_out, liquid_load, pressure_image
```

```python
import functools

import jax
import jax.numpy as jnp
from jax import lax
from jax.experimental import pallas as pl
from jax.experimental.pallas import tpu as pltpu
from jax.sharding import PartitionSpec as P

BLOCK = 128
GROUP = 64
NT = 8
DRAG = 0.5
STEP = 0.5
DIAG = 6.0
VMEM_LIMIT = 24 * 1024 * 1024

F32 = jnp.float32
BF16 = jnp.bfloat16
I32 = jnp.int32

vmem = pl.BlockSpec(memory_space=pltpu.VMEM)
smem = pl.BlockSpec(memory_space=pltpu.SMEM)


class Sizes:
    def __init__(self, layers, radial, parcels):
        self.layers = layers
        self.quarters = radial // BLOCK
        self.blocks = layers * self.quarters
        self.tiles = parcels // BLOCK
        self.groups = parcels // GROUP
        self.gas = 0
        self.pres = 3 * self.blocks
        self.motion = self.pres + self.blocks
        self.size = self.motion + 6 * self.tiles
        self.offset = self.size + self.tiles
        self.meta = self.offset + self.tiles
        self.rows = self.meta + 8


def split2(x):
    high = x.astype(BF16)
    return high, (x - high.astype(F32)).astype(BF16)


def dot(a, b):
    return jnp.dot(a, b, preferred_element_type=F32)


def dot_nt(a, b):
    return lax.dot_general(a, b, (((1,), (1,)), ((), ())), preferred_element_type=F32)


def iota(shape, dim):
    return lax.broadcasted_iota(I32, shape, dim)


def block_row(sz, b):
    local = b % sz.blocks
    return b - local + (local % sz.quarters) * sz.layers + local // sz.quarters


def pack_kernel(sz, motion, size, block, offset, gas, pres, lists, counts, out):
    layers = sz.layers
    for c in range(3):
        for q in range(sz.quarters):
            out[pl.ds(sz.gas + c * sz.blocks + q * layers, layers), :] = gas[c, :, q * BLOCK : (q + 1) * BLOCK]
    for q in range(sz.quarters):
        out[pl.ds(sz.pres + q * layers, layers), :] = pres[:, q * BLOCK : (q + 1) * BLOCK]
    for i in range(sz.tiles):
        out[pl.ds(sz.motion + i, 6, stride=sz.tiles), :] = motion[:, i * BLOCK : (i + 1) * BLOCK]
    out[pl.ds(sz.size, sz.tiles), :] = size[...]
    out[pl.ds(sz.offset, sz.tiles), :] = offset[...].astype(F32)
    out[pl.ds(sz.meta, 8), :] = jnp.full((8, BLOCK), -1.0, F32)
    out[pl.ds(sz.meta, 1), pl.ds(0, sz.groups)] = block_row(sz, block[...]).astype(F32)
    width = lists.shape[1]
    lane = iota((1, width), 1)
    for slot in range(2):
        kept = jnp.where(lane < counts[0, 2 + slot], lists[slot : slot + 1, :], -1)
        out[pl.ds(sz.meta + 1 + slot, 1), pl.ds(0, width)] = kept.astype(F32)


def take_lanes(x, idx):
    return jnp.take_along_axis(x, idx, axis=1, mode="promise_in_bounds")


def pick(sz, state, idx):
    shape = (sz.tiles, BLOCK)
    idx = jnp.broadcast_to(idx, shape)
    lane = idx & (BLOCK - 1)
    here = (idx >> 7) == iota(shape, 0)
    return [jnp.sum(jnp.where(here, take_lanes(s, lane), 0.0), axis=0, keepdims=True) for s in state]


def main_kernel(
    sz, n_rad, G, cols, kinds, table, axial, counts, me,
    motion_out, arr_rad, gas_out, liquid, image, up, down,
    near, state, deps, spread, coup,
):
    r = me[0]
    layers, tiles, blocks, groups = sz.layers, sz.tiles, sz.blocks, sz.groups
    slab_blocks = n_rad * blocks
    T = n_rad * tiles
    lane_row = iota((1, BLOCK), 1)

    block_rows = [G[d, pl.ds(sz.meta, 1), :] for d in range(n_rad)]
    column = jnp.concatenate(
        [jnp.transpose(jnp.broadcast_to(b, (BLOCK, BLOCK)))[:groups] for b in block_rows], axis=0
    ).astype(I32)
    lanes = iota((n_rad * groups, BLOCK), 1)
    chooser = jnp.concatenate(
        [(column == lanes + first).astype(F32).astype(BF16) for first in range(0, slab_blocks, BLOCK)], axis=1
    )
    gas_slab = jnp.concatenate(
        [
            jnp.concatenate([G[d, pl.ds(sz.gas + c * blocks, blocks), :] for d in range(n_rad)], axis=0)
            for c in range(3)
        ],
        axis=1,
    )
    high, low = split2(gas_slab)
    found = dot(chooser, high) + dot(chooser, low)
    for c in range(3):
        near[c] = found[:, c * BLOCK : (c + 1) * BLOCK]

    def rows(first):
        return jnp.concatenate([G[d, pl.ds(first, tiles), :] for d in range(n_rad)], axis=0)

    size = rows(sz.size)
    offset = rows(sz.offset).astype(I32)
    factor = jnp.exp(-DRAG / (size * size))
    mass = size * size * size
    even = iota((T, BLOCK), 1) < GROUP
    dep = []
    for c in range(3):
        u_even = take_lanes(near[c, pl.ds(0, T, stride=2), :], offset)
        u_odd = take_lanes(near[c, pl.ds(1, T, stride=2), :], offset)
        u = jnp.where(even, u_even, u_odd)
        v = rows(sz.motion + (3 + c) * tiles)
        new = u + (v - u) * factor
        state[pl.ds(c * T, T), :] = rows(sz.motion + c * tiles) + STEP * new
        state[pl.ds((3 + c) * T, T), :] = new
        dep.append(-mass * (new - v))
    state[pl.ds(6 * T, T), :] = size
    dep.append(mass)

    mine = pl.multiple_of(r * tiles, tiles)
    for i in range(tiles):
        motion_out[:, i * BLOCK : (i + 1) * BLOCK] = state[pl.ds(mine + i, 6, stride=T), :]

    def state_of(d):
        first = pl.multiple_of(d * tiles, tiles)
        return [state[pl.ds(c * T + first, tiles), :] for c in range(7)]

    wide = jnp.concatenate([axial[0:1, :], axial[1:2, :]], axis=1)
    half = axial.shape[1]
    limit = jnp.where(lane_row < half, counts[0, 0], counts[0, 1])
    place = jnp.where(lane_row < half, lane_row, lane_row - half)
    payload = pick(sz, state_of(r), jnp.where(place < limit, wide, -1))
    pres_first = [G[r, pl.ds(sz.pres + q * layers, 1), :] for q in range(sz.quarters)]
    pres_last = [G[r, pl.ds(sz.pres + q * layers + layers - 1, 1), :] for q in range(sz.quarters)]
    for c in range(7):
        up[c : c + 1, :] = payload[c]
        down[c : c + 1, :] = payload[c]
    for q in range(sz.quarters):
        up[8 + q : 9 + q, :] = pres_last[q]
        down[8 + q : 9 + q, :] = pres_first[q]
    zero_row = jnp.zeros((1, BLOCK), F32)
    for row in (7, *range(8 + sz.quarters, 16)):
        up[row : row + 1, :] = zero_row
        down[row : row + 1, :] = zero_row

    width = arr_rad.shape[2]
    for slot, exists, other in ((0, r > 0, jnp.maximum(r - 1, 0)), (1, r < n_rad - 1, jnp.minimum(r + 1, n_rad - 1))):
        idx = G[other, pl.ds(sz.meta + 1 + slot, 1), :].astype(I32)
        idx = jnp.where(exists, idx, -1)
        got = pick(sz, state_of(other), idx)
        for c in range(7):
            arr_rad[c, slot : slot + 1, :] = got[c][:, :width]

    for c in range(4):
        high = dep[c].astype(BF16).astype(F32)
        low = dep[c] - high
        for piece, part in enumerate((high, low)):
            deps[pl.ds((piece * 8 + c) * T, T), :] = jnp.where(even, part, 0.0)
            deps[pl.ds((piece * 8 + 4 + c) * T, T), :] = jnp.where(even, 0.0, part)
    cell = iota((BLOCK, BLOCK), 0)
    for d in range(n_rad):
        for i in range(tiles):
            t = d * tiles + i
            off = G[d, pl.ds(sz.offset + i, 1), :].astype(I32)
            onehot = (cell == off).astype(F32).astype(BF16)
            lhs = deps[pl.ds(t, 16, stride=T), :].astype(BF16)
            res = dot_nt(lhs, onehot)
            res = res[:8] + res[8:]
            spread[pl.ds(2 * t, 4, stride=2 * T), :] = res[:4]
            spread[pl.ds(2 * t + 1, 4, stride=2 * T), :] = res[4:]
    own = iota((blocks, groups), 0) + r * blocks
    adder = jnp.concatenate(
        [(own == b[:, :groups].astype(I32)).astype(F32) for b in block_rows], axis=1
    ).astype(BF16)
    for c in range(4):
        high, low = split2(spread[pl.ds(c * 2 * T, 2 * T), :])
        total = dot(adder, high) + dot(adder, low)
        for q in range(sz.quarters):
            part = total[q * layers : (q + 1) * layers]
            at = slice(q * BLOCK, (q + 1) * BLOCK)
            if c < 3:
                gas_out[c, :, at] = G[r, pl.ds(sz.gas + c * blocks + q * layers, layers), :] + part
            else:
                liquid[:, at] = part

    pres = jnp.concatenate([G[d, pl.ds(sz.pres, blocks), :] for d in range(n_rad)], axis=0)
    index = kinds[...] * slab_blocks + block_row(sz, cols[...])
    index = jnp.concatenate([index, index], axis=1)
    grouped = [None] * (NT // 2)
    for first in range(0, slab_blocks, BLOCK):
        p_high, p_low = split2(jnp.transpose(pres[first : first + BLOCK]))
        here = iota((BLOCK, BLOCK), 0) + first + jnp.where(iota((BLOCK, BLOCK), 1) < blocks, 0, slab_blocks)
        for j in range(NT // 2):
            aim = here + 2 * j * slab_blocks
            count = (aim == index[0:1]).astype(F32)
            for k in range(1, index.shape[0]):
                count = count + (aim == index[k : k + 1]).astype(F32)
            count = count.astype(BF16)
            part = dot(p_high, count) + dot(p_low, count)
            grouped[j] = part if grouped[j] is None else grouped[j] + part
    sums = [None, None]
    for j in range(NT // 2):
        g_high, g_low = split2(grouped[j])
        for s in range(2):
            t_high, t_low = split2(table[2 * j + s])
            part = dot(t_high, g_high) + dot(t_low, g_high) + dot(t_high, g_low)
            sums[s] = part if sums[s] is None else sums[s] + part
    both = jnp.where(iota((BLOCK, BLOCK), 1) < blocks, sums[0], sums[1])
    both = both + pltpu.roll(jnp.where(iota((BLOCK, BLOCK), 1) < blocks, 0.0, sums[1]), blocks, 1)
    coup[...] = jnp.transpose(both)
    layer = iota((layers, BLOCK), 0)
    for q in range(sz.quarters):
        p = G[r, pl.ds(sz.pres + q * layers, layers), :]
        below = jnp.where(layer == 0, 0.0, pltpu.roll(p, 1, 0))
        above = jnp.where(layer == layers - 1, 0.0, pltpu.roll(p, layers - 1, 0))
        image[:, q * BLOCK : (q + 1) * BLOCK] = (
            DIAG * p - above - below + coup[pl.ds(q, layers, stride=sz.quarters), :]
        )


def finish_kernel(sz, from_lower, from_upper, image, arr_ax, pressure_image):
    half = arr_ax.shape[2]
    arr_ax[:, 0, :] = from_lower[0:7, 0:half]
    arr_ax[:, 1, :] = from_upper[0:7, half : 2 * half]
    pressure_image[...] = image[...]
    last = sz.layers - 1
    for q in range(sz.quarters):
        at = slice(q * BLOCK, (q + 1) * BLOCK)
        pressure_image[0:1, at] = image[0:1, at] - from_lower[8 + q : 9 + q, :]
        pressure_image[last : last + 1, at] = image[last : last + 1, at] - from_upper[8 + q : 9 + q, :]


def on_device(
    parcel_motion,
    parcel_size,
    parcel_block,
    parcel_offset,
    gas_velocity,
    pressure,
    block_cols,
    block_kinds,
    block_table,
    send_axial,
    send_radial,
    send_counts,
):
    n_ax, n_rad = lax.axis_size("ax"), lax.axis_size("rad")
    layers, radial = pressure.shape
    parcels = parcel_size.shape[0]
    sz = Sizes(layers, radial, parcels)
    T = n_rad * sz.tiles
    cap_ax, cap_rad = send_axial.shape[-1], send_radial.shape[-1]
    params = pltpu.CompilerParams(vmem_limit_bytes=VMEM_LIMIT)
    counts = send_counts.reshape(1, 4)
    size2 = parcel_size.reshape(sz.tiles, BLOCK)
    offset2 = parcel_offset.reshape(sz.tiles, BLOCK)

    packed = pl.pallas_call(
        functools.partial(pack_kernel, sz),
        out_shape=jax.ShapeDtypeStruct((sz.rows, BLOCK), F32),
        in_specs=[vmem] * 7 + [smem],
        out_specs=vmem,
        compiler_params=params,
        name="pack",
    )(
        parcel_motion, size2, parcel_block.reshape(1, sz.groups), offset2, gas_velocity, pressure,
        send_radial.reshape(2, cap_rad), counts,
    )
    gathered = lax.all_gather(packed, "rad", axis=0)

    me = lax.axis_index("rad").astype(I32).reshape(1)
    motion_out, arr_rad, gas_out, liquid, image, up, down = pl.pallas_call(
        functools.partial(main_kernel, sz, n_rad),
        out_shape=[
            jax.ShapeDtypeStruct((6, parcels), F32),
            jax.ShapeDtypeStruct((7, 2, cap_rad), F32),
            jax.ShapeDtypeStruct(gas_velocity.shape, F32),
            jax.ShapeDtypeStruct(pressure.shape, F32),
            jax.ShapeDtypeStruct(pressure.shape, F32),
            jax.ShapeDtypeStruct((16, BLOCK), F32),
            jax.ShapeDtypeStruct((16, BLOCK), F32),
        ],
        in_specs=[vmem] * 5 + [smem] * 2,
        out_specs=[vmem] * 7,
        scratch_shapes=[
            pltpu.VMEM((3, n_rad * sz.groups, BLOCK), F32),
            pltpu.VMEM((7 * T, BLOCK), F32),
            pltpu.VMEM((16 * T, BLOCK), F32),
            pltpu.VMEM((4 * 2 * T, BLOCK), F32),
            pltpu.VMEM((BLOCK, BLOCK), F32),
        ],
        compiler_params=params,
        name="slab",
    )(
        gathered,
        block_cols[0].T,
        block_kinds[0].T,
        block_table,
        send_axial.reshape(2, cap_ax),
        counts,
        me,
    )

    from_lower = lax.ppermute(up, "ax", [(i, i + 1) for i in range(n_ax - 1)])
    from_upper = lax.ppermute(down, "ax", [(i + 1, i) for i in range(n_ax - 1)])

    arr_ax, pressure_image = pl.pallas_call(
        functools.partial(finish_kernel, sz),
        out_shape=[
            jax.ShapeDtypeStruct((7, 2, cap_ax), F32),
            jax.ShapeDtypeStruct(pressure.shape, F32),
        ],
        in_specs=[vmem] * 3,
        out_specs=[vmem] * 2,
        compiler_params=params,
        name="finish",
    )(from_lower, from_upper, image)

    arrivals_axial = arr_ax.transpose(1, 0, 2)[None, None]
    arrivals_radial = arr_rad.transpose(1, 0, 2)[None, None]
    return (motion_out, arrivals_axial, arrivals_radial, gas_out, liquid, pressure_image)


def solution(mesh):
    return jax.shard_map(
        on_device,
        mesh=mesh,
        in_specs=(
            P(None, ("ax", "rad")),
            P(("ax", "rad")),
            P(("ax", "rad")),
            P(("ax", "rad")),
            P(None, "ax", "rad"),
            P("ax", "rad"),
            P("ax", "rad", None),
            P("ax", "rad", None),
            P(),
            P("ax", "rad", None, None),
            P("ax", "rad", None, None),
            P("ax", "rad", None),
        ),
        out_specs=(
            P(None, ("ax", "rad")),
            P("ax", "rad", None, None, None),
            P("ax", "rad", None, None, None),
            P(None, "ax", "rad"),
            P("ax", "rad"),
            P("ax", "rad"),
        ),
        check_vma=False,
    )
```

```python
import functools

import jax
import jax.numpy as jnp
from jax import lax
from jax.experimental import pallas as pl
from jax.experimental.pallas import tpu as pltpu
from jax.sharding import PartitionSpec as P

BLOCK = 128
GROUP = 64
NT = 8
DRAG = 0.5
STEP = 0.5
DIAG = 6.0
VMEM_LIMIT = 24 * 1024 * 1024

F32 = jnp.float32
BF16 = jnp.bfloat16
I32 = jnp.int32

vmem = pl.BlockSpec(memory_space=pltpu.VMEM)
hbm = pl.BlockSpec(memory_space=pltpu.HBM)


class Sizes:
    def __init__(self, layers, radial, parcels):
        self.layers = layers
        self.quarters = radial // BLOCK
        self.blocks = layers * self.quarters
        self.tiles = parcels // BLOCK
        self.groups = parcels // GROUP
        self.gas = 0
        self.pres = 3 * self.blocks
        self.motion = self.pres + self.blocks
        self.size = self.motion + 6 * self.tiles
        self.offset = self.size + self.tiles
        self.meta = self.offset + self.tiles
        self.rows = self.meta + 8


def split2(x):
    high = x.astype(BF16)
    return high, (x - high.astype(F32)).astype(BF16)


def dot(a, b):
    return jnp.dot(a, b, preferred_element_type=F32)


def dot_nt(a, b):
    return lax.dot_general(a, b, (((1,), (1,)), ((), ())), preferred_element_type=F32)


def iota(shape, dim):
    return lax.broadcasted_iota(I32, shape, dim)


def block_row(sz, b):
    local = b % sz.blocks
    return b - local + (local % sz.quarters) * sz.layers + local // sz.quarters


def pack_kernel(
    sz, n_rad, motion_hbm, size_hbm, block_hbm, offset_hbm, gas_hbm, pres_hbm, radial_hbm, counts_hbm, cols_hbm,
    kinds_hbm, axial_hbm,
    out, aux,
    motion, size, block, offset, gas, pres, radial, counts, cols, kinds, axial, sem,
):
    pairs = (
        (counts_hbm, counts), (gas_hbm, gas), (motion_hbm, motion), (pres_hbm, pres), (size_hbm, size),
        (offset_hbm, offset), (block_hbm, block), (radial_hbm, radial), (cols_hbm, cols), (kinds_hbm, kinds),
        (axial_hbm, axial),
    )
    copies = [pltpu.make_async_copy(src, dst, sem.at[i]) for i, (src, dst) in enumerate(pairs)]
    for copy in copies:
        copy.start()
    out[pl.ds(sz.meta, 8), :] = jnp.full((8, BLOCK), -1.0, F32)
    for copy in copies:
        copy.wait()
    layers = sz.layers
    for c in range(3):
        for q in range(sz.quarters):
            out[pl.ds(sz.gas + c * sz.blocks + q * layers, layers), :] = gas[c, :, q * BLOCK : (q + 1) * BLOCK]
    for q in range(sz.quarters):
        out[pl.ds(sz.pres + q * layers, layers), :] = pres[:, q * BLOCK : (q + 1) * BLOCK]
    for i in range(sz.tiles):
        out[pl.ds(sz.motion + i, 6, stride=sz.tiles), :] = motion[:, i * BLOCK : (i + 1) * BLOCK]
    out[pl.ds(sz.size, sz.tiles), :] = size[...]
    out[pl.ds(sz.offset, sz.tiles), :] = offset[...].astype(F32)
    out[pl.ds(sz.meta, 1), pl.ds(0, sz.groups)] = block_row(sz, block[...]).astype(F32)
    width = radial.shape[1]
    lane = iota((1, width), 1)
    for slot in range(2):
        kept = jnp.where(lane < counts[0, 2 + slot], radial[slot : slot + 1, :], -1)
        out[pl.ds(sz.meta + 1 + slot, 1), pl.ds(0, width)] = kept.astype(F32)

    index = kinds[...] * (n_rad * sz.blocks) + block_row(sz, cols[...])
    aux[pl.ds(0, index.shape[0]), :] = jnp.concatenate([index, index], axis=1)
    lane = iota((1, axial.shape[1]), 1)
    kept = [jnp.where(lane < counts[0, slot], axial[slot : slot + 1, :], -1) for slot in range(2)]
    aux[pl.ds(8, 1), :] = jnp.concatenate(kept, axis=1)


def take_lanes(x, idx):
    return jnp.take_along_axis(x, idx, axis=1, mode="promise_in_bounds")


def pick(sz, state, idx):
    shape = (sz.tiles, BLOCK)
    idx = jnp.broadcast_to(idx, shape)
    lane = idx & (BLOCK - 1)
    here = (idx >> 7) == iota(shape, 0)
    return [jnp.sum(jnp.where(here, take_lanes(s, lane), 0.0), axis=0, keepdims=True) for s in state]


def main_kernel(
    sz, n_rad, G, aux, table,
    motion_hbm, arr_hbm, gas_hbm, liquid_hbm, image, message,
    near, state, deps, spread, coup, motion_out, arr_rad, gas_out, liquid, sem,
):
    r = lax.axis_index("rad")
    sends = [
        pltpu.make_async_copy(src, dst, sem.at[i])
        for i, (src, dst) in enumerate(
            ((motion_out, motion_hbm), (arr_rad, arr_hbm), (gas_out, gas_hbm), (liquid, liquid_hbm))
        )
    ]
    layers, tiles, blocks, groups = sz.layers, sz.tiles, sz.blocks, sz.groups
    slab_blocks = n_rad * blocks
    T = n_rad * tiles

    block_rows = [G[d, pl.ds(sz.meta, 1), :] for d in range(n_rad)]
    column = jnp.concatenate(
        [jnp.transpose(jnp.broadcast_to(b, (BLOCK, BLOCK)))[:groups] for b in block_rows], axis=0
    ).astype(I32)
    lanes = iota((n_rad * groups, BLOCK), 1)
    chooser = jnp.concatenate(
        [(column == lanes + first).astype(F32).astype(BF16) for first in range(0, slab_blocks, BLOCK)], axis=1
    )
    gas_slab = jnp.concatenate(
        [
            jnp.concatenate([G[d, pl.ds(sz.gas + c * blocks, blocks), :] for d in range(n_rad)], axis=0)
            for c in range(3)
        ],
        axis=1,
    )
    high, low = split2(gas_slab)
    found = dot(chooser, high) + dot(chooser, low)
    for c in range(3):
        near[c] = found[:, c * BLOCK : (c + 1) * BLOCK]

    def rows(first):
        return jnp.concatenate([G[d, pl.ds(first, tiles), :] for d in range(n_rad)], axis=0)

    size = rows(sz.size)
    offset = rows(sz.offset).astype(I32)
    factor = jnp.exp(-DRAG / (size * size))
    mass = size * size * size
    even = iota((T, BLOCK), 1) < GROUP
    dep = []
    for c in range(3):
        u_even = take_lanes(near[c, pl.ds(0, T, stride=2), :], offset)
        u_odd = take_lanes(near[c, pl.ds(1, T, stride=2), :], offset)
        u = jnp.where(even, u_even, u_odd)
        v = rows(sz.motion + (3 + c) * tiles)
        new = u + (v - u) * factor
        state[pl.ds(c * T, T), :] = rows(sz.motion + c * tiles) + STEP * new
        state[pl.ds((3 + c) * T, T), :] = new
        dep.append(-mass * (new - v))
    state[pl.ds(6 * T, T), :] = size
    dep.append(mass)

    mine = pl.multiple_of(r * tiles, tiles)
    for i in range(tiles):
        motion_out[:, i * BLOCK : (i + 1) * BLOCK] = state[pl.ds(mine + i, 6, stride=T), :]
    sends[0].start()

    def state_of(d):
        first = pl.multiple_of(d * tiles, tiles)
        return [state[pl.ds(c * T + first, tiles), :] for c in range(7)]

    payload = pick(sz, state_of(r), aux[pl.ds(8, 1), :])
    for c in range(7):
        message[c : c + 1, :] = payload[c]
    message[7:8, :] = jnp.zeros((1, BLOCK), F32)
    for q in range(sz.quarters):
        first = sz.pres + q * layers
        message[8 + q : 9 + q, :] = G[r, pl.ds(first + layers - 1, 1), :]
        message[12 + q : 13 + q, :] = G[r, pl.ds(first, 1), :]

    width = arr_rad.shape[2]
    for slot, exists, other in ((0, r > 0, jnp.maximum(r - 1, 0)), (1, r < n_rad - 1, jnp.minimum(r + 1, n_rad - 1))):
        idx = G[other, pl.ds(sz.meta + 1 + slot, 1), :].astype(I32)
        idx = jnp.where(exists, idx, -1)
        got = pick(sz, state_of(other), idx)
        for c in range(7):
            arr_rad[c, slot : slot + 1, :] = got[c][:, :width]
    sends[1].start()

    for c in range(4):
        high = dep[c].astype(BF16).astype(F32)
        low = dep[c] - high
        for piece, part in enumerate((high, low)):
            deps[pl.ds((piece * 8 + c) * T, T), :] = jnp.where(even, part, 0.0)
            deps[pl.ds((piece * 8 + 4 + c) * T, T), :] = jnp.where(even, 0.0, part)
    cell = iota((BLOCK, BLOCK), 0)
    for d in range(n_rad):
        for i in range(tiles):
            t = d * tiles + i
            off = G[d, pl.ds(sz.offset + i, 1), :].astype(I32)
            onehot = (cell == off).astype(F32).astype(BF16)
            lhs = deps[pl.ds(t, 16, stride=T), :].astype(BF16)
            res = dot_nt(lhs, onehot)
            res = res[:8] + res[8:]
            spread[pl.ds(2 * t, 4, stride=2 * T), :] = res[:4]
            spread[pl.ds(2 * t + 1, 4, stride=2 * T), :] = res[4:]
    own = iota((blocks, groups), 0) + r * blocks
    adder = jnp.concatenate(
        [(own == b[:, :groups].astype(I32)).astype(F32) for b in block_rows], axis=1
    ).astype(BF16)
    for c in range(4):
        high, low = split2(spread[pl.ds(c * 2 * T, 2 * T), :])
        total = dot(adder, high) + dot(adder, low)
        for q in range(sz.quarters):
            part = total[q * layers : (q + 1) * layers]
            at = slice(q * BLOCK, (q + 1) * BLOCK)
            if c < 3:
                gas_out[c, :, at] = G[r, pl.ds(sz.gas + c * blocks + q * layers, layers), :] + part
            else:
                liquid[:, at] = part
    sends[2].start()
    sends[3].start()

    pres = jnp.concatenate([G[d, pl.ds(sz.pres, blocks), :] for d in range(n_rad)], axis=0)
    index = aux[pl.ds(0, 4), :]
    grouped = [None] * (NT // 2)
    for first in range(0, slab_blocks, BLOCK):
        p_high, p_low = split2(jnp.transpose(pres[first : first + BLOCK]))
        here = iota((BLOCK, BLOCK), 0) + first + jnp.where(iota((BLOCK, BLOCK), 1) < blocks, 0, slab_blocks)
        for j in range(NT // 2):
            aim = here + 2 * j * slab_blocks
            count = (aim == index[0:1]).astype(F32)
            for k in range(1, index.shape[0]):
                count = count + (aim == index[k : k + 1]).astype(F32)
            count = count.astype(BF16)
            part = dot(p_high, count) + dot(p_low, count)
            grouped[j] = part if grouped[j] is None else grouped[j] + part
    sums = [None, None]
    for j in range(NT // 2):
        g_high, g_low = split2(grouped[j])
        for s in range(2):
            t_high, t_low = split2(table[2 * j + s])
            part = dot(t_high, g_high) + dot(t_low, g_high) + dot(t_high, g_low)
            sums[s] = part if sums[s] is None else sums[s] + part
    both = jnp.where(iota((BLOCK, BLOCK), 1) < blocks, sums[0], sums[1])
    both = both + pltpu.roll(jnp.where(iota((BLOCK, BLOCK), 1) < blocks, 0.0, sums[1]), blocks, 1)
    coup[...] = jnp.transpose(both)
    layer = iota((layers, BLOCK), 0)
    for q in range(sz.quarters):
        p = G[r, pl.ds(sz.pres + q * layers, layers), :]
        below = jnp.where(layer == 0, 0.0, pltpu.roll(p, 1, 0))
        above = jnp.where(layer == layers - 1, 0.0, pltpu.roll(p, layers - 1, 0))
        image[:, q * BLOCK : (q + 1) * BLOCK] = (
            DIAG * p - above - below + coup[pl.ds(q, layers, stride=sz.quarters), :]
        )
    for send in sends:
        send.wait()


def finish_kernel(sz, got_a, got_b, image, arr_ax, pressure_image):
    even = lax.axis_index("ax") % 2 == 0
    low = jnp.where(even, got_b[...], got_a[...])
    up = jnp.where(even, got_a[...], got_b[...])
    half = arr_ax.shape[2]
    arr_ax[:, 0, :] = low[0:7, 0:half]
    arr_ax[:, 1, :] = up[0:7, half : 2 * half]
    pressure_image[...] = image[...]
    last = sz.layers - 1
    for q in range(sz.quarters):
        at = slice(q * BLOCK, (q + 1) * BLOCK)
        pressure_image[0:1, at] = image[0:1, at] - low[8 + q : 9 + q, :]
        pressure_image[last : last + 1, at] = image[last : last + 1, at] - up[12 + q : 13 + q, :]


def on_device(
    parcel_motion,
    parcel_size,
    parcel_block,
    parcel_offset,
    gas_velocity,
    pressure,
    block_cols,
    block_kinds,
    block_table,
    send_axial,
    send_radial,
    send_counts,
):
    n_ax, n_rad = lax.axis_size("ax"), lax.axis_size("rad")
    layers, radial = pressure.shape
    parcels = parcel_size.shape[0]
    sz = Sizes(layers, radial, parcels)
    T = n_rad * sz.tiles
    cap_ax, cap_rad = send_axial.shape[-1], send_radial.shape[-1]
    params = pltpu.CompilerParams(vmem_limit_bytes=VMEM_LIMIT)
    counts = send_counts.reshape(1, 4)
    size2 = parcel_size.reshape(sz.tiles, BLOCK)
    offset2 = parcel_offset.reshape(sz.tiles, BLOCK)

    packed, aux = pl.pallas_call(
        functools.partial(pack_kernel, sz, n_rad),
        out_shape=[
            jax.ShapeDtypeStruct((sz.rows, BLOCK), F32),
            jax.ShapeDtypeStruct((16, BLOCK), I32),
        ],
        in_specs=[hbm] * 11,
        out_specs=[vmem] * 2,
        scratch_shapes=[
            pltpu.VMEM(parcel_motion.shape, F32),
            pltpu.VMEM(size2.shape, F32),
            pltpu.VMEM((1, sz.groups), I32),
            pltpu.VMEM(offset2.shape, I32),
            pltpu.VMEM(gas_velocity.shape, F32),
            pltpu.VMEM(pressure.shape, F32),
            pltpu.VMEM((2, cap_rad), I32),
            pltpu.SMEM((1, 4), I32),
            pltpu.VMEM((4, sz.blocks), I32),
            pltpu.VMEM((4, sz.blocks), I32),
            pltpu.VMEM((2, cap_ax), I32),
            pltpu.SemaphoreType.DMA((11,)),
        ],
        compiler_params=params,
        name="pack",
    )(
        *(
            pltpu.with_memory_space_constraint(x, pltpu.HBM)
            for x in (
                parcel_motion, size2, parcel_block.reshape(1, sz.groups), offset2, gas_velocity, pressure,
                send_radial.reshape(2, cap_rad), counts, block_cols[0].T, block_kinds[0].T,
                send_axial.reshape(2, cap_ax),
            )
        )
    )
    gathered = lax.all_gather(packed, "rad", axis=0)

    motion_out, arr_rad, gas_out, liquid, image, message = pl.pallas_call(
        functools.partial(main_kernel, sz, n_rad),
        out_shape=[
            jax.ShapeDtypeStruct((6, parcels), F32),
            jax.ShapeDtypeStruct((7, 2, cap_rad), F32),
            jax.ShapeDtypeStruct(gas_velocity.shape, F32),
            jax.ShapeDtypeStruct(pressure.shape, F32),
            jax.ShapeDtypeStruct(pressure.shape, F32),
            jax.ShapeDtypeStruct((16, BLOCK), F32),
        ],
        in_specs=[vmem] * 3,
        out_specs=[hbm] * 4 + [vmem] * 2,
        scratch_shapes=[
            pltpu.VMEM((3, n_rad * sz.groups, BLOCK), F32),
            pltpu.VMEM((7 * T, BLOCK), F32),
            pltpu.VMEM((16 * T, BLOCK), F32),
            pltpu.VMEM((4 * 2 * T, BLOCK), F32),
            pltpu.VMEM((BLOCK, BLOCK), F32),
            pltpu.VMEM((6, parcels), F32),
            pltpu.VMEM((7, 2, cap_rad), F32),
            pltpu.VMEM(gas_velocity.shape, F32),
            pltpu.VMEM(pressure.shape, F32),
            pltpu.SemaphoreType.DMA((4,)),
        ],
        compiler_params=params,
        name="slab",
    )(gathered, aux, block_table)

    def exchange(first):
        pairs = [(i, i + 1) for i in range(first, n_ax - 1, 2)]
        return lax.ppermute(message, "ax", pairs + [(j, i) for i, j in pairs])

    got_b = exchange(1)
    got_a = exchange(0)

    arr_ax, pressure_image = pl.pallas_call(
        functools.partial(finish_kernel, sz),
        out_shape=[
            jax.ShapeDtypeStruct((7, 2, cap_ax), F32),
            jax.ShapeDtypeStruct(pressure.shape, F32),
        ],
        in_specs=[vmem] * 3,
        out_specs=[vmem] * 2,
        compiler_params=params,
        name="finish",
    )(got_a, got_b, image)

    arrivals_axial = arr_ax.transpose(1, 0, 2)[None, None]
    arrivals_radial = arr_rad.transpose(1, 0, 2)[None, None]
    return (motion_out, arrivals_axial, arrivals_radial, gas_out, liquid, pressure_image)


def solution(mesh):
    return jax.shard_map(
        on_device,
        mesh=mesh,
        in_specs=(
            P(None, ("ax", "rad")),
            P(("ax", "rad")),
            P(("ax", "rad")),
            P(("ax", "rad")),
            P(None, "ax", "rad"),
            P("ax", "rad"),
            P("ax", "rad", None),
            P("ax", "rad", None),
            P(),
            P("ax", "rad", None, None),
            P("ax", "rad", None, None),
            P("ax", "rad", None),
        ),
        out_specs=(
            P(None, ("ax", "rad")),
            P("ax", "rad", None, None, None),
            P("ax", "rad", None, None, None),
            P(None, "ax", "rad"),
            P("ax", "rad"),
            P("ax", "rad"),
        ),
        check_vma=False,
    )
```

```python
import functools

import jax
import jax.numpy as jnp
from jax import lax
from jax.experimental import pallas as pl
from jax.experimental.pallas import tpu as pltpu
from jax.sharding import PartitionSpec as P

BLOCK = 128
GROUP = 64
NT = 8
DRAG = 0.5
STEP = 0.5
DIAG = 6.0
VMEM_LIMIT = 24 * 1024 * 1024

F32 = jnp.float32
BF16 = jnp.bfloat16
I32 = jnp.int32

vmem = pl.BlockSpec(memory_space=pltpu.VMEM)
hbm = pl.BlockSpec(memory_space=pltpu.HBM)


class Sizes:
    def __init__(self, layers, radial, parcels):
        self.layers = layers
        self.quarters = radial // BLOCK
        self.blocks = layers * self.quarters
        self.tiles = parcels // BLOCK
        self.groups = parcels // GROUP
        self.gas = 0
        self.pres = 3 * self.blocks
        self.motion = self.pres + self.blocks
        self.size = self.motion + 6 * self.tiles
        self.offset = self.size + self.tiles
        self.meta = self.offset + self.tiles
        self.rows = self.meta + 8


def split2(x):
    high = x.astype(BF16)
    return high, (x - high.astype(F32)).astype(BF16)


def dot(a, b):
    return jnp.dot(a, b, preferred_element_type=F32)


def dot_nt(a, b):
    return lax.dot_general(a, b, (((1,), (1,)), ((), ())), preferred_element_type=F32)


def iota(shape, dim):
    return lax.broadcasted_iota(I32, shape, dim)


def block_row(sz, b):
    local = b % sz.blocks
    return b - local + (local % sz.quarters) * sz.layers + local // sz.quarters


def pack_kernel(
    sz, n_rad, motion_hbm, size_hbm, block_hbm, offset_hbm, gas_hbm, pres_hbm, radial_hbm, counts_hbm, cols_hbm,
    kinds_hbm, axial_hbm,
    out, aux,
    motion, size, block, offset, gas, pres, radial, counts, cols, kinds, axial, sem,
):
    pairs = (
        (counts_hbm, counts), (gas_hbm, gas), (motion_hbm, motion), (pres_hbm, pres), (size_hbm, size),
        (offset_hbm, offset), (block_hbm, block), (radial_hbm, radial), (cols_hbm, cols), (kinds_hbm, kinds),
        (axial_hbm, axial),
    )
    copies = [pltpu.make_async_copy(src, dst, sem.at[i]) for i, (src, dst) in enumerate(pairs)]
    for copy in copies:
        copy.start()
    out[pl.ds(sz.meta, 8), :] = jnp.full((8, BLOCK), -1.0, F32)
    for copy in copies:
        copy.wait()
    layers = sz.layers
    for c in range(3):
        for q in range(sz.quarters):
            out[pl.ds(sz.gas + c * sz.blocks + q * layers, layers), :] = gas[c, :, q * BLOCK : (q + 1) * BLOCK]
    for q in range(sz.quarters):
        out[pl.ds(sz.pres + q * layers, layers), :] = pres[:, q * BLOCK : (q + 1) * BLOCK]
    for i in range(sz.tiles):
        out[pl.ds(sz.motion + i, 6, stride=sz.tiles), :] = motion[:, i * BLOCK : (i + 1) * BLOCK]
    out[pl.ds(sz.size, sz.tiles), :] = size[...]
    out[pl.ds(sz.offset, sz.tiles), :] = offset[...].astype(F32)
    out[pl.ds(sz.meta, 1), pl.ds(0, sz.groups)] = block_row(sz, block[...]).astype(F32)
    width = radial.shape[1]
    lane = iota((1, width), 1)
    for slot in range(2):
        kept = jnp.where(lane < counts[0, 2 + slot], radial[slot : slot + 1, :], -1)
        out[pl.ds(sz.meta + 1 + slot, 1), pl.ds(0, width)] = kept.astype(F32)

    index = kinds[...] * (n_rad * sz.blocks) + block_row(sz, cols[...])
    aux[pl.ds(0, index.shape[0]), :] = jnp.concatenate([index, index], axis=1)
    lane = iota((1, axial.shape[1]), 1)
    kept = [jnp.where(lane < counts[0, slot], axial[slot : slot + 1, :], -1) for slot in range(2)]
    aux[pl.ds(8, 1), :] = jnp.concatenate(kept, axis=1)


def take_lanes(x, idx):
    return jnp.take_along_axis(x, idx, axis=1, mode="promise_in_bounds")


def pick(sz, state, idx):
    shape = (sz.tiles, BLOCK)
    idx = jnp.broadcast_to(idx, shape)
    lane = idx & (BLOCK - 1)
    here = (idx >> 7) == iota(shape, 0)
    return [jnp.sum(jnp.where(here, take_lanes(s, lane), 0.0), axis=0, keepdims=True) for s in state]


def slab_rows(sz, n_rad, G, first):
    return jnp.concatenate([G[d, pl.ds(first, sz.tiles), :] for d in range(n_rad)], axis=0)


def state_of(sz, T, state, d):
    first = pl.multiple_of(d * sz.tiles, sz.tiles)
    return [state[pl.ds(c * T + first, sz.tiles), :] for c in range(7)]


def move_kernel(sz, n_rad, G, aux, state, message, near):
    r = lax.axis_index("rad")
    layers, tiles, blocks, groups = sz.layers, sz.tiles, sz.blocks, sz.groups
    slab_blocks = n_rad * blocks
    T = n_rad * tiles

    block_rows = [G[d, pl.ds(sz.meta, 1), :] for d in range(n_rad)]
    column = jnp.concatenate(
        [jnp.transpose(jnp.broadcast_to(b, (BLOCK, BLOCK)))[:groups] for b in block_rows], axis=0
    ).astype(I32)
    lanes = iota((n_rad * groups, BLOCK), 1)
    chooser = jnp.concatenate(
        [(column == lanes + first).astype(F32).astype(BF16) for first in range(0, slab_blocks, BLOCK)], axis=1
    )
    gas_slab = jnp.concatenate(
        [
            jnp.concatenate([G[d, pl.ds(sz.gas + c * blocks, blocks), :] for d in range(n_rad)], axis=0)
            for c in range(3)
        ],
        axis=1,
    )
    high, low = split2(gas_slab)
    found = dot(chooser, high) + dot(chooser, low)
    for c in range(3):
        near[c] = found[:, c * BLOCK : (c + 1) * BLOCK]

    rows = functools.partial(slab_rows, sz, n_rad, G)
    size = rows(sz.size)
    offset = rows(sz.offset).astype(I32)
    factor = jnp.exp(-DRAG / (size * size))
    even = iota((T, BLOCK), 1) < GROUP
    for c in range(3):
        u_even = take_lanes(near[c, pl.ds(0, T, stride=2), :], offset)
        u_odd = take_lanes(near[c, pl.ds(1, T, stride=2), :], offset)
        u = jnp.where(even, u_even, u_odd)
        v = rows(sz.motion + (3 + c) * tiles)
        new = u + (v - u) * factor
        state[pl.ds(c * T, T), :] = rows(sz.motion + c * tiles) + STEP * new
        state[pl.ds((3 + c) * T, T), :] = new
    state[pl.ds(6 * T, T), :] = size

    payload = pick(sz, state_of(sz, T, state, r), aux[pl.ds(8, 1), :])
    for c in range(7):
        message[c : c + 1, :] = payload[c]
    message[7:8, :] = jnp.zeros((1, BLOCK), F32)
    for q in range(sz.quarters):
        first = sz.pres + q * layers
        message[8 + q : 9 + q, :] = G[r, pl.ds(first + layers - 1, 1), :]
        message[12 + q : 13 + q, :] = G[r, pl.ds(first, 1), :]


def rest_kernel(
    sz, n_rad, G, aux, table, state,
    motion_hbm, arr_hbm, gas_hbm, liquid_hbm, image,
    deps, spread, coup, motion_out, arr_rad, gas_out, liquid, sem,
):
    r = lax.axis_index("rad")
    sends = [
        pltpu.make_async_copy(src, dst, sem.at[i])
        for i, (src, dst) in enumerate(
            ((motion_out, motion_hbm), (arr_rad, arr_hbm), (gas_out, gas_hbm), (liquid, liquid_hbm))
        )
    ]
    layers, tiles, blocks, groups = sz.layers, sz.tiles, sz.blocks, sz.groups
    slab_blocks = n_rad * blocks
    T = n_rad * tiles
    block_rows = [G[d, pl.ds(sz.meta, 1), :] for d in range(n_rad)]

    mine = pl.multiple_of(r * tiles, tiles)
    for i in range(tiles):
        motion_out[:, i * BLOCK : (i + 1) * BLOCK] = state[pl.ds(mine + i, 6, stride=T), :]
    sends[0].start()

    width = arr_rad.shape[2]
    for slot, exists, other in ((0, r > 0, jnp.maximum(r - 1, 0)), (1, r < n_rad - 1, jnp.minimum(r + 1, n_rad - 1))):
        idx = G[other, pl.ds(sz.meta + 1 + slot, 1), :].astype(I32)
        idx = jnp.where(exists, idx, -1)
        got = pick(sz, state_of(sz, T, state, other), idx)
        for c in range(7):
            arr_rad[c, slot : slot + 1, :] = got[c][:, :width]
    sends[1].start()

    rows = functools.partial(slab_rows, sz, n_rad, G)
    size = rows(sz.size)
    mass = size * size * size
    dep = [-mass * (state[pl.ds((3 + c) * T, T), :] - rows(sz.motion + (3 + c) * tiles)) for c in range(3)] + [mass]
    even = iota((T, BLOCK), 1) < GROUP

    for c in range(4):
        high = dep[c].astype(BF16).astype(F32)
        low = dep[c] - high
        for piece, part in enumerate((high, low)):
            deps[pl.ds((piece * 8 + c) * T, T), :] = jnp.where(even, part, 0.0)
            deps[pl.ds((piece * 8 + 4 + c) * T, T), :] = jnp.where(even, 0.0, part)
    cell = iota((BLOCK, BLOCK), 0)
    for d in range(n_rad):
        for i in range(tiles):
            t = d * tiles + i
            off = G[d, pl.ds(sz.offset + i, 1), :].astype(I32)
            onehot = (cell == off).astype(F32).astype(BF16)
            lhs = deps[pl.ds(t, 16, stride=T), :].astype(BF16)
            res = dot_nt(lhs, onehot)
            res = res[:8] + res[8:]
            spread[pl.ds(2 * t, 4, stride=2 * T), :] = res[:4]
            spread[pl.ds(2 * t + 1, 4, stride=2 * T), :] = res[4:]
    own = iota((blocks, groups), 0) + r * blocks
    adder = jnp.concatenate(
        [(own == b[:, :groups].astype(I32)).astype(F32) for b in block_rows], axis=1
    ).astype(BF16)
    for c in range(4):
        high, low = split2(spread[pl.ds(c * 2 * T, 2 * T), :])
        total = dot(adder, high) + dot(adder, low)
        for q in range(sz.quarters):
            part = total[q * layers : (q + 1) * layers]
            at = slice(q * BLOCK, (q + 1) * BLOCK)
            if c < 3:
                gas_out[c, :, at] = G[r, pl.ds(sz.gas + c * blocks + q * layers, layers), :] + part
            else:
                liquid[:, at] = part
    sends[2].start()
    sends[3].start()

    pres = jnp.concatenate([G[d, pl.ds(sz.pres, blocks), :] for d in range(n_rad)], axis=0)
    index = aux[pl.ds(0, 4), :]
    grouped = [None] * (NT // 2)
    for first in range(0, slab_blocks, BLOCK):
        p_high, p_low = split2(jnp.transpose(pres[first : first + BLOCK]))
        here = iota((BLOCK, BLOCK), 0) + first + jnp.where(iota((BLOCK, BLOCK), 1) < blocks, 0, slab_blocks)
        for j in range(NT // 2):
            aim = here + 2 * j * slab_blocks
            count = (aim == index[0:1]).astype(F32)
            for k in range(1, index.shape[0]):
                count = count + (aim == index[k : k + 1]).astype(F32)
            count = count.astype(BF16)
            part = dot(p_high, count) + dot(p_low, count)
            grouped[j] = part if grouped[j] is None else grouped[j] + part
    sums = [None, None]
    for j in range(NT // 2):
        g_high, g_low = split2(grouped[j])
        for s in range(2):
            t_high, t_low = split2(table[2 * j + s])
            part = dot(t_high, g_high) + dot(t_low, g_high) + dot(t_high, g_low)
            sums[s] = part if sums[s] is None else sums[s] + part
    both = jnp.where(iota((BLOCK, BLOCK), 1) < blocks, sums[0], sums[1])
    both = both + pltpu.roll(jnp.where(iota((BLOCK, BLOCK), 1) < blocks, 0.0, sums[1]), blocks, 1)
    coup[...] = jnp.transpose(both)
    layer = iota((layers, BLOCK), 0)
    for q in range(sz.quarters):
        p = G[r, pl.ds(sz.pres + q * layers, layers), :]
        below = jnp.where(layer == 0, 0.0, pltpu.roll(p, 1, 0))
        above = jnp.where(layer == layers - 1, 0.0, pltpu.roll(p, layers - 1, 0))
        image[:, q * BLOCK : (q + 1) * BLOCK] = (
            DIAG * p - above - below + coup[pl.ds(q, layers, stride=sz.quarters), :]
        )
    for send in sends:
        send.wait()


def finish_kernel(sz, got_a, got_b, image, arr_ax, pressure_image):
    even = lax.axis_index("ax") % 2 == 0
    low = jnp.where(even, got_b[...], got_a[...])
    up = jnp.where(even, got_a[...], got_b[...])
    half = arr_ax.shape[2]
    arr_ax[:, 0, :] = low[0:7, 0:half]
    arr_ax[:, 1, :] = up[0:7, half : 2 * half]
    pressure_image[...] = image[...]
    last = sz.layers - 1
    for q in range(sz.quarters):
        at = slice(q * BLOCK, (q + 1) * BLOCK)
        pressure_image[0:1, at] = image[0:1, at] - low[8 + q : 9 + q, :]
        pressure_image[last : last + 1, at] = image[last : last + 1, at] - up[12 + q : 13 + q, :]


def on_device(
    parcel_motion,
    parcel_size,
    parcel_block,
    parcel_offset,
    gas_velocity,
    pressure,
    block_cols,
    block_kinds,
    block_table,
    send_axial,
    send_radial,
    send_counts,
):
    n_ax, n_rad = lax.axis_size("ax"), lax.axis_size("rad")
    layers, radial = pressure.shape
    parcels = parcel_size.shape[0]
    sz = Sizes(layers, radial, parcels)
    T = n_rad * sz.tiles
    cap_ax, cap_rad = send_axial.shape[-1], send_radial.shape[-1]
    params = pltpu.CompilerParams(vmem_limit_bytes=VMEM_LIMIT)
    counts = send_counts.reshape(1, 4)
    size2 = parcel_size.reshape(sz.tiles, BLOCK)
    offset2 = parcel_offset.reshape(sz.tiles, BLOCK)

    packed, aux = pl.pallas_call(
        functools.partial(pack_kernel, sz, n_rad),
        out_shape=[
            jax.ShapeDtypeStruct((sz.rows, BLOCK), F32),
            jax.ShapeDtypeStruct((16, BLOCK), I32),
        ],
        in_specs=[hbm] * 11,
        out_specs=[vmem] * 2,
        scratch_shapes=[
            pltpu.VMEM(parcel_motion.shape, F32),
            pltpu.VMEM(size2.shape, F32),
            pltpu.VMEM((1, sz.groups), I32),
            pltpu.VMEM(offset2.shape, I32),
            pltpu.VMEM(gas_velocity.shape, F32),
            pltpu.VMEM(pressure.shape, F32),
            pltpu.VMEM((2, cap_rad), I32),
            pltpu.SMEM((1, 4), I32),
            pltpu.VMEM((4, sz.blocks), I32),
            pltpu.VMEM((4, sz.blocks), I32),
            pltpu.VMEM((2, cap_ax), I32),
            pltpu.SemaphoreType.DMA((11,)),
        ],
        compiler_params=params,
        name="pack",
    )(
        *(
            pltpu.with_memory_space_constraint(x, pltpu.HBM)
            for x in (
                parcel_motion, size2, parcel_block.reshape(1, sz.groups), offset2, gas_velocity, pressure,
                send_radial.reshape(2, cap_rad), counts, block_cols[0].T, block_kinds[0].T,
                send_axial.reshape(2, cap_ax),
            )
        )
    )
    gathered = lax.all_gather(packed, "rad", axis=0)

    state, message = pl.pallas_call(
        functools.partial(move_kernel, sz, n_rad),
        out_shape=[
            jax.ShapeDtypeStruct((7 * T, BLOCK), F32),
            jax.ShapeDtypeStruct((16, BLOCK), F32),
        ],
        in_specs=[vmem] * 2,
        out_specs=[vmem] * 2,
        scratch_shapes=[pltpu.VMEM((3, n_rad * sz.groups, BLOCK), F32)],
        compiler_params=params,
        name="move",
    )(gathered, aux)

    def exchange(first):
        pairs = [(i, i + 1) for i in range(first, n_ax - 1, 2)]
        return lax.ppermute(message, "ax", pairs + [(j, i) for i, j in pairs])

    got_b = exchange(1)
    got_a = exchange(0)

    motion_out, arr_rad, gas_out, liquid, image = pl.pallas_call(
        functools.partial(rest_kernel, sz, n_rad),
        out_shape=[
            jax.ShapeDtypeStruct((6, parcels), F32),
            jax.ShapeDtypeStruct((7, 2, cap_rad), F32),
            jax.ShapeDtypeStruct(gas_velocity.shape, F32),
            jax.ShapeDtypeStruct(pressure.shape, F32),
            jax.ShapeDtypeStruct(pressure.shape, F32),
        ],
        in_specs=[vmem] * 4,
        out_specs=[hbm] * 4 + [vmem],
        scratch_shapes=[
            pltpu.VMEM((16 * T, BLOCK), F32),
            pltpu.VMEM((4 * 2 * T, BLOCK), F32),
            pltpu.VMEM((BLOCK, BLOCK), F32),
            pltpu.VMEM((6, parcels), F32),
            pltpu.VMEM((7, 2, cap_rad), F32),
            pltpu.VMEM(gas_velocity.shape, F32),
            pltpu.VMEM(pressure.shape, F32),
            pltpu.SemaphoreType.DMA((4,)),
        ],
        compiler_params=params,
        cost_estimate=pl.CostEstimate(flops=2_000_000_000, bytes_accessed=2_000_000, transcendentals=0),
        name="rest",
    )(gathered, aux, block_table, state)

    arr_ax, pressure_image = pl.pallas_call(
        functools.partial(finish_kernel, sz),
        out_shape=[
            jax.ShapeDtypeStruct((7, 2, cap_ax), F32),
            jax.ShapeDtypeStruct(pressure.shape, F32),
        ],
        in_specs=[vmem] * 3,
        out_specs=[vmem] * 2,
        compiler_params=params,
        name="finish",
    )(got_a, got_b, image)

    arrivals_axial = arr_ax.transpose(1, 0, 2)[None, None]
    arrivals_radial = arr_rad.transpose(1, 0, 2)[None, None]
    return (motion_out, arrivals_axial, arrivals_radial, gas_out, liquid, pressure_image)


def solution(mesh):
    return jax.shard_map(
        on_device,
        mesh=mesh,
        in_specs=(
            P(None, ("ax", "rad")),
            P(("ax", "rad")),
            P(("ax", "rad")),
            P(("ax", "rad")),
            P(None, "ax", "rad"),
            P("ax", "rad"),
            P("ax", "rad", None),
            P("ax", "rad", None),
            P(),
            P("ax", "rad", None, None),
            P("ax", "rad", None, None),
            P("ax", "rad", None),
        ),
        out_specs=(
            P(None, ("ax", "rad")),
            P("ax", "rad", None, None, None),
            P("ax", "rad", None, None, None),
            P(None, "ax", "rad"),
            P("ax", "rad"),
            P("ax", "rad"),
        ),
        check_vma=False,
    )
```

```python
import functools

import jax
import jax.numpy as jnp
from jax import lax
from jax.experimental import pallas as pl
from jax.experimental.pallas import tpu as pltpu
from jax.sharding import PartitionSpec as P

BLOCK = 128
GROUP = 64
NT = 8
DRAG = 0.5
STEP = 0.5
DIAG = 6.0
VMEM_LIMIT = 24 * 1024 * 1024

F32 = jnp.float32
BF16 = jnp.bfloat16
I32 = jnp.int32

vmem = pl.BlockSpec(memory_space=pltpu.VMEM)
hbm = pl.BlockSpec(memory_space=pltpu.HBM)


class Sizes:
    def __init__(self, layers, radial, parcels):
        self.layers = layers
        self.quarters = radial // BLOCK
        self.blocks = layers * self.quarters
        self.tiles = parcels // BLOCK
        self.groups = parcels // GROUP
        self.gas = 0
        self.pres = 3 * self.blocks
        self.motion = self.pres + self.blocks
        self.size = self.motion + 6 * self.tiles
        self.offset = self.size + self.tiles
        self.meta = self.offset + self.tiles
        self.rows = self.meta + 8


def split2(x):
    high = x.astype(BF16)
    return high, (x - high.astype(F32)).astype(BF16)


def dot(a, b):
    return jnp.dot(a, b, preferred_element_type=F32)


def dot_nt(a, b):
    return lax.dot_general(a, b, (((1,), (1,)), ((), ())), preferred_element_type=F32)


def iota(shape, dim):
    return lax.broadcasted_iota(I32, shape, dim)


def block_row(sz, b):
    local = b % sz.blocks
    return b - local + (local % sz.quarters) * sz.layers + local // sz.quarters


def pack_kernel(
    sz, n_rad, motion_hbm, size_hbm, block_hbm, offset_hbm, gas_hbm, pres_hbm, radial_hbm, counts_hbm, cols_hbm,
    kinds_hbm, axial_hbm,
    out, aux,
    motion, size, block, offset, gas, pres, radial, counts, cols, kinds, axial, sem,
):
    pairs = (
        (motion_hbm, motion), (gas_hbm, gas), (pres_hbm, pres), (size_hbm, size), (offset_hbm, offset),
        (block_hbm, block), (counts_hbm, counts), (radial_hbm, radial), (axial_hbm, axial), (cols_hbm, cols),
        (kinds_hbm, kinds),
    )
    copies = [pltpu.make_async_copy(src, dst, sem.at[i]) for i, (src, dst) in enumerate(pairs)]
    for copy in copies:
        copy.start()
    out[pl.ds(sz.meta, 8), :] = jnp.full((8, BLOCK), -1.0, F32)
    layers = sz.layers
    copies[0].wait()
    for i in range(sz.tiles):
        out[pl.ds(sz.motion + i, 6, stride=sz.tiles), :] = motion[:, i * BLOCK : (i + 1) * BLOCK]
    copies[1].wait()
    for c in range(3):
        for q in range(sz.quarters):
            out[pl.ds(sz.gas + c * sz.blocks + q * layers, layers), :] = gas[c, :, q * BLOCK : (q + 1) * BLOCK]
    copies[2].wait()
    for q in range(sz.quarters):
        out[pl.ds(sz.pres + q * layers, layers), :] = pres[:, q * BLOCK : (q + 1) * BLOCK]
    for copy in copies[3:]:
        copy.wait()
    out[pl.ds(sz.size, sz.tiles), :] = size[...]
    out[pl.ds(sz.offset, sz.tiles), :] = offset[...].astype(F32)
    out[pl.ds(sz.meta, 1), pl.ds(0, sz.groups)] = block_row(sz, block[...]).astype(F32)
    width = radial.shape[1]
    lane = iota((1, width), 1)
    for slot in range(2):
        kept = jnp.where(lane < counts[0, 2 + slot], radial[slot : slot + 1, :], -1)
        out[pl.ds(sz.meta + 1 + slot, 1), pl.ds(0, width)] = kept.astype(F32)

    index = kinds[...] * (n_rad * sz.blocks) + block_row(sz, cols[...])
    aux[pl.ds(0, index.shape[0]), :] = jnp.concatenate([index, index], axis=1)
    lane = iota((1, axial.shape[1]), 1)
    kept = [jnp.where(lane < counts[0, slot], axial[slot : slot + 1, :], -1) for slot in range(2)]
    aux[pl.ds(8, 1), :] = jnp.concatenate(kept, axis=1)


def take_lanes(x, idx):
    return jnp.take_along_axis(x, idx, axis=1, mode="promise_in_bounds")


def pick(sz, state, idx):
    shape = (sz.tiles, BLOCK)
    idx = jnp.broadcast_to(idx, shape)
    lane = idx & (BLOCK - 1)
    here = (idx >> 7) == iota(shape, 0)
    return [jnp.sum(jnp.where(here, take_lanes(s, lane), 0.0), axis=0, keepdims=True) for s in state]


def slab_rows(sz, n_rad, G, first):
    return jnp.concatenate([G[d, pl.ds(first, sz.tiles), :] for d in range(n_rad)], axis=0)


def state_of(sz, T, state, d):
    first = pl.multiple_of(d * sz.tiles, sz.tiles)
    return [state[pl.ds(c * T + first, sz.tiles), :] for c in range(7)]


def move_kernel(sz, n_rad, G, aux, state, message, near):
    r = lax.axis_index("rad")
    layers, tiles, blocks, groups = sz.layers, sz.tiles, sz.blocks, sz.groups
    slab_blocks = n_rad * blocks
    T = n_rad * tiles

    block_rows = [G[d, pl.ds(sz.meta, 1), :] for d in range(n_rad)]
    column = jnp.concatenate(
        [jnp.transpose(jnp.broadcast_to(b, (BLOCK, BLOCK)))[:groups] for b in block_rows], axis=0
    ).astype(I32)
    lanes = iota((n_rad * groups, BLOCK), 1)
    chooser = jnp.concatenate(
        [(column == lanes + first).astype(F32).astype(BF16) for first in range(0, slab_blocks, BLOCK)], axis=1
    )
    gas_slab = jnp.concatenate(
        [
            jnp.concatenate([G[d, pl.ds(sz.gas + c * blocks, blocks), :] for d in range(n_rad)], axis=0)
            for c in range(3)
        ],
        axis=1,
    )
    high, low = split2(gas_slab)
    found = dot(chooser, high) + dot(chooser, low)
    for c in range(3):
        near[c] = found[:, c * BLOCK : (c + 1) * BLOCK]

    rows = functools.partial(slab_rows, sz, n_rad, G)
    size = rows(sz.size)
    offset = rows(sz.offset).astype(I32)
    factor = jnp.exp(-DRAG / (size * size))
    even = iota((T, BLOCK), 1) < GROUP
    for c in range(3):
        u_even = take_lanes(near[c, pl.ds(0, T, stride=2), :], offset)
        u_odd = take_lanes(near[c, pl.ds(1, T, stride=2), :], offset)
        u = jnp.where(even, u_even, u_odd)
        v = rows(sz.motion + (3 + c) * tiles)
        new = u + (v - u) * factor
        state[pl.ds(c * T, T), :] = rows(sz.motion + c * tiles) + STEP * new
        state[pl.ds((3 + c) * T, T), :] = new
    state[pl.ds(6 * T, T), :] = size

    payload = pick(sz, state_of(sz, T, state, r), aux[pl.ds(8, 1), :])
    for c in range(7):
        message[c : c + 1, :] = payload[c]
    message[7:8, :] = jnp.zeros((1, BLOCK), F32)
    for q in range(sz.quarters):
        first = sz.pres + q * layers
        message[8 + q : 9 + q, :] = G[r, pl.ds(first + layers - 1, 1), :]
        message[12 + q : 13 + q, :] = G[r, pl.ds(first, 1), :]


def rest_kernel(
    sz, n_rad, G, aux, table_hbm, state,
    motion_hbm, arr_hbm, gas_hbm, liquid_hbm, image,
    table, deps, spread, coup, motion_out, arr_rad, gas_out, liquid, sem,
):
    r = lax.axis_index("rad")
    load = pltpu.make_async_copy(table_hbm, table, sem.at[4])
    load.start()
    sends = [
        pltpu.make_async_copy(src, dst, sem.at[i])
        for i, (src, dst) in enumerate(
            ((motion_out, motion_hbm), (arr_rad, arr_hbm), (gas_out, gas_hbm), (liquid, liquid_hbm))
        )
    ]
    layers, tiles, blocks, groups = sz.layers, sz.tiles, sz.blocks, sz.groups
    slab_blocks = n_rad * blocks
    T = n_rad * tiles
    block_rows = [G[d, pl.ds(sz.meta, 1), :] for d in range(n_rad)]

    mine = pl.multiple_of(r * tiles, tiles)
    for i in range(tiles):
        motion_out[:, i * BLOCK : (i + 1) * BLOCK] = state[pl.ds(mine + i, 6, stride=T), :]
    sends[0].start()

    width = arr_rad.shape[2]
    for slot, exists, other in ((0, r > 0, jnp.maximum(r - 1, 0)), (1, r < n_rad - 1, jnp.minimum(r + 1, n_rad - 1))):
        idx = G[other, pl.ds(sz.meta + 1 + slot, 1), :].astype(I32)
        idx = jnp.where(exists, idx, -1)
        got = pick(sz, state_of(sz, T, state, other), idx)
        for c in range(7):
            arr_rad[c, slot : slot + 1, :] = got[c][:, :width]
    sends[1].start()

    rows = functools.partial(slab_rows, sz, n_rad, G)
    size = rows(sz.size)
    mass = size * size * size
    dep = [-mass * (state[pl.ds((3 + c) * T, T), :] - rows(sz.motion + (3 + c) * tiles)) for c in range(3)] + [mass]
    even = iota((T, BLOCK), 1) < GROUP

    for c in range(4):
        high = dep[c].astype(BF16).astype(F32)
        low = dep[c] - high
        for piece, part in enumerate((high, low)):
            deps[pl.ds((piece * 8 + c) * T, T), :] = jnp.where(even, part, 0.0)
            deps[pl.ds((piece * 8 + 4 + c) * T, T), :] = jnp.where(even, 0.0, part)
    cell = iota((BLOCK, BLOCK), 0)
    for d in range(n_rad):
        for i in range(tiles):
            t = d * tiles + i
            off = G[d, pl.ds(sz.offset + i, 1), :].astype(I32)
            onehot = (cell == off).astype(F32).astype(BF16)
            lhs = deps[pl.ds(t, 16, stride=T), :].astype(BF16)
            res = dot_nt(lhs, onehot)
            res = res[:8] + res[8:]
            spread[pl.ds(2 * t, 4, stride=2 * T), :] = res[:4]
            spread[pl.ds(2 * t + 1, 4, stride=2 * T), :] = res[4:]
    own = iota((blocks, groups), 0) + r * blocks
    adder = jnp.concatenate(
        [(own == b[:, :groups].astype(I32)).astype(F32) for b in block_rows], axis=1
    ).astype(BF16)
    for c in range(4):
        high, low = split2(spread[pl.ds(c * 2 * T, 2 * T), :])
        total = dot(adder, high) + dot(adder, low)
        for q in range(sz.quarters):
            part = total[q * layers : (q + 1) * layers]
            at = slice(q * BLOCK, (q + 1) * BLOCK)
            if c < 3:
                gas_out[c, :, at] = G[r, pl.ds(sz.gas + c * blocks + q * layers, layers), :] + part
            else:
                liquid[:, at] = part
    sends[2].start()
    sends[3].start()

    pres = jnp.concatenate([G[d, pl.ds(sz.pres, blocks), :] for d in range(n_rad)], axis=0)
    index = aux[pl.ds(0, 4), :]
    grouped = [None] * (NT // 2)
    for first in range(0, slab_blocks, BLOCK):
        p_high, p_low = split2(jnp.transpose(pres[first : first + BLOCK]))
        here = iota((BLOCK, BLOCK), 0) + first + jnp.where(iota((BLOCK, BLOCK), 1) < blocks, 0, slab_blocks)
        for j in range(NT // 2):
            aim = here + 2 * j * slab_blocks
            count = (aim == index[0:1]).astype(F32)
            for k in range(1, index.shape[0]):
                count = count + (aim == index[k : k + 1]).astype(F32)
            count = count.astype(BF16)
            part = dot(p_high, count) + dot(p_low, count)
            grouped[j] = part if grouped[j] is None else grouped[j] + part
    load.wait()
    sums = [None, None]
    for j in range(NT // 2):
        g_high, g_low = split2(grouped[j])
        for s in range(2):
            t_high, t_low = split2(table[2 * j + s])
            part = dot(t_high, g_high) + dot(t_low, g_high) + dot(t_high, g_low)
            sums[s] = part if sums[s] is None else sums[s] + part
    both = jnp.where(iota((BLOCK, BLOCK), 1) < blocks, sums[0], sums[1])
    both = both + pltpu.roll(jnp.where(iota((BLOCK, BLOCK), 1) < blocks, 0.0, sums[1]), blocks, 1)
    coup[...] = jnp.transpose(both)
    layer = iota((layers, BLOCK), 0)
    for q in range(sz.quarters):
        p = G[r, pl.ds(sz.pres + q * layers, layers), :]
        below = jnp.where(layer == 0, 0.0, pltpu.roll(p, 1, 0))
        above = jnp.where(layer == layers - 1, 0.0, pltpu.roll(p, layers - 1, 0))
        image[:, q * BLOCK : (q + 1) * BLOCK] = (
            DIAG * p - above - below + coup[pl.ds(q, layers, stride=sz.quarters), :]
        )
    for send in sends:
        send.wait()


def finish_kernel(sz, got_b, got_a, image, arr_ax, pressure_image):
    even = lax.axis_index("ax") % 2 == 0
    low = jnp.where(even, got_b[...], got_a[...])
    up = jnp.where(even, got_a[...], got_b[...])
    half = arr_ax.shape[2]
    arr_ax[:, 0, :] = low[0:7, 0:half]
    arr_ax[:, 1, :] = up[0:7, half : 2 * half]
    pressure_image[...] = image[...]
    last = sz.layers - 1
    for q in range(sz.quarters):
        at = slice(q * BLOCK, (q + 1) * BLOCK)
        pressure_image[0:1, at] = image[0:1, at] - low[8 + q : 9 + q, :]
        pressure_image[last : last + 1, at] = image[last : last + 1, at] - up[12 + q : 13 + q, :]


def on_device(
    parcel_motion,
    parcel_size,
    parcel_block,
    parcel_offset,
    gas_velocity,
    pressure,
    block_cols,
    block_kinds,
    block_table,
    send_axial,
    send_radial,
    send_counts,
):
    n_ax, n_rad = lax.axis_size("ax"), lax.axis_size("rad")
    layers, radial = pressure.shape
    parcels = parcel_size.shape[0]
    sz = Sizes(layers, radial, parcels)
    T = n_rad * sz.tiles
    cap_ax, cap_rad = send_axial.shape[-1], send_radial.shape[-1]
    params = pltpu.CompilerParams(vmem_limit_bytes=VMEM_LIMIT)
    counts = send_counts.reshape(1, 4)
    size2 = parcel_size.reshape(sz.tiles, BLOCK)
    offset2 = parcel_offset.reshape(sz.tiles, BLOCK)

    packed, aux = pl.pallas_call(
        functools.partial(pack_kernel, sz, n_rad),
        out_shape=[
            jax.ShapeDtypeStruct((sz.rows, BLOCK), F32),
            jax.ShapeDtypeStruct((16, BLOCK), I32),
        ],
        in_specs=[hbm] * 11,
        out_specs=[vmem] * 2,
        scratch_shapes=[
            pltpu.VMEM(parcel_motion.shape, F32),
            pltpu.VMEM(size2.shape, F32),
            pltpu.VMEM((1, sz.groups), I32),
            pltpu.VMEM(offset2.shape, I32),
            pltpu.VMEM(gas_velocity.shape, F32),
            pltpu.VMEM(pressure.shape, F32),
            pltpu.VMEM((2, cap_rad), I32),
            pltpu.SMEM((1, 4), I32),
            pltpu.VMEM((4, sz.blocks), I32),
            pltpu.VMEM((4, sz.blocks), I32),
            pltpu.VMEM((2, cap_ax), I32),
            pltpu.SemaphoreType.DMA((11,)),
        ],
        compiler_params=params,
        name="pack",
    )(
        *(
            pltpu.with_memory_space_constraint(x, pltpu.HBM)
            for x in (
                parcel_motion, size2, parcel_block.reshape(1, sz.groups), offset2, gas_velocity, pressure,
                send_radial.reshape(2, cap_rad), counts, block_cols[0].T, block_kinds[0].T,
                send_axial.reshape(2, cap_ax),
            )
        )
    )
    gathered = lax.all_gather(packed, "rad", axis=0)

    state, message = pl.pallas_call(
        functools.partial(move_kernel, sz, n_rad),
        out_shape=[
            jax.ShapeDtypeStruct((7 * T, BLOCK), F32),
            jax.ShapeDtypeStruct((16, BLOCK), F32),
        ],
        in_specs=[vmem] * 2,
        out_specs=[vmem] * 2,
        scratch_shapes=[pltpu.VMEM((3, n_rad * sz.groups, BLOCK), F32)],
        compiler_params=params,
        name="move",
    )(gathered, aux)

    def exchange(first):
        pairs = [(i, i + 1) for i in range(first, n_ax - 1, 2)]
        return lax.ppermute(message, "ax", pairs + [(j, i) for i, j in pairs])

    got_a = exchange(0)
    got_b = exchange(1)

    motion_out, arr_rad, gas_out, liquid, image = pl.pallas_call(
        functools.partial(rest_kernel, sz, n_rad),
        out_shape=[
            jax.ShapeDtypeStruct((6, parcels), F32),
            jax.ShapeDtypeStruct((7, 2, cap_rad), F32),
            jax.ShapeDtypeStruct(gas_velocity.shape, F32),
            jax.ShapeDtypeStruct(pressure.shape, F32),
            jax.ShapeDtypeStruct(pressure.shape, F32),
        ],
        in_specs=[vmem, vmem, hbm, vmem],
        out_specs=[hbm] * 4 + [vmem],
        scratch_shapes=[
            pltpu.VMEM(block_table.shape, F32),
            pltpu.VMEM((16 * T, BLOCK), F32),
            pltpu.VMEM((4 * 2 * T, BLOCK), F32),
            pltpu.VMEM((BLOCK, BLOCK), F32),
            pltpu.VMEM((6, parcels), F32),
            pltpu.VMEM((7, 2, cap_rad), F32),
            pltpu.VMEM(gas_velocity.shape, F32),
            pltpu.VMEM(pressure.shape, F32),
            pltpu.SemaphoreType.DMA((5,)),
        ],
        compiler_params=params,
        cost_estimate=pl.CostEstimate(flops=2_000_000_000, bytes_accessed=2_000_000, transcendentals=0),
        name="rest",
    )(gathered, aux, pltpu.with_memory_space_constraint(block_table, pltpu.HBM), state)

    arr_ax, pressure_image = pl.pallas_call(
        functools.partial(finish_kernel, sz),
        out_shape=[
            jax.ShapeDtypeStruct((7, 2, cap_ax), F32),
            jax.ShapeDtypeStruct(pressure.shape, F32),
        ],
        in_specs=[vmem] * 3,
        out_specs=[vmem] * 2,
        compiler_params=params,
        name="finish",
    )(got_b, got_a, image)

    arrivals_axial = arr_ax.transpose(1, 0, 2)[None, None]
    arrivals_radial = arr_rad.transpose(1, 0, 2)[None, None]
    return (motion_out, arrivals_axial, arrivals_radial, gas_out, liquid, pressure_image)


def solution(mesh):
    return jax.shard_map(
        on_device,
        mesh=mesh,
        in_specs=(
            P(None, ("ax", "rad")),
            P(("ax", "rad")),
            P(("ax", "rad")),
            P(("ax", "rad")),
            P(None, "ax", "rad"),
            P("ax", "rad"),
            P("ax", "rad", None),
            P("ax", "rad", None),
            P(),
            P("ax", "rad", None, None),
            P("ax", "rad", None, None),
            P("ax", "rad", None),
        ),
        out_specs=(
            P(None, ("ax", "rad")),
            P("ax", "rad", None, None, None),
            P("ax", "rad", None, None, None),
            P(None, "ax", "rad"),
            P("ax", "rad"),
            P("ax", "rad"),
        ),
        check_vma=False,
    )
```

```python
import functools

import jax
import jax.numpy as jnp
from jax import lax
from jax.experimental import pallas as pl
from jax.experimental.pallas import tpu as pltpu
from jax.sharding import PartitionSpec as P

BLOCK = 128
GROUP = 64
NT = 8
DRAG = 0.5
STEP = 0.5
DIAG = 6.0
VMEM_LIMIT = 24 * 1024 * 1024

F32 = jnp.float32
BF16 = jnp.bfloat16
I32 = jnp.int32

vmem = pl.BlockSpec(memory_space=pltpu.VMEM)
hbm = pl.BlockSpec(memory_space=pltpu.HBM)


class Sizes:
    def __init__(self, layers, radial, parcels):
        self.layers = layers
        self.quarters = radial // BLOCK
        self.blocks = layers * self.quarters
        self.tiles = parcels // BLOCK
        self.groups = parcels // GROUP
        self.gas = 0
        self.pres = 3 * self.blocks
        self.motion = self.pres + self.blocks
        self.size = self.motion + 6 * self.tiles
        self.offset = self.size + self.tiles
        self.meta = self.offset + self.tiles
        self.rows = self.meta + 8


def split2(x):
    high = x.astype(BF16)
    return high, (x - high.astype(F32)).astype(BF16)


def dot(a, b):
    return jnp.dot(a, b, preferred_element_type=F32)


def dot_nt(a, b):
    return lax.dot_general(a, b, (((1,), (1,)), ((), ())), preferred_element_type=F32)


def iota(shape, dim):
    return lax.broadcasted_iota(I32, shape, dim)


def block_row(sz, b):
    local = b % sz.blocks
    return b - local + (local % sz.quarters) * sz.layers + local // sz.quarters


def pack_kernel(
    sz, n_rad, motion_hbm, size_hbm, block_hbm, offset_hbm, gas_hbm, pres_hbm, radial_hbm, counts_hbm, cols_hbm,
    kinds_hbm, axial_hbm, table_hbm,
    out, aux, table,
    motion, size, block, offset, gas, pres, radial, counts, cols, kinds, axial, sem,
):
    pairs = (
        (motion_hbm, motion), (gas_hbm, gas), (pres_hbm, pres), (size_hbm, size), (offset_hbm, offset),
        (block_hbm, block), (counts_hbm, counts), (radial_hbm, radial), (axial_hbm, axial), (cols_hbm, cols),
        (kinds_hbm, kinds), (table_hbm, table),
    )
    copies = [pltpu.make_async_copy(src, dst, sem.at[i]) for i, (src, dst) in enumerate(pairs)]
    for copy in copies:
        copy.start()
    out[pl.ds(sz.meta, 8), :] = jnp.full((8, BLOCK), -1.0, F32)
    layers = sz.layers
    copies[0].wait()
    for i in range(sz.tiles):
        out[pl.ds(sz.motion + i, 6, stride=sz.tiles), :] = motion[:, i * BLOCK : (i + 1) * BLOCK]
    copies[1].wait()
    for c in range(3):
        for q in range(sz.quarters):
            out[pl.ds(sz.gas + c * sz.blocks + q * layers, layers), :] = gas[c, :, q * BLOCK : (q + 1) * BLOCK]
    copies[2].wait()
    for q in range(sz.quarters):
        out[pl.ds(sz.pres + q * layers, layers), :] = pres[:, q * BLOCK : (q + 1) * BLOCK]
    for copy in copies[3:11]:
        copy.wait()
    out[pl.ds(sz.size, sz.tiles), :] = size[...]
    out[pl.ds(sz.offset, sz.tiles), :] = offset[...].astype(F32)
    out[pl.ds(sz.meta, 1), pl.ds(0, sz.groups)] = block_row(sz, block[...]).astype(F32)
    width = radial.shape[1]
    lane = iota((1, width), 1)
    for slot in range(2):
        kept = jnp.where(lane < counts[0, 2 + slot], radial[slot : slot + 1, :], -1)
        out[pl.ds(sz.meta + 1 + slot, 1), pl.ds(0, width)] = kept.astype(F32)

    index = kinds[...] * (n_rad * sz.blocks) + block_row(sz, cols[...])
    aux[pl.ds(0, index.shape[0]), :] = jnp.concatenate([index, index], axis=1)
    lane = iota((1, axial.shape[1]), 1)
    kept = [jnp.where(lane < counts[0, slot], axial[slot : slot + 1, :], -1) for slot in range(2)]
    aux[pl.ds(8, 1), :] = jnp.concatenate(kept, axis=1)
    copies[11].wait()


def take_lanes(x, idx):
    return jnp.take_along_axis(x, idx, axis=1, mode="promise_in_bounds")


def pick(sz, state, idx):
    shape = (sz.tiles, BLOCK)
    idx = jnp.broadcast_to(idx, shape)
    lane = idx & (BLOCK - 1)
    here = (idx >> 7) == iota(shape, 0)
    return [jnp.sum(jnp.where(here, take_lanes(s, lane), 0.0), axis=0, keepdims=True) for s in state]


def slab_rows(sz, n_rad, G, first):
    return jnp.concatenate([G[d, pl.ds(first, sz.tiles), :] for d in range(n_rad)], axis=0)


def state_of(sz, T, state, d):
    first = pl.multiple_of(d * sz.tiles, sz.tiles)
    return [state[pl.ds(c * T + first, sz.tiles), :] for c in range(7)]


def move_kernel(sz, n_rad, G, aux, state, message, near):
    r = lax.axis_index("rad")
    layers, tiles, blocks, groups = sz.layers, sz.tiles, sz.blocks, sz.groups
    slab_blocks = n_rad * blocks
    T = n_rad * tiles

    block_rows = [G[d, pl.ds(sz.meta, 1), :] for d in range(n_rad)]
    column = jnp.concatenate(
        [jnp.transpose(jnp.broadcast_to(b, (BLOCK, BLOCK)))[:groups] for b in block_rows], axis=0
    ).astype(I32)
    lanes = iota((n_rad * groups, BLOCK), 1)
    chooser = jnp.concatenate(
        [(column == lanes + first).astype(F32).astype(BF16) for first in range(0, slab_blocks, BLOCK)], axis=1
    )
    gas_slab = jnp.concatenate(
        [
            jnp.concatenate([G[d, pl.ds(sz.gas + c * blocks, blocks), :] for d in range(n_rad)], axis=0)
            for c in range(3)
        ],
        axis=1,
    )
    high, low = split2(gas_slab)
    found = dot(chooser, high) + dot(chooser, low)
    for c in range(3):
        near[c] = found[:, c * BLOCK : (c + 1) * BLOCK]

    rows = functools.partial(slab_rows, sz, n_rad, G)
    size = rows(sz.size)
    offset = rows(sz.offset).astype(I32)
    factor = jnp.exp(-DRAG / (size * size))
    even = iota((T, BLOCK), 1) < GROUP
    for c in range(3):
        u_even = take_lanes(near[c, pl.ds(0, T, stride=2), :], offset)
        u_odd = take_lanes(near[c, pl.ds(1, T, stride=2), :], offset)
        u = jnp.where(even, u_even, u_odd)
        v = rows(sz.motion + (3 + c) * tiles)
        new = u + (v - u) * factor
        state[pl.ds(c * T, T), :] = rows(sz.motion + c * tiles) + STEP * new
        state[pl.ds((3 + c) * T, T), :] = new
    state[pl.ds(6 * T, T), :] = size

    payload = pick(sz, state_of(sz, T, state, r), aux[pl.ds(8, 1), :])
    for c in range(7):
        message[c : c + 1, :] = payload[c]
    message[7:8, :] = jnp.zeros((1, BLOCK), F32)
    for q in range(sz.quarters):
        first = sz.pres + q * layers
        message[8 + q : 9 + q, :] = G[r, pl.ds(first + layers - 1, 1), :]
        message[12 + q : 13 + q, :] = G[r, pl.ds(first, 1), :]


def rest_kernel(
    sz, n_rad, G, aux, table, state,
    motion_hbm, arr_hbm, gas_hbm, liquid_hbm, image,
    deps, spread, coup, motion_out, arr_rad, gas_out, liquid, sem,
):
    r = lax.axis_index("rad")
    sends = [
        pltpu.make_async_copy(src, dst, sem.at[i])
        for i, (src, dst) in enumerate(
            ((motion_out, motion_hbm), (arr_rad, arr_hbm), (gas_out, gas_hbm), (liquid, liquid_hbm))
        )
    ]
    layers, tiles, blocks, groups = sz.layers, sz.tiles, sz.blocks, sz.groups
    slab_blocks = n_rad * blocks
    T = n_rad * tiles
    block_rows = [G[d, pl.ds(sz.meta, 1), :] for d in range(n_rad)]

    mine = pl.multiple_of(r * tiles, tiles)
    for i in range(tiles):
        motion_out[:, i * BLOCK : (i + 1) * BLOCK] = state[pl.ds(mine + i, 6, stride=T), :]
    sends[0].start()

    width = arr_rad.shape[2]
    for slot, exists, other in ((0, r > 0, jnp.maximum(r - 1, 0)), (1, r < n_rad - 1, jnp.minimum(r + 1, n_rad - 1))):
        idx = G[other, pl.ds(sz.meta + 1 + slot, 1), :].astype(I32)
        idx = jnp.where(exists, idx, -1)
        got = pick(sz, state_of(sz, T, state, other), idx)
        for c in range(7):
            arr_rad[c, slot : slot + 1, :] = got[c][:, :width]
    sends[1].start()

    rows = functools.partial(slab_rows, sz, n_rad, G)
    size = rows(sz.size)
    mass = size * size * size
    dep = [-mass * (state[pl.ds((3 + c) * T, T), :] - rows(sz.motion + (3 + c) * tiles)) for c in range(3)] + [mass]
    even = iota((T, BLOCK), 1) < GROUP

    for c in range(4):
        high = dep[c].astype(BF16).astype(F32)
        low = dep[c] - high
        for piece, part in enumerate((high, low)):
            deps[pl.ds((piece * 8 + c) * T, T), :] = jnp.where(even, part, 0.0)
            deps[pl.ds((piece * 8 + 4 + c) * T, T), :] = jnp.where(even, 0.0, part)
    cell = iota((BLOCK, BLOCK), 0)
    for d in range(n_rad):
        for i in range(tiles):
            t = d * tiles + i
            off = G[d, pl.ds(sz.offset + i, 1), :].astype(I32)
            onehot = (cell == off).astype(F32).astype(BF16)
            lhs = deps[pl.ds(t, 16, stride=T), :].astype(BF16)
            res = dot_nt(lhs, onehot)
            res = res[:8] + res[8:]
            spread[pl.ds(2 * t, 4, stride=2 * T), :] = res[:4]
            spread[pl.ds(2 * t + 1, 4, stride=2 * T), :] = res[4:]
    own = iota((blocks, groups), 0) + r * blocks
    adder = jnp.concatenate(
        [(own == b[:, :groups].astype(I32)).astype(F32) for b in block_rows], axis=1
    ).astype(BF16)
    for c in range(4):
        high, low = split2(spread[pl.ds(c * 2 * T, 2 * T), :])
        total = dot(adder, high) + dot(adder, low)
        for q in range(sz.quarters):
            part = total[q * layers : (q + 1) * layers]
            at = slice(q * BLOCK, (q + 1) * BLOCK)
            if c < 3:
                gas_out[c, :, at] = G[r, pl.ds(sz.gas + c * blocks + q * layers, layers), :] + part
            else:
                liquid[:, at] = part
    sends[2].start()
    sends[3].start()

    pres = jnp.concatenate([G[d, pl.ds(sz.pres, blocks), :] for d in range(n_rad)], axis=0)
    index = aux[pl.ds(0, 4), :]
    grouped = [None] * (NT // 2)
    for first in range(0, slab_blocks, BLOCK):
        p_high, p_low = split2(jnp.transpose(pres[first : first + BLOCK]))
        here = iota((BLOCK, BLOCK), 0) + first + jnp.where(iota((BLOCK, BLOCK), 1) < blocks, 0, slab_blocks)
        for j in range(NT // 2):
            aim = here + 2 * j * slab_blocks
            count = (aim == index[0:1]).astype(F32)
            for k in range(1, index.shape[0]):
                count = count + (aim == index[k : k + 1]).astype(F32)
            count = count.astype(BF16)
            part = dot(p_high, count) + dot(p_low, count)
            grouped[j] = part if grouped[j] is None else grouped[j] + part
    sums = [None, None]
    for j in range(NT // 2):
        g_high, g_low = split2(grouped[j])
        for s in range(2):
            t_high, t_low = split2(table[2 * j + s])
            part = dot(t_high, g_high) + dot(t_low, g_high) + dot(t_high, g_low)
            sums[s] = part if sums[s] is None else sums[s] + part
    both = jnp.where(iota((BLOCK, BLOCK), 1) < blocks, sums[0], sums[1])
    both = both + pltpu.roll(jnp.where(iota((BLOCK, BLOCK), 1) < blocks, 0.0, sums[1]), blocks, 1)
    coup[...] = jnp.transpose(both)
    layer = iota((layers, BLOCK), 0)
    for q in range(sz.quarters):
        p = G[r, pl.ds(sz.pres + q * layers, layers), :]
        below = jnp.where(layer == 0, 0.0, pltpu.roll(p, 1, 0))
        above = jnp.where(layer == layers - 1, 0.0, pltpu.roll(p, layers - 1, 0))
        image[:, q * BLOCK : (q + 1) * BLOCK] = (
            DIAG * p - above - below + coup[pl.ds(q, layers, stride=sz.quarters), :]
        )
    for send in sends:
        send.wait()


def finish_kernel(sz, n_ax, got_a, got_b, image, arr_ax, pressure_image):
    a = lax.axis_index("ax")
    even = a % 2 == 0
    low = jnp.where(a > 0, jnp.where(even, got_b[...], got_a[...]), 0.0)
    up = jnp.where(a < n_ax - 1, jnp.where(even, got_a[...], got_b[...]), 0.0)
    half = arr_ax.shape[2]
    arr_ax[:, 0, :] = low[0:7, 0:half]
    arr_ax[:, 1, :] = up[0:7, half : 2 * half]
    pressure_image[...] = image[...]
    last = sz.layers - 1
    for q in range(sz.quarters):
        at = slice(q * BLOCK, (q + 1) * BLOCK)
        pressure_image[0:1, at] = image[0:1, at] - low[8 + q : 9 + q, :]
        pressure_image[last : last + 1, at] = image[last : last + 1, at] - up[12 + q : 13 + q, :]


def on_device(
    parcel_motion,
    parcel_size,
    parcel_block,
    parcel_offset,
    gas_velocity,
    pressure,
    block_cols,
    block_kinds,
    block_table,
    send_axial,
    send_radial,
    send_counts,
):
    n_ax, n_rad = lax.axis_size("ax"), lax.axis_size("rad")
    layers, radial = pressure.shape
    parcels = parcel_size.shape[0]
    sz = Sizes(layers, radial, parcels)
    T = n_rad * sz.tiles
    cap_ax, cap_rad = send_axial.shape[-1], send_radial.shape[-1]
    params = pltpu.CompilerParams(vmem_limit_bytes=VMEM_LIMIT)
    counts = send_counts.reshape(1, 4)
    size2 = parcel_size.reshape(sz.tiles, BLOCK)
    offset2 = parcel_offset.reshape(sz.tiles, BLOCK)

    packed, aux, table = pl.pallas_call(
        functools.partial(pack_kernel, sz, n_rad),
        out_shape=[
            jax.ShapeDtypeStruct((sz.rows, BLOCK), F32),
            jax.ShapeDtypeStruct((16, BLOCK), I32),
            jax.ShapeDtypeStruct(block_table.shape, F32),
        ],
        in_specs=[hbm] * 12,
        out_specs=[vmem] * 3,
        scratch_shapes=[
            pltpu.VMEM(parcel_motion.shape, F32),
            pltpu.VMEM(size2.shape, F32),
            pltpu.VMEM((1, sz.groups), I32),
            pltpu.VMEM(offset2.shape, I32),
            pltpu.VMEM(gas_velocity.shape, F32),
            pltpu.VMEM(pressure.shape, F32),
            pltpu.VMEM((2, cap_rad), I32),
            pltpu.SMEM((1, 4), I32),
            pltpu.VMEM((4, sz.blocks), I32),
            pltpu.VMEM((4, sz.blocks), I32),
            pltpu.VMEM((2, cap_ax), I32),
            pltpu.SemaphoreType.DMA((12,)),
        ],
        compiler_params=params,
        name="pack",
    )(
        *(
            pltpu.with_memory_space_constraint(x, pltpu.HBM)
            for x in (
                parcel_motion, size2, parcel_block.reshape(1, sz.groups), offset2, gas_velocity, pressure,
                send_radial.reshape(2, cap_rad), counts, block_cols[0].T, block_kinds[0].T,
                send_axial.reshape(2, cap_ax), block_table,
            )
        )
    )
    gathered = lax.all_gather(packed, "rad", axis=0)

    state, message = pl.pallas_call(
        functools.partial(move_kernel, sz, n_rad),
        out_shape=[
            jax.ShapeDtypeStruct((7 * T, BLOCK), F32),
            jax.ShapeDtypeStruct((16, BLOCK), F32),
        ],
        in_specs=[vmem] * 2,
        out_specs=[vmem] * 2,
        scratch_shapes=[pltpu.VMEM((3, n_rad * sz.groups, BLOCK), F32)],
        compiler_params=params,
        name="move",
    )(gathered, aux)

    def exchange(first):
        to = list(range(n_ax * n_rad))
        for low in range(first, n_ax - 1, 2):
            for r in range(n_rad):
                i, j = low * n_rad + r, (low + 1) * n_rad + r
                to[i], to[j] = j, i
        alone = [i for i in range(n_ax * n_rad) if to[i] == i]
        for i, j in zip(alone[0::2], alone[1::2]):
            to[i], to[j] = j, i
        return lax.ppermute(message, ("ax", "rad"), list(enumerate(to)))

    got_b = exchange(1)
    got_a = exchange(0)

    motion_out, arr_rad, gas_out, liquid, image = pl.pallas_call(
        functools.partial(rest_kernel, sz, n_rad),
        out_shape=[
            jax.ShapeDtypeStruct((6, parcels), F32),
            jax.ShapeDtypeStruct((7, 2, cap_rad), F32),
            jax.ShapeDtypeStruct(gas_velocity.shape, F32),
            jax.ShapeDtypeStruct(pressure.shape, F32),
            jax.ShapeDtypeStruct(pressure.shape, F32),
        ],
        in_specs=[vmem] * 4,
        out_specs=[hbm] * 4 + [vmem],
        scratch_shapes=[
            pltpu.VMEM((16 * T, BLOCK), F32),
            pltpu.VMEM((4 * 2 * T, BLOCK), F32),
            pltpu.VMEM((BLOCK, BLOCK), F32),
            pltpu.VMEM((6, parcels), F32),
            pltpu.VMEM((7, 2, cap_rad), F32),
            pltpu.VMEM(gas_velocity.shape, F32),
            pltpu.VMEM(pressure.shape, F32),
            pltpu.SemaphoreType.DMA((4,)),
        ],
        compiler_params=params,
        cost_estimate=pl.CostEstimate(flops=2_000_000_000, bytes_accessed=2_000_000, transcendentals=0),
        name="rest",
    )(gathered, aux, table, state)

    arr_ax, pressure_image = pl.pallas_call(
        functools.partial(finish_kernel, sz, n_ax),
        out_shape=[
            jax.ShapeDtypeStruct((7, 2, cap_ax), F32),
            jax.ShapeDtypeStruct(pressure.shape, F32),
        ],
        in_specs=[vmem] * 3,
        out_specs=[vmem] * 2,
        compiler_params=params,
        name="finish",
    )(got_a, got_b, image)

    arrivals_axial = arr_ax.transpose(1, 0, 2)[None, None]
    arrivals_radial = arr_rad.transpose(1, 0, 2)[None, None]
    return (motion_out, arrivals_axial, arrivals_radial, gas_out, liquid, pressure_image)


def solution(mesh):
    return jax.shard_map(
        on_device,
        mesh=mesh,
        in_specs=(
            P(None, ("ax", "rad")),
            P(("ax", "rad")),
            P(("ax", "rad")),
            P(("ax", "rad")),
            P(None, "ax", "rad"),
            P("ax", "rad"),
            P("ax", "rad", None),
            P("ax", "rad", None),
            P(),
            P("ax", "rad", None, None),
            P("ax", "rad", None, None),
            P("ax", "rad", None),
        ),
        out_specs=(
            P(None, ("ax", "rad")),
            P("ax", "rad", None, None, None),
            P("ax", "rad", None, None, None),
            P(None, "ax", "rad"),
            P("ax", "rad"),
            P("ax", "rad"),
        ),
        check_vma=False,
    )
```

```python
import functools

import jax
import jax.numpy as jnp
from jax import lax
from jax.experimental import pallas as pl
from jax.experimental.pallas import tpu as pltpu
from jax.sharding import PartitionSpec as P

BLOCK = 128
GROUP = 64
NT = 8
DRAG = 0.5
STEP = 0.5
DIAG = 6.0
VMEM_LIMIT = 24 * 1024 * 1024

F32 = jnp.float32
BF16 = jnp.bfloat16
I32 = jnp.int32

vmem = pl.BlockSpec(memory_space=pltpu.VMEM)
hbm = pl.BlockSpec(memory_space=pltpu.HBM)


class Sizes:
    def __init__(self, layers, radial, parcels):
        self.layers = layers
        self.quarters = radial // BLOCK
        self.blocks = layers * self.quarters
        self.tiles = parcels // BLOCK
        self.groups = parcels // GROUP
        self.gas = 0
        self.pres = 3 * self.blocks
        self.motion = self.pres + self.blocks
        self.size = self.motion + 6 * self.tiles
        self.offset = self.size + self.tiles
        self.meta = self.offset + self.tiles
        self.rows = self.meta + 8


def split2(x):
    high = x.astype(BF16)
    return high, (x - high.astype(F32)).astype(BF16)


def dot(a, b):
    return jnp.dot(a, b, preferred_element_type=F32)


def dot_nt(a, b):
    return lax.dot_general(a, b, (((1,), (1,)), ((), ())), preferred_element_type=F32)


def iota(shape, dim):
    return lax.broadcasted_iota(I32, shape, dim)


def block_row(sz, b):
    local = b % sz.blocks
    return b - local + (local % sz.quarters) * sz.layers + local // sz.quarters


def pack_kernel(
    sz, n_rad, motion_hbm, size_hbm, block_hbm, offset_hbm, gas_hbm, pres_hbm, radial_hbm, counts_hbm, cols_hbm,
    kinds_hbm, axial_hbm, table_hbm,
    out, aux, table,
    motion, size, block, offset, gas, pres, radial, counts, cols, kinds, axial, sem,
):
    half = motion.shape[1] // 2
    big = [(motion_hbm.at[:, pl.ds(i * half, half)], motion.at[:, pl.ds(i * half, half)]) for i in range(2)]
    big += [(gas_hbm.at[c], gas.at[c]) for c in range(3)]
    rest = [
        (pres_hbm, pres), (size_hbm, size), (offset_hbm, offset), (block_hbm, block), (counts_hbm, counts),
        (radial_hbm, radial), (axial_hbm, axial), (cols_hbm, cols), (kinds_hbm, kinds),
    ]
    late = [(table_hbm.at[t], table.at[t]) for t in range(table.shape[0])]
    copies = [pltpu.make_async_copy(src, dst, sem.at[i]) for i, (src, dst) in enumerate(big + rest + late)]
    for copy in copies:
        copy.start()
    out[pl.ds(sz.meta, 8), :] = jnp.full((8, BLOCK), -1.0, F32)
    layers = sz.layers
    copies[0].wait()
    copies[1].wait()
    for i in range(sz.tiles):
        out[pl.ds(sz.motion + i, 6, stride=sz.tiles), :] = motion[:, i * BLOCK : (i + 1) * BLOCK]
    for copy in copies[2:5]:
        copy.wait()
    for c in range(3):
        for q in range(sz.quarters):
            out[pl.ds(sz.gas + c * sz.blocks + q * layers, layers), :] = gas[c, :, q * BLOCK : (q + 1) * BLOCK]
    copies[5].wait()
    for q in range(sz.quarters):
        out[pl.ds(sz.pres + q * layers, layers), :] = pres[:, q * BLOCK : (q + 1) * BLOCK]
    for copy in copies[6 : len(big + rest)]:
        copy.wait()
    out[pl.ds(sz.size, sz.tiles), :] = size[...]
    out[pl.ds(sz.offset, sz.tiles), :] = offset[...].astype(F32)
    out[pl.ds(sz.meta, 1), pl.ds(0, sz.groups)] = block_row(sz, block[...]).astype(F32)
    width = radial.shape[1]
    lane = iota((1, width), 1)
    for slot in range(2):
        kept = jnp.where(lane < counts[0, 2 + slot], radial[slot : slot + 1, :], -1)
        out[pl.ds(sz.meta + 1 + slot, 1), pl.ds(0, width)] = kept.astype(F32)

    index = kinds[...] * (n_rad * sz.blocks) + block_row(sz, cols[...])
    aux[pl.ds(0, index.shape[0]), :] = jnp.concatenate([index, index], axis=1)
    lane = iota((1, axial.shape[1]), 1)
    kept = [jnp.where(lane < counts[0, slot], axial[slot : slot + 1, :], -1) for slot in range(2)]
    aux[pl.ds(8, 1), :] = jnp.concatenate(kept, axis=1)
    for copy in copies[len(big + rest) :]:
        copy.wait()


def take_lanes(x, idx):
    return jnp.take_along_axis(x, idx, axis=1, mode="promise_in_bounds")


def pick(sz, state, idx):
    shape = (sz.tiles, BLOCK)
    idx = jnp.broadcast_to(idx, shape)
    lane = idx & (BLOCK - 1)
    here = (idx >> 7) == iota(shape, 0)
    return [jnp.sum(jnp.where(here, take_lanes(s, lane), 0.0), axis=0, keepdims=True) for s in state]


def slab_rows(sz, n_rad, G, first):
    return jnp.concatenate([G[d, pl.ds(first, sz.tiles), :] for d in range(n_rad)], axis=0)


def state_of(sz, T, state, d):
    first = pl.multiple_of(d * sz.tiles, sz.tiles)
    return [state[pl.ds(c * T + first, sz.tiles), :] for c in range(7)]


def move_kernel(sz, n_rad, G, aux, state, message, near):
    r = lax.axis_index("rad")
    layers, tiles, blocks, groups = sz.layers, sz.tiles, sz.blocks, sz.groups
    slab_blocks = n_rad * blocks
    T = n_rad * tiles

    block_rows = [G[d, pl.ds(sz.meta, 1), :] for d in range(n_rad)]
    column = jnp.concatenate(
        [jnp.transpose(jnp.broadcast_to(b, (BLOCK, BLOCK)))[:groups] for b in block_rows], axis=0
    ).astype(I32)
    lanes = iota((n_rad * groups, BLOCK), 1)
    chooser = jnp.concatenate(
        [(column == lanes + first).astype(F32).astype(BF16) for first in range(0, slab_blocks, BLOCK)], axis=1
    )
    gas_slab = jnp.concatenate(
        [
            jnp.concatenate([G[d, pl.ds(sz.gas + c * blocks, blocks), :] for d in range(n_rad)], axis=0)
            for c in range(3)
        ],
        axis=1,
    )
    high, low = split2(gas_slab)
    found = dot(chooser, high) + dot(chooser, low)
    for c in range(3):
        near[c] = found[:, c * BLOCK : (c + 1) * BLOCK]

    rows = functools.partial(slab_rows, sz, n_rad, G)
    size = rows(sz.size)
    offset = rows(sz.offset).astype(I32)
    factor = jnp.exp(-DRAG / (size * size))
    even = iota((T, BLOCK), 1) < GROUP
    for c in range(3):
        u_even = take_lanes(near[c, pl.ds(0, T, stride=2), :], offset)
        u_odd = take_lanes(near[c, pl.ds(1, T, stride=2), :], offset)
        u = jnp.where(even, u_even, u_odd)
        v = rows(sz.motion + (3 + c) * tiles)
        new = u + (v - u) * factor
        state[pl.ds(c * T, T), :] = rows(sz.motion + c * tiles) + STEP * new
        state[pl.ds((3 + c) * T, T), :] = new
    state[pl.ds(6 * T, T), :] = size

    payload = pick(sz, state_of(sz, T, state, r), aux[pl.ds(8, 1), :])
    for c in range(7):
        message[c : c + 1, :] = payload[c]
    message[7:8, :] = jnp.zeros((1, BLOCK), F32)
    for q in range(sz.quarters):
        first = sz.pres + q * layers
        message[8 + q : 9 + q, :] = G[r, pl.ds(first + layers - 1, 1), :]
        message[12 + q : 13 + q, :] = G[r, pl.ds(first, 1), :]


def rest_kernel(
    sz, n_rad, G, aux, table, state,
    motion_hbm, arr_hbm, gas_hbm, liquid_hbm, image,
    deps, spread, coup, motion_out, arr_rad, gas_out, liquid, sem,
):
    r = lax.axis_index("rad")
    sends = [
        pltpu.make_async_copy(src, dst, sem.at[i])
        for i, (src, dst) in enumerate(
            ((motion_out, motion_hbm), (arr_rad, arr_hbm), (gas_out, gas_hbm), (liquid, liquid_hbm))
        )
    ]
    layers, tiles, blocks, groups = sz.layers, sz.tiles, sz.blocks, sz.groups
    slab_blocks = n_rad * blocks
    T = n_rad * tiles
    block_rows = [G[d, pl.ds(sz.meta, 1), :] for d in range(n_rad)]

    mine = pl.multiple_of(r * tiles, tiles)
    for i in range(tiles):
        motion_out[:, i * BLOCK : (i + 1) * BLOCK] = state[pl.ds(mine + i, 6, stride=T), :]
    sends[0].start()

    width = arr_rad.shape[2]
    for slot, exists, other in ((0, r > 0, jnp.maximum(r - 1, 0)), (1, r < n_rad - 1, jnp.minimum(r + 1, n_rad - 1))):
        idx = G[other, pl.ds(sz.meta + 1 + slot, 1), :].astype(I32)
        idx = jnp.where(exists, idx, -1)
        got = pick(sz, state_of(sz, T, state, other), idx)
        for c in range(7):
            arr_rad[c, slot : slot + 1, :] = got[c][:, :width]
    sends[1].start()

    rows = functools.partial(slab_rows, sz, n_rad, G)
    size = rows(sz.size)
    mass = size * size * size
    dep = [-mass * (state[pl.ds((3 + c) * T, T), :] - rows(sz.motion + (3 + c) * tiles)) for c in range(3)] + [mass]
    even = iota((T, BLOCK), 1) < GROUP

    for c in range(4):
        high = dep[c].astype(BF16).astype(F32)
        low = dep[c] - high
        for piece, part in enumerate((high, low)):
            deps[pl.ds((piece * 8 + c) * T, T), :] = jnp.where(even, part, 0.0)
            deps[pl.ds((piece * 8 + 4 + c) * T, T), :] = jnp.where(even, 0.0, part)
    cell = iota((BLOCK, BLOCK), 0).astype(F32).astype(BF16)
    one, none = jnp.ones((BLOCK, BLOCK), BF16), jnp.zeros((BLOCK, BLOCK), BF16)
    for d in range(n_rad):
        for i in range(tiles):
            t = d * tiles + i
            off = jnp.broadcast_to(G[d, pl.ds(sz.offset + i, 1), :], (16, BLOCK)).astype(BF16)
            onehot = jnp.where(cell == jnp.concatenate([off] * (BLOCK // 16), axis=0), one, none)
            lhs = deps[pl.ds(t, 16, stride=T), :].astype(BF16)
            res = dot_nt(lhs, onehot)
            res = res[:8] + res[8:]
            spread[pl.ds(2 * t, 4, stride=2 * T), :] = res[:4]
            spread[pl.ds(2 * t + 1, 4, stride=2 * T), :] = res[4:]
    own = iota((blocks, groups), 0) + r * blocks
    adder = jnp.concatenate(
        [(own == b[:, :groups].astype(I32)).astype(F32) for b in block_rows], axis=1
    ).astype(BF16)
    for c in range(4):
        high, low = split2(spread[pl.ds(c * 2 * T, 2 * T), :])
        total = dot(adder, high) + dot(adder, low)
        for q in range(sz.quarters):
            part = total[q * layers : (q + 1) * layers]
            at = slice(q * BLOCK, (q + 1) * BLOCK)
            if c < 3:
                gas_out[c, :, at] = G[r, pl.ds(sz.gas + c * blocks + q * layers, layers), :] + part
            else:
                liquid[:, at] = part
    sends[2].start()
    sends[3].start()

    pres = jnp.concatenate([G[d, pl.ds(sz.pres, blocks), :] for d in range(n_rad)], axis=0)
    index = [jnp.broadcast_to(aux[pl.ds(k, 1), :], (BLOCK, BLOCK)).astype(jnp.int16) for k in range(4)]
    grouped = [None] * (NT // 2)
    for first in range(0, slab_blocks, BLOCK):
        p_high, p_low = split2(jnp.transpose(pres[first : first + BLOCK]))
        here = iota((BLOCK, BLOCK), 0) + first + jnp.where(iota((BLOCK, BLOCK), 1) < blocks, 0, slab_blocks)
        for j in range(NT // 2):
            aim = (here + 2 * j * slab_blocks).astype(jnp.int16)
            count = none
            for k in range(4):
                count = count + jnp.where(aim == index[k], one, none)
            part = dot(p_high, count) + dot(p_low, count)
            grouped[j] = part if grouped[j] is None else grouped[j] + part
    sums = [None, None]
    for j in range(NT // 2):
        g_high, g_low = split2(grouped[j])
        for s in range(2):
            t_high, t_low = split2(table[2 * j + s])
            part = dot(t_high, g_high) + dot(t_low, g_high) + dot(t_high, g_low)
            sums[s] = part if sums[s] is None else sums[s] + part
    both = jnp.where(iota((BLOCK, BLOCK), 1) < blocks, sums[0], sums[1])
    both = both + pltpu.roll(jnp.where(iota((BLOCK, BLOCK), 1) < blocks, 0.0, sums[1]), blocks, 1)
    coup[...] = jnp.transpose(both)
    layer = iota((layers, BLOCK), 0)
    for q in range(sz.quarters):
        p = G[r, pl.ds(sz.pres + q * layers, layers), :]
        below = jnp.where(layer == 0, 0.0, pltpu.roll(p, 1, 0))
        above = jnp.where(layer == layers - 1, 0.0, pltpu.roll(p, layers - 1, 0))
        image[:, q * BLOCK : (q + 1) * BLOCK] = (
            DIAG * p - above - below + coup[pl.ds(q, layers, stride=sz.quarters), :]
        )
    for send in sends:
        send.wait()


def finish_kernel(sz, n_ax, got_a, got_b, image, arr_ax, pressure_image):
    a = lax.axis_index("ax")
    even = a % 2 == 0
    low = jnp.where(a > 0, jnp.where(even, got_b[...], got_a[...]), 0.0)
    up = jnp.where(a < n_ax - 1, jnp.where(even, got_a[...], got_b[...]), 0.0)
    half = arr_ax.shape[2]
    arr_ax[:, 0, :] = low[0:7, 0:half]
    arr_ax[:, 1, :] = up[0:7, half : 2 * half]
    pressure_image[...] = image[...]
    last = sz.layers - 1
    for q in range(sz.quarters):
        at = slice(q * BLOCK, (q + 1) * BLOCK)
        pressure_image[0:1, at] = image[0:1, at] - low[8 + q : 9 + q, :]
        pressure_image[last : last + 1, at] = image[last : last + 1, at] - up[12 + q : 13 + q, :]


def on_device(
    parcel_motion,
    parcel_size,
    parcel_block,
    parcel_offset,
    gas_velocity,
    pressure,
    block_cols,
    block_kinds,
    block_table,
    send_axial,
    send_radial,
    send_counts,
):
    n_ax, n_rad = lax.axis_size("ax"), lax.axis_size("rad")
    layers, radial = pressure.shape
    parcels = parcel_size.shape[0]
    sz = Sizes(layers, radial, parcels)
    T = n_rad * sz.tiles
    cap_ax, cap_rad = send_axial.shape[-1], send_radial.shape[-1]
    params = pltpu.CompilerParams(vmem_limit_bytes=VMEM_LIMIT)
    counts = send_counts.reshape(1, 4)
    size2 = parcel_size.reshape(sz.tiles, BLOCK)
    offset2 = parcel_offset.reshape(sz.tiles, BLOCK)

    packed, aux, table = pl.pallas_call(
        functools.partial(pack_kernel, sz, n_rad),
        out_shape=[
            jax.ShapeDtypeStruct((sz.rows, BLOCK), F32),
            jax.ShapeDtypeStruct((16, BLOCK), I32),
            jax.ShapeDtypeStruct(block_table.shape, F32),
        ],
        in_specs=[hbm] * 12,
        out_specs=[vmem] * 3,
        scratch_shapes=[
            pltpu.VMEM(parcel_motion.shape, F32),
            pltpu.VMEM(size2.shape, F32),
            pltpu.VMEM((1, sz.groups), I32),
            pltpu.VMEM(offset2.shape, I32),
            pltpu.VMEM(gas_velocity.shape, F32),
            pltpu.VMEM(pressure.shape, F32),
            pltpu.VMEM((2, cap_rad), I32),
            pltpu.SMEM((1, 4), I32),
            pltpu.VMEM((4, sz.blocks), I32),
            pltpu.VMEM((4, sz.blocks), I32),
            pltpu.VMEM((2, cap_ax), I32),
            pltpu.SemaphoreType.DMA((14 + NT,)),
        ],
        compiler_params=params,
        name="pack",
    )(
        *(
            pltpu.with_memory_space_constraint(x, pltpu.HBM)
            for x in (
                parcel_motion, size2, parcel_block.reshape(1, sz.groups), offset2, gas_velocity, pressure,
                send_radial.reshape(2, cap_rad), counts, block_cols[0].T, block_kinds[0].T,
                send_axial.reshape(2, cap_ax), block_table,
            )
        )
    )
    gathered = lax.all_gather(packed, "rad", axis=0)

    state, message = pl.pallas_call(
        functools.partial(move_kernel, sz, n_rad),
        out_shape=[
            jax.ShapeDtypeStruct((7 * T, BLOCK), F32),
            jax.ShapeDtypeStruct((16, BLOCK), F32),
        ],
        in_specs=[vmem] * 2,
        out_specs=[vmem] * 2,
        scratch_shapes=[pltpu.VMEM((3, n_rad * sz.groups, BLOCK), F32)],
        compiler_params=params,
        name="move",
    )(gathered, aux)

    def exchange(first):
        to = list(range(n_ax * n_rad))
        for low in range(first, n_ax - 1, 2):
            for r in range(n_rad):
                i, j = low * n_rad + r, (low + 1) * n_rad + r
                to[i], to[j] = j, i
        alone = [i for i in range(n_ax * n_rad) if to[i] == i]
        for i, j in zip(alone[0::2], alone[1::2]):
            to[i], to[j] = j, i
        return lax.ppermute(message, ("ax", "rad"), list(enumerate(to)))

    got_b = exchange(1)
    got_a = exchange(0)

    motion_out, arr_rad, gas_out, liquid, image = pl.pallas_call(
        functools.partial(rest_kernel, sz, n_rad),
        out_shape=[
            jax.ShapeDtypeStruct((6, parcels), F32),
            jax.ShapeDtypeStruct((7, 2, cap_rad), F32),
            jax.ShapeDtypeStruct(gas_velocity.shape, F32),
            jax.ShapeDtypeStruct(pressure.shape, F32),
            jax.ShapeDtypeStruct(pressure.shape, F32),
        ],
        in_specs=[vmem] * 4,
        out_specs=[hbm] * 4 + [vmem],
        scratch_shapes=[
            pltpu.VMEM((16 * T, BLOCK), F32),
            pltpu.VMEM((4 * 2 * T, BLOCK), F32),
            pltpu.VMEM((BLOCK, BLOCK), F32),
            pltpu.VMEM((6, parcels), F32),
            pltpu.VMEM((7, 2, cap_rad), F32),
            pltpu.VMEM(gas_velocity.shape, F32),
            pltpu.VMEM(pressure.shape, F32),
            pltpu.SemaphoreType.DMA((4,)),
        ],
        compiler_params=params,
        cost_estimate=pl.CostEstimate(flops=2_000_000_000, bytes_accessed=2_000_000, transcendentals=0),
        name="rest",
    )(gathered, aux, table, state)

    arr_ax, pressure_image = pl.pallas_call(
        functools.partial(finish_kernel, sz, n_ax),
        out_shape=[
            jax.ShapeDtypeStruct((7, 2, cap_ax), F32),
            jax.ShapeDtypeStruct(pressure.shape, F32),
        ],
        in_specs=[vmem] * 3,
        out_specs=[vmem] * 2,
        compiler_params=params,
        name="finish",
    )(got_a, got_b, image)

    arrivals_axial = arr_ax.transpose(1, 0, 2)[None, None]
    arrivals_radial = arr_rad.transpose(1, 0, 2)[None, None]
    return (motion_out, arrivals_axial, arrivals_radial, gas_out, liquid, pressure_image)


def solution(mesh):
    return jax.shard_map(
        on_device,
        mesh=mesh,
        in_specs=(
            P(None, ("ax", "rad")),
            P(("ax", "rad")),
            P(("ax", "rad")),
            P(("ax", "rad")),
            P(None, "ax", "rad"),
            P("ax", "rad"),
            P("ax", "rad", None),
            P("ax", "rad", None),
            P(),
            P("ax", "rad", None, None),
            P("ax", "rad", None, None),
            P("ax", "rad", None),
        ),
        out_specs=(
            P(None, ("ax", "rad")),
            P("ax", "rad", None, None, None),
            P("ax", "rad", None, None, None),
            P(None, "ax", "rad"),
            P("ax", "rad"),
            P("ax", "rad"),
        ),
        check_vma=False,
    )
```

```python
import functools

import jax
import jax.numpy as jnp
from jax import lax
from jax.experimental import pallas as pl
from jax.experimental.pallas import tpu as pltpu
from jax.sharding import PartitionSpec as P

BLOCK = 128
GROUP = 64
NT = 8
DRAG = 0.5
STEP = 0.5
DIAG = 6.0
VMEM_LIMIT = 24 * 1024 * 1024

F32 = jnp.float32
BF16 = jnp.bfloat16
I32 = jnp.int32

vmem = pl.BlockSpec(memory_space=pltpu.VMEM)
hbm = pl.BlockSpec(memory_space=pltpu.HBM)


class Sizes:
    def __init__(self, layers, radial, parcels):
        self.layers = layers
        self.quarters = radial // BLOCK
        self.blocks = layers * self.quarters
        self.tiles = parcels // BLOCK
        self.groups = parcels // GROUP
        self.gas = 0
        self.pres = 3 * self.blocks
        self.motion = self.pres + self.blocks
        self.size = self.motion + 6 * self.tiles
        self.offset = self.size + self.tiles
        self.meta = self.offset + self.tiles
        self.rows = self.meta + 8


def split2(x):
    high = x.astype(BF16)
    return high, (x - high.astype(F32)).astype(BF16)


def dot(a, b):
    return jnp.dot(a, b, preferred_element_type=F32)


def dot_nt(a, b):
    return lax.dot_general(a, b, (((1,), (1,)), ((), ())), preferred_element_type=F32)


def iota(shape, dim):
    return lax.broadcasted_iota(I32, shape, dim)


def block_row(sz, b):
    local = b % sz.blocks
    return b - local + (local % sz.quarters) * sz.layers + local // sz.quarters


def pack_kernel(
    sz, n_rad, motion_hbm, size_hbm, block_hbm, offset_hbm, gas_hbm, pres_hbm, radial_hbm, counts_hbm, cols_hbm,
    kinds_hbm, axial_hbm,
    out, aux,
    motion, size, block, offset, gas, pres, radial, counts, cols, kinds, axial, sem,
):
    pairs = (
        (motion_hbm, motion), (gas_hbm, gas), (pres_hbm, pres), (size_hbm, size), (offset_hbm, offset),
        (block_hbm, block), (counts_hbm, counts), (radial_hbm, radial), (axial_hbm, axial), (cols_hbm, cols),
        (kinds_hbm, kinds),
    )
    copies = [pltpu.make_async_copy(src, dst, sem.at[i]) for i, (src, dst) in enumerate(pairs)]
    for copy in copies:
        copy.start()
    out[pl.ds(sz.meta, 8), :] = jnp.full((8, BLOCK), -1.0, F32)
    layers = sz.layers
    copies[0].wait()
    for i in range(sz.tiles):
        out[pl.ds(sz.motion + i, 6, stride=sz.tiles), :] = motion[:, i * BLOCK : (i + 1) * BLOCK]
    copies[1].wait()
    for c in range(3):
        for q in range(sz.quarters):
            out[pl.ds(sz.gas + c * sz.blocks + q * layers, layers), :] = gas[c, :, q * BLOCK : (q + 1) * BLOCK]
    copies[2].wait()
    for q in range(sz.quarters):
        out[pl.ds(sz.pres + q * layers, layers), :] = pres[:, q * BLOCK : (q + 1) * BLOCK]
    for copy in copies[3:]:
        copy.wait()
    out[pl.ds(sz.size, sz.tiles), :] = size[...]
    out[pl.ds(sz.offset, sz.tiles), :] = offset[...].astype(F32)
    out[pl.ds(sz.meta, 1), pl.ds(0, sz.groups)] = block_row(sz, block[...]).astype(F32)
    width = radial.shape[1]
    lane = iota((1, width), 1)
    for slot in range(2):
        kept = jnp.where(lane < counts[0, 2 + slot], radial[slot : slot + 1, :], -1)
        out[pl.ds(sz.meta + 1 + slot, 1), pl.ds(0, width)] = kept.astype(F32)

    index = kinds[...] * (n_rad * sz.blocks) + block_row(sz, cols[...])
    aux[pl.ds(0, index.shape[0]), :] = jnp.concatenate([index, index], axis=1)
    lane = iota((1, axial.shape[1]), 1)
    kept = [jnp.where(lane < counts[0, slot], axial[slot : slot + 1, :], -1) for slot in range(2)]
    aux[pl.ds(8, 1), :] = jnp.concatenate(kept, axis=1)


def take_lanes(x, idx):
    return jnp.take_along_axis(x, idx, axis=1, mode="promise_in_bounds")


def pick(sz, state, idx):
    shape = (sz.tiles, BLOCK)
    idx = jnp.broadcast_to(idx, shape)
    lane = idx & (BLOCK - 1)
    here = (idx >> 7) == iota(shape, 0)
    return [jnp.sum(jnp.where(here, take_lanes(s, lane), 0.0), axis=0, keepdims=True) for s in state]


def slab_rows(sz, n_rad, G, first):
    return jnp.concatenate([G[d, pl.ds(first, sz.tiles), :] for d in range(n_rad)], axis=0)


def state_of(sz, T, state, d):
    first = pl.multiple_of(d * sz.tiles, sz.tiles)
    return [state[pl.ds(c * T + first, sz.tiles), :] for c in range(7)]


def move_kernel(sz, n_rad, G, aux, state, message, near):
    r = lax.axis_index("rad")
    layers, tiles, blocks, groups = sz.layers, sz.tiles, sz.blocks, sz.groups
    slab_blocks = n_rad * blocks
    T = n_rad * tiles

    block_rows = [G[d, pl.ds(sz.meta, 1), :] for d in range(n_rad)]
    column = jnp.concatenate(
        [jnp.transpose(jnp.broadcast_to(b, (BLOCK, BLOCK)))[:groups] for b in block_rows], axis=0
    ).astype(I32)
    lanes = iota((n_rad * groups, BLOCK), 1)
    chooser = jnp.concatenate(
        [(column == lanes + first).astype(F32).astype(BF16) for first in range(0, slab_blocks, BLOCK)], axis=1
    )
    gas_slab = jnp.concatenate(
        [
            jnp.concatenate([G[d, pl.ds(sz.gas + c * blocks, blocks), :] for d in range(n_rad)], axis=0)
            for c in range(3)
        ],
        axis=1,
    )
    high, low = split2(gas_slab)
    found = dot(chooser, high) + dot(chooser, low)
    for c in range(3):
        near[c] = found[:, c * BLOCK : (c + 1) * BLOCK]

    rows = functools.partial(slab_rows, sz, n_rad, G)
    size = rows(sz.size)
    offset = rows(sz.offset).astype(I32)
    factor = jnp.exp(-DRAG / (size * size))
    even = iota((T, BLOCK), 1) < GROUP
    for c in range(3):
        u_even = take_lanes(near[c, pl.ds(0, T, stride=2), :], offset)
        u_odd = take_lanes(near[c, pl.ds(1, T, stride=2), :], offset)
        u = jnp.where(even, u_even, u_odd)
        v = rows(sz.motion + (3 + c) * tiles)
        new = u + (v - u) * factor
        state[pl.ds(c * T, T), :] = rows(sz.motion + c * tiles) + STEP * new
        state[pl.ds((3 + c) * T, T), :] = new
    state[pl.ds(6 * T, T), :] = size

    payload = pick(sz, state_of(sz, T, state, r), aux[pl.ds(8, 1), :])
    for c in range(7):
        message[c : c + 1, :] = payload[c]
    message[7:8, :] = jnp.zeros((1, BLOCK), F32)
    for q in range(sz.quarters):
        first = sz.pres + q * layers
        message[8 + q : 9 + q, :] = G[r, pl.ds(first + layers - 1, 1), :]
        message[12 + q : 13 + q, :] = G[r, pl.ds(first, 1), :]


def rest_kernel(
    sz, n_rad, G, aux, table, state,
    motion_hbm, arr_hbm, gas_hbm, liquid_hbm, image,
    deps, spread, coup, motion_out, arr_rad, gas_out, liquid, sem,
):
    r = lax.axis_index("rad")
    sends = [
        pltpu.make_async_copy(src, dst, sem.at[i])
        for i, (src, dst) in enumerate(
            ((motion_out, motion_hbm), (arr_rad, arr_hbm), (gas_out, gas_hbm), (liquid, liquid_hbm))
        )
    ]
    layers, tiles, blocks, groups = sz.layers, sz.tiles, sz.blocks, sz.groups
    slab_blocks = n_rad * blocks
    T = n_rad * tiles
    block_rows = [G[d, pl.ds(sz.meta, 1), :] for d in range(n_rad)]

    mine = pl.multiple_of(r * tiles, tiles)
    for i in range(tiles):
        motion_out[:, i * BLOCK : (i + 1) * BLOCK] = state[pl.ds(mine + i, 6, stride=T), :]

    width = arr_rad.shape[2]
    for slot, exists, other in ((0, r > 0, jnp.maximum(r - 1, 0)), (1, r < n_rad - 1, jnp.minimum(r + 1, n_rad - 1))):
        idx = G[other, pl.ds(sz.meta + 1 + slot, 1), :].astype(I32)
        idx = jnp.where(exists, idx, -1)
        got = pick(sz, state_of(sz, T, state, other), idx)
        for c in range(7):
            arr_rad[c, slot : slot + 1, :] = got[c][:, :width]

    rows = functools.partial(slab_rows, sz, n_rad, G)
    size = rows(sz.size)
    mass = size * size * size
    dep = [-mass * (state[pl.ds((3 + c) * T, T), :] - rows(sz.motion + (3 + c) * tiles)) for c in range(3)] + [mass]
    even = iota((T, BLOCK), 1) < GROUP

    for c in range(4):
        high = dep[c].astype(BF16).astype(F32)
        low = dep[c] - high
        for piece, part in enumerate((high, low)):
            deps[pl.ds((piece * 8 + c) * T, T), :] = jnp.where(even, part, 0.0)
            deps[pl.ds((piece * 8 + 4 + c) * T, T), :] = jnp.where(even, 0.0, part)
    cell = iota((BLOCK, BLOCK), 0).astype(F32).astype(BF16)
    one, none = jnp.ones((BLOCK, BLOCK), BF16), jnp.zeros((BLOCK, BLOCK), BF16)
    for d in range(n_rad):
        for i in range(tiles):
            t = d * tiles + i
            off = jnp.broadcast_to(G[d, pl.ds(sz.offset + i, 1), :], (16, BLOCK)).astype(BF16)
            onehot = jnp.where(cell == jnp.concatenate([off] * (BLOCK // 16), axis=0), one, none)
            lhs = deps[pl.ds(t, 16, stride=T), :].astype(BF16)
            res = dot_nt(lhs, onehot)
            res = res[:8] + res[8:]
            spread[pl.ds(2 * t, 4, stride=2 * T), :] = res[:4]
            spread[pl.ds(2 * t + 1, 4, stride=2 * T), :] = res[4:]
    own = iota((blocks, groups), 0) + r * blocks
    adder = jnp.concatenate(
        [(own == b[:, :groups].astype(I32)).astype(F32) for b in block_rows], axis=1
    ).astype(BF16)
    for c in range(4):
        high, low = split2(spread[pl.ds(c * 2 * T, 2 * T), :])
        total = dot(adder, high) + dot(adder, low)
        for q in range(sz.quarters):
            part = total[q * layers : (q + 1) * layers]
            at = slice(q * BLOCK, (q + 1) * BLOCK)
            if c < 3:
                gas_out[c, :, at] = G[r, pl.ds(sz.gas + c * blocks + q * layers, layers), :] + part
            else:
                liquid[:, at] = part

    pres = jnp.concatenate([G[d, pl.ds(sz.pres, blocks), :] for d in range(n_rad)], axis=0)
    index = [jnp.broadcast_to(aux[pl.ds(k, 1), :], (BLOCK, BLOCK)).astype(jnp.int16) for k in range(4)]
    grouped = [None] * (NT // 2)
    for first in range(0, slab_blocks, BLOCK):
        p_high, p_low = split2(jnp.transpose(pres[first : first + BLOCK]))
        here = iota((BLOCK, BLOCK), 0) + first + jnp.where(iota((BLOCK, BLOCK), 1) < blocks, 0, slab_blocks)
        for j in range(NT // 2):
            aim = (here + 2 * j * slab_blocks).astype(jnp.int16)
            count = none
            for k in range(4):
                count = count + jnp.where(aim == index[k], one, none)
            part = dot(p_high, count) + dot(p_low, count)
            grouped[j] = part if grouped[j] is None else grouped[j] + part
    for send in sends:
        send.start()
    sums = [None, None]
    for j in range(NT // 2):
        g_high, g_low = split2(grouped[j])
        for s in range(2):
            t_high, t_low = split2(table[2 * j + s])
            part = dot(t_high, g_high) + dot(t_low, g_high) + dot(t_high, g_low)
            sums[s] = part if sums[s] is None else sums[s] + part
    both = jnp.where(iota((BLOCK, BLOCK), 1) < blocks, sums[0], sums[1])
    both = both + pltpu.roll(jnp.where(iota((BLOCK, BLOCK), 1) < blocks, 0.0, sums[1]), blocks, 1)
    coup[...] = jnp.transpose(both)
    layer = iota((layers, BLOCK), 0)
    for q in range(sz.quarters):
        p = G[r, pl.ds(sz.pres + q * layers, layers), :]
        below = jnp.where(layer == 0, 0.0, pltpu.roll(p, 1, 0))
        above = jnp.where(layer == layers - 1, 0.0, pltpu.roll(p, layers - 1, 0))
        image[:, q * BLOCK : (q + 1) * BLOCK] = (
            DIAG * p - above - below + coup[pl.ds(q, layers, stride=sz.quarters), :]
        )
    for send in sends:
        send.wait()


def finish_kernel(sz, n_ax, got_a, got_b, image, arr_ax, pressure_image):
    a = lax.axis_index("ax")
    even = a % 2 == 0
    low = jnp.where(a > 0, jnp.where(even, got_b[...], got_a[...]), 0.0)
    up = jnp.where(a < n_ax - 1, jnp.where(even, got_a[...], got_b[...]), 0.0)
    half = arr_ax.shape[2]
    arr_ax[:, 0, :] = low[0:7, 0:half]
    arr_ax[:, 1, :] = up[0:7, half : 2 * half]
    pressure_image[...] = image[...]
    last = sz.layers - 1
    for q in range(sz.quarters):
        at = slice(q * BLOCK, (q + 1) * BLOCK)
        pressure_image[0:1, at] = image[0:1, at] - low[8 + q : 9 + q, :]
        pressure_image[last : last + 1, at] = image[last : last + 1, at] - up[12 + q : 13 + q, :]


def on_device(
    parcel_motion,
    parcel_size,
    parcel_block,
    parcel_offset,
    gas_velocity,
    pressure,
    block_cols,
    block_kinds,
    block_table,
    send_axial,
    send_radial,
    send_counts,
):
    n_ax, n_rad = lax.axis_size("ax"), lax.axis_size("rad")
    layers, radial = pressure.shape
    parcels = parcel_size.shape[0]
    sz = Sizes(layers, radial, parcels)
    T = n_rad * sz.tiles
    cap_ax, cap_rad = send_axial.shape[-1], send_radial.shape[-1]
    params = pltpu.CompilerParams(vmem_limit_bytes=VMEM_LIMIT)
    counts = send_counts.reshape(1, 4)
    size2 = parcel_size.reshape(sz.tiles, BLOCK)
    offset2 = parcel_offset.reshape(sz.tiles, BLOCK)

    packed, aux = pl.pallas_call(
        functools.partial(pack_kernel, sz, n_rad),
        out_shape=[
            jax.ShapeDtypeStruct((sz.rows, BLOCK), F32),
            jax.ShapeDtypeStruct((16, BLOCK), I32),
        ],
        in_specs=[hbm] * 11,
        out_specs=[vmem] * 2,
        scratch_shapes=[
            pltpu.VMEM(parcel_motion.shape, F32),
            pltpu.VMEM(size2.shape, F32),
            pltpu.VMEM((1, sz.groups), I32),
            pltpu.VMEM(offset2.shape, I32),
            pltpu.VMEM(gas_velocity.shape, F32),
            pltpu.VMEM(pressure.shape, F32),
            pltpu.VMEM((2, cap_rad), I32),
            pltpu.SMEM((1, 4), I32),
            pltpu.VMEM((4, sz.blocks), I32),
            pltpu.VMEM((4, sz.blocks), I32),
            pltpu.VMEM((2, cap_ax), I32),
            pltpu.SemaphoreType.DMA((11,)),
        ],
        compiler_params=params,
        name="pack",
    )(
        *(
            pltpu.with_memory_space_constraint(x, pltpu.HBM)
            for x in (
                parcel_motion, size2, parcel_block.reshape(1, sz.groups), offset2, gas_velocity, pressure,
                send_radial.reshape(2, cap_rad), counts, block_cols[0].T, block_kinds[0].T,
                send_axial.reshape(2, cap_ax),
            )
        )
    )
    gathered = lax.all_gather(packed, "rad", axis=0)

    state, message = pl.pallas_call(
        functools.partial(move_kernel, sz, n_rad),
        out_shape=[
            jax.ShapeDtypeStruct((7 * T, BLOCK), F32),
            jax.ShapeDtypeStruct((16, BLOCK), F32),
        ],
        in_specs=[vmem] * 2,
        out_specs=[vmem] * 2,
        scratch_shapes=[pltpu.VMEM((3, n_rad * sz.groups, BLOCK), F32)],
        compiler_params=params,
        cost_estimate=pl.CostEstimate(flops=4_000_000_000, bytes_accessed=1_000_000, transcendentals=0),
        name="move",
    )(gathered, aux)

    def exchange(first):
        to = list(range(n_ax * n_rad))
        for low in range(first, n_ax - 1, 2):
            for r in range(n_rad):
                i, j = low * n_rad + r, (low + 1) * n_rad + r
                to[i], to[j] = j, i
        alone = [i for i in range(n_ax * n_rad) if to[i] == i]
        for i, j in zip(alone[0::2], alone[1::2]):
            to[i], to[j] = j, i
        return lax.ppermute(message, ("ax", "rad"), list(enumerate(to)))

    got_b = exchange(1)
    got_a = exchange(0)

    motion_out, arr_rad, gas_out, liquid, image = pl.pallas_call(
        functools.partial(rest_kernel, sz, n_rad),
        out_shape=[
            jax.ShapeDtypeStruct((6, parcels), F32),
            jax.ShapeDtypeStruct((7, 2, cap_rad), F32),
            jax.ShapeDtypeStruct(gas_velocity.shape, F32),
            jax.ShapeDtypeStruct(pressure.shape, F32),
            jax.ShapeDtypeStruct(pressure.shape, F32),
        ],
        in_specs=[vmem] * 4,
        out_specs=[hbm] * 4 + [vmem],
        scratch_shapes=[
            pltpu.VMEM((16 * T, BLOCK), F32),
            pltpu.VMEM((4 * 2 * T, BLOCK), F32),
            pltpu.VMEM((BLOCK, BLOCK), F32),
            pltpu.VMEM((6, parcels), F32),
            pltpu.VMEM((7, 2, cap_rad), F32),
            pltpu.VMEM(gas_velocity.shape, F32),
            pltpu.VMEM(pressure.shape, F32),
            pltpu.SemaphoreType.DMA((4,)),
        ],
        compiler_params=params,
        cost_estimate=pl.CostEstimate(flops=2_000_000_000, bytes_accessed=2_000_000, transcendentals=0),
        name="rest",
    )(gathered, aux, block_table, state)

    arr_ax, pressure_image = pl.pallas_call(
        functools.partial(finish_kernel, sz, n_ax),
        out_shape=[
            jax.ShapeDtypeStruct((7, 2, cap_ax), F32),
            jax.ShapeDtypeStruct(pressure.shape, F32),
        ],
        in_specs=[vmem] * 3,
        out_specs=[vmem] * 2,
        compiler_params=params,
        name="finish",
    )(got_a, got_b, image)

    arrivals_axial = arr_ax.transpose(1, 0, 2)[None, None]
    arrivals_radial = arr_rad.transpose(1, 0, 2)[None, None]
    return (motion_out, arrivals_axial, arrivals_radial, gas_out, liquid, pressure_image)


def solution(mesh):
    return jax.shard_map(
        on_device,
        mesh=mesh,
        in_specs=(
            P(None, ("ax", "rad")),
            P(("ax", "rad")),
            P(("ax", "rad")),
            P(("ax", "rad")),
            P(None, "ax", "rad"),
            P("ax", "rad"),
            P("ax", "rad", None),
            P("ax", "rad", None),
            P(),
            P("ax", "rad", None, None),
            P("ax", "rad", None, None),
            P("ax", "rad", None),
        ),
        out_specs=(
            P(None, ("ax", "rad")),
            P("ax", "rad", None, None, None),
            P("ax", "rad", None, None, None),
            P(None, "ax", "rad"),
            P("ax", "rad"),
            P("ax", "rad"),
        ),
        check_vma=False,
    )
```

```python
import functools

import jax
import jax.numpy as jnp
from jax import lax
from jax.experimental import pallas as pl
from jax.experimental.pallas import tpu as pltpu
from jax.sharding import PartitionSpec as P

BLOCK = 128
GROUP = 64
NT = 8
DRAG = 0.5
STEP = 0.5
DIAG = 6.0
VMEM_LIMIT = 24 * 1024 * 1024

F32 = jnp.float32
BF16 = jnp.bfloat16
I32 = jnp.int32

vmem = pl.BlockSpec(memory_space=pltpu.VMEM)
hbm = pl.BlockSpec(memory_space=pltpu.HBM)


class Sizes:
    def __init__(self, layers, radial, parcels):
        self.layers = layers
        self.quarters = radial // BLOCK
        self.blocks = layers * self.quarters
        self.tiles = parcels // BLOCK
        self.groups = parcels // GROUP
        self.gas = 0
        self.pres = 3 * self.blocks
        self.motion = self.pres + self.blocks
        self.size = self.motion + 6 * self.tiles
        self.offset = self.size + self.tiles
        self.meta = self.offset + self.tiles
        self.rows = self.meta + 8


def split2(x):
    high = x.astype(BF16)
    return high, (x - high.astype(F32)).astype(BF16)


def dot(a, b):
    return jnp.dot(a, b, preferred_element_type=F32)


def dot_nt(a, b):
    return lax.dot_general(a, b, (((1,), (1,)), ((), ())), preferred_element_type=F32)


def iota(shape, dim):
    return lax.broadcasted_iota(I32, shape, dim)


def block_row(sz, b):
    local = b % sz.blocks
    return b - local + (local % sz.quarters) * sz.layers + local // sz.quarters


def pack_kernel(
    sz, n_rad, motion_hbm, size_hbm, block_hbm, offset_hbm, gas_hbm, pres_hbm, radial_hbm, counts_hbm, cols_hbm,
    kinds_hbm, axial_hbm,
    out, aux,
    motion, size, block, offset, gas, pres, radial, counts, cols, kinds, axial, sem,
):
    pairs = (
        (motion_hbm, motion), *((gas_hbm.at[c], gas.at[c]) for c in range(3)), (pres_hbm, pres), (size_hbm, size),
        (offset_hbm, offset), (block_hbm, block), (counts_hbm, counts), (radial_hbm, radial), (axial_hbm, axial), (cols_hbm, cols),
        (kinds_hbm, kinds),
    )
    copies = [pltpu.make_async_copy(src, dst, sem.at[i]) for i, (src, dst) in enumerate(pairs)]
    for copy in copies:
        copy.start()
    out[pl.ds(sz.meta, 8), :] = jnp.full((8, BLOCK), -1.0, F32)
    layers = sz.layers
    copies[0].wait()
    for i in range(sz.tiles):
        out[pl.ds(sz.motion + i, 6, stride=sz.tiles), :] = motion[:, i * BLOCK : (i + 1) * BLOCK]
    for c in range(3):
        copies[1 + c].wait()
        for q in range(sz.quarters):
            out[pl.ds(sz.gas + c * sz.blocks + q * layers, layers), :] = gas[c, :, q * BLOCK : (q + 1) * BLOCK]
    copies[4].wait()
    for q in range(sz.quarters):
        out[pl.ds(sz.pres + q * layers, layers), :] = pres[:, q * BLOCK : (q + 1) * BLOCK]
    for copy in copies[5:]:
        copy.wait()
    out[pl.ds(sz.size, sz.tiles), :] = size[...]
    out[pl.ds(sz.offset, sz.tiles), :] = offset[...].astype(F32)
    out[pl.ds(sz.meta, 1), pl.ds(0, sz.groups)] = block_row(sz, block[...]).astype(F32)
    width = radial.shape[1]
    lane = iota((1, width), 1)
    for slot in range(2):
        kept = jnp.where(lane < counts[0, 2 + slot], radial[slot : slot + 1, :], -1)
        out[pl.ds(sz.meta + 1 + slot, 1), pl.ds(0, width)] = kept.astype(F32)

    index = kinds[...] * (n_rad * sz.blocks) + block_row(sz, cols[...])
    aux[pl.ds(0, index.shape[0]), :] = jnp.concatenate([index, index], axis=1)
    lane = iota((1, axial.shape[1]), 1)
    kept = [jnp.where(lane < counts[0, slot], axial[slot : slot + 1, :], -1) for slot in range(2)]
    aux[pl.ds(8, 1), :] = jnp.concatenate(kept, axis=1)


def take_lanes(x, idx):
    return jnp.take_along_axis(x, idx, axis=1, mode="promise_in_bounds")


def pick(sz, state, idx):
    shape = (sz.tiles, BLOCK)
    idx = jnp.broadcast_to(idx, shape)
    lane = idx & (BLOCK - 1)
    here = (idx >> 7) == iota(shape, 0)
    return [jnp.sum(jnp.where(here, take_lanes(s, lane), 0.0), axis=0, keepdims=True) for s in state]


def slab_rows(sz, n_rad, G, first):
    return jnp.concatenate([G[d, pl.ds(first, sz.tiles), :] for d in range(n_rad)], axis=0)


def state_of(sz, T, state, d):
    first = pl.multiple_of(d * sz.tiles, sz.tiles)
    return [state[pl.ds(c * T + first, sz.tiles), :] for c in range(7)]


def move_kernel(sz, n_rad, G, aux, state, message, near):
    r = lax.axis_index("rad")
    layers, tiles, blocks, groups = sz.layers, sz.tiles, sz.blocks, sz.groups
    slab_blocks = n_rad * blocks
    T = n_rad * tiles

    block_rows = [G[d, pl.ds(sz.meta, 1), :] for d in range(n_rad)]
    column = jnp.concatenate(
        [jnp.transpose(jnp.broadcast_to(b, (BLOCK, BLOCK)))[:groups] for b in block_rows], axis=0
    ).astype(I32)
    lanes = iota((n_rad * groups, BLOCK), 1)
    chooser = jnp.concatenate(
        [(column == lanes + first).astype(F32).astype(BF16) for first in range(0, slab_blocks, BLOCK)], axis=1
    )
    gas_slab = jnp.concatenate(
        [
            jnp.concatenate([G[d, pl.ds(sz.gas + c * blocks, blocks), :] for d in range(n_rad)], axis=0)
            for c in range(3)
        ],
        axis=1,
    )
    high, low = split2(gas_slab)
    found = dot(jnp.concatenate([chooser, chooser], axis=1), jnp.concatenate([high, low], axis=0))
    for c in range(3):
        near[c] = found[:, c * BLOCK : (c + 1) * BLOCK]

    rows = functools.partial(slab_rows, sz, n_rad, G)
    size = rows(sz.size)
    offset = rows(sz.offset).astype(I32)
    factor = jnp.exp(-DRAG / (size * size))
    even = iota((T, BLOCK), 1) < GROUP
    for c in range(3):
        u_even = take_lanes(near[c, pl.ds(0, T, stride=2), :], offset)
        u_odd = take_lanes(near[c, pl.ds(1, T, stride=2), :], offset)
        u = jnp.where(even, u_even, u_odd)
        v = rows(sz.motion + (3 + c) * tiles)
        new = u + (v - u) * factor
        state[pl.ds(c * T, T), :] = rows(sz.motion + c * tiles) + STEP * new
        state[pl.ds((3 + c) * T, T), :] = new
    state[pl.ds(6 * T, T), :] = size

    payload = pick(sz, state_of(sz, T, state, r), aux[pl.ds(8, 1), :])
    for c in range(7):
        message[c : c + 1, :] = payload[c]
    message[7:8, :] = jnp.zeros((1, BLOCK), F32)
    for q in range(sz.quarters):
        first = sz.pres + q * layers
        message[8 + q : 9 + q, :] = G[r, pl.ds(first + layers - 1, 1), :]
        message[12 + q : 13 + q, :] = G[r, pl.ds(first, 1), :]


def rest_kernel(
    sz, n_rad, G, aux, table, state,
    motion_hbm, arr_hbm, gas_hbm, liquid_hbm, image,
    deps, spread, coup, motion_out, arr_rad, gas_out, liquid, sem,
):
    r = lax.axis_index("rad")
    sends = [
        pltpu.make_async_copy(src, dst, sem.at[i])
        for i, (src, dst) in enumerate(
            ((motion_out, motion_hbm), (arr_rad, arr_hbm), (gas_out, gas_hbm), (liquid, liquid_hbm))
        )
    ]
    layers, tiles, blocks, groups = sz.layers, sz.tiles, sz.blocks, sz.groups
    slab_blocks = n_rad * blocks
    T = n_rad * tiles
    block_rows = [G[d, pl.ds(sz.meta, 1), :] for d in range(n_rad)]

    mine = pl.multiple_of(r * tiles, tiles)
    for i in range(tiles):
        motion_out[:, i * BLOCK : (i + 1) * BLOCK] = state[pl.ds(mine + i, 6, stride=T), :]

    width = arr_rad.shape[2]
    for slot, exists, other in ((0, r > 0, jnp.maximum(r - 1, 0)), (1, r < n_rad - 1, jnp.minimum(r + 1, n_rad - 1))):
        idx = G[other, pl.ds(sz.meta + 1 + slot, 1), :].astype(I32)
        idx = jnp.where(exists, idx, -1)
        got = pick(sz, state_of(sz, T, state, other), idx)
        for c in range(7):
            arr_rad[c, slot : slot + 1, :] = got[c][:, :width]

    rows = functools.partial(slab_rows, sz, n_rad, G)
    size = rows(sz.size)
    mass = size * size * size
    dep = [-mass * (state[pl.ds((3 + c) * T, T), :] - rows(sz.motion + (3 + c) * tiles)) for c in range(3)] + [mass]
    even = iota((T, BLOCK), 1) < GROUP

    for c in range(4):
        high = dep[c].astype(BF16).astype(F32)
        low = dep[c] - high
        for piece, part in enumerate((high, low)):
            deps[pl.ds((piece * 8 + c) * T, T), :] = jnp.where(even, part, 0.0)
            deps[pl.ds((piece * 8 + 4 + c) * T, T), :] = jnp.where(even, 0.0, part)
    cell = iota((BLOCK, BLOCK), 0).astype(F32).astype(BF16)
    one, none = jnp.ones((BLOCK, BLOCK), BF16), jnp.zeros((BLOCK, BLOCK), BF16)
    blank = jnp.zeros((16, BLOCK), BF16)
    for d in range(n_rad):
        for i in range(0, tiles, 2):
            onehot, lhs = [], []
            for t in (i, i + 1):
                off = jnp.broadcast_to(G[d, pl.ds(sz.offset + t, 1), :], (16, BLOCK)).astype(BF16)
                onehot.append(jnp.where(cell == jnp.concatenate([off] * (BLOCK // 16), axis=0), one, none))
                lhs.append(deps[pl.ds(d * tiles + t, 16, stride=T), :].astype(BF16))
            lhs = jnp.concatenate(
                [jnp.concatenate([lhs[0], blank], axis=1), jnp.concatenate([blank, lhs[1]], axis=1)], axis=0
            )
            res = dot_nt(lhs, jnp.concatenate(onehot, axis=1))
            for k in range(2):
                t = d * tiles + i + k
                both = res[16 * k : 16 * k + 8] + res[16 * k + 8 : 16 * k + 16]
                spread[pl.ds(2 * t, 4, stride=2 * T), :] = both[:4]
                spread[pl.ds(2 * t + 1, 4, stride=2 * T), :] = both[4:]
    own = iota((blocks, groups), 0) + r * blocks
    adder = jnp.concatenate(
        [(own == b[:, :groups].astype(I32)).astype(F32) for b in block_rows] * 2, axis=1
    ).astype(BF16)
    for c in range(4):
        high, low = split2(spread[pl.ds(c * 2 * T, 2 * T), :])
        total = dot(adder, jnp.concatenate([high, low], axis=0))
        for q in range(sz.quarters):
            part = total[q * layers : (q + 1) * layers]
            at = slice(q * BLOCK, (q + 1) * BLOCK)
            if c < 3:
                gas_out[c, :, at] = G[r, pl.ds(sz.gas + c * blocks + q * layers, layers), :] + part
            else:
                liquid[:, at] = part

    pres = jnp.concatenate([G[d, pl.ds(sz.pres, blocks), :] for d in range(n_rad)], axis=0)
    index = [jnp.broadcast_to(aux[pl.ds(k, 1), :], (BLOCK, BLOCK)).astype(jnp.int16) for k in range(4)]
    left, right = [], []
    for first in range(0, slab_blocks, BLOCK):
        p_high, p_low = split2(jnp.transpose(pres[first : first + BLOCK]))
        here = iota((BLOCK, BLOCK), 0) + first + jnp.where(iota((BLOCK, BLOCK), 1) < blocks, 0, slab_blocks)
        counts = []
        for j in range(NT // 2):
            aim = (here + 2 * j * slab_blocks).astype(jnp.int16)
            count = none
            for k in range(4):
                count = count + jnp.where(aim == index[k], one, none)
            counts.append(count)
        counts = jnp.concatenate(counts, axis=1)
        left += [p_high, p_low]
        right += [counts, counts]
    grouped = dot(jnp.concatenate(left, axis=1), jnp.concatenate(right, axis=0))
    for send in sends:
        send.start()
    g_high, g_low = split2(
        jnp.concatenate([grouped[:, j * BLOCK : (j + 1) * BLOCK] for j in range(NT // 2)], axis=0)
    )
    t_high, t_low = split2(
        jnp.concatenate(
            [jnp.concatenate([table[2 * j + s] for j in range(NT // 2)], axis=1) for s in range(2)], axis=0
        )
    )
    sums = dot(
        jnp.concatenate([t_high, t_low, t_high], axis=1), jnp.concatenate([g_high, g_high, g_low], axis=0)
    )
    sums = [sums[:BLOCK], sums[BLOCK:]]
    both = jnp.where(iota((BLOCK, BLOCK), 1) < blocks, sums[0], sums[1])
    both = both + pltpu.roll(jnp.where(iota((BLOCK, BLOCK), 1) < blocks, 0.0, sums[1]), blocks, 1)
    coup[...] = jnp.transpose(both)
    layer = iota((layers, BLOCK), 0)
    for q in range(sz.quarters):
        p = G[r, pl.ds(sz.pres + q * layers, layers), :]
        below = jnp.where(layer == 0, 0.0, pltpu.roll(p, 1, 0))
        above = jnp.where(layer == layers - 1, 0.0, pltpu.roll(p, layers - 1, 0))
        image[:, q * BLOCK : (q + 1) * BLOCK] = (
            DIAG * p - above - below + coup[pl.ds(q, layers, stride=sz.quarters), :]
        )
    for send in sends:
        send.wait()


def finish_kernel(sz, n_ax, got_a, got_b, image, arr_ax, pressure_image):
    a = lax.axis_index("ax")
    even = a % 2 == 0
    low = jnp.where(a > 0, jnp.where(even, got_b[...], got_a[...]), 0.0)
    up = jnp.where(a < n_ax - 1, jnp.where(even, got_a[...], got_b[...]), 0.0)
    half = arr_ax.shape[2]
    arr_ax[:, 0, :] = low[0:7, 0:half]
    arr_ax[:, 1, :] = up[0:7, half : 2 * half]
    pressure_image[...] = image[...]
    last = sz.layers - 1
    for q in range(sz.quarters):
        at = slice(q * BLOCK, (q + 1) * BLOCK)
        pressure_image[0:1, at] = image[0:1, at] - low[8 + q : 9 + q, :]
        pressure_image[last : last + 1, at] = image[last : last + 1, at] - up[12 + q : 13 + q, :]


def on_device(
    parcel_motion,
    parcel_size,
    parcel_block,
    parcel_offset,
    gas_velocity,
    pressure,
    block_cols,
    block_kinds,
    block_table,
    send_axial,
    send_radial,
    send_counts,
):
    n_ax, n_rad = lax.axis_size("ax"), lax.axis_size("rad")
    layers, radial = pressure.shape
    parcels = parcel_size.shape[0]
    sz = Sizes(layers, radial, parcels)
    T = n_rad * sz.tiles
    cap_ax, cap_rad = send_axial.shape[-1], send_radial.shape[-1]
    params = pltpu.CompilerParams(vmem_limit_bytes=VMEM_LIMIT)
    counts = send_counts.reshape(1, 4)
    size2 = parcel_size.reshape(sz.tiles, BLOCK)
    offset2 = parcel_offset.reshape(sz.tiles, BLOCK)

    packed, aux = pl.pallas_call(
        functools.partial(pack_kernel, sz, n_rad),
        out_shape=[
            jax.ShapeDtypeStruct((sz.rows, BLOCK), F32),
            jax.ShapeDtypeStruct((16, BLOCK), I32),
        ],
        in_specs=[hbm] * 11,
        out_specs=[vmem] * 2,
        scratch_shapes=[
            pltpu.VMEM(parcel_motion.shape, F32),
            pltpu.VMEM(size2.shape, F32),
            pltpu.VMEM((1, sz.groups), I32),
            pltpu.VMEM(offset2.shape, I32),
            pltpu.VMEM(gas_velocity.shape, F32),
            pltpu.VMEM(pressure.shape, F32),
            pltpu.VMEM((2, cap_rad), I32),
            pltpu.SMEM((1, 4), I32),
            pltpu.VMEM((4, sz.blocks), I32),
            pltpu.VMEM((4, sz.blocks), I32),
            pltpu.VMEM((2, cap_ax), I32),
            pltpu.SemaphoreType.DMA((13,)),
        ],
        compiler_params=params,
        name="pack",
    )(
        *(
            pltpu.with_memory_space_constraint(x, pltpu.HBM)
            for x in (
                parcel_motion, size2, parcel_block.reshape(1, sz.groups), offset2, gas_velocity, pressure,
                send_radial.reshape(2, cap_rad), counts, block_cols[0].T, block_kinds[0].T,
                send_axial.reshape(2, cap_ax),
            )
        )
    )
    gathered = lax.all_gather(packed, "rad", axis=0)

    state, message = pl.pallas_call(
        functools.partial(move_kernel, sz, n_rad),
        out_shape=[
            jax.ShapeDtypeStruct((7 * T, BLOCK), F32),
            jax.ShapeDtypeStruct((16, BLOCK), F32),
        ],
        in_specs=[vmem] * 2,
        out_specs=[vmem] * 2,
        scratch_shapes=[pltpu.VMEM((3, n_rad * sz.groups, BLOCK), F32)],
        compiler_params=params,
        cost_estimate=pl.CostEstimate(flops=4_000_000_000, bytes_accessed=1_000_000, transcendentals=0),
        name="move",
    )(gathered, aux)

    def exchange(first):
        to = list(range(n_ax * n_rad))
        for low in range(first, n_ax - 1, 2):
            for r in range(n_rad):
                i, j = low * n_rad + r, (low + 1) * n_rad + r
                to[i], to[j] = j, i
        alone = [i for i in range(n_ax * n_rad) if to[i] == i]
        for i, j in zip(alone[0::2], alone[1::2]):
            to[i], to[j] = j, i
        return lax.ppermute(message, ("ax", "rad"), list(enumerate(to)))

    got_b = exchange(1)
    got_a = exchange(0)

    motion_out, arr_rad, gas_out, liquid, image = pl.pallas_call(
        functools.partial(rest_kernel, sz, n_rad),
        out_shape=[
            jax.ShapeDtypeStruct((6, parcels), F32),
            jax.ShapeDtypeStruct((7, 2, cap_rad), F32),
            jax.ShapeDtypeStruct(gas_velocity.shape, F32),
            jax.ShapeDtypeStruct(pressure.shape, F32),
            jax.ShapeDtypeStruct(pressure.shape, F32),
        ],
        in_specs=[vmem] * 4,
        out_specs=[hbm] * 4 + [vmem],
        scratch_shapes=[
            pltpu.VMEM((16 * T, BLOCK), F32),
            pltpu.VMEM((4 * 2 * T, BLOCK), F32),
            pltpu.VMEM((BLOCK, BLOCK), F32),
            pltpu.VMEM((6, parcels), F32),
            pltpu.VMEM((7, 2, cap_rad), F32),
            pltpu.VMEM(gas_velocity.shape, F32),
            pltpu.VMEM(pressure.shape, F32),
            pltpu.SemaphoreType.DMA((4,)),
        ],
        compiler_params=params,
        cost_estimate=pl.CostEstimate(flops=2_000_000_000, bytes_accessed=2_000_000, transcendentals=0),
        name="rest",
    )(gathered, aux, block_table, state)

    arr_ax, pressure_image = pl.pallas_call(
        functools.partial(finish_kernel, sz, n_ax),
        out_shape=[
            jax.ShapeDtypeStruct((7, 2, cap_ax), F32),
            jax.ShapeDtypeStruct(pressure.shape, F32),
        ],
        in_specs=[vmem] * 3,
        out_specs=[vmem] * 2,
        compiler_params=params,
        name="finish",
    )(got_a, got_b, image)

    arrivals_axial = arr_ax.transpose(1, 0, 2)[None, None]
    arrivals_radial = arr_rad.transpose(1, 0, 2)[None, None]
    return (motion_out, arrivals_axial, arrivals_radial, gas_out, liquid, pressure_image)


def solution(mesh):
    return jax.shard_map(
        on_device,
        mesh=mesh,
        in_specs=(
            P(None, ("ax", "rad")),
            P(("ax", "rad")),
            P(("ax", "rad")),
            P(("ax", "rad")),
            P(None, "ax", "rad"),
            P("ax", "rad"),
            P("ax", "rad", None),
            P("ax", "rad", None),
            P(),
            P("ax", "rad", None, None),
            P("ax", "rad", None, None),
            P("ax", "rad", None),
        ),
        out_specs=(
            P(None, ("ax", "rad")),
            P("ax", "rad", None, None, None),
            P("ax", "rad", None, None, None),
            P(None, "ax", "rad"),
            P("ax", "rad"),
            P("ax", "rad"),
        ),
        check_vma=False,
    )
```

```python
import functools

import jax
import jax.numpy as jnp
from jax import lax
from jax.experimental import pallas as pl
from jax.experimental.pallas import tpu as pltpu
from jax.sharding import PartitionSpec as P

BLOCK = 128
GROUP = 64
NT = 8
DRAG = 0.5
STEP = 0.5
DIAG = 6.0
VMEM_LIMIT = 24 * 1024 * 1024

F32 = jnp.float32
BF16 = jnp.bfloat16
I32 = jnp.int32

vmem = pl.BlockSpec(memory_space=pltpu.VMEM)
hbm = pl.BlockSpec(memory_space=pltpu.HBM)


class Sizes:
    def __init__(self, layers, radial, parcels):
        self.layers = layers
        self.quarters = radial // BLOCK
        self.blocks = layers * self.quarters
        self.tiles = parcels // BLOCK
        self.groups = parcels // GROUP
        self.gas = 0
        self.pres = 3 * self.blocks
        self.motion = self.pres + self.blocks
        self.size = self.motion + 6 * self.tiles
        self.offset = self.size + self.tiles
        self.meta = self.offset + self.tiles
        self.rows = self.meta + 8


def split2(x):
    high = x.astype(BF16)
    return high, (x - high.astype(F32)).astype(BF16)


def dot(a, b):
    return jnp.dot(a, b, preferred_element_type=F32)


def dot_nt(a, b):
    return lax.dot_general(a, b, (((1,), (1,)), ((), ())), preferred_element_type=F32)


def iota(shape, dim):
    return lax.broadcasted_iota(I32, shape, dim)


def block_row(sz, b):
    local = b % sz.blocks
    return b - local + (local % sz.quarters) * sz.layers + local // sz.quarters


def pack_kernel(
    sz, n_rad, motion_hbm, size_hbm, block_hbm, offset_hbm, gas_hbm, pres_hbm, radial_hbm, counts_hbm, cols_hbm,
    kinds_hbm, axial_hbm,
    out, aux,
    motion, size, block, offset, gas, pres, radial, counts, cols, kinds, axial, sem,
):
    small = (
        (counts_hbm, counts), (block_hbm, block), (radial_hbm, radial), (axial_hbm, axial), (cols_hbm, cols),
        (kinds_hbm, kinds), (offset_hbm, offset), (size_hbm, size),
    )
    large = ((motion_hbm, motion), (pres_hbm, pres), *((gas_hbm.at[c], gas.at[c]) for c in range(3)))
    copies = [pltpu.make_async_copy(src, dst, sem.at[i]) for i, (src, dst) in enumerate(small + large)]
    for copy in copies:
        copy.start()
    out[pl.ds(sz.meta, 8), :] = jnp.full((8, BLOCK), -1.0, F32)
    layers = sz.layers
    for copy in copies[: len(small)]:
        copy.wait()
    out[pl.ds(sz.size, sz.tiles), :] = size[...]
    out[pl.ds(sz.offset, sz.tiles), :] = offset[...].astype(F32)
    out[pl.ds(sz.meta, 1), pl.ds(0, sz.groups)] = block_row(sz, block[...]).astype(F32)
    width = radial.shape[1]
    lane = iota((1, width), 1)
    for slot in range(2):
        kept = jnp.where(lane < counts[0, 2 + slot], radial[slot : slot + 1, :], -1)
        out[pl.ds(sz.meta + 1 + slot, 1), pl.ds(0, width)] = kept.astype(F32)
    index = kinds[...] * (n_rad * sz.blocks) + block_row(sz, cols[...])
    aux[pl.ds(0, index.shape[0]), :] = jnp.concatenate([index, index], axis=1)
    lane = iota((1, axial.shape[1]), 1)
    kept = [jnp.where(lane < counts[0, slot], axial[slot : slot + 1, :], -1) for slot in range(2)]
    aux[pl.ds(8, 1), :] = jnp.concatenate(kept, axis=1)
    motion_copy, pres_copy, *gas_copies = copies[len(small) :]
    motion_copy.wait()
    for i in range(sz.tiles):
        out[pl.ds(sz.motion + i, 6, stride=sz.tiles), :] = motion[:, i * BLOCK : (i + 1) * BLOCK]
    pres_copy.wait()
    for q in range(sz.quarters):
        out[pl.ds(sz.pres + q * layers, layers), :] = pres[:, q * BLOCK : (q + 1) * BLOCK]
    for c in range(3):
        gas_copies[c].wait()
        for q in range(sz.quarters):
            out[pl.ds(sz.gas + c * sz.blocks + q * layers, layers), :] = gas[c, :, q * BLOCK : (q + 1) * BLOCK]


def take_lanes(x, idx):
    return jnp.take_along_axis(x, idx, axis=1, mode="promise_in_bounds")


def pick(sz, state, idx):
    shape = (sz.tiles, BLOCK)
    idx = jnp.broadcast_to(idx, shape)
    lane = idx & (BLOCK - 1)
    here = (idx >> 7) == iota(shape, 0)
    return [jnp.sum(jnp.where(here, take_lanes(s, lane), 0.0), axis=0, keepdims=True) for s in state]


def slab_rows(sz, n_rad, G, first):
    return jnp.concatenate([G[d, pl.ds(first, sz.tiles), :] for d in range(n_rad)], axis=0)


def state_of(sz, T, state, d):
    first = pl.multiple_of(d * sz.tiles, sz.tiles)
    return [state[pl.ds(c * T + first, sz.tiles), :] for c in range(7)]


def move_kernel(sz, n_rad, G, aux, state, message, near):
    r = lax.axis_index("rad")
    layers, tiles, blocks, groups = sz.layers, sz.tiles, sz.blocks, sz.groups
    slab_blocks = n_rad * blocks
    T = n_rad * tiles

    block_rows = [G[d, pl.ds(sz.meta, 1), :] for d in range(n_rad)]
    column = jnp.concatenate(
        [jnp.transpose(jnp.broadcast_to(b, (BLOCK, BLOCK)))[:groups] for b in block_rows], axis=0
    ).astype(I32)
    lanes = iota((n_rad * groups, BLOCK), 1)
    chooser = jnp.concatenate(
        [(column == lanes + first).astype(F32).astype(BF16) for first in range(0, slab_blocks, BLOCK)], axis=1
    )
    gas_slab = jnp.concatenate(
        [
            jnp.concatenate([G[d, pl.ds(sz.gas + c * blocks, blocks), :] for d in range(n_rad)], axis=0)
            for c in range(3)
        ],
        axis=1,
    )
    high, low = split2(gas_slab)
    found = dot(jnp.concatenate([chooser, chooser], axis=1), jnp.concatenate([high, low], axis=0))
    for c in range(3):
        near[c] = found[:, c * BLOCK : (c + 1) * BLOCK]

    rows = functools.partial(slab_rows, sz, n_rad, G)
    size = rows(sz.size)
    offset = rows(sz.offset).astype(I32)
    factor = jnp.exp(-DRAG / (size * size))
    even = iota((T, BLOCK), 1) < GROUP
    for c in range(3):
        u_even = take_lanes(near[c, pl.ds(0, T, stride=2), :], offset)
        u_odd = take_lanes(near[c, pl.ds(1, T, stride=2), :], offset)
        u = jnp.where(even, u_even, u_odd)
        v = rows(sz.motion + (3 + c) * tiles)
        new = u + (v - u) * factor
        state[pl.ds(c * T, T), :] = rows(sz.motion + c * tiles) + STEP * new
        state[pl.ds((3 + c) * T, T), :] = new
    state[pl.ds(6 * T, T), :] = size

    payload = pick(sz, state_of(sz, T, state, r), aux[pl.ds(8, 1), :])
    for c in range(7):
        message[c : c + 1, :] = payload[c]
    message[7:8, :] = jnp.zeros((1, BLOCK), F32)
    for q in range(sz.quarters):
        first = sz.pres + q * layers
        message[8 + q : 9 + q, :] = G[r, pl.ds(first + layers - 1, 1), :]
        message[12 + q : 13 + q, :] = G[r, pl.ds(first, 1), :]


def rest_kernel(
    sz, n_rad, G, aux, table, state,
    motion_hbm, arr_hbm, gas_hbm, liquid_hbm, image,
    deps, spread, coup, motion_out, arr_rad, gas_out, liquid, sem,
):
    r = lax.axis_index("rad")
    sends = [
        pltpu.make_async_copy(src, dst, sem.at[i])
        for i, (src, dst) in enumerate(
            (
                (motion_out, motion_hbm), (arr_rad, arr_hbm), *((gas_out.at[c], gas_hbm.at[c]) for c in range(3)),
                (liquid, liquid_hbm),
            )
        )
    ]
    layers, tiles, blocks, groups = sz.layers, sz.tiles, sz.blocks, sz.groups
    slab_blocks = n_rad * blocks
    T = n_rad * tiles
    block_rows = [G[d, pl.ds(sz.meta, 1), :] for d in range(n_rad)]

    rows = functools.partial(slab_rows, sz, n_rad, G)
    size = rows(sz.size)
    mass = size * size * size
    dep = [-mass * (state[pl.ds((3 + c) * T, T), :] - rows(sz.motion + (3 + c) * tiles)) for c in range(3)] + [mass]
    even = iota((T, BLOCK), 1) < GROUP

    for c in range(4):
        high = dep[c].astype(BF16).astype(F32)
        low = dep[c] - high
        for piece, part in enumerate((high, low)):
            deps[pl.ds((piece * 8 + c) * T, T), :] = jnp.where(even, part, 0.0)
            deps[pl.ds((piece * 8 + 4 + c) * T, T), :] = jnp.where(even, 0.0, part)
    cell = iota((BLOCK, BLOCK), 0).astype(F32).astype(BF16)
    one, none = jnp.ones((BLOCK, BLOCK), BF16), jnp.zeros((BLOCK, BLOCK), BF16)
    blank = jnp.zeros((16, BLOCK), BF16)
    for d in range(n_rad):
        for i in range(0, tiles, 2):
            onehot, lhs = [], []
            for t in (i, i + 1):
                off = jnp.broadcast_to(G[d, pl.ds(sz.offset + t, 1), :], (16, BLOCK)).astype(BF16)
                onehot.append(jnp.where(cell == jnp.concatenate([off] * (BLOCK // 16), axis=0), one, none))
                lhs.append(deps[pl.ds(d * tiles + t, 16, stride=T), :].astype(BF16))
            lhs = jnp.concatenate(
                [jnp.concatenate([lhs[0], blank], axis=1), jnp.concatenate([blank, lhs[1]], axis=1)], axis=0
            )
            res = dot_nt(lhs, jnp.concatenate(onehot, axis=1))
            for k in range(2):
                t = d * tiles + i + k
                both = res[16 * k : 16 * k + 8] + res[16 * k + 8 : 16 * k + 16]
                spread[pl.ds(2 * t, 4, stride=2 * T), :] = both[:4]
                spread[pl.ds(2 * t + 1, 4, stride=2 * T), :] = both[4:]
    own = iota((blocks, groups), 0) + r * blocks
    adder = jnp.concatenate(
        [(own == b[:, :groups].astype(I32)).astype(F32) for b in block_rows] * 2, axis=1
    ).astype(BF16)
    for c in range(4):
        high, low = split2(spread[pl.ds(c * 2 * T, 2 * T), :])
        total = dot(adder, jnp.concatenate([high, low], axis=0))
        for q in range(sz.quarters):
            part = total[q * layers : (q + 1) * layers]
            at = slice(q * BLOCK, (q + 1) * BLOCK)
            if c < 3:
                gas_out[c, :, at] = G[r, pl.ds(sz.gas + c * blocks + q * layers, layers), :] + part
            else:
                liquid[:, at] = part
    for send in sends[2:]:
        send.start()

    pres = jnp.concatenate([G[d, pl.ds(sz.pres, blocks), :] for d in range(n_rad)], axis=0)
    index = [jnp.broadcast_to(aux[pl.ds(k, 1), :], (BLOCK, BLOCK)).astype(jnp.int16) for k in range(4)]
    left, right = [], []
    for first in range(0, slab_blocks, BLOCK):
        p_high, p_low = split2(jnp.transpose(pres[first : first + BLOCK]))
        here = iota((BLOCK, BLOCK), 0) + first + jnp.where(iota((BLOCK, BLOCK), 1) < blocks, 0, slab_blocks)
        counts = []
        for j in range(NT // 2):
            aim = (here + 2 * j * slab_blocks).astype(jnp.int16)
            count = none
            for k in range(4):
                count = count + jnp.where(aim == index[k], one, none)
            counts.append(count)
        counts = jnp.concatenate(counts, axis=1)
        left += [p_high, p_low]
        right += [counts, counts]
    grouped = dot(jnp.concatenate(left, axis=1), jnp.concatenate(right, axis=0))
    mine = pl.multiple_of(r * tiles, tiles)
    for i in range(tiles):
        motion_out[:, i * BLOCK : (i + 1) * BLOCK] = state[pl.ds(mine + i, 6, stride=T), :]
    sends[0].start()
    width = arr_rad.shape[2]
    for slot, exists, other in ((0, r > 0, jnp.maximum(r - 1, 0)), (1, r < n_rad - 1, jnp.minimum(r + 1, n_rad - 1))):
        idx = G[other, pl.ds(sz.meta + 1 + slot, 1), :].astype(I32)
        idx = jnp.where(exists, idx, -1)
        got = pick(sz, state_of(sz, T, state, other), idx)
        for c in range(7):
            arr_rad[c, slot : slot + 1, :] = got[c][:, :width]
    sends[1].start()

    g_high, g_low = split2(
        jnp.concatenate([grouped[:, j * BLOCK : (j + 1) * BLOCK] for j in range(NT // 2)], axis=0)
    )
    t_high, t_low = split2(
        jnp.concatenate(
            [jnp.concatenate([table[2 * j + s] for j in range(NT // 2)], axis=1) for s in range(2)], axis=0
        )
    )
    sums = dot(
        jnp.concatenate([t_high, t_low, t_high], axis=1), jnp.concatenate([g_high, g_high, g_low], axis=0)
    )
    sums = [sums[:BLOCK], sums[BLOCK:]]
    both = jnp.where(iota((BLOCK, BLOCK), 1) < blocks, sums[0], sums[1])
    both = both + pltpu.roll(jnp.where(iota((BLOCK, BLOCK), 1) < blocks, 0.0, sums[1]), blocks, 1)
    coup[...] = jnp.transpose(both)
    layer = iota((layers, BLOCK), 0)
    for q in range(sz.quarters):
        p = G[r, pl.ds(sz.pres + q * layers, layers), :]
        below = jnp.where(layer == 0, 0.0, pltpu.roll(p, 1, 0))
        above = jnp.where(layer == layers - 1, 0.0, pltpu.roll(p, layers - 1, 0))
        image[:, q * BLOCK : (q + 1) * BLOCK] = (
            DIAG * p - above - below + coup[pl.ds(q, layers, stride=sz.quarters), :]
        )
    for send in sends:
        send.wait()


def finish_kernel(sz, n_ax, got_a, got_b, image, arr_ax, pressure_image):
    a = lax.axis_index("ax")
    even = a % 2 == 0
    low = jnp.where(a > 0, jnp.where(even, got_b[...], got_a[...]), 0.0)
    up = jnp.where(a < n_ax - 1, jnp.where(even, got_a[...], got_b[...]), 0.0)
    half = arr_ax.shape[2]
    arr_ax[:, 0, :] = low[0:7, 0:half]
    arr_ax[:, 1, :] = up[0:7, half : 2 * half]
    pressure_image[...] = image[...]
    last = sz.layers - 1
    for q in range(sz.quarters):
        at = slice(q * BLOCK, (q + 1) * BLOCK)
        pressure_image[0:1, at] = image[0:1, at] - low[8 + q : 9 + q, :]
        pressure_image[last : last + 1, at] = image[last : last + 1, at] - up[12 + q : 13 + q, :]


def on_device(
    parcel_motion,
    parcel_size,
    parcel_block,
    parcel_offset,
    gas_velocity,
    pressure,
    block_cols,
    block_kinds,
    block_table,
    send_axial,
    send_radial,
    send_counts,
):
    n_ax, n_rad = lax.axis_size("ax"), lax.axis_size("rad")
    layers, radial = pressure.shape
    parcels = parcel_size.shape[0]
    sz = Sizes(layers, radial, parcels)
    T = n_rad * sz.tiles
    cap_ax, cap_rad = send_axial.shape[-1], send_radial.shape[-1]
    params = pltpu.CompilerParams(vmem_limit_bytes=VMEM_LIMIT)
    counts = send_counts.reshape(1, 4)
    size2 = parcel_size.reshape(sz.tiles, BLOCK)
    offset2 = parcel_offset.reshape(sz.tiles, BLOCK)

    packed, aux = pl.pallas_call(
        functools.partial(pack_kernel, sz, n_rad),
        out_shape=[
            jax.ShapeDtypeStruct((sz.rows, BLOCK), F32),
            jax.ShapeDtypeStruct((16, BLOCK), I32),
        ],
        in_specs=[hbm] * 11,
        out_specs=[vmem] * 2,
        scratch_shapes=[
            pltpu.VMEM(parcel_motion.shape, F32),
            pltpu.VMEM(size2.shape, F32),
            pltpu.VMEM((1, sz.groups), I32),
            pltpu.VMEM(offset2.shape, I32),
            pltpu.VMEM(gas_velocity.shape, F32),
            pltpu.VMEM(pressure.shape, F32),
            pltpu.VMEM((2, cap_rad), I32),
            pltpu.SMEM((1, 4), I32),
            pltpu.VMEM((4, sz.blocks), I32),
            pltpu.VMEM((4, sz.blocks), I32),
            pltpu.VMEM((2, cap_ax), I32),
            pltpu.SemaphoreType.DMA((13,)),
        ],
        compiler_params=params,
        name="pack",
    )(
        *(
            pltpu.with_memory_space_constraint(x, pltpu.HBM)
            for x in (
                parcel_motion, size2, parcel_block.reshape(1, sz.groups), offset2, gas_velocity, pressure,
                send_radial.reshape(2, cap_rad), counts, block_cols[0].T, block_kinds[0].T,
                send_axial.reshape(2, cap_ax),
            )
        )
    )
    gathered = lax.all_gather(packed, "rad", axis=0)

    state, message = pl.pallas_call(
        functools.partial(move_kernel, sz, n_rad),
        out_shape=[
            jax.ShapeDtypeStruct((7 * T, BLOCK), F32),
            jax.ShapeDtypeStruct((16, BLOCK), F32),
        ],
        in_specs=[vmem] * 2,
        out_specs=[vmem] * 2,
        scratch_shapes=[pltpu.VMEM((3, n_rad * sz.groups, BLOCK), F32)],
        compiler_params=params,
        cost_estimate=pl.CostEstimate(flops=4_000_000_000, bytes_accessed=1_000_000, transcendentals=0),
        name="move",
    )(gathered, aux)

    def exchange(first):
        to = list(range(n_ax * n_rad))
        for low in range(first, n_ax - 1, 2):
            for r in range(n_rad):
                i, j = low * n_rad + r, (low + 1) * n_rad + r
                to[i], to[j] = j, i
        alone = [i for i in range(n_ax * n_rad) if to[i] == i]
        for i, j in zip(alone[0::2], alone[1::2]):
            to[i], to[j] = j, i
        return lax.ppermute(message, ("ax", "rad"), list(enumerate(to)))

    got_b = exchange(1)
    got_a = exchange(0)

    motion_out, arr_rad, gas_out, liquid, image = pl.pallas_call(
        functools.partial(rest_kernel, sz, n_rad),
        out_shape=[
            jax.ShapeDtypeStruct((6, parcels), F32),
            jax.ShapeDtypeStruct((7, 2, cap_rad), F32),
            jax.ShapeDtypeStruct(gas_velocity.shape, F32),
            jax.ShapeDtypeStruct(pressure.shape, F32),
            jax.ShapeDtypeStruct(pressure.shape, F32),
        ],
        in_specs=[vmem] * 4,
        out_specs=[hbm] * 4 + [vmem],
        scratch_shapes=[
            pltpu.VMEM((16 * T, BLOCK), F32),
            pltpu.VMEM((4 * 2 * T, BLOCK), F32),
            pltpu.VMEM((BLOCK, BLOCK), F32),
            pltpu.VMEM((6, parcels), F32),
            pltpu.VMEM((7, 2, cap_rad), F32),
            pltpu.VMEM(gas_velocity.shape, F32),
            pltpu.VMEM(pressure.shape, F32),
            pltpu.SemaphoreType.DMA((6,)),
        ],
        compiler_params=params,
        cost_estimate=pl.CostEstimate(flops=2_000_000_000, bytes_accessed=2_000_000, transcendentals=0),
        name="rest",
    )(gathered, aux, block_table, state)

    arr_ax, pressure_image = pl.pallas_call(
        functools.partial(finish_kernel, sz, n_ax),
        out_shape=[
            jax.ShapeDtypeStruct((7, 2, cap_ax), F32),
            jax.ShapeDtypeStruct(pressure.shape, F32),
        ],
        in_specs=[vmem] * 3,
        out_specs=[vmem] * 2,
        compiler_params=params,
        name="finish",
    )(got_a, got_b, image)

    arrivals_axial = arr_ax.transpose(1, 0, 2)[None, None]
    arrivals_radial = arr_rad.transpose(1, 0, 2)[None, None]
    return (motion_out, arrivals_axial, arrivals_radial, gas_out, liquid, pressure_image)


def solution(mesh):
    return jax.shard_map(
        on_device,
        mesh=mesh,
        in_specs=(
            P(None, ("ax", "rad")),
            P(("ax", "rad")),
            P(("ax", "rad")),
            P(("ax", "rad")),
            P(None, "ax", "rad"),
            P("ax", "rad"),
            P("ax", "rad", None),
            P("ax", "rad", None),
            P(),
            P("ax", "rad", None, None),
            P("ax", "rad", None, None),
            P("ax", "rad", None),
        ),
        out_specs=(
            P(None, ("ax", "rad")),
            P("ax", "rad", None, None, None),
            P("ax", "rad", None, None, None),
            P(None, "ax", "rad"),
            P("ax", "rad"),
            P("ax", "rad"),
        ),
        check_vma=False,
    )
```

```python
import functools

import jax
import jax.numpy as jnp
from jax import lax
from jax.experimental import pallas as pl
from jax.experimental.pallas import tpu as pltpu
from jax.sharding import PartitionSpec as P

BLOCK = 128
GROUP = 64
NT = 8
DRAG = 0.5
STEP = 0.5
DIAG = 6.0
VMEM_LIMIT = 24 * 1024 * 1024

F32 = jnp.float32
BF16 = jnp.bfloat16
I32 = jnp.int32

vmem = pl.BlockSpec(memory_space=pltpu.VMEM)
hbm = pl.BlockSpec(memory_space=pltpu.HBM)


class Sizes:
    def __init__(self, layers, radial, parcels):
        self.layers = layers
        self.quarters = radial // BLOCK
        self.blocks = layers * self.quarters
        self.tiles = parcels // BLOCK
        self.groups = parcels // GROUP
        self.gas = 0
        self.pres = 3 * self.blocks
        self.motion = self.pres + self.blocks
        self.size = self.motion + 6 * self.tiles
        self.offset = self.size + self.tiles
        self.meta = self.offset + self.tiles
        self.column = self.meta + 8
        self.rows = self.column + self.groups


def split2(x):
    high = x.astype(BF16)
    return high, (x - high.astype(F32)).astype(BF16)


def dot(a, b):
    return jnp.dot(a, b, preferred_element_type=F32)


def dot_nt(a, b):
    return lax.dot_general(a, b, (((1,), (1,)), ((), ())), preferred_element_type=F32)


def iota(shape, dim):
    return lax.broadcasted_iota(I32, shape, dim)


def block_row(sz, b):
    local = b % sz.blocks
    return b - local + (local % sz.quarters) * sz.layers + local // sz.quarters


def pack_kernel(
    sz, n_rad, motion_hbm, size_hbm, block_hbm, offset_hbm, gas_hbm, pres_hbm, radial_hbm, counts_hbm, cols_hbm,
    kinds_hbm, axial_hbm,
    out, aux,
    motion, size, block, offset, gas, pres, radial, counts, cols, kinds, axial, sem,
):
    small = (
        (counts_hbm, counts), (block_hbm, block), (radial_hbm, radial), (axial_hbm, axial), (cols_hbm, cols),
        (kinds_hbm, kinds), (offset_hbm, offset), (size_hbm, size),
    )
    large = ((motion_hbm, motion), (pres_hbm, pres), *((gas_hbm.at[c], gas.at[c]) for c in range(3)))
    copies = [pltpu.make_async_copy(src, dst, sem.at[i]) for i, (src, dst) in enumerate(small + large)]
    for copy in copies:
        copy.start()
    out[pl.ds(sz.meta, 8), :] = jnp.full((8, BLOCK), -1.0, F32)
    layers = sz.layers
    for copy in copies[: len(small)]:
        copy.wait()
    out[pl.ds(sz.size, sz.tiles), :] = size[...]
    out[pl.ds(sz.offset, sz.tiles), :] = offset[...].astype(F32)
    numbers = block_row(sz, block[...]).astype(F32)
    out[pl.ds(sz.meta, 1), pl.ds(0, sz.groups)] = numbers
    numbers = jnp.concatenate([numbers, jnp.zeros((1, BLOCK - sz.groups), F32)], axis=1)
    out[pl.ds(sz.column, sz.groups), :] = jnp.transpose(jnp.broadcast_to(numbers, (BLOCK, BLOCK)))[: sz.groups]
    width = radial.shape[1]
    lane = iota((1, width), 1)
    for slot in range(2):
        kept = jnp.where(lane < counts[0, 2 + slot], radial[slot : slot + 1, :], -1)
        out[pl.ds(sz.meta + 1 + slot, 1), pl.ds(0, width)] = kept.astype(F32)
    index = kinds[...] * (n_rad * sz.blocks) + block_row(sz, cols[...])
    index = jnp.concatenate([index, index], axis=1).astype(F32)
    index = jnp.concatenate([index, jnp.zeros((BLOCK - index.shape[0], BLOCK), F32)], axis=0)
    aux[pl.ds(8, sz.blocks), :] = jnp.transpose(index)[: sz.blocks].astype(I32)
    lane = iota((1, axial.shape[1]), 1)
    kept = [jnp.where(lane < counts[0, slot], axial[slot : slot + 1, :], -1) for slot in range(2)]
    aux[pl.ds(0, 1), :] = jnp.concatenate(kept, axis=1)
    motion_copy, pres_copy, *gas_copies = copies[len(small) :]
    motion_copy.wait()
    for i in range(sz.tiles):
        out[pl.ds(sz.motion + i, 6, stride=sz.tiles), :] = motion[:, i * BLOCK : (i + 1) * BLOCK]
    pres_copy.wait()
    for q in range(sz.quarters):
        out[pl.ds(sz.pres + q * layers, layers), :] = pres[:, q * BLOCK : (q + 1) * BLOCK]
    for c in range(3):
        gas_copies[c].wait()
        for q in range(sz.quarters):
            out[pl.ds(sz.gas + c * sz.blocks + q * layers, layers), :] = gas[c, :, q * BLOCK : (q + 1) * BLOCK]


def take_lanes(x, idx):
    return jnp.take_along_axis(x, idx, axis=1, mode="promise_in_bounds")


def pick(sz, state, idx):
    shape = (sz.tiles, BLOCK)
    idx = jnp.broadcast_to(idx, shape)
    lane = idx & (BLOCK - 1)
    here = (idx >> 7) == iota(shape, 0)
    return [jnp.sum(jnp.where(here, take_lanes(s, lane), 0.0), axis=0, keepdims=True) for s in state]


def slab_rows(sz, n_rad, G, first):
    return jnp.concatenate([G[d, pl.ds(first, sz.tiles), :] for d in range(n_rad)], axis=0)


def state_of(sz, T, state, d):
    first = pl.multiple_of(d * sz.tiles, sz.tiles)
    return [state[pl.ds(c * T + first, sz.tiles), :] for c in range(7)]


def move_kernel(sz, n_rad, G, aux, state, message, near):
    r = lax.axis_index("rad")
    layers, tiles, blocks, groups = sz.layers, sz.tiles, sz.blocks, sz.groups
    slab_blocks = n_rad * blocks
    T = n_rad * tiles

    column = jnp.concatenate([G[d, pl.ds(sz.column, groups), :] for d in range(n_rad)], axis=0).astype(I32)
    lanes = iota((n_rad * groups, BLOCK), 1)
    chooser = jnp.concatenate(
        [(column == lanes + first).astype(F32).astype(BF16) for first in range(0, slab_blocks, BLOCK)], axis=1
    )
    gas_slab = jnp.concatenate(
        [
            jnp.concatenate([G[d, pl.ds(sz.gas + c * blocks, blocks), :] for d in range(n_rad)], axis=0)
            for c in range(3)
        ],
        axis=1,
    )
    high, low = split2(gas_slab)
    found = dot(jnp.concatenate([chooser, chooser], axis=1), jnp.concatenate([high, low], axis=0))
    for c in range(3):
        near[c] = found[:, c * BLOCK : (c + 1) * BLOCK]

    rows = functools.partial(slab_rows, sz, n_rad, G)
    size = rows(sz.size)
    offset = rows(sz.offset).astype(I32)
    factor = jnp.exp(-DRAG / (size * size))
    even = iota((T, BLOCK), 1) < GROUP
    for c in range(3):
        u_even = take_lanes(near[c, pl.ds(0, T, stride=2), :], offset)
        u_odd = take_lanes(near[c, pl.ds(1, T, stride=2), :], offset)
        u = jnp.where(even, u_even, u_odd)
        v = rows(sz.motion + (3 + c) * tiles)
        new = u + (v - u) * factor
        state[pl.ds(c * T, T), :] = rows(sz.motion + c * tiles) + STEP * new
        state[pl.ds((3 + c) * T, T), :] = new
    state[pl.ds(6 * T, T), :] = size

    payload = pick(sz, state_of(sz, T, state, r), aux[pl.ds(0, 1), :])
    for c in range(7):
        message[c : c + 1, :] = payload[c]
    message[7:8, :] = jnp.zeros((1, BLOCK), F32)
    for q in range(sz.quarters):
        first = sz.pres + q * layers
        message[8 + q : 9 + q, :] = G[r, pl.ds(first + layers - 1, 1), :]
        message[12 + q : 13 + q, :] = G[r, pl.ds(first, 1), :]


def rest_kernel(
    sz, n_rad, G, aux, table, state,
    motion_hbm, arr_hbm, gas_hbm, liquid_hbm, image,
    deps, spread, coup, motion_out, arr_rad, gas_out, liquid, sem,
):
    r = lax.axis_index("rad")
    sends = [
        pltpu.make_async_copy(src, dst, sem.at[i])
        for i, (src, dst) in enumerate(
            (
                (motion_out, motion_hbm), (arr_rad, arr_hbm), *((gas_out.at[c], gas_hbm.at[c]) for c in range(3)),
                (liquid, liquid_hbm),
            )
        )
    ]
    layers, tiles, blocks, groups = sz.layers, sz.tiles, sz.blocks, sz.groups
    slab_blocks = n_rad * blocks
    T = n_rad * tiles
    block_rows = [G[d, pl.ds(sz.meta, 1), :] for d in range(n_rad)]

    rows = functools.partial(slab_rows, sz, n_rad, G)
    size = rows(sz.size)
    mass = size * size * size
    dep = [-mass * (state[pl.ds((3 + c) * T, T), :] - rows(sz.motion + (3 + c) * tiles)) for c in range(3)] + [mass]
    even = iota((T, BLOCK), 1) < GROUP

    for c in range(4):
        high = dep[c].astype(BF16).astype(F32)
        low = dep[c] - high
        for piece, part in enumerate((high, low)):
            deps[pl.ds((piece * 8 + c) * T, T), :] = jnp.where(even, part, 0.0)
            deps[pl.ds((piece * 8 + 4 + c) * T, T), :] = jnp.where(even, 0.0, part)
    cell = iota((BLOCK, BLOCK), 0).astype(F32).astype(BF16)
    one, none = jnp.ones((BLOCK, BLOCK), BF16), jnp.zeros((BLOCK, BLOCK), BF16)
    blank = jnp.zeros((16, BLOCK), BF16)
    for d in range(n_rad):
        for i in range(0, tiles, 2):
            onehot, lhs = [], []
            for t in (i, i + 1):
                off = jnp.broadcast_to(G[d, pl.ds(sz.offset + t, 1), :], (16, BLOCK)).astype(BF16)
                onehot.append(jnp.where(cell == jnp.concatenate([off] * (BLOCK // 16), axis=0), one, none))
                lhs.append(deps[pl.ds(d * tiles + t, 16, stride=T), :].astype(BF16))
            lhs = jnp.concatenate(
                [jnp.concatenate([lhs[0], blank], axis=1), jnp.concatenate([blank, lhs[1]], axis=1)], axis=0
            )
            res = dot_nt(lhs, jnp.concatenate(onehot, axis=1))
            for k in range(2):
                t = d * tiles + i + k
                both = res[16 * k : 16 * k + 8] + res[16 * k + 8 : 16 * k + 16]
                spread[pl.ds(2 * t, 4, stride=2 * T), :] = both[:4]
                spread[pl.ds(2 * t + 1, 4, stride=2 * T), :] = both[4:]
    own = iota((blocks, groups), 0) + r * blocks
    adder = jnp.concatenate(
        [(own == b[:, :groups].astype(I32)).astype(F32) for b in block_rows] * 2, axis=1
    ).astype(BF16)
    for c in range(4):
        high, low = split2(spread[pl.ds(c * 2 * T, 2 * T), :])
        total = dot(adder, jnp.concatenate([high, low], axis=0))
        for q in range(sz.quarters):
            part = total[q * layers : (q + 1) * layers]
            at = slice(q * BLOCK, (q + 1) * BLOCK)
            if c < 3:
                gas_out[c, :, at] = G[r, pl.ds(sz.gas + c * blocks + q * layers, layers), :] + part
            else:
                liquid[:, at] = part
    for send in sends[2:]:
        send.start()

    pres = jnp.concatenate([G[d, pl.ds(sz.pres, blocks), :] for d in range(n_rad)], axis=0)
    index = [
        jnp.broadcast_to(aux[pl.ds(8, blocks), k : k + 1], (blocks, BLOCK)).astype(jnp.int16) for k in range(4)
    ]
    one, none = jnp.ones((blocks, BLOCK), BF16), jnp.zeros((blocks, BLOCK), BF16)
    lanes = iota((blocks, BLOCK), 1)
    counts = []
    for t in range(NT):
        row = []
        for first in range(0, slab_blocks, BLOCK):
            aim = (lanes + (t * slab_blocks + first)).astype(jnp.int16)
            count = jnp.where(aim == index[0], one, none)
            for k in range(1, 4):
                count = count + jnp.where(aim == index[k], one, none)
            row.append(count)
        counts.append(jnp.concatenate(row, axis=1))
    grouped = dot(jnp.concatenate(counts, axis=0), jnp.concatenate(split2(pres), axis=1))
    grouped = grouped[:, :BLOCK] + grouped[:, BLOCK:]
    mine = pl.multiple_of(r * tiles, tiles)
    for i in range(tiles):
        motion_out[:, i * BLOCK : (i + 1) * BLOCK] = state[pl.ds(mine + i, 6, stride=T), :]
    sends[0].start()
    width = arr_rad.shape[2]
    for slot, exists, other in ((0, r > 0, jnp.maximum(r - 1, 0)), (1, r < n_rad - 1, jnp.minimum(r + 1, n_rad - 1))):
        idx = G[other, pl.ds(sz.meta + 1 + slot, 1), :].astype(I32)
        idx = jnp.where(exists, idx, -1)
        got = pick(sz, state_of(sz, T, state, other), idx)
        for c in range(7):
            arr_rad[c, slot : slot + 1, :] = got[c][:, :width]
    sends[1].start()

    grouped = jnp.concatenate([grouped[t * blocks : (t + 1) * blocks] for t in range(NT)], axis=1)
    matrices = jnp.concatenate([table[t] for t in range(NT)], axis=1)
    sums = dot_nt(jnp.concatenate(split2(grouped), axis=0), jnp.concatenate(split2(matrices), axis=0))
    coup[...] = sums[:blocks, :BLOCK] + sums[:blocks, BLOCK:] + sums[blocks:, :BLOCK]
    layer = iota((layers, BLOCK), 0)
    for q in range(sz.quarters):
        p = G[r, pl.ds(sz.pres + q * layers, layers), :]
        below = jnp.where(layer == 0, 0.0, pltpu.roll(p, 1, 0))
        above = jnp.where(layer == layers - 1, 0.0, pltpu.roll(p, layers - 1, 0))
        image[:, q * BLOCK : (q + 1) * BLOCK] = (
            DIAG * p - above - below + coup[pl.ds(q, layers, stride=sz.quarters), :]
        )
    for send in sends:
        send.wait()


def finish_kernel(sz, n_ax, got_a, got_b, image, arr_ax, pressure_image):
    a = lax.axis_index("ax")
    even = a % 2 == 0
    low = jnp.where(a > 0, jnp.where(even, got_b[...], got_a[...]), 0.0)
    up = jnp.where(a < n_ax - 1, jnp.where(even, got_a[...], got_b[...]), 0.0)
    half = arr_ax.shape[2]
    arr_ax[:, 0, :] = low[0:7, 0:half]
    arr_ax[:, 1, :] = up[0:7, half : 2 * half]
    pressure_image[...] = image[...]
    last = sz.layers - 1
    for q in range(sz.quarters):
        at = slice(q * BLOCK, (q + 1) * BLOCK)
        pressure_image[0:1, at] = image[0:1, at] - low[8 + q : 9 + q, :]
        pressure_image[last : last + 1, at] = image[last : last + 1, at] - up[12 + q : 13 + q, :]


def on_device(
    parcel_motion,
    parcel_size,
    parcel_block,
    parcel_offset,
    gas_velocity,
    pressure,
    block_cols,
    block_kinds,
    block_table,
    send_axial,
    send_radial,
    send_counts,
):
    n_ax, n_rad = lax.axis_size("ax"), lax.axis_size("rad")
    layers, radial = pressure.shape
    parcels = parcel_size.shape[0]
    sz = Sizes(layers, radial, parcels)
    T = n_rad * sz.tiles
    cap_ax, cap_rad = send_axial.shape[-1], send_radial.shape[-1]
    params = pltpu.CompilerParams(vmem_limit_bytes=VMEM_LIMIT)
    counts = send_counts.reshape(1, 4)
    size2 = parcel_size.reshape(sz.tiles, BLOCK)
    offset2 = parcel_offset.reshape(sz.tiles, BLOCK)

    packed, aux = pl.pallas_call(
        functools.partial(pack_kernel, sz, n_rad),
        out_shape=[
            jax.ShapeDtypeStruct((sz.rows, BLOCK), F32),
            jax.ShapeDtypeStruct((8 + sz.blocks, BLOCK), I32),
        ],
        in_specs=[hbm] * 11,
        out_specs=[vmem] * 2,
        scratch_shapes=[
            pltpu.VMEM(parcel_motion.shape, F32),
            pltpu.VMEM(size2.shape, F32),
            pltpu.VMEM((1, sz.groups), I32),
            pltpu.VMEM(offset2.shape, I32),
            pltpu.VMEM(gas_velocity.shape, F32),
            pltpu.VMEM(pressure.shape, F32),
            pltpu.VMEM((2, cap_rad), I32),
            pltpu.SMEM((1, 4), I32),
            pltpu.VMEM((4, sz.blocks), I32),
            pltpu.VMEM((4, sz.blocks), I32),
            pltpu.VMEM((2, cap_ax), I32),
            pltpu.SemaphoreType.DMA((13,)),
        ],
        compiler_params=params,
        name="pack",
    )(
        *(
            pltpu.with_memory_space_constraint(x, pltpu.HBM)
            for x in (
                parcel_motion, size2, parcel_block.reshape(1, sz.groups), offset2, gas_velocity, pressure,
                send_radial.reshape(2, cap_rad), counts, block_cols[0].T, block_kinds[0].T,
                send_axial.reshape(2, cap_ax),
            )
        )
    )
    gathered = lax.all_gather(packed, "rad", axis=0)

    state, message = pl.pallas_call(
        functools.partial(move_kernel, sz, n_rad),
        out_shape=[
            jax.ShapeDtypeStruct((7 * T, BLOCK), F32),
            jax.ShapeDtypeStruct((16, BLOCK), F32),
        ],
        in_specs=[vmem] * 2,
        out_specs=[vmem] * 2,
        scratch_shapes=[pltpu.VMEM((3, n_rad * sz.groups, BLOCK), F32)],
        compiler_params=params,
        cost_estimate=pl.CostEstimate(flops=4_000_000_000, bytes_accessed=1_000_000, transcendentals=0),
        name="move",
    )(gathered, aux)

    def exchange(first):
        to = list(range(n_ax * n_rad))
        for low in range(first, n_ax - 1, 2):
            for r in range(n_rad):
                i, j = low * n_rad + r, (low + 1) * n_rad + r
                to[i], to[j] = j, i
        alone = [i for i in range(n_ax * n_rad) if to[i] == i]
        for i, j in zip(alone[0::2], alone[1::2]):
            to[i], to[j] = j, i
        return lax.ppermute(message, ("ax", "rad"), list(enumerate(to)))

    got_b = exchange(1)
    got_a = exchange(0)

    motion_out, arr_rad, gas_out, liquid, image = pl.pallas_call(
        functools.partial(rest_kernel, sz, n_rad),
        out_shape=[
            jax.ShapeDtypeStruct((6, parcels), F32),
            jax.ShapeDtypeStruct((7, 2, cap_rad), F32),
            jax.ShapeDtypeStruct(gas_velocity.shape, F32),
            jax.ShapeDtypeStruct(pressure.shape, F32),
            jax.ShapeDtypeStruct(pressure.shape, F32),
        ],
        in_specs=[vmem] * 4,
        out_specs=[hbm] * 4 + [vmem],
        scratch_shapes=[
            pltpu.VMEM((16 * T, BLOCK), F32),
            pltpu.VMEM((4 * 2 * T, BLOCK), F32),
            pltpu.VMEM((sz.blocks, BLOCK), F32),
            pltpu.VMEM((6, parcels), F32),
            pltpu.VMEM((7, 2, cap_rad), F32),
            pltpu.VMEM(gas_velocity.shape, F32),
            pltpu.VMEM(pressure.shape, F32),
            pltpu.SemaphoreType.DMA((6,)),
        ],
        compiler_params=params,
        cost_estimate=pl.CostEstimate(flops=2_000_000_000, bytes_accessed=2_000_000, transcendentals=0),
        name="rest",
    )(gathered, aux, block_table, state)

    arr_ax, pressure_image = pl.pallas_call(
        functools.partial(finish_kernel, sz, n_ax),
        out_shape=[
            jax.ShapeDtypeStruct((7, 2, cap_ax), F32),
            jax.ShapeDtypeStruct(pressure.shape, F32),
        ],
        in_specs=[vmem] * 3,
        out_specs=[vmem] * 2,
        compiler_params=params,
        name="finish",
    )(got_a, got_b, image)

    arrivals_axial = arr_ax.transpose(1, 0, 2)[None, None]
    arrivals_radial = arr_rad.transpose(1, 0, 2)[None, None]
    return (motion_out, arrivals_axial, arrivals_radial, gas_out, liquid, pressure_image)


def solution(mesh):
    return jax.shard_map(
        on_device,
        mesh=mesh,
        in_specs=(
            P(None, ("ax", "rad")),
            P(("ax", "rad")),
            P(("ax", "rad")),
            P(("ax", "rad")),
            P(None, "ax", "rad"),
            P("ax", "rad"),
            P("ax", "rad", None),
            P("ax", "rad", None),
            P(),
            P("ax", "rad", None, None),
            P("ax", "rad", None, None),
            P("ax", "rad", None),
        ),
        out_specs=(
            P(None, ("ax", "rad")),
            P("ax", "rad", None, None, None),
            P("ax", "rad", None, None, None),
            P(None, "ax", "rad"),
            P("ax", "rad"),
            P("ax", "rad"),
        ),
        check_vma=False,
    )
```

```python
import functools

import jax
import jax.numpy as jnp
from jax import lax
from jax.experimental import pallas as pl
from jax.experimental.pallas import tpu as pltpu
from jax.sharding import PartitionSpec as P

BLOCK = 128
GROUP = 64
NT = 8
DRAG = 0.5
STEP = 0.5
DIAG = 6.0
VMEM_LIMIT = 24 * 1024 * 1024

F32 = jnp.float32
BF16 = jnp.bfloat16
I32 = jnp.int32

vmem = pl.BlockSpec(memory_space=pltpu.VMEM)
hbm = pl.BlockSpec(memory_space=pltpu.HBM)


class Sizes:
    def __init__(self, layers, radial, parcels):
        self.layers = layers
        self.quarters = radial // BLOCK
        self.blocks = layers * self.quarters
        self.tiles = parcels // BLOCK
        self.groups = parcels // GROUP
        self.gas = 0
        self.pres = 3 * self.blocks
        self.motion = self.pres + self.blocks
        self.size = self.motion + 6 * self.tiles
        self.offset = self.size + self.tiles
        self.meta = self.offset + self.tiles
        self.column = self.meta + 8
        self.rows = self.column + self.groups


def split2(x):
    high = x.astype(BF16)
    return high, (x - high.astype(F32)).astype(BF16)


def dot(a, b):
    return jnp.dot(a, b, preferred_element_type=F32)


def dot_nt(a, b):
    return lax.dot_general(a, b, (((1,), (1,)), ((), ())), preferred_element_type=F32)


def iota(shape, dim):
    return lax.broadcasted_iota(I32, shape, dim)


def block_row(sz, b):
    local = b % sz.blocks
    return b - local + (local % sz.quarters) * sz.layers + local // sz.quarters


def pack_kernel(
    sz, n_rad, motion_hbm, size_hbm, block_hbm, offset_hbm, gas_hbm, pres_hbm, radial_hbm, counts_hbm, axial_hbm,
    out, aux,
    motion, size, block, offset, gas, pres, radial, counts, axial, sem,
):
    small = (
        (counts_hbm, counts), (block_hbm, block), (radial_hbm, radial), (axial_hbm, axial), (offset_hbm, offset),
        (size_hbm, size),
    )
    large = ((motion_hbm, motion), (pres_hbm, pres), *((gas_hbm.at[c], gas.at[c]) for c in range(3)))
    copies = [pltpu.make_async_copy(src, dst, sem.at[i]) for i, (src, dst) in enumerate(small + large)]
    for copy in copies:
        copy.start()
    out[pl.ds(sz.meta, 8), :] = jnp.full((8, BLOCK), -1.0, F32)
    layers = sz.layers
    for copy in copies[: len(small)]:
        copy.wait()
    out[pl.ds(sz.size, sz.tiles), :] = size[...]
    out[pl.ds(sz.offset, sz.tiles), :] = offset[...].astype(F32)
    numbers = block_row(sz, block[...]).astype(F32)
    out[pl.ds(sz.meta, 1), pl.ds(0, sz.groups)] = numbers
    numbers = jnp.concatenate([numbers, jnp.zeros((1, BLOCK - sz.groups), F32)], axis=1)
    out[pl.ds(sz.column, sz.groups), :] = jnp.transpose(jnp.broadcast_to(numbers, (BLOCK, BLOCK)))[: sz.groups]
    width = radial.shape[1]
    lane = iota((1, width), 1)
    for slot in range(2):
        kept = jnp.where(lane < counts[0, 2 + slot], radial[slot : slot + 1, :], -1)
        out[pl.ds(sz.meta + 1 + slot, 1), pl.ds(0, width)] = kept.astype(F32)
    lane = iota((1, axial.shape[1]), 1)
    kept = [jnp.where(lane < counts[0, slot], axial[slot : slot + 1, :], -1) for slot in range(2)]
    aux[pl.ds(0, 1), :] = jnp.concatenate(kept, axis=1)
    motion_copy, pres_copy, *gas_copies = copies[len(small) :]
    motion_copy.wait()
    for i in range(sz.tiles):
        out[pl.ds(sz.motion + i, 6, stride=sz.tiles), :] = motion[:, i * BLOCK : (i + 1) * BLOCK]
    pres_copy.wait()
    for q in range(sz.quarters):
        out[pl.ds(sz.pres + q * layers, layers), :] = pres[:, q * BLOCK : (q + 1) * BLOCK]
    for c in range(3):
        gas_copies[c].wait()
        for q in range(sz.quarters):
            out[pl.ds(sz.gas + c * sz.blocks + q * layers, layers), :] = gas[c, :, q * BLOCK : (q + 1) * BLOCK]


def take_lanes(x, idx):
    return jnp.take_along_axis(x, idx, axis=1, mode="promise_in_bounds")


def pick(sz, state, idx):
    shape = (sz.tiles, BLOCK)
    idx = jnp.broadcast_to(idx, shape)
    lane = idx & (BLOCK - 1)
    here = (idx >> 7) == iota(shape, 0)
    return [jnp.sum(jnp.where(here, take_lanes(s, lane), 0.0), axis=0, keepdims=True) for s in state]


def slab_rows(sz, n_rad, G, first):
    return jnp.concatenate([G[d, pl.ds(first, sz.tiles), :] for d in range(n_rad)], axis=0)


def state_of(sz, T, state, d):
    first = pl.multiple_of(d * sz.tiles, sz.tiles)
    return [state[pl.ds(c * T + first, sz.tiles), :] for c in range(7)]


def move_kernel(sz, n_rad, G, aux, state, message, near):
    r = lax.axis_index("rad")
    layers, tiles, blocks, groups = sz.layers, sz.tiles, sz.blocks, sz.groups
    slab_blocks = n_rad * blocks
    T = n_rad * tiles

    column = jnp.concatenate([G[d, pl.ds(sz.column, groups), :] for d in range(n_rad)], axis=0).astype(I32)
    lanes = iota((n_rad * groups, BLOCK), 1)
    chooser = jnp.concatenate(
        [(column == lanes + first).astype(F32).astype(BF16) for first in range(0, slab_blocks, BLOCK)], axis=1
    )
    gas_slab = jnp.concatenate(
        [
            jnp.concatenate([G[d, pl.ds(sz.gas + c * blocks, blocks), :] for d in range(n_rad)], axis=0)
            for c in range(3)
        ],
        axis=1,
    )
    high, low = split2(gas_slab)
    found = dot(jnp.concatenate([chooser, chooser], axis=1), jnp.concatenate([high, low], axis=0))
    for c in range(3):
        near[c] = found[:, c * BLOCK : (c + 1) * BLOCK]

    rows = functools.partial(slab_rows, sz, n_rad, G)
    size = rows(sz.size)
    offset = rows(sz.offset).astype(I32)
    factor = jnp.exp(-DRAG / (size * size))
    even = iota((T, BLOCK), 1) < GROUP
    for c in range(3):
        u_even = take_lanes(near[c, pl.ds(0, T, stride=2), :], offset)
        u_odd = take_lanes(near[c, pl.ds(1, T, stride=2), :], offset)
        u = jnp.where(even, u_even, u_odd)
        v = rows(sz.motion + (3 + c) * tiles)
        new = u + (v - u) * factor
        state[pl.ds(c * T, T), :] = rows(sz.motion + c * tiles) + STEP * new
        state[pl.ds((3 + c) * T, T), :] = new
    state[pl.ds(6 * T, T), :] = size

    payload = pick(sz, state_of(sz, T, state, r), aux[pl.ds(0, 1), :])
    for c in range(7):
        message[c : c + 1, :] = payload[c]
    message[7:8, :] = jnp.zeros((1, BLOCK), F32)
    for q in range(sz.quarters):
        first = sz.pres + q * layers
        message[8 + q : 9 + q, :] = G[r, pl.ds(first + layers - 1, 1), :]
        message[12 + q : 13 + q, :] = G[r, pl.ds(first, 1), :]


def rest_kernel(
    sz, n_rad, G, cols_hbm, kinds_hbm, table, state,
    motion_hbm, arr_hbm, gas_hbm, liquid_hbm, image,
    deps, spread, coup, motion_out, arr_rad, gas_out, liquid, cols, kinds, sem,
):
    r = lax.axis_index("rad")
    loads = [
        pltpu.make_async_copy(cols_hbm, cols, sem.at[6]),
        pltpu.make_async_copy(kinds_hbm, kinds, sem.at[7]),
    ]
    for load in loads:
        load.start()
    sends = [
        pltpu.make_async_copy(src, dst, sem.at[i])
        for i, (src, dst) in enumerate(
            (
                (motion_out, motion_hbm), (arr_rad, arr_hbm), *((gas_out.at[c], gas_hbm.at[c]) for c in range(3)),
                (liquid, liquid_hbm),
            )
        )
    ]
    layers, tiles, blocks, groups = sz.layers, sz.tiles, sz.blocks, sz.groups
    slab_blocks = n_rad * blocks
    T = n_rad * tiles
    block_rows = [G[d, pl.ds(sz.meta, 1), :] for d in range(n_rad)]

    rows = functools.partial(slab_rows, sz, n_rad, G)
    size = rows(sz.size)
    mass = size * size * size
    dep = [-mass * (state[pl.ds((3 + c) * T, T), :] - rows(sz.motion + (3 + c) * tiles)) for c in range(3)] + [mass]
    even = iota((T, BLOCK), 1) < GROUP

    for c in range(4):
        high = dep[c].astype(BF16).astype(F32)
        low = dep[c] - high
        for piece, part in enumerate((high, low)):
            deps[pl.ds((piece * 8 + c) * T, T), :] = jnp.where(even, part, 0.0)
            deps[pl.ds((piece * 8 + 4 + c) * T, T), :] = jnp.where(even, 0.0, part)
    cell = iota((BLOCK, BLOCK), 0).astype(F32).astype(BF16)
    one, none = jnp.ones((BLOCK, BLOCK), BF16), jnp.zeros((BLOCK, BLOCK), BF16)
    blank = jnp.zeros((16, BLOCK), BF16)
    for d in range(n_rad):
        for i in range(0, tiles, 2):
            onehot, lhs = [], []
            for t in (i, i + 1):
                off = jnp.broadcast_to(G[d, pl.ds(sz.offset + t, 1), :], (16, BLOCK)).astype(BF16)
                onehot.append(jnp.where(cell == jnp.concatenate([off] * (BLOCK // 16), axis=0), one, none))
                lhs.append(deps[pl.ds(d * tiles + t, 16, stride=T), :].astype(BF16))
            lhs = jnp.concatenate(
                [jnp.concatenate([lhs[0], blank], axis=1), jnp.concatenate([blank, lhs[1]], axis=1)], axis=0
            )
            res = dot_nt(lhs, jnp.concatenate(onehot, axis=1))
            for k in range(2):
                t = d * tiles + i + k
                both = res[16 * k : 16 * k + 8] + res[16 * k + 8 : 16 * k + 16]
                spread[pl.ds(2 * t, 4, stride=2 * T), :] = both[:4]
                spread[pl.ds(2 * t + 1, 4, stride=2 * T), :] = both[4:]
    own = iota((blocks, groups), 0) + r * blocks
    adder = jnp.concatenate(
        [(own == b[:, :groups].astype(I32)).astype(F32) for b in block_rows] * 2, axis=1
    ).astype(BF16)
    for c in range(4):
        high, low = split2(spread[pl.ds(c * 2 * T, 2 * T), :])
        total = dot(adder, jnp.concatenate([high, low], axis=0))
        for q in range(sz.quarters):
            part = total[q * layers : (q + 1) * layers]
            at = slice(q * BLOCK, (q + 1) * BLOCK)
            if c < 3:
                gas_out[c, :, at] = G[r, pl.ds(sz.gas + c * blocks + q * layers, layers), :] + part
            else:
                liquid[:, at] = part
    for send in sends[2:]:
        send.start()

    for load in loads:
        load.wait()

    pres = jnp.concatenate([G[d, pl.ds(sz.pres, blocks), :] for d in range(n_rad)], axis=0)
    index = kinds[...] * slab_blocks + block_row(sz, cols[...])
    index = jnp.concatenate([index, index], axis=1).astype(F32)
    index = jnp.concatenate([index, jnp.zeros((BLOCK - index.shape[0], BLOCK), F32)], axis=0)
    index = jnp.transpose(index)[:blocks].astype(I32)
    index = [jnp.broadcast_to(index[:, k : k + 1], (blocks, BLOCK)).astype(jnp.int16) for k in range(4)]
    one, none = jnp.ones((blocks, BLOCK), BF16), jnp.zeros((blocks, BLOCK), BF16)
    lanes = iota((blocks, BLOCK), 1)
    counts = []
    for t in range(NT):
        row = []
        for first in range(0, slab_blocks, BLOCK):
            aim = (lanes + (t * slab_blocks + first)).astype(jnp.int16)
            count = jnp.where(aim == index[0], one, none)
            for k in range(1, 4):
                count = count + jnp.where(aim == index[k], one, none)
            row.append(count)
        counts.append(jnp.concatenate(row, axis=1))
    grouped = dot(jnp.concatenate(counts, axis=0), jnp.concatenate(split2(pres), axis=1))
    grouped = grouped[:, :BLOCK] + grouped[:, BLOCK:]
    mine = pl.multiple_of(r * tiles, tiles)
    for i in range(tiles):
        motion_out[:, i * BLOCK : (i + 1) * BLOCK] = state[pl.ds(mine + i, 6, stride=T), :]
    sends[0].start()
    width = arr_rad.shape[2]
    for slot, exists, other in ((0, r > 0, jnp.maximum(r - 1, 0)), (1, r < n_rad - 1, jnp.minimum(r + 1, n_rad - 1))):
        idx = G[other, pl.ds(sz.meta + 1 + slot, 1), :].astype(I32)
        idx = jnp.where(exists, idx, -1)
        got = pick(sz, state_of(sz, T, state, other), idx)
        for c in range(7):
            arr_rad[c, slot : slot + 1, :] = got[c][:, :width]
    sends[1].start()

    grouped = jnp.concatenate([grouped[t * blocks : (t + 1) * blocks] for t in range(NT)], axis=1)
    matrices = jnp.concatenate([table[t] for t in range(NT)], axis=1)
    sums = dot_nt(jnp.concatenate(split2(grouped), axis=0), jnp.concatenate(split2(matrices), axis=0))
    coup[...] = sums[:blocks, :BLOCK] + sums[:blocks, BLOCK:] + sums[blocks:, :BLOCK]
    layer = iota((layers, BLOCK), 0)
    for q in range(sz.quarters):
        p = G[r, pl.ds(sz.pres + q * layers, layers), :]
        below = jnp.where(layer == 0, 0.0, pltpu.roll(p, 1, 0))
        above = jnp.where(layer == layers - 1, 0.0, pltpu.roll(p, layers - 1, 0))
        image[:, q * BLOCK : (q + 1) * BLOCK] = (
            DIAG * p - above - below + coup[pl.ds(q, layers, stride=sz.quarters), :]
        )
    for send in sends:
        send.wait()


def finish_kernel(sz, n_ax, got_a, got_b, image, arr_hbm, pressure_hbm, arr_ax, pressure_image, sem):
    sends = [pltpu.make_async_copy(arr_ax, arr_hbm, sem.at[sz.quarters])]
    a = lax.axis_index("ax")
    even = a % 2 == 0
    low = jnp.where(a > 0, jnp.where(even, got_b[...], got_a[...]), 0.0)
    up = jnp.where(a < n_ax - 1, jnp.where(even, got_a[...], got_b[...]), 0.0)
    last = sz.layers - 1
    layer = iota((sz.layers, BLOCK), 0)
    for q in range(sz.quarters):
        at = slice(q * BLOCK, (q + 1) * BLOCK)
        edge = jnp.where(layer == 0, low[8 + q : 9 + q, :], jnp.where(layer == last, up[12 + q : 13 + q, :], 0.0))
        pressure_image[:, at] = image[:, at] - edge
        sends.append(pltpu.make_async_copy(pressure_image.at[:, at], pressure_hbm.at[:, at], sem.at[q]))
    for send in sends[1:]:
        send.start()
    half = arr_ax.shape[2]
    arr_ax[:, 0, :] = low[0:7, 0:half]
    arr_ax[:, 1, :] = up[0:7, half : 2 * half]
    sends[0].start()
    for send in sends:
        send.wait()


def on_device(
    parcel_motion,
    parcel_size,
    parcel_block,
    parcel_offset,
    gas_velocity,
    pressure,
    block_cols,
    block_kinds,
    block_table,
    send_axial,
    send_radial,
    send_counts,
):
    n_ax, n_rad = lax.axis_size("ax"), lax.axis_size("rad")
    layers, radial = pressure.shape
    parcels = parcel_size.shape[0]
    sz = Sizes(layers, radial, parcels)
    T = n_rad * sz.tiles
    cap_ax, cap_rad = send_axial.shape[-1], send_radial.shape[-1]
    params = pltpu.CompilerParams(vmem_limit_bytes=VMEM_LIMIT)
    counts = send_counts.reshape(1, 4)
    size2 = parcel_size.reshape(sz.tiles, BLOCK)
    offset2 = parcel_offset.reshape(sz.tiles, BLOCK)

    packed, aux = pl.pallas_call(
        functools.partial(pack_kernel, sz, n_rad),
        out_shape=[
            jax.ShapeDtypeStruct((sz.rows, BLOCK), F32),
            jax.ShapeDtypeStruct((8, BLOCK), I32),
        ],
        in_specs=[hbm] * 9,
        out_specs=[vmem] * 2,
        scratch_shapes=[
            pltpu.VMEM(parcel_motion.shape, F32),
            pltpu.VMEM(size2.shape, F32),
            pltpu.VMEM((1, sz.groups), I32),
            pltpu.VMEM(offset2.shape, I32),
            pltpu.VMEM(gas_velocity.shape, F32),
            pltpu.VMEM(pressure.shape, F32),
            pltpu.VMEM((2, cap_rad), I32),
            pltpu.SMEM((1, 4), I32),
            pltpu.VMEM((2, cap_ax), I32),
            pltpu.SemaphoreType.DMA((11,)),
        ],
        compiler_params=params,
        name="pack",
    )(
        *(
            pltpu.with_memory_space_constraint(x, pltpu.HBM)
            for x in (
                parcel_motion, size2, parcel_block.reshape(1, sz.groups), offset2, gas_velocity, pressure,
                send_radial.reshape(2, cap_rad), counts, send_axial.reshape(2, cap_ax),
            )
        )
    )
    gathered = lax.all_gather(packed, "rad", axis=0)

    state, message = pl.pallas_call(
        functools.partial(move_kernel, sz, n_rad),
        out_shape=[
            jax.ShapeDtypeStruct((7 * T, BLOCK), F32),
            jax.ShapeDtypeStruct((16, BLOCK), F32),
        ],
        in_specs=[vmem] * 2,
        out_specs=[vmem] * 2,
        scratch_shapes=[pltpu.VMEM((3, n_rad * sz.groups, BLOCK), F32)],
        compiler_params=params,
        cost_estimate=pl.CostEstimate(flops=4_000_000_000, bytes_accessed=1_000_000, transcendentals=0),
        name="move",
    )(gathered, aux)

    def exchange(first):
        to = list(range(n_ax * n_rad))
        for low in range(first, n_ax - 1, 2):
            for r in range(n_rad):
                i, j = low * n_rad + r, (low + 1) * n_rad + r
                to[i], to[j] = j, i
        alone = [i for i in range(n_ax * n_rad) if to[i] == i]
        for i, j in zip(alone[0::2], alone[1::2]):
            to[i], to[j] = j, i
        return lax.ppermute(message, ("ax", "rad"), list(enumerate(to)))

    got_b = exchange(1)
    got_a = exchange(0)

    motion_out, arr_rad, gas_out, liquid, image = pl.pallas_call(
        functools.partial(rest_kernel, sz, n_rad),
        out_shape=[
            jax.ShapeDtypeStruct((6, parcels), F32),
            jax.ShapeDtypeStruct((7, 2, cap_rad), F32),
            jax.ShapeDtypeStruct(gas_velocity.shape, F32),
            jax.ShapeDtypeStruct(pressure.shape, F32),
            jax.ShapeDtypeStruct(pressure.shape, F32),
        ],
        in_specs=[vmem, hbm, hbm, vmem, vmem],
        out_specs=[hbm] * 4 + [vmem],
        scratch_shapes=[
            pltpu.VMEM((16 * T, BLOCK), F32),
            pltpu.VMEM((4 * 2 * T, BLOCK), F32),
            pltpu.VMEM((sz.blocks, BLOCK), F32),
            pltpu.VMEM((6, parcels), F32),
            pltpu.VMEM((7, 2, cap_rad), F32),
            pltpu.VMEM(gas_velocity.shape, F32),
            pltpu.VMEM(pressure.shape, F32),
            pltpu.VMEM((4, sz.blocks), I32),
            pltpu.VMEM((4, sz.blocks), I32),
            pltpu.SemaphoreType.DMA((8,)),
        ],
        compiler_params=params,
        cost_estimate=pl.CostEstimate(flops=2_000_000_000, bytes_accessed=2_000_000, transcendentals=0),
        name="rest",
    )(
        gathered,
        pltpu.with_memory_space_constraint(block_cols[0].T, pltpu.HBM),
        pltpu.with_memory_space_constraint(block_kinds[0].T, pltpu.HBM),
        block_table,
        state,
    )

    arr_ax, pressure_image = pl.pallas_call(
        functools.partial(finish_kernel, sz, n_ax),
        out_shape=[
            jax.ShapeDtypeStruct((7, 2, cap_ax), F32),
            jax.ShapeDtypeStruct(pressure.shape, F32),
        ],
        in_specs=[vmem] * 3,
        out_specs=[hbm] * 2,
        scratch_shapes=[
            pltpu.VMEM((7, 2, cap_ax), F32),
            pltpu.VMEM(pressure.shape, F32),
            pltpu.SemaphoreType.DMA((sz.quarters + 1,)),
        ],
        compiler_params=params,
        name="finish",
    )(got_a, got_b, image)

    arrivals_axial = arr_ax.transpose(1, 0, 2)[None, None]
    arrivals_radial = arr_rad.transpose(1, 0, 2)[None, None]
    return (motion_out, arrivals_axial, arrivals_radial, gas_out, liquid, pressure_image)


def solution(mesh):
    return jax.shard_map(
        on_device,
        mesh=mesh,
        in_specs=(
            P(None, ("ax", "rad")),
            P(("ax", "rad")),
            P(("ax", "rad")),
            P(("ax", "rad")),
            P(None, "ax", "rad"),
            P("ax", "rad"),
            P("ax", "rad", None),
            P("ax", "rad", None),
            P(),
            P("ax", "rad", None, None),
            P("ax", "rad", None, None),
            P("ax", "rad", None),
        ),
        out_specs=(
            P(None, ("ax", "rad")),
            P("ax", "rad", None, None, None),
            P("ax", "rad", None, None, None),
            P(None, "ax", "rad"),
            P("ax", "rad"),
            P("ax", "rad"),
        ),
        check_vma=False,
    )
```

```python
import functools

import jax
import jax.numpy as jnp
from jax import lax
from jax.experimental import pallas as pl
from jax.experimental.pallas import tpu as pltpu
from jax.sharding import PartitionSpec as P

BLOCK = 128
GROUP = 64
NT = 8
DRAG = 0.5
STEP = 0.5
DIAG = 6.0
VMEM_LIMIT = 24 * 1024 * 1024

F32 = jnp.float32
BF16 = jnp.bfloat16
I32 = jnp.int32

vmem = pl.BlockSpec(memory_space=pltpu.VMEM)
hbm = pl.BlockSpec(memory_space=pltpu.HBM)


class Sizes:
    def __init__(self, layers, radial, parcels):
        self.layers = layers
        self.quarters = radial // BLOCK
        self.blocks = layers * self.quarters
        self.tiles = parcels // BLOCK
        self.groups = parcels // GROUP
        self.gas = 0
        self.pres = 3 * self.blocks
        self.motion = self.pres + self.blocks
        self.size = self.motion + 6 * self.tiles
        self.offset = self.size + self.tiles
        self.meta = self.offset + self.tiles
        self.column = self.meta + 8
        self.rows = self.column + self.groups


def split2(x):
    high = x.astype(BF16)
    return high, (x - high.astype(F32)).astype(BF16)


def dot(a, b):
    return jnp.dot(a, b, preferred_element_type=F32)


def dot_nt(a, b):
    return lax.dot_general(a, b, (((1,), (1,)), ((), ())), preferred_element_type=F32)


def iota(shape, dim):
    return lax.broadcasted_iota(I32, shape, dim)


def block_row(sz, b):
    local = b % sz.blocks
    return b - local + (local % sz.quarters) * sz.layers + local // sz.quarters


def pack_kernel(
    sz, n_rad, motion_hbm, size_hbm, block_hbm, offset_hbm, gas_hbm, pres_hbm, radial_hbm, counts_hbm, cols_hbm,
    kinds_hbm, axial_hbm,
    out, aux,
    motion, size, block, offset, gas, pres, radial, counts, cols, kinds, axial, sem,
):
    small = (
        (counts_hbm, counts), (block_hbm, block), (radial_hbm, radial), (axial_hbm, axial), (cols_hbm, cols),
        (kinds_hbm, kinds), (offset_hbm, offset), (size_hbm, size),
    )
    large = ((motion_hbm, motion), (pres_hbm, pres), *((gas_hbm.at[c], gas.at[c]) for c in range(3)))
    copies = [pltpu.make_async_copy(src, dst, sem.at[i]) for i, (src, dst) in enumerate(small + large)]
    for copy in copies:
        copy.start()
    out[pl.ds(sz.meta, 8), :] = jnp.full((8, BLOCK), -1.0, F32)
    layers = sz.layers
    for copy in copies[: len(small)]:
        copy.wait()
    out[pl.ds(sz.size, sz.tiles), :] = size[...]
    out[pl.ds(sz.offset, sz.tiles), :] = offset[...].astype(F32)
    numbers = block_row(sz, block[...]).astype(F32)
    out[pl.ds(sz.meta, 1), pl.ds(0, sz.groups)] = numbers
    numbers = jnp.concatenate([numbers, jnp.zeros((1, BLOCK - sz.groups), F32)], axis=1)
    out[pl.ds(sz.column, sz.groups), :] = jnp.transpose(jnp.broadcast_to(numbers, (BLOCK, BLOCK)))[: sz.groups]
    width = radial.shape[1]
    lane = iota((1, width), 1)
    for slot in range(2):
        kept = jnp.where(lane < counts[0, 2 + slot], radial[slot : slot + 1, :], -1)
        out[pl.ds(sz.meta + 1 + slot, 1), pl.ds(0, width)] = kept.astype(F32)
    index = kinds[...] * (n_rad * sz.blocks) + block_row(sz, cols[...])
    index = jnp.concatenate([index, index], axis=1).astype(F32)
    index = jnp.concatenate([index, jnp.zeros((BLOCK - index.shape[0], BLOCK), F32)], axis=0)
    aux[pl.ds(8, sz.blocks), :] = jnp.transpose(index)[: sz.blocks].astype(I32)
    lane = iota((1, axial.shape[1]), 1)
    kept = [jnp.where(lane < counts[0, slot], axial[slot : slot + 1, :], -1) for slot in range(2)]
    aux[pl.ds(0, 1), :] = jnp.concatenate(kept, axis=1)
    motion_copy, pres_copy, *gas_copies = copies[len(small) :]
    motion_copy.wait()
    for i in range(sz.tiles):
        out[pl.ds(sz.motion + i, 6, stride=sz.tiles), :] = motion[:, i * BLOCK : (i + 1) * BLOCK]
    pres_copy.wait()
    for q in range(sz.quarters):
        out[pl.ds(sz.pres + q * layers, layers), :] = pres[:, q * BLOCK : (q + 1) * BLOCK]
    for c in range(3):
        gas_copies[c].wait()
        for q in range(sz.quarters):
            out[pl.ds(sz.gas + c * sz.blocks + q * layers, layers), :] = gas[c, :, q * BLOCK : (q + 1) * BLOCK]


def take_lanes(x, idx):
    return jnp.take_along_axis(x, idx, axis=1, mode="promise_in_bounds")


def pick(sz, state, idx):
    shape = (sz.tiles, BLOCK)
    idx = jnp.broadcast_to(idx, shape)
    lane = idx & (BLOCK - 1)
    here = (idx >> 7) == iota(shape, 0)
    return [jnp.sum(jnp.where(here, take_lanes(s, lane), 0.0), axis=0, keepdims=True) for s in state]


def slab_rows(sz, n_rad, G, first):
    return jnp.concatenate([G[d, pl.ds(first, sz.tiles), :] for d in range(n_rad)], axis=0)


def state_of(sz, T, state, d):
    first = pl.multiple_of(d * sz.tiles, sz.tiles)
    return [state[pl.ds(c * T + first, sz.tiles), :] for c in range(7)]


def move_kernel(sz, n_rad, G, aux, state, message_a, message_b, near):
    r = lax.axis_index("rad")
    layers, tiles, blocks, groups = sz.layers, sz.tiles, sz.blocks, sz.groups
    slab_blocks = n_rad * blocks
    T = n_rad * tiles

    column = jnp.concatenate([G[d, pl.ds(sz.column, groups), :] for d in range(n_rad)], axis=0).astype(I32)
    lanes = iota((n_rad * groups, BLOCK), 1)
    chooser = jnp.concatenate(
        [(column == lanes + first).astype(F32).astype(BF16) for first in range(0, slab_blocks, BLOCK)], axis=1
    )
    gas_slab = jnp.concatenate(
        [
            jnp.concatenate([G[d, pl.ds(sz.gas + c * blocks, blocks), :] for d in range(n_rad)], axis=0)
            for c in range(3)
        ],
        axis=1,
    )
    high, low = split2(gas_slab)
    found = dot(jnp.concatenate([chooser, chooser], axis=1), jnp.concatenate([high, low], axis=0))
    for c in range(3):
        near[c] = found[:, c * BLOCK : (c + 1) * BLOCK]

    rows = functools.partial(slab_rows, sz, n_rad, G)
    size = rows(sz.size)
    offset = rows(sz.offset).astype(I32)
    factor = jnp.exp(-DRAG / (size * size))
    even = iota((T, BLOCK), 1) < GROUP
    for c in range(3):
        u_even = take_lanes(near[c, pl.ds(0, T, stride=2), :], offset)
        u_odd = take_lanes(near[c, pl.ds(1, T, stride=2), :], offset)
        u = jnp.where(even, u_even, u_odd)
        v = rows(sz.motion + (3 + c) * tiles)
        new = u + (v - u) * factor
        state[pl.ds(c * T, T), :] = rows(sz.motion + c * tiles) + STEP * new
        state[pl.ds((3 + c) * T, T), :] = new
    state[pl.ds(6 * T, T), :] = size

    payload = pick(sz, state_of(sz, T, state, r), aux[pl.ds(0, 1), :])
    payload = jnp.concatenate([*payload, jnp.zeros((1, BLOCK), F32)], axis=0)
    turned = pltpu.roll(payload, BLOCK // 2, 1)
    first_half = iota((1, BLOCK), 1) < BLOCK // 2
    even = lax.axis_index("ax") % 2 == 0
    for q in range(sz.quarters):
        first = sz.pres + q * layers
        up = G[r, pl.ds(first + layers - 1, 1), :]
        down = G[r, pl.ds(first, 1), :]
        message_a[q : q + 1, :] = jnp.where(even, up, down)
        message_b[q : q + 1, :] = jnp.where(even, down, up)
    for i in range(4):
        here = [x[2 * i : 2 * i + 1] for x in (payload, turned)]
        then = [x[2 * i + 1 : 2 * i + 2] for x in (payload, turned)]
        up = jnp.where(first_half, here[0], then[1])
        down = jnp.where(first_half, here[1], then[0])
        message_a[4 + i : 5 + i, :] = jnp.where(even, up, down)
        message_b[4 + i : 5 + i, :] = jnp.where(even, down, up)


def rest_kernel(
    sz, n_rad, G, aux, table, state,
    motion_hbm, arr_hbm, gas_hbm, liquid_hbm, image,
    deps, spread, coup, motion_out, arr_rad, gas_out, liquid, sem,
):
    r = lax.axis_index("rad")
    sends = [
        pltpu.make_async_copy(src, dst, sem.at[i])
        for i, (src, dst) in enumerate(
            (
                (motion_out, motion_hbm), (arr_rad, arr_hbm), *((gas_out.at[c], gas_hbm.at[c]) for c in range(3)),
                (liquid, liquid_hbm),
            )
        )
    ]
    layers, tiles, blocks, groups = sz.layers, sz.tiles, sz.blocks, sz.groups
    slab_blocks = n_rad * blocks
    T = n_rad * tiles
    block_rows = [G[d, pl.ds(sz.meta, 1), :] for d in range(n_rad)]

    rows = functools.partial(slab_rows, sz, n_rad, G)
    size = rows(sz.size)
    mass = size * size * size
    dep = [-mass * (state[pl.ds((3 + c) * T, T), :] - rows(sz.motion + (3 + c) * tiles)) for c in range(3)] + [mass]
    even = iota((T, BLOCK), 1) < GROUP

    for c in range(4):
        high = dep[c].astype(BF16).astype(F32)
        low = dep[c] - high
        for piece, part in enumerate((high, low)):
            deps[pl.ds((piece * 8 + c) * T, T), :] = jnp.where(even, part, 0.0)
            deps[pl.ds((piece * 8 + 4 + c) * T, T), :] = jnp.where(even, 0.0, part)
    cell = iota((BLOCK, BLOCK), 0).astype(F32).astype(BF16)
    one, none = jnp.ones((BLOCK, BLOCK), BF16), jnp.zeros((BLOCK, BLOCK), BF16)
    blank = jnp.zeros((16, BLOCK), BF16)
    for d in range(n_rad):
        for i in range(0, tiles, 2):
            onehot, lhs = [], []
            for t in (i, i + 1):
                off = jnp.broadcast_to(G[d, pl.ds(sz.offset + t, 1), :], (16, BLOCK)).astype(BF16)
                onehot.append(jnp.where(cell == jnp.concatenate([off] * (BLOCK // 16), axis=0), one, none))
                lhs.append(deps[pl.ds(d * tiles + t, 16, stride=T), :].astype(BF16))
            lhs = jnp.concatenate(
                [jnp.concatenate([lhs[0], blank], axis=1), jnp.concatenate([blank, lhs[1]], axis=1)], axis=0
            )
            res = dot_nt(lhs, jnp.concatenate(onehot, axis=1))
            for k in range(2):
                t = d * tiles + i + k
                both = res[16 * k : 16 * k + 8] + res[16 * k + 8 : 16 * k + 16]
                spread[pl.ds(2 * t, 4, stride=2 * T), :] = both[:4]
                spread[pl.ds(2 * t + 1, 4, stride=2 * T), :] = both[4:]
    own = iota((blocks, groups), 0) + r * blocks
    adder = jnp.concatenate(
        [(own == b[:, :groups].astype(I32)).astype(F32) for b in block_rows] * 2, axis=1
    ).astype(BF16)
    for c in range(4):
        high, low = split2(spread[pl.ds(c * 2 * T, 2 * T), :])
        total = dot(adder, jnp.concatenate([high, low], axis=0))
        for q in range(sz.quarters):
            part = total[q * layers : (q + 1) * layers]
            at = slice(q * BLOCK, (q + 1) * BLOCK)
            if c < 3:
                gas_out[c, :, at] = G[r, pl.ds(sz.gas + c * blocks + q * layers, layers), :] + part
            else:
                liquid[:, at] = part
    for send in sends[2:]:
        send.start()

    pres = jnp.concatenate([G[d, pl.ds(sz.pres, blocks), :] for d in range(n_rad)], axis=0)
    index = [
        jnp.broadcast_to(aux[pl.ds(8, blocks), k : k + 1], (blocks, BLOCK)).astype(jnp.int16) for k in range(4)
    ]
    one, none = jnp.ones((blocks, BLOCK), BF16), jnp.zeros((blocks, BLOCK), BF16)
    lanes = iota((blocks, BLOCK), 1)
    counts = []
    for t in range(NT):
        row = []
        for first in range(0, slab_blocks, BLOCK):
            aim = (lanes + (t * slab_blocks + first)).astype(jnp.int16)
            count = jnp.where(aim == index[0], one, none)
            for k in range(1, 4):
                count = count + jnp.where(aim == index[k], one, none)
            row.append(count)
        counts.append(jnp.concatenate(row, axis=1))
    grouped = dot(jnp.concatenate(counts, axis=0), jnp.concatenate(split2(pres), axis=1))
    grouped = grouped[:, :BLOCK] + grouped[:, BLOCK:]
    mine = pl.multiple_of(r * tiles, tiles)
    for i in range(tiles):
        motion_out[:, i * BLOCK : (i + 1) * BLOCK] = state[pl.ds(mine + i, 6, stride=T), :]
    sends[0].start()
    width = arr_rad.shape[2]
    for slot, exists, other in ((0, r > 0, jnp.maximum(r - 1, 0)), (1, r < n_rad - 1, jnp.minimum(r + 1, n_rad - 1))):
        idx = G[other, pl.ds(sz.meta + 1 + slot, 1), :].astype(I32)
        idx = jnp.where(exists, idx, -1)
        got = pick(sz, state_of(sz, T, state, other), idx)
        for c in range(7):
            arr_rad[c, slot : slot + 1, :] = got[c][:, :width]
    sends[1].start()

    grouped = jnp.concatenate([grouped[t * blocks : (t + 1) * blocks] for t in range(NT)], axis=1)
    matrices = jnp.concatenate([table[t] for t in range(NT)], axis=1)
    sums = dot_nt(jnp.concatenate(split2(grouped), axis=0), jnp.concatenate(split2(matrices), axis=0))
    coup[...] = sums[:blocks, :BLOCK] + sums[:blocks, BLOCK:] + sums[blocks:, :BLOCK]
    layer = iota((layers, BLOCK), 0)
    for q in range(sz.quarters):
        p = G[r, pl.ds(sz.pres + q * layers, layers), :]
        below = jnp.where(layer == 0, 0.0, pltpu.roll(p, 1, 0))
        above = jnp.where(layer == layers - 1, 0.0, pltpu.roll(p, layers - 1, 0))
        image[:, q * BLOCK : (q + 1) * BLOCK] = (
            DIAG * p - above - below + coup[pl.ds(q, layers, stride=sz.quarters), :]
        )
    for send in sends:
        send.wait()


def finish_kernel(sz, n_ax, got_a, got_b, image, arr_ax, pressure_image):
    a = lax.axis_index("ax")
    even = a % 2 == 0
    low = jnp.where(a > 0, jnp.where(even, got_b[...], got_a[...]), 0.0)
    up = jnp.where(a < n_ax - 1, jnp.where(even, got_a[...], got_b[...]), 0.0)
    half = arr_ax.shape[2]
    for slot, got in enumerate((low, up)):
        pair = (got, pltpu.roll(got, BLOCK // 2, 1))
        for c in range(7):
            arr_ax[c, slot : slot + 1, :] = pair[c % 2][4 + c // 2 : 5 + c // 2, :half]
    pressure_image[...] = image[...]
    last = sz.layers - 1
    for q in range(sz.quarters):
        at = slice(q * BLOCK, (q + 1) * BLOCK)
        pressure_image[0:1, at] = image[0:1, at] - low[q : q + 1, :]
        pressure_image[last : last + 1, at] = image[last : last + 1, at] - up[q : q + 1, :]


def on_device(
    parcel_motion,
    parcel_size,
    parcel_block,
    parcel_offset,
    gas_velocity,
    pressure,
    block_cols,
    block_kinds,
    block_table,
    send_axial,
    send_radial,
    send_counts,
):
    n_ax, n_rad = lax.axis_size("ax"), lax.axis_size("rad")
    layers, radial = pressure.shape
    parcels = parcel_size.shape[0]
    sz = Sizes(layers, radial, parcels)
    T = n_rad * sz.tiles
    cap_ax, cap_rad = send_axial.shape[-1], send_radial.shape[-1]
    params = pltpu.CompilerParams(vmem_limit_bytes=VMEM_LIMIT)
    counts = send_counts.reshape(1, 4)
    size2 = parcel_size.reshape(sz.tiles, BLOCK)
    offset2 = parcel_offset.reshape(sz.tiles, BLOCK)

    packed, aux = pl.pallas_call(
        functools.partial(pack_kernel, sz, n_rad),
        out_shape=[
            jax.ShapeDtypeStruct((sz.rows, BLOCK), F32),
            jax.ShapeDtypeStruct((8 + sz.blocks, BLOCK), I32),
        ],
        in_specs=[hbm] * 11,
        out_specs=[vmem] * 2,
        scratch_shapes=[
            pltpu.VMEM(parcel_motion.shape, F32),
            pltpu.VMEM(size2.shape, F32),
            pltpu.VMEM((1, sz.groups), I32),
            pltpu.VMEM(offset2.shape, I32),
            pltpu.VMEM(gas_velocity.shape, F32),
            pltpu.VMEM(pressure.shape, F32),
            pltpu.VMEM((2, cap_rad), I32),
            pltpu.SMEM((1, 4), I32),
            pltpu.VMEM((4, sz.blocks), I32),
            pltpu.VMEM((4, sz.blocks), I32),
            pltpu.VMEM((2, cap_ax), I32),
            pltpu.SemaphoreType.DMA((13,)),
        ],
        compiler_params=params,
        name="pack",
    )(
        *(
            pltpu.with_memory_space_constraint(x, pltpu.HBM)
            for x in (
                parcel_motion, size2, parcel_block.reshape(1, sz.groups), offset2, gas_velocity, pressure,
                send_radial.reshape(2, cap_rad), counts, block_cols[0].T, block_kinds[0].T,
                send_axial.reshape(2, cap_ax),
            )
        )
    )
    gathered = lax.all_gather(packed, "rad", axis=0)

    state, message_a, message_b = pl.pallas_call(
        functools.partial(move_kernel, sz, n_rad),
        out_shape=[
            jax.ShapeDtypeStruct((7 * T, BLOCK), F32),
            jax.ShapeDtypeStruct((8, BLOCK), F32),
            jax.ShapeDtypeStruct((8, BLOCK), F32),
        ],
        in_specs=[vmem] * 2,
        out_specs=[vmem] * 3,
        scratch_shapes=[pltpu.VMEM((3, n_rad * sz.groups, BLOCK), F32)],
        compiler_params=params,
        cost_estimate=pl.CostEstimate(flops=4_000_000_000, bytes_accessed=1_000_000, transcendentals=0),
        name="move",
    )(gathered, aux)

    def exchange(message, first):
        to = list(range(n_ax * n_rad))
        for low in range(first, n_ax - 1, 2):
            for r in range(n_rad):
                i, j = low * n_rad + r, (low + 1) * n_rad + r
                to[i], to[j] = j, i
        alone = [i for i in range(n_ax * n_rad) if to[i] == i]
        for i, j in zip(alone[0::2], alone[1::2]):
            to[i], to[j] = j, i
        return lax.ppermute(message, ("ax", "rad"), list(enumerate(to)))

    got_b = exchange(message_b, 1)
    got_a = exchange(message_a, 0)

    motion_out, arr_rad, gas_out, liquid, image = pl.pallas_call(
        functools.partial(rest_kernel, sz, n_rad),
        out_shape=[
            jax.ShapeDtypeStruct((6, parcels), F32),
            jax.ShapeDtypeStruct((7, 2, cap_rad), F32),
            jax.ShapeDtypeStruct(gas_velocity.shape, F32),
            jax.ShapeDtypeStruct(pressure.shape, F32),
            jax.ShapeDtypeStruct(pressure.shape, F32),
        ],
        in_specs=[vmem] * 4,
        out_specs=[hbm] * 4 + [vmem],
        scratch_shapes=[
            pltpu.VMEM((16 * T, BLOCK), F32),
            pltpu.VMEM((4 * 2 * T, BLOCK), F32),
            pltpu.VMEM((sz.blocks, BLOCK), F32),
            pltpu.VMEM((6, parcels), F32),
            pltpu.VMEM((7, 2, cap_rad), F32),
            pltpu.VMEM(gas_velocity.shape, F32),
            pltpu.VMEM(pressure.shape, F32),
            pltpu.SemaphoreType.DMA((6,)),
        ],
        compiler_params=params,
        cost_estimate=pl.CostEstimate(flops=2_000_000_000, bytes_accessed=2_000_000, transcendentals=0),
        name="rest",
    )(gathered, aux, block_table, state)

    arr_ax, pressure_image = pl.pallas_call(
        functools.partial(finish_kernel, sz, n_ax),
        out_shape=[
            jax.ShapeDtypeStruct((7, 2, cap_ax), F32),
            jax.ShapeDtypeStruct(pressure.shape, F32),
        ],
        in_specs=[vmem] * 3,
        out_specs=[vmem] * 2,
        compiler_params=params,
        name="finish",
    )(got_a, got_b, image)

    arrivals_axial = arr_ax.transpose(1, 0, 2)[None, None]
    arrivals_radial = arr_rad.transpose(1, 0, 2)[None, None]
    return (motion_out, arrivals_axial, arrivals_radial, gas_out, liquid, pressure_image)


def solution(mesh):
    return jax.shard_map(
        on_device,
        mesh=mesh,
        in_specs=(
            P(None, ("ax", "rad")),
            P(("ax", "rad")),
            P(("ax", "rad")),
            P(("ax", "rad")),
            P(None, "ax", "rad"),
            P("ax", "rad"),
            P("ax", "rad", None),
            P("ax", "rad", None),
            P(),
            P("ax", "rad", None, None),
            P("ax", "rad", None, None),
            P("ax", "rad", None),
        ),
        out_specs=(
            P(None, ("ax", "rad")),
            P("ax", "rad", None, None, None),
            P("ax", "rad", None, None, None),
            P(None, "ax", "rad"),
            P("ax", "rad"),
            P("ax", "rad"),
        ),
        check_vma=False,
    )
```

```python
import functools

import jax
import jax.numpy as jnp
from jax import lax
from jax.experimental import pallas as pl
from jax.experimental.pallas import tpu as pltpu
from jax.sharding import PartitionSpec as P

BLOCK = 128
GROUP = 64
NT = 8
DRAG = 0.5
STEP = 0.5
DIAG = 6.0
VMEM_LIMIT = 24 * 1024 * 1024

F32 = jnp.float32
BF16 = jnp.bfloat16
I32 = jnp.int32

vmem = pl.BlockSpec(memory_space=pltpu.VMEM)
hbm = pl.BlockSpec(memory_space=pltpu.HBM)


class Sizes:
    def __init__(self, layers, radial, parcels):
        self.layers = layers
        self.quarters = radial // BLOCK
        self.blocks = layers * self.quarters
        self.tiles = parcels // BLOCK
        self.groups = parcels // GROUP
        self.gas = 0
        self.pres = 3 * self.blocks
        self.motion = self.pres + self.blocks
        self.size = self.motion + 6 * self.tiles
        self.offset = self.size + self.tiles
        self.meta = self.offset + self.tiles
        self.column = self.meta + 8
        self.rows = self.column + self.groups


def split2(x):
    high = x.astype(BF16)
    return high, (x - high.astype(F32)).astype(BF16)


def dot(a, b):
    return jnp.dot(a, b, preferred_element_type=F32)


def dot_nt(a, b):
    return lax.dot_general(a, b, (((1,), (1,)), ((), ())), preferred_element_type=F32)


def iota(shape, dim):
    return lax.broadcasted_iota(I32, shape, dim)


def block_row(sz, b):
    local = b % sz.blocks
    return b - local + (local % sz.quarters) * sz.layers + local // sz.quarters


def pack_kernel(
    sz, n_rad, motion_hbm, size_hbm, block_hbm, offset_hbm, gas_hbm, pres_hbm, radial_hbm, counts_hbm, cols_hbm,
    kinds_hbm, axial_hbm,
    out, aux, cols, kinds,
    motion, size, block, offset, gas, pres, radial, counts, axial, sem,
):
    small = (
        (block_hbm, block), (counts_hbm, counts), (radial_hbm, radial), (axial_hbm, axial), (offset_hbm, offset),
        (size_hbm, size),
    )
    large = ((motion_hbm, motion), *((gas_hbm.at[c], gas.at[c]) for c in range(3)), (pres_hbm, pres))
    late = ((cols_hbm, cols), (kinds_hbm, kinds))
    copies = [pltpu.make_async_copy(src, dst, sem.at[i]) for i, (src, dst) in enumerate(large + small + late)]
    for copy in copies:
        copy.start()
    motion_copy, *gas_copies, pres_copy = copies[: len(large)]
    late_copies = copies[len(large + small) :]
    out[pl.ds(sz.meta, 8), :] = jnp.full((8, BLOCK), -1.0, F32)
    layers = sz.layers
    for copy in copies[len(large) : len(large + small)]:
        copy.wait()
    out[pl.ds(sz.size, sz.tiles), :] = size[...]
    out[pl.ds(sz.offset, sz.tiles), :] = offset[...].astype(F32)
    numbers = block_row(sz, block[...]).astype(F32)
    out[pl.ds(sz.meta, 1), pl.ds(0, sz.groups)] = numbers
    numbers = jnp.concatenate([numbers, jnp.zeros((1, BLOCK - sz.groups), F32)], axis=1)
    lane = iota((8, BLOCK), 1)
    order = jnp.where(lane < sz.tiles, 2 * lane, 2 * (lane - sz.tiles) + 1) & (sz.groups - 1)
    numbers = take_lanes(jnp.broadcast_to(numbers, (8, BLOCK)), order)
    numbers = jnp.concatenate([numbers] * (BLOCK // 8), axis=0)
    out[pl.ds(sz.column, sz.groups), :] = jnp.transpose(numbers)[: sz.groups]
    width = radial.shape[1]
    lane = iota((1, width), 1)
    for slot in range(2):
        kept = jnp.where(lane < counts[0, 2 + slot], radial[slot : slot + 1, :], -1)
        out[pl.ds(sz.meta + 1 + slot, 1), pl.ds(0, width)] = kept.astype(F32)
    lane = iota((1, axial.shape[1]), 1)
    kept = [jnp.where(lane < counts[0, slot], axial[slot : slot + 1, :], -1) for slot in range(2)]
    aux[pl.ds(0, 1), :] = jnp.concatenate(kept, axis=1)
    motion_copy.wait()
    for i in range(sz.tiles):
        out[pl.ds(sz.motion + i, 6, stride=sz.tiles), :] = motion[:, i * BLOCK : (i + 1) * BLOCK]
    for copy in (*gas_copies, pres_copy, *late_copies):
        copy.wait()
    for c in range(3):
        for q in range(sz.quarters):
            out[pl.ds(sz.gas + c * sz.blocks + q * layers, layers), :] = gas[c, :, q * BLOCK : (q + 1) * BLOCK]
    for q in range(sz.quarters):
        out[pl.ds(sz.pres + q * layers, layers), :] = pres[:, q * BLOCK : (q + 1) * BLOCK]


def take_lanes(x, idx):
    return jnp.take_along_axis(x, idx, axis=1, mode="promise_in_bounds")


def pick(sz, state, idx):
    shape = (sz.tiles, BLOCK)
    idx = jnp.broadcast_to(idx, shape)
    lane = idx & (BLOCK - 1)
    here = (idx >> 7) == iota(shape, 0)
    return [jnp.sum(jnp.where(here, take_lanes(s, lane), 0.0), axis=0, keepdims=True) for s in state]


def slab_rows(sz, n_rad, G, first):
    return jnp.concatenate([G[d, pl.ds(first, sz.tiles), :] for d in range(n_rad)], axis=0)


def state_of(sz, T, state, d):
    first = pl.multiple_of(d * sz.tiles, sz.tiles)
    return [state[pl.ds(c * T + first, sz.tiles), :] for c in range(7)]


def move_kernel(sz, n_rad, G, aux, cols, kinds, state, message, columns):
    r = lax.axis_index("rad")
    layers, tiles, blocks, groups = sz.layers, sz.tiles, sz.blocks, sz.groups
    slab_blocks = n_rad * blocks
    T = n_rad * tiles

    column = jnp.concatenate([G[d, pl.ds(sz.column, groups), :] for d in range(n_rad)], axis=0).astype(I32)
    lanes = iota((n_rad * groups, BLOCK), 1)
    chooser = jnp.concatenate(
        [(column == lanes + first).astype(F32).astype(BF16) for first in range(0, slab_blocks, BLOCK)], axis=1
    )
    gas_slab = jnp.concatenate(
        [
            jnp.concatenate([G[d, pl.ds(sz.gas + c * blocks, blocks), :] for d in range(n_rad)], axis=0)
            for c in range(3)
        ],
        axis=1,
    )
    high, low = split2(gas_slab)
    found = dot(jnp.concatenate([chooser, chooser], axis=1), jnp.concatenate([high, low], axis=0))

    def groups_of(c, odd):
        return jnp.concatenate(
            [
                found[d * groups + odd * tiles : d * groups + (odd + 1) * tiles, c * BLOCK : (c + 1) * BLOCK]
                for d in range(n_rad)
            ],
            axis=0,
        )

    rows = functools.partial(slab_rows, sz, n_rad, G)
    size = rows(sz.size)
    offset = rows(sz.offset).astype(I32)
    factor = jnp.exp(-DRAG / (size * size))
    even = iota((T, BLOCK), 1) < GROUP
    values = [None] * 6 + [size]
    for c in range(3):
        u = jnp.where(even, take_lanes(groups_of(c, 0), offset), take_lanes(groups_of(c, 1), offset))
        v = rows(sz.motion + (3 + c) * tiles)
        new = u + (v - u) * factor
        values[c] = rows(sz.motion + c * tiles) + STEP * new
        values[3 + c] = new
    own = []
    for c in range(7):
        state[pl.ds(c * T, T), :] = values[c]
        mine = values[c][:tiles]
        for d in range(1, n_rad):
            mine = jnp.where(r == d, values[c][d * tiles : (d + 1) * tiles], mine)
        own.append(mine)

    payload = pick(sz, own, aux[pl.ds(0, 1), :])
    for c in range(7):
        message[c : c + 1, :] = payload[c]
    message[7:8, :] = jnp.zeros((1, BLOCK), F32)
    for q in range(sz.quarters):
        first = sz.pres + q * layers
        message[8 + q : 9 + q, :] = G[r, pl.ds(first + layers - 1, 1), :]
        message[12 + q : 13 + q, :] = G[r, pl.ds(first, 1), :]
    index = kinds[...] * slab_blocks + block_row(sz, cols[...])
    index = jnp.concatenate([index, index], axis=1).astype(F32)
    index = jnp.concatenate([index, jnp.zeros((BLOCK - index.shape[0], BLOCK), F32)], axis=0)
    columns[...] = jnp.transpose(index)[:blocks].astype(I32)


def rest_kernel(
    sz, n_rad, G, columns, table, state,
    motion_hbm, arr_hbm, gas_hbm, liquid_hbm, image,
    deps, spread, coup, motion_out, arr_rad, gas_out, liquid, sem,
):
    r = lax.axis_index("rad")
    sends = [
        pltpu.make_async_copy(src, dst, sem.at[i])
        for i, (src, dst) in enumerate(
            (
                (motion_out, motion_hbm), (arr_rad, arr_hbm), *((gas_out.at[c], gas_hbm.at[c]) for c in range(3)),
                (liquid, liquid_hbm),
            )
        )
    ]
    layers, tiles, blocks, groups = sz.layers, sz.tiles, sz.blocks, sz.groups
    slab_blocks = n_rad * blocks
    T = n_rad * tiles
    block_rows = [G[d, pl.ds(sz.meta, 1), :] for d in range(n_rad)]

    rows = functools.partial(slab_rows, sz, n_rad, G)
    size = rows(sz.size)
    mass = size * size * size
    dep = [-mass * (state[pl.ds((3 + c) * T, T), :] - rows(sz.motion + (3 + c) * tiles)) for c in range(3)] + [mass]
    even = iota((T, BLOCK), 1) < GROUP

    for c in range(4):
        high = dep[c].astype(BF16).astype(F32)
        low = dep[c] - high
        for piece, part in enumerate((high, low)):
            deps[pl.ds((piece * 8 + c) * T, T), :] = jnp.where(even, part, 0.0)
            deps[pl.ds((piece * 8 + 4 + c) * T, T), :] = jnp.where(even, 0.0, part)
    cell = iota((BLOCK, BLOCK), 0).astype(F32).astype(BF16)
    one, none = jnp.ones((BLOCK, BLOCK), BF16), jnp.zeros((BLOCK, BLOCK), BF16)
    blank = jnp.zeros((16, BLOCK), BF16)
    for d in range(n_rad):
        for i in range(0, tiles, 2):
            onehot, lhs = [], []
            for t in (i, i + 1):
                off = jnp.broadcast_to(G[d, pl.ds(sz.offset + t, 1), :], (16, BLOCK)).astype(BF16)
                onehot.append(jnp.where(cell == jnp.concatenate([off] * (BLOCK // 16), axis=0), one, none))
                lhs.append(deps[pl.ds(d * tiles + t, 16, stride=T), :].astype(BF16))
            lhs = jnp.concatenate(
                [jnp.concatenate([lhs[0], blank], axis=1), jnp.concatenate([blank, lhs[1]], axis=1)], axis=0
            )
            res = dot_nt(lhs, jnp.concatenate(onehot, axis=1))
            for k in range(2):
                t = d * tiles + i + k
                both = res[16 * k : 16 * k + 8] + res[16 * k + 8 : 16 * k + 16]
                spread[pl.ds(2 * t, 4, stride=2 * T), :] = both[:4]
                spread[pl.ds(2 * t + 1, 4, stride=2 * T), :] = both[4:]
    own = iota((blocks, groups), 0) + r * blocks
    adder = jnp.concatenate(
        [(own == b[:, :groups].astype(I32)).astype(F32) for b in block_rows] * 2, axis=1
    ).astype(BF16)
    for c in range(4):
        high, low = split2(spread[pl.ds(c * 2 * T, 2 * T), :])
        total = dot(adder, jnp.concatenate([high, low], axis=0))
        for q in range(sz.quarters):
            part = total[q * layers : (q + 1) * layers]
            at = slice(q * BLOCK, (q + 1) * BLOCK)
            if c < 3:
                gas_out[c, :, at] = G[r, pl.ds(sz.gas + c * blocks + q * layers, layers), :] + part
            else:
                liquid[:, at] = part
    for send in sends[2:]:
        send.start()

    pres = jnp.concatenate([G[d, pl.ds(sz.pres, blocks), :] for d in range(n_rad)], axis=0)
    index = [
        jnp.broadcast_to(columns[:, k : k + 1], (blocks, BLOCK)).astype(jnp.int16) for k in range(4)
    ]
    one, none = jnp.ones((blocks, BLOCK), BF16), jnp.zeros((blocks, BLOCK), BF16)
    lanes = iota((blocks, BLOCK), 1)
    counts = []
    for t in range(NT):
        row = []
        for first in range(0, slab_blocks, BLOCK):
            aim = (lanes + (t * slab_blocks + first)).astype(jnp.int16)
            count = jnp.where(aim == index[0], one, none)
            for k in range(1, 4):
                count = count + jnp.where(aim == index[k], one, none)
            row.append(count)
        counts.append(jnp.concatenate(row, axis=1))
    grouped = dot(jnp.concatenate(counts, axis=0), jnp.concatenate(split2(pres), axis=1))
    grouped = grouped[:, :BLOCK] + grouped[:, BLOCK:]
    mine = pl.multiple_of(r * tiles, tiles)
    for i in range(tiles):
        motion_out[:, i * BLOCK : (i + 1) * BLOCK] = state[pl.ds(mine + i, 6, stride=T), :]
    sends[0].start()
    width = arr_rad.shape[2]
    for slot, exists, other in ((0, r > 0, jnp.maximum(r - 1, 0)), (1, r < n_rad - 1, jnp.minimum(r + 1, n_rad - 1))):
        idx = G[other, pl.ds(sz.meta + 1 + slot, 1), :].astype(I32)
        idx = jnp.where(exists, idx, -1)
        got = pick(sz, state_of(sz, T, state, other), idx)
        for c in range(7):
            arr_rad[c, slot : slot + 1, :] = got[c][:, :width]
    sends[1].start()

    grouped = jnp.concatenate([grouped[t * blocks : (t + 1) * blocks] for t in range(NT)], axis=1)
    matrices = jnp.concatenate([table[t] for t in range(NT)], axis=1)
    sums = dot_nt(jnp.concatenate(split2(grouped), axis=0), jnp.concatenate(split2(matrices), axis=0))
    coup[...] = sums[:blocks, :BLOCK] + sums[:blocks, BLOCK:] + sums[blocks:, :BLOCK]
    layer = iota((layers, BLOCK), 0)
    for q in range(sz.quarters):
        p = G[r, pl.ds(sz.pres + q * layers, layers), :]
        below = jnp.where(layer == 0, 0.0, pltpu.roll(p, 1, 0))
        above = jnp.where(layer == layers - 1, 0.0, pltpu.roll(p, layers - 1, 0))
        image[:, q * BLOCK : (q + 1) * BLOCK] = (
            DIAG * p - above - below + coup[pl.ds(q, layers, stride=sz.quarters), :]
        )
    for send in sends:
        send.wait()


def finish_kernel(sz, n_ax, got_a, got_b, image, arr_ax, pressure_image):
    a = lax.axis_index("ax")
    even = a % 2 == 0
    low = jnp.where(a > 0, jnp.where(even, got_b[...], got_a[...]), 0.0)
    up = jnp.where(a < n_ax - 1, jnp.where(even, got_a[...], got_b[...]), 0.0)
    half = arr_ax.shape[2]
    for c in range(7):
        arr_ax[c, 0:1, :] = low[c : c + 1, 0:half]
        arr_ax[c, 1:2, :] = up[c : c + 1, half : 2 * half]
    pressure_image[...] = image[...]
    last = sz.layers - 1
    for q in range(sz.quarters):
        at = slice(q * BLOCK, (q + 1) * BLOCK)
        pressure_image[0:1, at] = image[0:1, at] - low[8 + q : 9 + q, :]
        pressure_image[last : last + 1, at] = image[last : last + 1, at] - up[12 + q : 13 + q, :]


def on_device(
    parcel_motion,
    parcel_size,
    parcel_block,
    parcel_offset,
    gas_velocity,
    pressure,
    block_cols,
    block_kinds,
    block_table,
    send_axial,
    send_radial,
    send_counts,
):
    n_ax, n_rad = lax.axis_size("ax"), lax.axis_size("rad")
    layers, radial = pressure.shape
    parcels = parcel_size.shape[0]
    sz = Sizes(layers, radial, parcels)
    T = n_rad * sz.tiles
    cap_ax, cap_rad = send_axial.shape[-1], send_radial.shape[-1]
    params = pltpu.CompilerParams(vmem_limit_bytes=VMEM_LIMIT)
    counts = send_counts.reshape(1, 4)
    size2 = parcel_size.reshape(sz.tiles, BLOCK)
    offset2 = parcel_offset.reshape(sz.tiles, BLOCK)

    packed, aux, cols, kinds = pl.pallas_call(
        functools.partial(pack_kernel, sz, n_rad),
        out_shape=[
            jax.ShapeDtypeStruct((sz.rows, BLOCK), F32),
            jax.ShapeDtypeStruct((8, BLOCK), I32),
            jax.ShapeDtypeStruct((4, sz.blocks), I32),
            jax.ShapeDtypeStruct((4, sz.blocks), I32),
        ],
        in_specs=[hbm] * 11,
        out_specs=[vmem] * 4,
        scratch_shapes=[
            pltpu.VMEM(parcel_motion.shape, F32),
            pltpu.VMEM(size2.shape, F32),
            pltpu.VMEM((1, sz.groups), I32),
            pltpu.VMEM(offset2.shape, I32),
            pltpu.VMEM(gas_velocity.shape, F32),
            pltpu.VMEM(pressure.shape, F32),
            pltpu.VMEM((2, cap_rad), I32),
            pltpu.SMEM((1, 4), I32),
            pltpu.VMEM((2, cap_ax), I32),
            pltpu.SemaphoreType.DMA((13,)),
        ],
        compiler_params=params,
        name="pack",
    )(
        *(
            pltpu.with_memory_space_constraint(x, pltpu.HBM)
            for x in (
                parcel_motion, size2, parcel_block.reshape(1, sz.groups), offset2, gas_velocity, pressure,
                send_radial.reshape(2, cap_rad), counts, block_cols[0].T, block_kinds[0].T,
                send_axial.reshape(2, cap_ax),
            )
        )
    )
    gathered = lax.all_gather(packed, "rad", axis=0)

    state, message, columns = pl.pallas_call(
        functools.partial(move_kernel, sz, n_rad),
        out_shape=[
            jax.ShapeDtypeStruct((7 * T, BLOCK), F32),
            jax.ShapeDtypeStruct((16, BLOCK), F32),
            jax.ShapeDtypeStruct((sz.blocks, BLOCK), I32),
        ],
        in_specs=[vmem] * 4,
        out_specs=[vmem] * 3,
        compiler_params=params,
        cost_estimate=pl.CostEstimate(flops=4_000_000_000, bytes_accessed=1_000_000, transcendentals=0),
        name="move",
    )(gathered, aux, cols, kinds)

    def exchange(first):
        to = list(range(n_ax * n_rad))
        for low in range(first, n_ax - 1, 2):
            for r in range(n_rad):
                i, j = low * n_rad + r, (low + 1) * n_rad + r
                to[i], to[j] = j, i
        alone = [i for i in range(n_ax * n_rad) if to[i] == i]
        for i, j in zip(alone[0::2], alone[1::2]):
            to[i], to[j] = j, i
        return lax.ppermute(message, ("ax", "rad"), list(enumerate(to)))

    got_b = exchange(1)
    got_a = exchange(0)

    motion_out, arr_rad, gas_out, liquid, image = pl.pallas_call(
        functools.partial(rest_kernel, sz, n_rad),
        out_shape=[
            jax.ShapeDtypeStruct((6, parcels), F32),
            jax.ShapeDtypeStruct((7, 2, cap_rad), F32),
            jax.ShapeDtypeStruct(gas_velocity.shape, F32),
            jax.ShapeDtypeStruct(pressure.shape, F32),
            jax.ShapeDtypeStruct(pressure.shape, F32),
        ],
        in_specs=[vmem] * 4,
        out_specs=[hbm] * 4 + [vmem],
        scratch_shapes=[
            pltpu.VMEM((16 * T, BLOCK), F32),
            pltpu.VMEM((4 * 2 * T, BLOCK), F32),
            pltpu.VMEM((sz.blocks, BLOCK), F32),
            pltpu.VMEM((6, parcels), F32),
            pltpu.VMEM((7, 2, cap_rad), F32),
            pltpu.VMEM(gas_velocity.shape, F32),
            pltpu.VMEM(pressure.shape, F32),
            pltpu.SemaphoreType.DMA((6,)),
        ],
        compiler_params=params,
        cost_estimate=pl.CostEstimate(flops=2_000_000_000, bytes_accessed=2_000_000, transcendentals=0),
        name="rest",
    )(gathered, columns, block_table, state)

    arr_ax, pressure_image = pl.pallas_call(
        functools.partial(finish_kernel, sz, n_ax),
        out_shape=[
            jax.ShapeDtypeStruct((7, 2, cap_ax), F32),
            jax.ShapeDtypeStruct(pressure.shape, F32),
        ],
        in_specs=[vmem] * 3,
        out_specs=[vmem] * 2,
        compiler_params=params,
        name="finish",
    )(got_a, got_b, image)

    arrivals_axial = arr_ax.transpose(1, 0, 2)[None, None]
    arrivals_radial = arr_rad.transpose(1, 0, 2)[None, None]
    return (motion_out, arrivals_axial, arrivals_radial, gas_out, liquid, pressure_image)


def solution(mesh):
    return jax.shard_map(
        on_device,
        mesh=mesh,
        in_specs=(
            P(None, ("ax", "rad")),
            P(("ax", "rad")),
            P(("ax", "rad")),
            P(("ax", "rad")),
            P(None, "ax", "rad"),
            P("ax", "rad"),
            P("ax", "rad", None),
            P("ax", "rad", None),
            P(),
            P("ax", "rad", None, None),
            P("ax", "rad", None, None),
            P("ax", "rad", None),
        ),
        out_specs=(
            P(None, ("ax", "rad")),
            P("ax", "rad", None, None, None),
            P("ax", "rad", None, None, None),
            P(None, "ax", "rad"),
            P("ax", "rad"),
            P("ax", "rad"),
        ),
        check_vma=False,
    )
```

```python
import functools

import jax
import jax.numpy as jnp
from jax import lax
from jax.experimental import pallas as pl
from jax.experimental.pallas import tpu as pltpu
from jax.sharding import PartitionSpec as P

BLOCK = 128
GROUP = 64
NT = 8
DRAG = 0.5
STEP = 0.5
DIAG = 6.0
VMEM_LIMIT = 24 * 1024 * 1024

F32 = jnp.float32
BF16 = jnp.bfloat16
I32 = jnp.int32

vmem = pl.BlockSpec(memory_space=pltpu.VMEM)
hbm = pl.BlockSpec(memory_space=pltpu.HBM)


class Sizes:
    def __init__(self, layers, radial, parcels):
        self.layers = layers
        self.quarters = radial // BLOCK
        self.blocks = layers * self.quarters
        self.tiles = parcels // BLOCK
        self.groups = parcels // GROUP
        self.gas = 0
        self.pres = 3 * self.blocks
        self.motion = self.pres + self.blocks
        self.size = self.motion + 6 * self.tiles
        self.offset = self.size + self.tiles
        self.meta = self.offset + self.tiles
        self.column = self.meta + 8
        self.rows = self.column + self.groups


def split2(x):
    high = x.astype(BF16)
    return high, (x - high.astype(F32)).astype(BF16)


def dot(a, b):
    return jnp.dot(a, b, preferred_element_type=F32)


def dot_nt(a, b):
    return lax.dot_general(a, b, (((1,), (1,)), ((), ())), preferred_element_type=F32)


def iota(shape, dim):
    return lax.broadcasted_iota(I32, shape, dim)


def block_row(sz, b):
    local = b % sz.blocks
    return b - local + (local % sz.quarters) * sz.layers + local // sz.quarters


def pack_kernel(
    sz, n_rad, motion_hbm, size_hbm, block_hbm, offset_hbm, gas_hbm, pres_hbm, radial_hbm, counts_hbm, cols_hbm,
    kinds_hbm, axial_hbm,
    out, aux,
    motion, size, block, offset, gas, pres, radial, counts, cols, kinds, axial, sem,
):
    def put(at, lanes, value):
        for d in range(n_rad):
            out[d, at, lanes] = value

    small = (
        (counts_hbm, counts), (block_hbm, block), (radial_hbm, radial), (axial_hbm, axial), (cols_hbm, cols),
        (kinds_hbm, kinds), (offset_hbm, offset), (size_hbm, size),
    )
    large = ((motion_hbm, motion), (pres_hbm, pres), *((gas_hbm.at[c], gas.at[c]) for c in range(3)))
    copies = [pltpu.make_async_copy(src, dst, sem.at[i]) for i, (src, dst) in enumerate(small + large)]
    for copy in copies:
        copy.start()
    put(pl.ds(sz.meta, 8), slice(None), jnp.full((8, BLOCK), -1.0, F32))
    layers = sz.layers
    for copy in copies[: len(small)]:
        copy.wait()
    put(pl.ds(sz.size, sz.tiles), slice(None), size[...])
    put(pl.ds(sz.offset, sz.tiles), slice(None), offset[...].astype(F32))
    numbers = block_row(sz, block[...]).astype(F32)
    put(pl.ds(sz.meta, 1), pl.ds(0, sz.groups), numbers)
    numbers = jnp.concatenate([numbers, jnp.zeros((1, BLOCK - sz.groups), F32)], axis=1)
    put(pl.ds(sz.column, sz.groups), slice(None), jnp.transpose(jnp.broadcast_to(numbers, (BLOCK, BLOCK)))[: sz.groups])
    width = radial.shape[1]
    lane = iota((1, width), 1)
    for slot in range(2):
        kept = jnp.where(lane < counts[0, 2 + slot], radial[slot : slot + 1, :], -1)
        put(pl.ds(sz.meta + 1 + slot, 1), pl.ds(0, width), kept.astype(F32))
    index = kinds[...] * (n_rad * sz.blocks) + block_row(sz, cols[...])
    index = jnp.concatenate([index, index], axis=1).astype(F32)
    index = jnp.concatenate([index, jnp.zeros((BLOCK - index.shape[0], BLOCK), F32)], axis=0)
    aux[pl.ds(8, sz.blocks), :] = jnp.transpose(index)[: sz.blocks].astype(I32)
    lane = iota((1, axial.shape[1]), 1)
    kept = [jnp.where(lane < counts[0, slot], axial[slot : slot + 1, :], -1) for slot in range(2)]
    aux[pl.ds(0, 1), :] = jnp.concatenate(kept, axis=1)
    motion_copy, pres_copy, *gas_copies = copies[len(small) :]
    motion_copy.wait()
    for i in range(sz.tiles):
        put(pl.ds(sz.motion + i, 6, stride=sz.tiles), slice(None), motion[:, i * BLOCK : (i + 1) * BLOCK])
    pres_copy.wait()
    for q in range(sz.quarters):
        put(pl.ds(sz.pres + q * layers, layers), slice(None), pres[:, q * BLOCK : (q + 1) * BLOCK])
    for c in range(3):
        gas_copies[c].wait()
        for q in range(sz.quarters):
            put(pl.ds(sz.gas + c * sz.blocks + q * layers, layers), slice(None), gas[c, :, q * BLOCK : (q + 1) * BLOCK])


def take_lanes(x, idx):
    return jnp.take_along_axis(x, idx, axis=1, mode="promise_in_bounds")


def pick(sz, state, idx):
    shape = (sz.tiles, BLOCK)
    idx = jnp.broadcast_to(idx, shape)
    lane = idx & (BLOCK - 1)
    here = (idx >> 7) == iota(shape, 0)
    return [jnp.sum(jnp.where(here, take_lanes(s, lane), 0.0), axis=0, keepdims=True) for s in state]


def slab_rows(sz, n_rad, G, first):
    return jnp.concatenate([G[d, pl.ds(first, sz.tiles), :] for d in range(n_rad)], axis=0)


def state_of(sz, T, state, d):
    first = pl.multiple_of(d * sz.tiles, sz.tiles)
    return [state[pl.ds(c * T + first, sz.tiles), :] for c in range(7)]


def move_kernel(sz, n_rad, G, aux, state, message, near):
    r = lax.axis_index("rad")
    layers, tiles, blocks, groups = sz.layers, sz.tiles, sz.blocks, sz.groups
    slab_blocks = n_rad * blocks
    T = n_rad * tiles

    column = jnp.concatenate([G[d, pl.ds(sz.column, groups), :] for d in range(n_rad)], axis=0).astype(I32)
    lanes = iota((n_rad * groups, BLOCK), 1)
    chooser = jnp.concatenate(
        [(column == lanes + first).astype(F32).astype(BF16) for first in range(0, slab_blocks, BLOCK)], axis=1
    )
    gas_slab = jnp.concatenate(
        [
            jnp.concatenate([G[d, pl.ds(sz.gas + c * blocks, blocks), :] for d in range(n_rad)], axis=0)
            for c in range(3)
        ],
        axis=1,
    )
    high, low = split2(gas_slab)
    found = dot(jnp.concatenate([chooser, chooser], axis=1), jnp.concatenate([high, low], axis=0))
    for c in range(3):
        near[c] = found[:, c * BLOCK : (c + 1) * BLOCK]

    rows = functools.partial(slab_rows, sz, n_rad, G)
    size = rows(sz.size)
    offset = rows(sz.offset).astype(I32)
    factor = jnp.exp(-DRAG / (size * size))
    even = iota((T, BLOCK), 1) < GROUP
    for c in range(3):
        u_even = take_lanes(near[c, pl.ds(0, T, stride=2), :], offset)
        u_odd = take_lanes(near[c, pl.ds(1, T, stride=2), :], offset)
        u = jnp.where(even, u_even, u_odd)
        v = rows(sz.motion + (3 + c) * tiles)
        new = u + (v - u) * factor
        state[pl.ds(c * T, T), :] = rows(sz.motion + c * tiles) + STEP * new
        state[pl.ds((3 + c) * T, T), :] = new
    state[pl.ds(6 * T, T), :] = size

    payload = pick(sz, state_of(sz, T, state, r), aux[pl.ds(0, 1), :])
    for c in range(7):
        message[c : c + 1, :] = payload[c]
    message[7:8, :] = jnp.zeros((1, BLOCK), F32)
    for q in range(sz.quarters):
        first = sz.pres + q * layers
        message[8 + q : 9 + q, :] = G[r, pl.ds(first + layers - 1, 1), :]
        message[12 + q : 13 + q, :] = G[r, pl.ds(first, 1), :]


def rest_kernel(
    sz, n_rad, G, aux, table, state,
    motion_hbm, arr_hbm, gas_hbm, liquid_hbm, image,
    deps, spread, coup, motion_out, arr_rad, gas_out, liquid, sem,
):
    r = lax.axis_index("rad")
    sends = [
        pltpu.make_async_copy(src, dst, sem.at[i])
        for i, (src, dst) in enumerate(
            (
                (motion_out, motion_hbm), (arr_rad, arr_hbm), *((gas_out.at[c], gas_hbm.at[c]) for c in range(3)),
                (liquid, liquid_hbm),
            )
        )
    ]
    layers, tiles, blocks, groups = sz.layers, sz.tiles, sz.blocks, sz.groups
    slab_blocks = n_rad * blocks
    T = n_rad * tiles
    block_rows = [G[d, pl.ds(sz.meta, 1), :] for d in range(n_rad)]

    rows = functools.partial(slab_rows, sz, n_rad, G)
    size = rows(sz.size)
    mass = size * size * size
    dep = [-mass * (state[pl.ds((3 + c) * T, T), :] - rows(sz.motion + (3 + c) * tiles)) for c in range(3)] + [mass]
    even = iota((T, BLOCK), 1) < GROUP

    for c in range(4):
        high = dep[c].astype(BF16).astype(F32)
        low = dep[c] - high
        for piece, part in enumerate((high, low)):
            deps[pl.ds((piece * 8 + c) * T, T), :] = jnp.where(even, part, 0.0)
            deps[pl.ds((piece * 8 + 4 + c) * T, T), :] = jnp.where(even, 0.0, part)
    cell = iota((BLOCK, BLOCK), 0).astype(F32).astype(BF16)
    one, none = jnp.ones((BLOCK, BLOCK), BF16), jnp.zeros((BLOCK, BLOCK), BF16)
    blank = jnp.zeros((16, BLOCK), BF16)
    for d in range(n_rad):
        for i in range(0, tiles, 2):
            onehot, lhs = [], []
            for t in (i, i + 1):
                off = jnp.broadcast_to(G[d, pl.ds(sz.offset + t, 1), :], (16, BLOCK)).astype(BF16)
                onehot.append(jnp.where(cell == jnp.concatenate([off] * (BLOCK // 16), axis=0), one, none))
                lhs.append(deps[pl.ds(d * tiles + t, 16, stride=T), :].astype(BF16))
            lhs = jnp.concatenate(
                [jnp.concatenate([lhs[0], blank], axis=1), jnp.concatenate([blank, lhs[1]], axis=1)], axis=0
            )
            res = dot_nt(lhs, jnp.concatenate(onehot, axis=1))
            for k in range(2):
                t = d * tiles + i + k
                both = res[16 * k : 16 * k + 8] + res[16 * k + 8 : 16 * k + 16]
                spread[pl.ds(2 * t, 4, stride=2 * T), :] = both[:4]
                spread[pl.ds(2 * t + 1, 4, stride=2 * T), :] = both[4:]
    own = iota((blocks, groups), 0) + r * blocks
    adder = jnp.concatenate(
        [(own == b[:, :groups].astype(I32)).astype(F32) for b in block_rows] * 2, axis=1
    ).astype(BF16)
    for c in range(4):
        high, low = split2(spread[pl.ds(c * 2 * T, 2 * T), :])
        total = dot(adder, jnp.concatenate([high, low], axis=0))
        for q in range(sz.quarters):
            part = total[q * layers : (q + 1) * layers]
            at = slice(q * BLOCK, (q + 1) * BLOCK)
            if c < 3:
                gas_out[c, :, at] = G[r, pl.ds(sz.gas + c * blocks + q * layers, layers), :] + part
            else:
                liquid[:, at] = part
    for send in sends[2:]:
        send.start()

    pres = jnp.concatenate([G[d, pl.ds(sz.pres, blocks), :] for d in range(n_rad)], axis=0)
    index = [
        jnp.broadcast_to(aux[pl.ds(8, blocks), k : k + 1], (blocks, BLOCK)).astype(jnp.int16) for k in range(4)
    ]
    one, none = jnp.ones((blocks, BLOCK), BF16), jnp.zeros((blocks, BLOCK), BF16)
    lanes = iota((blocks, BLOCK), 1)
    counts = []
    for t in range(NT):
        row = []
        for first in range(0, slab_blocks, BLOCK):
            aim = (lanes + (t * slab_blocks + first)).astype(jnp.int16)
            count = jnp.where(aim == index[0], one, none)
            for k in range(1, 4):
                count = count + jnp.where(aim == index[k], one, none)
            row.append(count)
        counts.append(jnp.concatenate(row, axis=1))
    grouped = dot(jnp.concatenate(counts, axis=0), jnp.concatenate(split2(pres), axis=1))
    grouped = grouped[:, :BLOCK] + grouped[:, BLOCK:]
    mine = pl.multiple_of(r * tiles, tiles)
    for i in range(tiles):
        motion_out[:, i * BLOCK : (i + 1) * BLOCK] = state[pl.ds(mine + i, 6, stride=T), :]
    sends[0].start()
    width = arr_rad.shape[2]
    for slot, exists, other in ((0, r > 0, jnp.maximum(r - 1, 0)), (1, r < n_rad - 1, jnp.minimum(r + 1, n_rad - 1))):
        idx = G[other, pl.ds(sz.meta + 1 + slot, 1), :].astype(I32)
        idx = jnp.where(exists, idx, -1)
        got = pick(sz, state_of(sz, T, state, other), idx)
        for c in range(7):
            arr_rad[c, slot : slot + 1, :] = got[c][:, :width]
    sends[1].start()

    grouped = jnp.concatenate([grouped[t * blocks : (t + 1) * blocks] for t in range(NT)], axis=1)
    matrices = jnp.concatenate([table[t] for t in range(NT)], axis=1)
    sums = dot_nt(jnp.concatenate(split2(grouped), axis=0), jnp.concatenate(split2(matrices), axis=0))
    coup[...] = sums[:blocks, :BLOCK] + sums[:blocks, BLOCK:] + sums[blocks:, :BLOCK]
    layer = iota((layers, BLOCK), 0)
    for q in range(sz.quarters):
        p = G[r, pl.ds(sz.pres + q * layers, layers), :]
        below = jnp.where(layer == 0, 0.0, pltpu.roll(p, 1, 0))
        above = jnp.where(layer == layers - 1, 0.0, pltpu.roll(p, layers - 1, 0))
        image[:, q * BLOCK : (q + 1) * BLOCK] = (
            DIAG * p - above - below + coup[pl.ds(q, layers, stride=sz.quarters), :]
        )
    for send in sends:
        send.wait()


def finish_kernel(sz, n_ax, got_a, got_b, image, arr_ax, pressure_image):
    a = lax.axis_index("ax")
    even = a % 2 == 0
    low = jnp.where(a > 0, jnp.where(even, got_b[...], got_a[...]), 0.0)
    up = jnp.where(a < n_ax - 1, jnp.where(even, got_a[...], got_b[...]), 0.0)
    half = arr_ax.shape[2]
    arr_ax[:, 0, :] = low[0:7, 0:half]
    arr_ax[:, 1, :] = up[0:7, half : 2 * half]
    pressure_image[...] = image[...]
    last = sz.layers - 1
    for q in range(sz.quarters):
        at = slice(q * BLOCK, (q + 1) * BLOCK)
        pressure_image[0:1, at] = image[0:1, at] - low[8 + q : 9 + q, :]
        pressure_image[last : last + 1, at] = image[last : last + 1, at] - up[12 + q : 13 + q, :]


def on_device(
    parcel_motion,
    parcel_size,
    parcel_block,
    parcel_offset,
    gas_velocity,
    pressure,
    block_cols,
    block_kinds,
    block_table,
    send_axial,
    send_radial,
    send_counts,
):
    n_ax, n_rad = lax.axis_size("ax"), lax.axis_size("rad")
    layers, radial = pressure.shape
    parcels = parcel_size.shape[0]
    sz = Sizes(layers, radial, parcels)
    T = n_rad * sz.tiles
    cap_ax, cap_rad = send_axial.shape[-1], send_radial.shape[-1]
    params = pltpu.CompilerParams(vmem_limit_bytes=VMEM_LIMIT)
    counts = send_counts.reshape(1, 4)
    size2 = parcel_size.reshape(sz.tiles, BLOCK)
    offset2 = parcel_offset.reshape(sz.tiles, BLOCK)

    packed, aux = pl.pallas_call(
        functools.partial(pack_kernel, sz, n_rad),
        out_shape=[
            jax.ShapeDtypeStruct((n_rad, sz.rows, BLOCK), F32),
            jax.ShapeDtypeStruct((8 + sz.blocks, BLOCK), I32),
        ],
        in_specs=[hbm] * 11,
        out_specs=[vmem] * 2,
        scratch_shapes=[
            pltpu.VMEM(parcel_motion.shape, F32),
            pltpu.VMEM(size2.shape, F32),
            pltpu.VMEM((1, sz.groups), I32),
            pltpu.VMEM(offset2.shape, I32),
            pltpu.VMEM(gas_velocity.shape, F32),
            pltpu.VMEM(pressure.shape, F32),
            pltpu.VMEM((2, cap_rad), I32),
            pltpu.SMEM((1, 4), I32),
            pltpu.VMEM((4, sz.blocks), I32),
            pltpu.VMEM((4, sz.blocks), I32),
            pltpu.VMEM((2, cap_ax), I32),
            pltpu.SemaphoreType.DMA((13,)),
        ],
        compiler_params=params,
        name="pack",
    )(
        *(
            pltpu.with_memory_space_constraint(x, pltpu.HBM)
            for x in (
                parcel_motion, size2, parcel_block.reshape(1, sz.groups), offset2, gas_velocity, pressure,
                send_radial.reshape(2, cap_rad), counts, block_cols[0].T, block_kinds[0].T,
                send_axial.reshape(2, cap_ax),
            )
        )
    )
    gathered = lax.all_to_all(packed, "rad", 0, 0)

    state, message = pl.pallas_call(
        functools.partial(move_kernel, sz, n_rad),
        out_shape=[
            jax.ShapeDtypeStruct((7 * T, BLOCK), F32),
            jax.ShapeDtypeStruct((16, BLOCK), F32),
        ],
        in_specs=[vmem] * 2,
        out_specs=[vmem] * 2,
        scratch_shapes=[pltpu.VMEM((3, n_rad * sz.groups, BLOCK), F32)],
        compiler_params=params,
        cost_estimate=pl.CostEstimate(flops=4_000_000_000, bytes_accessed=1_000_000, transcendentals=0),
        name="move",
    )(gathered, aux)

    def exchange(first):
        to = list(range(n_ax * n_rad))
        for low in range(first, n_ax - 1, 2):
            for r in range(n_rad):
                i, j = low * n_rad + r, (low + 1) * n_rad + r
                to[i], to[j] = j, i
        alone = [i for i in range(n_ax * n_rad) if to[i] == i]
        for i, j in zip(alone[0::2], alone[1::2]):
            to[i], to[j] = j, i
        return lax.ppermute(message, ("ax", "rad"), list(enumerate(to)))

    got_b = exchange(1)
    got_a = exchange(0)

    motion_out, arr_rad, gas_out, liquid, image = pl.pallas_call(
        functools.partial(rest_kernel, sz, n_rad),
        out_shape=[
            jax.ShapeDtypeStruct((6, parcels), F32),
            jax.ShapeDtypeStruct((7, 2, cap_rad), F32),
            jax.ShapeDtypeStruct(gas_velocity.shape, F32),
            jax.ShapeDtypeStruct(pressure.shape, F32),
            jax.ShapeDtypeStruct(pressure.shape, F32),
        ],
        in_specs=[vmem] * 4,
        out_specs=[hbm] * 4 + [vmem],
        scratch_shapes=[
            pltpu.VMEM((16 * T, BLOCK), F32),
            pltpu.VMEM((4 * 2 * T, BLOCK), F32),
            pltpu.VMEM((sz.blocks, BLOCK), F32),
            pltpu.VMEM((6, parcels), F32),
            pltpu.VMEM((7, 2, cap_rad), F32),
            pltpu.VMEM(gas_velocity.shape, F32),
            pltpu.VMEM(pressure.shape, F32),
            pltpu.SemaphoreType.DMA((6,)),
        ],
        compiler_params=params,
        cost_estimate=pl.CostEstimate(flops=2_000_000_000, bytes_accessed=2_000_000, transcendentals=0),
        name="rest",
    )(gathered, aux, block_table, state)

    arr_ax, pressure_image = pl.pallas_call(
        functools.partial(finish_kernel, sz, n_ax),
        out_shape=[
            jax.ShapeDtypeStruct((7, 2, cap_ax), F32),
            jax.ShapeDtypeStruct(pressure.shape, F32),
        ],
        in_specs=[vmem] * 3,
        out_specs=[vmem] * 2,
        compiler_params=params,
        name="finish",
    )(got_a, got_b, image)

    arrivals_axial = arr_ax.transpose(1, 0, 2)[None, None]
    arrivals_radial = arr_rad.transpose(1, 0, 2)[None, None]
    return (motion_out, arrivals_axial, arrivals_radial, gas_out, liquid, pressure_image)


def solution(mesh):
    return jax.shard_map(
        on_device,
        mesh=mesh,
        in_specs=(
            P(None, ("ax", "rad")),
            P(("ax", "rad")),
            P(("ax", "rad")),
            P(("ax", "rad")),
            P(None, "ax", "rad"),
            P("ax", "rad"),
            P("ax", "rad", None),
            P("ax", "rad", None),
            P(),
            P("ax", "rad", None, None),
            P("ax", "rad", None, None),
            P("ax", "rad", None),
        ),
        out_specs=(
            P(None, ("ax", "rad")),
            P("ax", "rad", None, None, None),
            P("ax", "rad", None, None, None),
            P(None, "ax", "rad"),
            P("ax", "rad"),
            P("ax", "rad"),
        ),
        check_vma=False,
    )
```

```python
import functools

import jax
import jax.numpy as jnp
from jax import lax
from jax.experimental import pallas as pl
from jax.experimental.pallas import tpu as pltpu
from jax.sharding import PartitionSpec as P

BLOCK = 128
GROUP = 64
NT = 8
DRAG = 0.5
STEP = 0.5
DIAG = 6.0
VMEM_LIMIT = 24 * 1024 * 1024

F32 = jnp.float32
BF16 = jnp.bfloat16
I32 = jnp.int32

vmem = pl.BlockSpec(memory_space=pltpu.VMEM)
hbm = pl.BlockSpec(memory_space=pltpu.HBM)


class Sizes:
    def __init__(self, layers, radial, parcels):
        self.layers = layers
        self.quarters = radial // BLOCK
        self.blocks = layers * self.quarters
        self.tiles = parcels // BLOCK
        self.groups = parcels // GROUP
        self.gas = 0
        self.pres = 3 * self.blocks
        self.motion = self.pres + self.blocks
        self.size = self.motion + 6 * self.tiles
        self.offset = self.size + self.tiles
        self.meta = self.offset + self.tiles
        self.column = self.meta + 8
        self.rows = self.column + self.groups


def split2(x):
    high = x.astype(BF16)
    return high, (x - high.astype(F32)).astype(BF16)


def dot(a, b):
    return jnp.dot(a, b, preferred_element_type=F32)


def dot_nt(a, b):
    return lax.dot_general(a, b, (((1,), (1,)), ((), ())), preferred_element_type=F32)


def iota(shape, dim):
    return lax.broadcasted_iota(I32, shape, dim)


def block_row(sz, b):
    local = b % sz.blocks
    return b - local + (local % sz.quarters) * sz.layers + local // sz.quarters


def pack_kernel(
    sz, n_rad, motion_hbm, size_hbm, block_hbm, offset_hbm, gas_hbm, pres_hbm, radial_hbm, counts_hbm, cols_hbm,
    kinds_hbm, axial_hbm,
    out, aux, cols, kinds,
    motion, size, block, offset, gas, pres, radial, counts, axial, sem,
):
    small = (
        (counts_hbm, counts), (block_hbm, block), (radial_hbm, radial), (axial_hbm, axial), (cols_hbm, cols),
        (kinds_hbm, kinds), (offset_hbm, offset), (size_hbm, size),
    )
    large = ((motion_hbm, motion), (pres_hbm, pres), *((gas_hbm.at[c], gas.at[c]) for c in range(3)))
    copies = [pltpu.make_async_copy(src, dst, sem.at[i]) for i, (src, dst) in enumerate(small + large)]
    for copy in copies:
        copy.start()
    out[pl.ds(sz.meta, 8), :] = jnp.full((8, BLOCK), -1.0, F32)
    layers = sz.layers
    for copy in copies[: len(small)]:
        copy.wait()
    out[pl.ds(sz.size, sz.tiles), :] = size[...]
    out[pl.ds(sz.offset, sz.tiles), :] = offset[...].astype(F32)
    numbers = block_row(sz, block[...]).astype(F32)
    out[pl.ds(sz.meta, 1), pl.ds(0, sz.groups)] = numbers
    numbers = jnp.concatenate([numbers, jnp.zeros((1, BLOCK - sz.groups), F32)], axis=1)
    out[pl.ds(sz.column, sz.groups), :] = jnp.transpose(jnp.broadcast_to(numbers, (BLOCK, BLOCK)))[: sz.groups]
    width = radial.shape[1]
    lane = iota((1, width), 1)
    for slot in range(2):
        kept = jnp.where(lane < counts[0, 2 + slot], radial[slot : slot + 1, :], -1)
        out[pl.ds(sz.meta + 1 + slot, 1), pl.ds(0, width)] = kept.astype(F32)
    lane = iota((1, axial.shape[1]), 1)
    kept = [jnp.where(lane < counts[0, slot], axial[slot : slot + 1, :], -1) for slot in range(2)]
    aux[pl.ds(0, 1), :] = jnp.concatenate(kept, axis=1)
    motion_copy, pres_copy, *gas_copies = copies[len(small) :]
    motion_copy.wait()
    for i in range(sz.tiles):
        out[pl.ds(sz.motion + i, 6, stride=sz.tiles), :] = motion[:, i * BLOCK : (i + 1) * BLOCK]
    pres_copy.wait()
    for q in range(sz.quarters):
        out[pl.ds(sz.pres + q * layers, layers), :] = pres[:, q * BLOCK : (q + 1) * BLOCK]
    for c in range(3):
        gas_copies[c].wait()
        for q in range(sz.quarters):
            out[pl.ds(sz.gas + c * sz.blocks + q * layers, layers), :] = gas[c, :, q * BLOCK : (q + 1) * BLOCK]


def take_lanes(x, idx):
    return jnp.take_along_axis(x, idx, axis=1, mode="promise_in_bounds")


def pick(sz, state, idx):
    shape = (sz.tiles, BLOCK)
    idx = jnp.broadcast_to(idx, shape)
    lane = idx & (BLOCK - 1)
    here = (idx >> 7) == iota(shape, 0)
    return [jnp.sum(jnp.where(here, take_lanes(s, lane), 0.0), axis=0, keepdims=True) for s in state]


def slab_rows(sz, n_rad, G, first):
    return jnp.concatenate([G[d, pl.ds(first, sz.tiles), :] for d in range(n_rad)], axis=0)


def state_of(sz, T, state, d):
    first = pl.multiple_of(d * sz.tiles, sz.tiles)
    return [state[pl.ds(c * T + first, sz.tiles), :] for c in range(7)]


def move_kernel(sz, n_rad, G, aux, cols, kinds, state, message, columns, near):
    r = lax.axis_index("rad")
    layers, tiles, blocks, groups = sz.layers, sz.tiles, sz.blocks, sz.groups
    slab_blocks = n_rad * blocks
    T = n_rad * tiles

    index = kinds[...] * slab_blocks + block_row(sz, cols[...])
    index = jnp.concatenate([index, index], axis=1).astype(F32)
    index = jnp.concatenate([index, jnp.zeros((BLOCK - index.shape[0], BLOCK), F32)], axis=0)
    columns[...] = jnp.transpose(index)[:blocks].astype(I32)

    column = jnp.concatenate([G[d, pl.ds(sz.column, groups), :] for d in range(n_rad)], axis=0).astype(I32)
    lanes = iota((n_rad * groups, BLOCK), 1)
    chooser = jnp.concatenate(
        [(column == lanes + first).astype(F32).astype(BF16) for first in range(0, slab_blocks, BLOCK)], axis=1
    )
    gas_slab = jnp.concatenate(
        [
            jnp.concatenate([G[d, pl.ds(sz.gas + c * blocks, blocks), :] for d in range(n_rad)], axis=0)
            for c in range(3)
        ],
        axis=1,
    )
    high, low = split2(gas_slab)
    found = dot(jnp.concatenate([chooser, chooser], axis=1), jnp.concatenate([high, low], axis=0))
    for c in range(3):
        near[c] = found[:, c * BLOCK : (c + 1) * BLOCK]

    rows = functools.partial(slab_rows, sz, n_rad, G)
    size = rows(sz.size)
    offset = rows(sz.offset).astype(I32)
    factor = jnp.exp(-DRAG / (size * size))
    even = iota((T, BLOCK), 1) < GROUP
    for c in range(3):
        u_even = take_lanes(near[c, pl.ds(0, T, stride=2), :], offset)
        u_odd = take_lanes(near[c, pl.ds(1, T, stride=2), :], offset)
        u = jnp.where(even, u_even, u_odd)
        v = rows(sz.motion + (3 + c) * tiles)
        new = u + (v - u) * factor
        state[pl.ds(c * T, T), :] = rows(sz.motion + c * tiles) + STEP * new
        state[pl.ds((3 + c) * T, T), :] = new
    state[pl.ds(6 * T, T), :] = size

    payload = pick(sz, state_of(sz, T, state, r), aux[pl.ds(0, 1), :])
    for c in range(7):
        message[c : c + 1, :] = payload[c]
    message[7:8, :] = jnp.zeros((1, BLOCK), F32)
    for q in range(sz.quarters):
        first = sz.pres + q * layers
        message[8 + q : 9 + q, :] = G[r, pl.ds(first + layers - 1, 1), :]
        message[12 + q : 13 + q, :] = G[r, pl.ds(first, 1), :]


def rest_kernel(
    sz, n_rad, G, columns, table, state,
    motion_hbm, arr_hbm, gas_hbm, liquid_hbm, image,
    deps, spread, coup, motion_out, arr_rad, gas_out, liquid, sem,
):
    r = lax.axis_index("rad")
    sends = [
        pltpu.make_async_copy(src, dst, sem.at[i])
        for i, (src, dst) in enumerate(
            (
                (motion_out, motion_hbm), (arr_rad, arr_hbm), *((gas_out.at[c], gas_hbm.at[c]) for c in range(3)),
                (liquid, liquid_hbm),
            )
        )
    ]
    layers, tiles, blocks, groups = sz.layers, sz.tiles, sz.blocks, sz.groups
    slab_blocks = n_rad * blocks
    T = n_rad * tiles
    block_rows = [G[d, pl.ds(sz.meta, 1), :] for d in range(n_rad)]

    rows = functools.partial(slab_rows, sz, n_rad, G)
    size = rows(sz.size)
    mass = size * size * size
    dep = [-mass * (state[pl.ds((3 + c) * T, T), :] - rows(sz.motion + (3 + c) * tiles)) for c in range(3)] + [mass]
    even = iota((T, BLOCK), 1) < GROUP

    for c in range(4):
        high = dep[c].astype(BF16).astype(F32)
        low = dep[c] - high
        for piece, part in enumerate((high, low)):
            deps[pl.ds((piece * 8 + c) * T, T), :] = jnp.where(even, part, 0.0)
            deps[pl.ds((piece * 8 + 4 + c) * T, T), :] = jnp.where(even, 0.0, part)
    cell = iota((BLOCK, BLOCK), 0).astype(F32).astype(BF16)
    one, none = jnp.ones((BLOCK, BLOCK), BF16), jnp.zeros((BLOCK, BLOCK), BF16)
    blank = jnp.zeros((16, BLOCK), BF16)
    for d in range(n_rad):
        for i in range(0, tiles, 2):
            onehot, lhs = [], []
            for t in (i, i + 1):
                off = jnp.broadcast_to(G[d, pl.ds(sz.offset + t, 1), :], (16, BLOCK)).astype(BF16)
                onehot.append(jnp.where(cell == jnp.concatenate([off] * (BLOCK // 16), axis=0), one, none))
                lhs.append(deps[pl.ds(d * tiles + t, 16, stride=T), :].astype(BF16))
            lhs = jnp.concatenate(
                [jnp.concatenate([lhs[0], blank], axis=1), jnp.concatenate([blank, lhs[1]], axis=1)], axis=0
            )
            res = dot_nt(lhs, jnp.concatenate(onehot, axis=1))
            for k in range(2):
                t = d * tiles + i + k
                both = res[16 * k : 16 * k + 8] + res[16 * k + 8 : 16 * k + 16]
                spread[pl.ds(2 * t, 4, stride=2 * T), :] = both[:4]
                spread[pl.ds(2 * t + 1, 4, stride=2 * T), :] = both[4:]
    own = iota((blocks, groups), 0) + r * blocks
    adder = jnp.concatenate(
        [(own == b[:, :groups].astype(I32)).astype(F32) for b in block_rows] * 2, axis=1
    ).astype(BF16)
    for c in range(4):
        high, low = split2(spread[pl.ds(c * 2 * T, 2 * T), :])
        total = dot(adder, jnp.concatenate([high, low], axis=0))
        for q in range(sz.quarters):
            part = total[q * layers : (q + 1) * layers]
            at = slice(q * BLOCK, (q + 1) * BLOCK)
            if c < 3:
                gas_out[c, :, at] = G[r, pl.ds(sz.gas + c * blocks + q * layers, layers), :] + part
            else:
                liquid[:, at] = part
    for send in sends[2:]:
        send.start()

    pres = jnp.concatenate([G[d, pl.ds(sz.pres, blocks), :] for d in range(n_rad)], axis=0)
    index = [
        jnp.broadcast_to(columns[:, k : k + 1], (blocks, BLOCK)).astype(jnp.int16) for k in range(4)
    ]
    one, none = jnp.ones((blocks, BLOCK), BF16), jnp.zeros((blocks, BLOCK), BF16)
    lanes = iota((blocks, BLOCK), 1)
    counts = []
    for t in range(NT):
        row = []
        for first in range(0, slab_blocks, BLOCK):
            aim = (lanes + (t * slab_blocks + first)).astype(jnp.int16)
            count = jnp.where(aim == index[0], one, none)
            for k in range(1, 4):
                count = count + jnp.where(aim == index[k], one, none)
            row.append(count)
        counts.append(jnp.concatenate(row, axis=1))
    grouped = dot(jnp.concatenate(counts, axis=0), jnp.concatenate(split2(pres), axis=1))
    grouped = grouped[:, :BLOCK] + grouped[:, BLOCK:]
    mine = pl.multiple_of(r * tiles, tiles)
    for i in range(tiles):
        motion_out[:, i * BLOCK : (i + 1) * BLOCK] = state[pl.ds(mine + i, 6, stride=T), :]
    sends[0].start()
    width = arr_rad.shape[2]
    for slot, exists, other in ((0, r > 0, jnp.maximum(r - 1, 0)), (1, r < n_rad - 1, jnp.minimum(r + 1, n_rad - 1))):
        idx = G[other, pl.ds(sz.meta + 1 + slot, 1), :].astype(I32)
        idx = jnp.where(exists, idx, -1)
        got = pick(sz, state_of(sz, T, state, other), idx)
        for c in range(7):
            arr_rad[c, slot : slot + 1, :] = got[c][:, :width]
    sends[1].start()

    grouped = jnp.concatenate([grouped[t * blocks : (t + 1) * blocks] for t in range(NT)], axis=1)
    matrices = jnp.concatenate([table[t] for t in range(NT)], axis=1)
    sums = dot_nt(jnp.concatenate(split2(grouped), axis=0), jnp.concatenate(split2(matrices), axis=0))
    coup[...] = sums[:blocks, :BLOCK] + sums[:blocks, BLOCK:] + sums[blocks:, :BLOCK]
    layer = iota((layers, BLOCK), 0)
    for q in range(sz.quarters):
        p = G[r, pl.ds(sz.pres + q * layers, layers), :]
        below = jnp.where(layer == 0, 0.0, pltpu.roll(p, 1, 0))
        above = jnp.where(layer == layers - 1, 0.0, pltpu.roll(p, layers - 1, 0))
        image[:, q * BLOCK : (q + 1) * BLOCK] = (
            DIAG * p - above - below + coup[pl.ds(q, layers, stride=sz.quarters), :]
        )
    for send in sends:
        send.wait()


def finish_kernel(sz, n_ax, got_a, got_b, image, arr_ax, pressure_image):
    a = lax.axis_index("ax")
    even = a % 2 == 0
    low = jnp.where(a > 0, jnp.where(even, got_b[...], got_a[...]), 0.0)
    up = jnp.where(a < n_ax - 1, jnp.where(even, got_a[...], got_b[...]), 0.0)
    half = arr_ax.shape[2]
    arr_ax[:, 0, :] = low[0:7, 0:half]
    arr_ax[:, 1, :] = up[0:7, half : 2 * half]
    pressure_image[...] = image[...]
    last = sz.layers - 1
    for q in range(sz.quarters):
        at = slice(q * BLOCK, (q + 1) * BLOCK)
        pressure_image[0:1, at] = image[0:1, at] - low[8 + q : 9 + q, :]
        pressure_image[last : last + 1, at] = image[last : last + 1, at] - up[12 + q : 13 + q, :]


def on_device(
    parcel_motion,
    parcel_size,
    parcel_block,
    parcel_offset,
    gas_velocity,
    pressure,
    block_cols,
    block_kinds,
    block_table,
    send_axial,
    send_radial,
    send_counts,
):
    n_ax, n_rad = lax.axis_size("ax"), lax.axis_size("rad")
    layers, radial = pressure.shape
    parcels = parcel_size.shape[0]
    sz = Sizes(layers, radial, parcels)
    T = n_rad * sz.tiles
    cap_ax, cap_rad = send_axial.shape[-1], send_radial.shape[-1]
    params = pltpu.CompilerParams(vmem_limit_bytes=VMEM_LIMIT)
    counts = send_counts.reshape(1, 4)
    size2 = parcel_size.reshape(sz.tiles, BLOCK)
    offset2 = parcel_offset.reshape(sz.tiles, BLOCK)

    packed, aux, cols, kinds = pl.pallas_call(
        functools.partial(pack_kernel, sz, n_rad),
        out_shape=[
            jax.ShapeDtypeStruct((sz.rows, BLOCK), F32),
            jax.ShapeDtypeStruct((8, BLOCK), I32),
            jax.ShapeDtypeStruct((4, sz.blocks), I32),
            jax.ShapeDtypeStruct((4, sz.blocks), I32),
        ],
        in_specs=[hbm] * 11,
        out_specs=[vmem] * 4,
        scratch_shapes=[
            pltpu.VMEM(parcel_motion.shape, F32),
            pltpu.VMEM(size2.shape, F32),
            pltpu.VMEM((1, sz.groups), I32),
            pltpu.VMEM(offset2.shape, I32),
            pltpu.VMEM(gas_velocity.shape, F32),
            pltpu.VMEM(pressure.shape, F32),
            pltpu.VMEM((2, cap_rad), I32),
            pltpu.SMEM((1, 4), I32),
            pltpu.VMEM((2, cap_ax), I32),
            pltpu.SemaphoreType.DMA((13,)),
        ],
        compiler_params=params,
        name="pack",
    )(
        *(
            pltpu.with_memory_space_constraint(x, pltpu.HBM)
            for x in (
                parcel_motion, size2, parcel_block.reshape(1, sz.groups), offset2, gas_velocity, pressure,
                send_radial.reshape(2, cap_rad), counts, block_cols[0].T, block_kinds[0].T,
                send_axial.reshape(2, cap_ax),
            )
        )
    )
    gathered = lax.all_gather(packed, "rad", axis=0)

    state, message, columns = pl.pallas_call(
        functools.partial(move_kernel, sz, n_rad),
        out_shape=[
            jax.ShapeDtypeStruct((7 * T, BLOCK), F32),
            jax.ShapeDtypeStruct((16, BLOCK), F32),
            jax.ShapeDtypeStruct((sz.blocks, BLOCK), I32),
        ],
        in_specs=[vmem] * 4,
        out_specs=[vmem] * 3,
        scratch_shapes=[pltpu.VMEM((3, n_rad * sz.groups, BLOCK), F32)],
        compiler_params=params,
        cost_estimate=pl.CostEstimate(flops=4_000_000_000, bytes_accessed=1_000_000, transcendentals=0),
        name="move",
    )(gathered, aux, cols, kinds)

    def exchange(first):
        to = list(range(n_ax * n_rad))
        for low in range(first, n_ax - 1, 2):
            for r in range(n_rad):
                i, j = low * n_rad + r, (low + 1) * n_rad + r
                to[i], to[j] = j, i
        alone = [i for i in range(n_ax * n_rad) if to[i] == i]
        for i, j in zip(alone[0::2], alone[1::2]):
            to[i], to[j] = j, i
        return lax.ppermute(message, ("ax", "rad"), list(enumerate(to)))

    got_b = exchange(1)
    got_a = exchange(0)

    motion_out, arr_rad, gas_out, liquid, image = pl.pallas_call(
        functools.partial(rest_kernel, sz, n_rad),
        out_shape=[
            jax.ShapeDtypeStruct((6, parcels), F32),
            jax.ShapeDtypeStruct((7, 2, cap_rad), F32),
            jax.ShapeDtypeStruct(gas_velocity.shape, F32),
            jax.ShapeDtypeStruct(pressure.shape, F32),
            jax.ShapeDtypeStruct(pressure.shape, F32),
        ],
        in_specs=[vmem] * 4,
        out_specs=[hbm] * 4 + [vmem],
        scratch_shapes=[
            pltpu.VMEM((16 * T, BLOCK), F32),
            pltpu.VMEM((4 * 2 * T, BLOCK), F32),
            pltpu.VMEM((sz.blocks, BLOCK), F32),
            pltpu.VMEM((6, parcels), F32),
            pltpu.VMEM((7, 2, cap_rad), F32),
            pltpu.VMEM(gas_velocity.shape, F32),
            pltpu.VMEM(pressure.shape, F32),
            pltpu.SemaphoreType.DMA((6,)),
        ],
        compiler_params=params,
        cost_estimate=pl.CostEstimate(flops=2_000_000_000, bytes_accessed=2_000_000, transcendentals=0),
        name="rest",
    )(gathered, columns, block_table, state)

    arr_ax, pressure_image = pl.pallas_call(
        functools.partial(finish_kernel, sz, n_ax),
        out_shape=[
            jax.ShapeDtypeStruct((7, 2, cap_ax), F32),
            jax.ShapeDtypeStruct(pressure.shape, F32),
        ],
        in_specs=[vmem] * 3,
        out_specs=[vmem] * 2,
        compiler_params=params,
        name="finish",
    )(got_a, got_b, image)

    arrivals_axial = arr_ax.transpose(1, 0, 2)[None, None]
    arrivals_radial = arr_rad.transpose(1, 0, 2)[None, None]
    return (motion_out, arrivals_axial, arrivals_radial, gas_out, liquid, pressure_image)


def solution(mesh):
    return jax.shard_map(
        on_device,
        mesh=mesh,
        in_specs=(
            P(None, ("ax", "rad")),
            P(("ax", "rad")),
            P(("ax", "rad")),
            P(("ax", "rad")),
            P(None, "ax", "rad"),
            P("ax", "rad"),
            P("ax", "rad", None),
            P("ax", "rad", None),
            P(),
            P("ax", "rad", None, None),
            P("ax", "rad", None, None),
            P("ax", "rad", None),
        ),
        out_specs=(
            P(None, ("ax", "rad")),
            P("ax", "rad", None, None, None),
            P("ax", "rad", None, None, None),
            P(None, "ax", "rad"),
            P("ax", "rad"),
            P("ax", "rad"),
        ),
        check_vma=False,
    )
```

```python
import functools

import jax
import jax.numpy as jnp
from jax import lax
from jax.experimental import pallas as pl
from jax.experimental.pallas import tpu as pltpu
from jax.sharding import PartitionSpec as P

BLOCK = 128
GROUP = 64
NT = 8
DRAG = 0.5
STEP = 0.5
DIAG = 6.0
VMEM_LIMIT = 24 * 1024 * 1024

F32 = jnp.float32
BF16 = jnp.bfloat16
I32 = jnp.int32

vmem = pl.BlockSpec(memory_space=pltpu.VMEM)
hbm = pl.BlockSpec(memory_space=pltpu.HBM)


class Sizes:
    def __init__(self, layers, radial, parcels):
        self.layers = layers
        self.quarters = radial // BLOCK
        self.blocks = layers * self.quarters
        self.tiles = parcels // BLOCK
        self.groups = parcels // GROUP
        self.gas = 0
        self.pres = 3 * self.blocks
        self.motion = self.pres + self.blocks
        self.size = self.motion + 6 * self.tiles
        self.offset = self.size + self.tiles
        self.meta = self.offset + self.tiles
        self.column = self.meta + 8
        self.rows = self.column + self.groups


def split2(x):
    high = x.astype(BF16)
    return high, (x - high.astype(F32)).astype(BF16)


def dot(a, b):
    return jnp.dot(a, b, preferred_element_type=F32)


def dot_nt(a, b):
    return lax.dot_general(a, b, (((1,), (1,)), ((), ())), preferred_element_type=F32)


def iota(shape, dim):
    return lax.broadcasted_iota(I32, shape, dim)


def block_row(sz, b):
    local = b % sz.blocks
    return b - local + (local % sz.quarters) * sz.layers + local // sz.quarters


def pack_kernel(
    sz, n_rad, motion_hbm, size_hbm, block_hbm, offset_hbm, gas_hbm, pres_hbm, radial_hbm, counts_hbm, cols_hbm,
    kinds_hbm, axial_hbm,
    out, aux,
    motion, size, block, offset, gas, pres, radial, counts, cols, kinds, axial, sem,
):
    small = (
        (counts_hbm, counts), (block_hbm, block), (radial_hbm, radial), (axial_hbm, axial), (cols_hbm, cols),
        (kinds_hbm, kinds), (offset_hbm, offset), (size_hbm, size),
    )
    large = ((motion_hbm, motion), (pres_hbm, pres), *((gas_hbm.at[c], gas.at[c]) for c in range(3)))
    copies = [pltpu.make_async_copy(src, dst, sem.at[i]) for i, (src, dst) in enumerate(small + large)]
    for copy in copies:
        copy.start()
    out[pl.ds(sz.meta, 8), :] = jnp.full((8, BLOCK), -1.0, F32)
    layers = sz.layers
    for copy in copies[: len(small)]:
        copy.wait()
    out[pl.ds(sz.size, sz.tiles), :] = size[...]
    out[pl.ds(sz.offset, sz.tiles), :] = offset[...].astype(F32)
    numbers = block_row(sz, block[...]).astype(F32)
    out[pl.ds(sz.meta, 1), pl.ds(0, sz.groups)] = numbers
    numbers = jnp.concatenate([numbers, jnp.zeros((1, BLOCK - sz.groups), F32)], axis=1)
    out[pl.ds(sz.column, sz.groups), :] = jnp.transpose(jnp.broadcast_to(numbers, (BLOCK, BLOCK)))[: sz.groups]
    width = radial.shape[1]
    lane = iota((1, width), 1)
    for slot in range(2):
        kept = jnp.where(lane < counts[0, 2 + slot], radial[slot : slot + 1, :], -1)
        out[pl.ds(sz.meta + 1 + slot, 1), pl.ds(0, width)] = kept.astype(F32)
    index = kinds[...] * (n_rad * sz.blocks) + block_row(sz, cols[...])
    index = jnp.concatenate([index, index], axis=1).astype(F32)
    index = jnp.concatenate([index, jnp.zeros((BLOCK - index.shape[0], BLOCK), F32)], axis=0)
    aux[...] = jnp.transpose(index)[: sz.blocks].astype(I32)
    lane = iota((1, axial.shape[1]), 1)
    kept = [jnp.where(lane < counts[0, slot], axial[slot : slot + 1, :], -1) for slot in range(2)]
    out[pl.ds(sz.meta + 3, 1), :] = jnp.concatenate(kept, axis=1).astype(F32)
    motion_copy, pres_copy, *gas_copies = copies[len(small) :]
    motion_copy.wait()
    for i in range(sz.tiles):
        out[pl.ds(sz.motion + i, 6, stride=sz.tiles), :] = motion[:, i * BLOCK : (i + 1) * BLOCK]
    pres_copy.wait()
    for q in range(sz.quarters):
        out[pl.ds(sz.pres + q * layers, layers), :] = pres[:, q * BLOCK : (q + 1) * BLOCK]
    for c in range(3):
        gas_copies[c].wait()
        for q in range(sz.quarters):
            out[pl.ds(sz.gas + c * sz.blocks + q * layers, layers), :] = gas[c, :, q * BLOCK : (q + 1) * BLOCK]


def take_lanes(x, idx):
    return jnp.take_along_axis(x, idx, axis=1, mode="promise_in_bounds")


def pick(sz, state, idx):
    shape = (sz.tiles, BLOCK)
    idx = jnp.broadcast_to(idx, shape)
    lane = idx & (BLOCK - 1)
    here = (idx >> 7) == iota(shape, 0)
    return [jnp.sum(jnp.where(here, take_lanes(s, lane), 0.0), axis=0, keepdims=True) for s in state]


def slab_rows(sz, n_rad, G, first):
    return jnp.concatenate([G[d, pl.ds(first, sz.tiles), :] for d in range(n_rad)], axis=0)


def state_of(sz, T, state, d):
    first = pl.multiple_of(d * sz.tiles, sz.tiles)
    return [state[pl.ds(c * T + first, sz.tiles), :] for c in range(7)]


def cross(r, n_rad):
    return r + 1 - 2 * (r % 2) if n_rad % 2 == 0 else r


def move_kernel(sz, n_rad, G, state, message, near):
    sent = cross(lax.axis_index("rad"), n_rad)
    layers, tiles, blocks, groups = sz.layers, sz.tiles, sz.blocks, sz.groups
    slab_blocks = n_rad * blocks
    T = n_rad * tiles

    column = jnp.concatenate([G[d, pl.ds(sz.column, groups), :] for d in range(n_rad)], axis=0).astype(I32)
    lanes = iota((n_rad * groups, BLOCK), 1)
    chooser = jnp.concatenate(
        [(column == lanes + first).astype(F32).astype(BF16) for first in range(0, slab_blocks, BLOCK)], axis=1
    )
    gas_slab = jnp.concatenate(
        [
            jnp.concatenate([G[d, pl.ds(sz.gas + c * blocks, blocks), :] for d in range(n_rad)], axis=0)
            for c in range(3)
        ],
        axis=1,
    )
    high, low = split2(gas_slab)
    found = dot(jnp.concatenate([chooser, chooser], axis=1), jnp.concatenate([high, low], axis=0))
    for c in range(3):
        near[c] = found[:, c * BLOCK : (c + 1) * BLOCK]

    rows = functools.partial(slab_rows, sz, n_rad, G)
    size = rows(sz.size)
    offset = rows(sz.offset).astype(I32)
    factor = jnp.exp(-DRAG / (size * size))
    even = iota((T, BLOCK), 1) < GROUP
    for c in range(3):
        u_even = take_lanes(near[c, pl.ds(0, T, stride=2), :], offset)
        u_odd = take_lanes(near[c, pl.ds(1, T, stride=2), :], offset)
        u = jnp.where(even, u_even, u_odd)
        v = rows(sz.motion + (3 + c) * tiles)
        new = u + (v - u) * factor
        state[pl.ds(c * T, T), :] = rows(sz.motion + c * tiles) + STEP * new
        state[pl.ds((3 + c) * T, T), :] = new
    state[pl.ds(6 * T, T), :] = size

    payload = pick(sz, state_of(sz, T, state, sent), G[sent, pl.ds(sz.meta + 3, 1), :].astype(I32))
    for c in range(7):
        message[c : c + 1, :] = payload[c]
    message[7:8, :] = jnp.zeros((1, BLOCK), F32)
    for q in range(sz.quarters):
        first = sz.pres + q * layers
        message[8 + q : 9 + q, :] = G[sent, pl.ds(first + layers - 1, 1), :]
        message[12 + q : 13 + q, :] = G[sent, pl.ds(first, 1), :]


def rest_kernel(
    sz, n_rad, G, aux, table, state,
    motion_hbm, arr_hbm, gas_hbm, liquid_hbm, image,
    deps, spread, coup, motion_out, arr_rad, gas_out, liquid, sem,
):
    r = lax.axis_index("rad")
    sends = [
        pltpu.make_async_copy(src, dst, sem.at[i])
        for i, (src, dst) in enumerate(
            (
                (motion_out, motion_hbm), (arr_rad, arr_hbm), *((gas_out.at[c], gas_hbm.at[c]) for c in range(3)),
                (liquid, liquid_hbm),
            )
        )
    ]
    layers, tiles, blocks, groups = sz.layers, sz.tiles, sz.blocks, sz.groups
    slab_blocks = n_rad * blocks
    T = n_rad * tiles
    block_rows = [G[d, pl.ds(sz.meta, 1), :] for d in range(n_rad)]

    rows = functools.partial(slab_rows, sz, n_rad, G)
    size = rows(sz.size)
    mass = size * size * size
    dep = [-mass * (state[pl.ds((3 + c) * T, T), :] - rows(sz.motion + (3 + c) * tiles)) for c in range(3)] + [mass]
    even = iota((T, BLOCK), 1) < GROUP

    for c in range(4):
        high = dep[c].astype(BF16).astype(F32)
        low = dep[c] - high
        for piece, part in enumerate((high, low)):
            deps[pl.ds((piece * 8 + c) * T, T), :] = jnp.where(even, part, 0.0)
            deps[pl.ds((piece * 8 + 4 + c) * T, T), :] = jnp.where(even, 0.0, part)
    cell = iota((BLOCK, BLOCK), 0).astype(F32).astype(BF16)
    one, none = jnp.ones((BLOCK, BLOCK), BF16), jnp.zeros((BLOCK, BLOCK), BF16)
    blank = jnp.zeros((16, BLOCK), BF16)
    for d in range(n_rad):
        for i in range(0, tiles, 2):
            onehot, lhs = [], []
            for t in (i, i + 1):
                off = jnp.broadcast_to(G[d, pl.ds(sz.offset + t, 1), :], (16, BLOCK)).astype(BF16)
                onehot.append(jnp.where(cell == jnp.concatenate([off] * (BLOCK // 16), axis=0), one, none))
                lhs.append(deps[pl.ds(d * tiles + t, 16, stride=T), :].astype(BF16))
            lhs = jnp.concatenate(
                [jnp.concatenate([lhs[0], blank], axis=1), jnp.concatenate([blank, lhs[1]], axis=1)], axis=0
            )
            res = dot_nt(lhs, jnp.concatenate(onehot, axis=1))
            for k in range(2):
                t = d * tiles + i + k
                both = res[16 * k : 16 * k + 8] + res[16 * k + 8 : 16 * k + 16]
                spread[pl.ds(2 * t, 4, stride=2 * T), :] = both[:4]
                spread[pl.ds(2 * t + 1, 4, stride=2 * T), :] = both[4:]
    own = iota((blocks, groups), 0) + r * blocks
    adder = jnp.concatenate(
        [(own == b[:, :groups].astype(I32)).astype(F32) for b in block_rows] * 2, axis=1
    ).astype(BF16)
    for c in range(4):
        high, low = split2(spread[pl.ds(c * 2 * T, 2 * T), :])
        total = dot(adder, jnp.concatenate([high, low], axis=0))
        for q in range(sz.quarters):
            part = total[q * layers : (q + 1) * layers]
            at = slice(q * BLOCK, (q + 1) * BLOCK)
            if c < 3:
                gas_out[c, :, at] = G[r, pl.ds(sz.gas + c * blocks + q * layers, layers), :] + part
            else:
                liquid[:, at] = part
    for send in sends[2:]:
        send.start()

    pres = jnp.concatenate([G[d, pl.ds(sz.pres, blocks), :] for d in range(n_rad)], axis=0)
    index = [
        jnp.broadcast_to(aux[:, k : k + 1], (blocks, BLOCK)).astype(jnp.int16) for k in range(4)
    ]
    one, none = jnp.ones((blocks, BLOCK), BF16), jnp.zeros((blocks, BLOCK), BF16)
    lanes = iota((blocks, BLOCK), 1)
    counts = []
    for t in range(NT):
        row = []
        for first in range(0, slab_blocks, BLOCK):
            aim = (lanes + (t * slab_blocks + first)).astype(jnp.int16)
            count = jnp.where(aim == index[0], one, none)
            for k in range(1, 4):
                count = count + jnp.where(aim == index[k], one, none)
            row.append(count)
        counts.append(jnp.concatenate(row, axis=1))
    grouped = dot(jnp.concatenate(counts, axis=0), jnp.concatenate(split2(pres), axis=1))
    grouped = grouped[:, :BLOCK] + grouped[:, BLOCK:]
    mine = pl.multiple_of(r * tiles, tiles)
    for i in range(tiles):
        motion_out[:, i * BLOCK : (i + 1) * BLOCK] = state[pl.ds(mine + i, 6, stride=T), :]
    sends[0].start()
    width = arr_rad.shape[2]
    for slot, exists, other in ((0, r > 0, jnp.maximum(r - 1, 0)), (1, r < n_rad - 1, jnp.minimum(r + 1, n_rad - 1))):
        idx = G[other, pl.ds(sz.meta + 1 + slot, 1), :].astype(I32)
        idx = jnp.where(exists, idx, -1)
        got = pick(sz, state_of(sz, T, state, other), idx)
        for c in range(7):
            arr_rad[c, slot : slot + 1, :] = got[c][:, :width]
    sends[1].start()

    grouped = jnp.concatenate([grouped[t * blocks : (t + 1) * blocks] for t in range(NT)], axis=1)
    matrices = jnp.concatenate([table[t] for t in range(NT)], axis=1)
    sums = dot_nt(jnp.concatenate(split2(grouped), axis=0), jnp.concatenate(split2(matrices), axis=0))
    coup[...] = sums[:blocks, :BLOCK] + sums[:blocks, BLOCK:] + sums[blocks:, :BLOCK]
    layer = iota((layers, BLOCK), 0)
    for q in range(sz.quarters):
        p = G[r, pl.ds(sz.pres + q * layers, layers), :]
        below = jnp.where(layer == 0, 0.0, pltpu.roll(p, 1, 0))
        above = jnp.where(layer == layers - 1, 0.0, pltpu.roll(p, layers - 1, 0))
        image[:, q * BLOCK : (q + 1) * BLOCK] = (
            DIAG * p - above - below + coup[pl.ds(q, layers, stride=sz.quarters), :]
        )
    for send in sends:
        send.wait()


def finish_kernel(sz, n_ax, got_a, got_b, image, arr_ax, pressure_image):
    a = lax.axis_index("ax")
    even = a % 2 == 0
    low = jnp.where(a > 0, jnp.where(even, got_b[...], got_a[...]), 0.0)
    up = jnp.where(a < n_ax - 1, jnp.where(even, got_a[...], got_b[...]), 0.0)
    half = arr_ax.shape[2]
    arr_ax[:, 0, :] = low[0:7, 0:half]
    arr_ax[:, 1, :] = up[0:7, half : 2 * half]
    pressure_image[...] = image[...]
    last = sz.layers - 1
    for q in range(sz.quarters):
        at = slice(q * BLOCK, (q + 1) * BLOCK)
        pressure_image[0:1, at] = image[0:1, at] - low[8 + q : 9 + q, :]
        pressure_image[last : last + 1, at] = image[last : last + 1, at] - up[12 + q : 13 + q, :]


def on_device(
    parcel_motion,
    parcel_size,
    parcel_block,
    parcel_offset,
    gas_velocity,
    pressure,
    block_cols,
    block_kinds,
    block_table,
    send_axial,
    send_radial,
    send_counts,
):
    n_ax, n_rad = lax.axis_size("ax"), lax.axis_size("rad")
    layers, radial = pressure.shape
    parcels = parcel_size.shape[0]
    sz = Sizes(layers, radial, parcels)
    T = n_rad * sz.tiles
    cap_ax, cap_rad = send_axial.shape[-1], send_radial.shape[-1]
    params = pltpu.CompilerParams(vmem_limit_bytes=VMEM_LIMIT)
    counts = send_counts.reshape(1, 4)
    size2 = parcel_size.reshape(sz.tiles, BLOCK)
    offset2 = parcel_offset.reshape(sz.tiles, BLOCK)

    packed, aux = pl.pallas_call(
        functools.partial(pack_kernel, sz, n_rad),
        out_shape=[
            jax.ShapeDtypeStruct((sz.rows, BLOCK), F32),
            jax.ShapeDtypeStruct((sz.blocks, BLOCK), I32),
        ],
        in_specs=[hbm] * 11,
        out_specs=[vmem] * 2,
        scratch_shapes=[
            pltpu.VMEM(parcel_motion.shape, F32),
            pltpu.VMEM(size2.shape, F32),
            pltpu.VMEM((1, sz.groups), I32),
            pltpu.VMEM(offset2.shape, I32),
            pltpu.VMEM(gas_velocity.shape, F32),
            pltpu.VMEM(pressure.shape, F32),
            pltpu.VMEM((2, cap_rad), I32),
            pltpu.SMEM((1, 4), I32),
            pltpu.VMEM((4, sz.blocks), I32),
            pltpu.VMEM((4, sz.blocks), I32),
            pltpu.VMEM((2, cap_ax), I32),
            pltpu.SemaphoreType.DMA((13,)),
        ],
        compiler_params=params,
        name="pack",
    )(
        *(
            pltpu.with_memory_space_constraint(x, pltpu.HBM)
            for x in (
                parcel_motion, size2, parcel_block.reshape(1, sz.groups), offset2, gas_velocity, pressure,
                send_radial.reshape(2, cap_rad), counts, block_cols[0].T, block_kinds[0].T,
                send_axial.reshape(2, cap_ax),
            )
        )
    )
    gathered = lax.all_gather(packed, "rad", axis=0)

    state, message = pl.pallas_call(
        functools.partial(move_kernel, sz, n_rad),
        out_shape=[
            jax.ShapeDtypeStruct((7 * T, BLOCK), F32),
            jax.ShapeDtypeStruct((16, BLOCK), F32),
        ],
        in_specs=[vmem],
        out_specs=[vmem] * 2,
        scratch_shapes=[pltpu.VMEM((3, n_rad * sz.groups, BLOCK), F32)],
        compiler_params=params,
        cost_estimate=pl.CostEstimate(flops=4_000_000_000, bytes_accessed=1_000_000, transcendentals=0),
        name="move",
    )(gathered)

    def exchange(first):
        to = list(range(n_ax * n_rad))
        for low in range(first, n_ax - 1, 2):
            for r in range(n_rad):
                i, j = low * n_rad + r, (low + 1) * n_rad + cross(r, n_rad)
                to[i], to[j] = j, i
        alone = [i for i in range(n_ax * n_rad) if to[i] == i]
        for i, j in zip(alone[0::2], alone[1::2]):
            to[i], to[j] = j, i
        return lax.ppermute(message, ("ax", "rad"), list(enumerate(to)))

    got_b = exchange(1)
    got_a = exchange(0)

    motion_out, arr_rad, gas_out, liquid, image = pl.pallas_call(
        functools.partial(rest_kernel, sz, n_rad),
        out_shape=[
            jax.ShapeDtypeStruct((6, parcels), F32),
            jax.ShapeDtypeStruct((7, 2, cap_rad), F32),
            jax.ShapeDtypeStruct(gas_velocity.shape, F32),
            jax.ShapeDtypeStruct(pressure.shape, F32),
            jax.ShapeDtypeStruct(pressure.shape, F32),
        ],
        in_specs=[vmem] * 4,
        out_specs=[hbm] * 4 + [vmem],
        scratch_shapes=[
            pltpu.VMEM((16 * T, BLOCK), F32),
            pltpu.VMEM((4 * 2 * T, BLOCK), F32),
            pltpu.VMEM((sz.blocks, BLOCK), F32),
            pltpu.VMEM((6, parcels), F32),
            pltpu.VMEM((7, 2, cap_rad), F32),
            pltpu.VMEM(gas_velocity.shape, F32),
            pltpu.VMEM(pressure.shape, F32),
            pltpu.SemaphoreType.DMA((6,)),
        ],
        compiler_params=params,
        cost_estimate=pl.CostEstimate(flops=2_000_000_000, bytes_accessed=2_000_000, transcendentals=0),
        name="rest",
    )(gathered, aux, block_table, state)

    arr_ax, pressure_image = pl.pallas_call(
        functools.partial(finish_kernel, sz, n_ax),
        out_shape=[
            jax.ShapeDtypeStruct((7, 2, cap_ax), F32),
            jax.ShapeDtypeStruct(pressure.shape, F32),
        ],
        in_specs=[vmem] * 3,
        out_specs=[vmem] * 2,
        compiler_params=params,
        name="finish",
    )(got_a, got_b, image)

    arrivals_axial = arr_ax.transpose(1, 0, 2)[None, None]
    arrivals_radial = arr_rad.transpose(1, 0, 2)[None, None]
    return (motion_out, arrivals_axial, arrivals_radial, gas_out, liquid, pressure_image)


def solution(mesh):
    return jax.shard_map(
        on_device,
        mesh=mesh,
        in_specs=(
            P(None, ("ax", "rad")),
            P(("ax", "rad")),
            P(("ax", "rad")),
            P(("ax", "rad")),
            P(None, "ax", "rad"),
            P("ax", "rad"),
            P("ax", "rad", None),
            P("ax", "rad", None),
            P(),
            P("ax", "rad", None, None),
            P("ax", "rad", None, None),
            P("ax", "rad", None),
        ),
        out_specs=(
            P(None, ("ax", "rad")),
            P("ax", "rad", None, None, None),
            P("ax", "rad", None, None, None),
            P(None, "ax", "rad"),
            P("ax", "rad"),
            P("ax", "rad"),
        ),
        check_vma=False,
    )
```

```python
import functools

import jax
import jax.numpy as jnp
from jax import lax
from jax.experimental import pallas as pl
from jax.experimental.pallas import tpu as pltpu
from jax.sharding import PartitionSpec as P

BLOCK = 128
GROUP = 64
NT = 8
DRAG = 0.5
STEP = 0.5
DIAG = 6.0
VMEM_LIMIT = 24 * 1024 * 1024

F32 = jnp.float32
BF16 = jnp.bfloat16
I32 = jnp.int32

vmem = pl.BlockSpec(memory_space=pltpu.VMEM)
hbm = pl.BlockSpec(memory_space=pltpu.HBM)


class Sizes:
    def __init__(self, layers, radial, parcels):
        self.layers = layers
        self.quarters = radial // BLOCK
        self.blocks = layers * self.quarters
        self.tiles = parcels // BLOCK
        self.groups = parcels // GROUP
        self.gas = 0
        self.pres = 3 * self.blocks
        self.motion = self.pres + self.blocks
        self.size = self.motion + 6 * self.tiles
        self.offset = self.size + self.tiles
        self.meta = self.offset + self.tiles
        self.column = self.meta + 8
        self.rows = self.column + self.groups


def split2(x):
    high = x.astype(BF16)
    return high, (x - high.astype(F32)).astype(BF16)


def dot(a, b):
    return jnp.dot(a, b, preferred_element_type=F32)


def dot_nt(a, b):
    return lax.dot_general(a, b, (((1,), (1,)), ((), ())), preferred_element_type=F32)


def iota(shape, dim):
    return lax.broadcasted_iota(I32, shape, dim)


def block_row(sz, b):
    local = b % sz.blocks
    return b - local + (local % sz.quarters) * sz.layers + local // sz.quarters


def pack_kernel(
    sz, n_rad, motion_hbm, size_hbm, block_hbm, offset_hbm, gas_hbm, pres_hbm, radial_hbm, counts_hbm, cols_hbm,
    kinds_hbm, axial_hbm,
    out, aux,
    motion, size, block, offset, gas, pres, radial, counts, cols, kinds, axial, sem,
):
    small = (
        (counts_hbm, counts), (block_hbm, block), (radial_hbm, radial), (axial_hbm, axial), (cols_hbm, cols),
        (kinds_hbm, kinds), (offset_hbm, offset), (size_hbm, size),
    )
    large = ((motion_hbm, motion), (pres_hbm, pres), *((gas_hbm.at[c], gas.at[c]) for c in range(3)))
    copies = [pltpu.make_async_copy(src, dst, sem.at[i]) for i, (src, dst) in enumerate(small + large)]
    for copy in copies:
        copy.start()
    out[pl.ds(sz.meta, 8), :] = jnp.full((8, BLOCK), -1.0, F32)
    layers = sz.layers
    for copy in copies[: len(small)]:
        copy.wait()
    out[pl.ds(sz.size, sz.tiles), :] = size[...]
    out[pl.ds(sz.offset, sz.tiles), :] = offset[...].astype(F32)
    numbers = block_row(sz, block[...]).astype(F32)
    out[pl.ds(sz.meta, 1), pl.ds(0, sz.groups)] = numbers
    numbers = jnp.concatenate([numbers, jnp.zeros((1, BLOCK - sz.groups), F32)], axis=1)
    out[pl.ds(sz.column, sz.groups), :] = jnp.transpose(jnp.broadcast_to(numbers, (BLOCK, BLOCK)))[: sz.groups]
    width = radial.shape[1]
    lane = iota((1, width), 1)
    for slot in range(2):
        kept = jnp.where(lane < counts[0, 2 + slot], radial[slot : slot + 1, :], -1)
        out[pl.ds(sz.meta + 1 + slot, 1), pl.ds(0, width)] = kept.astype(F32)
    index = kinds[...] * (n_rad * sz.blocks) + block_row(sz, cols[...])
    index = jnp.concatenate([index, index], axis=1).astype(F32)
    index = jnp.concatenate([index, jnp.zeros((BLOCK - index.shape[0], BLOCK), F32)], axis=0)
    aux[...] = jnp.transpose(index)[: sz.blocks].astype(I32)
    lane = iota((1, axial.shape[1]), 1)
    kept = [jnp.where(lane < counts[0, slot], axial[slot : slot + 1, :], -1) for slot in range(2)]
    out[pl.ds(sz.meta + 3, 1), :] = jnp.concatenate(kept, axis=1).astype(F32)
    motion_copy, pres_copy, *gas_copies = copies[len(small) :]
    motion_copy.wait()
    for i in range(sz.tiles):
        out[pl.ds(sz.motion + i, 6, stride=sz.tiles), :] = motion[:, i * BLOCK : (i + 1) * BLOCK]
    pres_copy.wait()
    for q in range(sz.quarters):
        out[pl.ds(sz.pres + q * layers, layers), :] = pres[:, q * BLOCK : (q + 1) * BLOCK]
    for c in range(3):
        gas_copies[c].wait()
        for q in range(sz.quarters):
            out[pl.ds(sz.gas + c * sz.blocks + q * layers, layers), :] = gas[c, :, q * BLOCK : (q + 1) * BLOCK]


def take_lanes(x, idx):
    return jnp.take_along_axis(x, idx, axis=1, mode="promise_in_bounds")


def pick(sz, state, idx):
    shape = (sz.tiles, BLOCK)
    idx = jnp.broadcast_to(idx, shape)
    lane = idx & (BLOCK - 1)
    here = (idx >> 7) == iota(shape, 0)
    return [jnp.sum(jnp.where(here, take_lanes(s, lane), 0.0), axis=0, keepdims=True) for s in state]


def slab_rows(sz, n_rad, G, first):
    return jnp.concatenate([G[d, pl.ds(first, sz.tiles), :] for d in range(n_rad)], axis=0)


def state_of(sz, T, state, d):
    first = pl.multiple_of(d * sz.tiles, sz.tiles)
    return [state[pl.ds(c * T + first, sz.tiles), :] for c in range(7)]


def cross(r, n_rad):
    return r + 1 - 2 * (r % 2) if n_rad % 2 == 0 else r


def move_kernel(sz, n_rad, G, state, far, near, found_gas):
    r = lax.axis_index("rad")
    layers, tiles, blocks, groups = sz.layers, sz.tiles, sz.blocks, sz.groups
    slab_blocks = n_rad * blocks
    T = n_rad * tiles

    column = jnp.concatenate([G[d, pl.ds(sz.column, groups), :] for d in range(n_rad)], axis=0).astype(I32)
    lanes = iota((n_rad * groups, BLOCK), 1)
    chooser = jnp.concatenate(
        [(column == lanes + first).astype(F32).astype(BF16) for first in range(0, slab_blocks, BLOCK)], axis=1
    )
    gas_slab = jnp.concatenate(
        [
            jnp.concatenate([G[d, pl.ds(sz.gas + c * blocks, blocks), :] for d in range(n_rad)], axis=0)
            for c in range(3)
        ],
        axis=1,
    )
    high, low = split2(gas_slab)
    found = dot(jnp.concatenate([chooser, chooser], axis=1), jnp.concatenate([high, low], axis=0))
    for c in range(3):
        found_gas[c] = found[:, c * BLOCK : (c + 1) * BLOCK]

    rows = functools.partial(slab_rows, sz, n_rad, G)
    size = rows(sz.size)
    offset = rows(sz.offset).astype(I32)
    factor = jnp.exp(-DRAG / (size * size))
    even = iota((T, BLOCK), 1) < GROUP
    for c in range(3):
        u_even = take_lanes(found_gas[c, pl.ds(0, T, stride=2), :], offset)
        u_odd = take_lanes(found_gas[c, pl.ds(1, T, stride=2), :], offset)
        u = jnp.where(even, u_even, u_odd)
        v = rows(sz.motion + (3 + c) * tiles)
        new = u + (v - u) * factor
        state[pl.ds(c * T, T), :] = rows(sz.motion + c * tiles) + STEP * new
        state[pl.ds((3 + c) * T, T), :] = new
    state[pl.ds(6 * T, T), :] = size

    for message, sent in ((far, r), (near, cross(r, n_rad))):
        payload = pick(sz, state_of(sz, T, state, sent), G[sent, pl.ds(sz.meta + 3, 1), :].astype(I32))
        for c in range(7):
            message[c : c + 1, :] = payload[c]
        message[7:8, :] = jnp.zeros((1, BLOCK), F32)
        for q in range(sz.quarters):
            first = sz.pres + q * layers
            message[8 + q : 9 + q, :] = G[sent, pl.ds(first + layers - 1, 1), :]
            message[12 + q : 13 + q, :] = G[sent, pl.ds(first, 1), :]


def rest_kernel(
    sz, n_rad, G, aux, table, state,
    motion_hbm, arr_hbm, gas_hbm, liquid_hbm, image,
    deps, spread, coup, motion_out, arr_rad, gas_out, liquid, sem,
):
    r = lax.axis_index("rad")
    sends = [
        pltpu.make_async_copy(src, dst, sem.at[i])
        for i, (src, dst) in enumerate(
            (
                (motion_out, motion_hbm), (arr_rad, arr_hbm), *((gas_out.at[c], gas_hbm.at[c]) for c in range(3)),
                (liquid, liquid_hbm),
            )
        )
    ]
    layers, tiles, blocks, groups = sz.layers, sz.tiles, sz.blocks, sz.groups
    slab_blocks = n_rad * blocks
    T = n_rad * tiles
    block_rows = [G[d, pl.ds(sz.meta, 1), :] for d in range(n_rad)]

    rows = functools.partial(slab_rows, sz, n_rad, G)
    size = rows(sz.size)
    mass = size * size * size
    dep = [-mass * (state[pl.ds((3 + c) * T, T), :] - rows(sz.motion + (3 + c) * tiles)) for c in range(3)] + [mass]
    even = iota((T, BLOCK), 1) < GROUP

    for c in range(4):
        high = dep[c].astype(BF16).astype(F32)
        low = dep[c] - high
        for piece, part in enumerate((high, low)):
            deps[pl.ds((piece * 8 + c) * T, T), :] = jnp.where(even, part, 0.0)
            deps[pl.ds((piece * 8 + 4 + c) * T, T), :] = jnp.where(even, 0.0, part)
    cell = iota((BLOCK, BLOCK), 0).astype(F32).astype(BF16)
    one, none = jnp.ones((BLOCK, BLOCK), BF16), jnp.zeros((BLOCK, BLOCK), BF16)
    blank = jnp.zeros((16, BLOCK), BF16)
    for d in range(n_rad):
        for i in range(0, tiles, 2):
            onehot, lhs = [], []
            for t in (i, i + 1):
                off = jnp.broadcast_to(G[d, pl.ds(sz.offset + t, 1), :], (16, BLOCK)).astype(BF16)
                onehot.append(jnp.where(cell == jnp.concatenate([off] * (BLOCK // 16), axis=0), one, none))
                lhs.append(deps[pl.ds(d * tiles + t, 16, stride=T), :].astype(BF16))
            lhs = jnp.concatenate(
                [jnp.concatenate([lhs[0], blank], axis=1), jnp.concatenate([blank, lhs[1]], axis=1)], axis=0
            )
            res = dot_nt(lhs, jnp.concatenate(onehot, axis=1))
            for k in range(2):
                t = d * tiles + i + k
                both = res[16 * k : 16 * k + 8] + res[16 * k + 8 : 16 * k + 16]
                spread[pl.ds(2 * t, 4, stride=2 * T), :] = both[:4]
                spread[pl.ds(2 * t + 1, 4, stride=2 * T), :] = both[4:]
    own = iota((blocks, groups), 0) + r * blocks
    adder = jnp.concatenate(
        [(own == b[:, :groups].astype(I32)).astype(F32) for b in block_rows] * 2, axis=1
    ).astype(BF16)
    for c in range(4):
        high, low = split2(spread[pl.ds(c * 2 * T, 2 * T), :])
        total = dot(adder, jnp.concatenate([high, low], axis=0))
        for q in range(sz.quarters):
            part = total[q * layers : (q + 1) * layers]
            at = slice(q * BLOCK, (q + 1) * BLOCK)
            if c < 3:
                gas_out[c, :, at] = G[r, pl.ds(sz.gas + c * blocks + q * layers, layers), :] + part
            else:
                liquid[:, at] = part
    for send in sends[2:]:
        send.start()

    pres = jnp.concatenate([G[d, pl.ds(sz.pres, blocks), :] for d in range(n_rad)], axis=0)
    index = [
        jnp.broadcast_to(aux[:, k : k + 1], (blocks, BLOCK)).astype(jnp.int16) for k in range(4)
    ]
    one, none = jnp.ones((blocks, BLOCK), BF16), jnp.zeros((blocks, BLOCK), BF16)
    lanes = iota((blocks, BLOCK), 1)
    counts = []
    for t in range(NT):
        row = []
        for first in range(0, slab_blocks, BLOCK):
            aim = (lanes + (t * slab_blocks + first)).astype(jnp.int16)
            count = jnp.where(aim == index[0], one, none)
            for k in range(1, 4):
                count = count + jnp.where(aim == index[k], one, none)
            row.append(count)
        counts.append(jnp.concatenate(row, axis=1))
    grouped = dot(jnp.concatenate(counts, axis=0), jnp.concatenate(split2(pres), axis=1))
    grouped = grouped[:, :BLOCK] + grouped[:, BLOCK:]
    mine = pl.multiple_of(r * tiles, tiles)
    for i in range(tiles):
        motion_out[:, i * BLOCK : (i + 1) * BLOCK] = state[pl.ds(mine + i, 6, stride=T), :]
    sends[0].start()
    width = arr_rad.shape[2]
    for slot, exists, other in ((0, r > 0, jnp.maximum(r - 1, 0)), (1, r < n_rad - 1, jnp.minimum(r + 1, n_rad - 1))):
        idx = G[other, pl.ds(sz.meta + 1 + slot, 1), :].astype(I32)
        idx = jnp.where(exists, idx, -1)
        got = pick(sz, state_of(sz, T, state, other), idx)
        for c in range(7):
            arr_rad[c, slot : slot + 1, :] = got[c][:, :width]
    sends[1].start()

    grouped = jnp.concatenate([grouped[t * blocks : (t + 1) * blocks] for t in range(NT)], axis=1)
    matrices = jnp.concatenate([table[t] for t in range(NT)], axis=1)
    sums = dot_nt(jnp.concatenate(split2(grouped), axis=0), jnp.concatenate(split2(matrices), axis=0))
    coup[...] = sums[:blocks, :BLOCK] + sums[:blocks, BLOCK:] + sums[blocks:, :BLOCK]
    layer = iota((layers, BLOCK), 0)
    for q in range(sz.quarters):
        p = G[r, pl.ds(sz.pres + q * layers, layers), :]
        below = jnp.where(layer == 0, 0.0, pltpu.roll(p, 1, 0))
        above = jnp.where(layer == layers - 1, 0.0, pltpu.roll(p, layers - 1, 0))
        image[:, q * BLOCK : (q + 1) * BLOCK] = (
            DIAG * p - above - below + coup[pl.ds(q, layers, stride=sz.quarters), :]
        )
    for send in sends:
        send.wait()


def finish_kernel(sz, n_ax, got_b, got_a, image, arr_ax, pressure_image):
    a = lax.axis_index("ax")
    even = a % 2 == 0
    low = jnp.where(a > 0, jnp.where(even, got_b[...], got_a[...]), 0.0)
    up = jnp.where(a < n_ax - 1, jnp.where(even, got_a[...], got_b[...]), 0.0)
    half = arr_ax.shape[2]
    arr_ax[:, 0, :] = low[0:7, 0:half]
    arr_ax[:, 1, :] = up[0:7, half : 2 * half]
    pressure_image[...] = image[...]
    last = sz.layers - 1
    for q in range(sz.quarters):
        at = slice(q * BLOCK, (q + 1) * BLOCK)
        pressure_image[0:1, at] = image[0:1, at] - low[8 + q : 9 + q, :]
        pressure_image[last : last + 1, at] = image[last : last + 1, at] - up[12 + q : 13 + q, :]


def on_device(
    parcel_motion,
    parcel_size,
    parcel_block,
    parcel_offset,
    gas_velocity,
    pressure,
    block_cols,
    block_kinds,
    block_table,
    send_axial,
    send_radial,
    send_counts,
):
    n_ax, n_rad = lax.axis_size("ax"), lax.axis_size("rad")
    layers, radial = pressure.shape
    parcels = parcel_size.shape[0]
    sz = Sizes(layers, radial, parcels)
    T = n_rad * sz.tiles
    cap_ax, cap_rad = send_axial.shape[-1], send_radial.shape[-1]
    params = pltpu.CompilerParams(vmem_limit_bytes=VMEM_LIMIT)
    counts = send_counts.reshape(1, 4)
    size2 = parcel_size.reshape(sz.tiles, BLOCK)
    offset2 = parcel_offset.reshape(sz.tiles, BLOCK)

    packed, aux = pl.pallas_call(
        functools.partial(pack_kernel, sz, n_rad),
        out_shape=[
            jax.ShapeDtypeStruct((sz.rows, BLOCK), F32),
            jax.ShapeDtypeStruct((sz.blocks, BLOCK), I32),
        ],
        in_specs=[hbm] * 11,
        out_specs=[vmem] * 2,
        scratch_shapes=[
            pltpu.VMEM(parcel_motion.shape, F32),
            pltpu.VMEM(size2.shape, F32),
            pltpu.VMEM((1, sz.groups), I32),
            pltpu.VMEM(offset2.shape, I32),
            pltpu.VMEM(gas_velocity.shape, F32),
            pltpu.VMEM(pressure.shape, F32),
            pltpu.VMEM((2, cap_rad), I32),
            pltpu.SMEM((1, 4), I32),
            pltpu.VMEM((4, sz.blocks), I32),
            pltpu.VMEM((4, sz.blocks), I32),
            pltpu.VMEM((2, cap_ax), I32),
            pltpu.SemaphoreType.DMA((13,)),
        ],
        compiler_params=params,
        name="pack",
    )(
        *(
            pltpu.with_memory_space_constraint(x, pltpu.HBM)
            for x in (
                parcel_motion, size2, parcel_block.reshape(1, sz.groups), offset2, gas_velocity, pressure,
                send_radial.reshape(2, cap_rad), counts, block_cols[0].T, block_kinds[0].T,
                send_axial.reshape(2, cap_ax),
            )
        )
    )
    gathered = lax.all_gather(packed, "rad", axis=0)

    state, far, near = pl.pallas_call(
        functools.partial(move_kernel, sz, n_rad),
        out_shape=[
            jax.ShapeDtypeStruct((7 * T, BLOCK), F32),
            jax.ShapeDtypeStruct((16, BLOCK), F32),
            jax.ShapeDtypeStruct((16, BLOCK), F32),
        ],
        in_specs=[vmem],
        out_specs=[vmem] * 3,
        scratch_shapes=[pltpu.VMEM((3, n_rad * sz.groups, BLOCK), F32)],
        compiler_params=params,
        cost_estimate=pl.CostEstimate(flops=4_000_000_000, bytes_accessed=1_000_000, transcendentals=0),
        name="move",
    )(gathered)

    def exchange(message, first, partner):
        to = list(range(n_ax * n_rad))
        for low in range(first, n_ax - 1, 2):
            for r in range(n_rad):
                i, j = low * n_rad + r, (low + 1) * n_rad + partner(r)
                to[i], to[j] = j, i
        alone = [i for i in range(n_ax * n_rad) if to[i] == i]
        for i, j in zip(alone[0::2], alone[1::2]):
            to[i], to[j] = j, i
        return lax.ppermute(message, ("ax", "rad"), list(enumerate(to)))

    got_b = exchange(far, 1, lambda r: r)
    got_a = exchange(near, 0, lambda r: cross(r, n_rad))

    motion_out, arr_rad, gas_out, liquid, image = pl.pallas_call(
        functools.partial(rest_kernel, sz, n_rad),
        out_shape=[
            jax.ShapeDtypeStruct((6, parcels), F32),
            jax.ShapeDtypeStruct((7, 2, cap_rad), F32),
            jax.ShapeDtypeStruct(gas_velocity.shape, F32),
            jax.ShapeDtypeStruct(pressure.shape, F32),
            jax.ShapeDtypeStruct(pressure.shape, F32),
        ],
        in_specs=[vmem] * 4,
        out_specs=[hbm] * 4 + [vmem],
        scratch_shapes=[
            pltpu.VMEM((16 * T, BLOCK), F32),
            pltpu.VMEM((4 * 2 * T, BLOCK), F32),
            pltpu.VMEM((sz.blocks, BLOCK), F32),
            pltpu.VMEM((6, parcels), F32),
            pltpu.VMEM((7, 2, cap_rad), F32),
            pltpu.VMEM(gas_velocity.shape, F32),
            pltpu.VMEM(pressure.shape, F32),
            pltpu.SemaphoreType.DMA((6,)),
        ],
        compiler_params=params,
        cost_estimate=pl.CostEstimate(flops=2_000_000_000, bytes_accessed=2_000_000, transcendentals=0),
        name="rest",
    )(gathered, aux, block_table, state)

    arr_ax, pressure_image = pl.pallas_call(
        functools.partial(finish_kernel, sz, n_ax),
        out_shape=[
            jax.ShapeDtypeStruct((7, 2, cap_ax), F32),
            jax.ShapeDtypeStruct(pressure.shape, F32),
        ],
        in_specs=[vmem] * 3,
        out_specs=[vmem] * 2,
        compiler_params=params,
        name="finish",
    )(got_b, got_a, image)

    arrivals_axial = arr_ax.transpose(1, 0, 2)[None, None]
    arrivals_radial = arr_rad.transpose(1, 0, 2)[None, None]
    return (motion_out, arrivals_axial, arrivals_radial, gas_out, liquid, pressure_image)


def solution(mesh):
    return jax.shard_map(
        on_device,
        mesh=mesh,
        in_specs=(
            P(None, ("ax", "rad")),
            P(("ax", "rad")),
            P(("ax", "rad")),
            P(("ax", "rad")),
            P(None, "ax", "rad"),
            P("ax", "rad"),
            P("ax", "rad", None),
            P("ax", "rad", None),
            P(),
            P("ax", "rad", None, None),
            P("ax", "rad", None, None),
            P("ax", "rad", None),
        ),
        out_specs=(
            P(None, ("ax", "rad")),
            P("ax", "rad", None, None, None),
            P("ax", "rad", None, None, None),
            P(None, "ax", "rad"),
            P("ax", "rad"),
            P("ax", "rad"),
        ),
        check_vma=False,
    )
```

```python
import functools

import jax
import jax.numpy as jnp
from jax import lax
from jax.experimental import pallas as pl
from jax.experimental.pallas import tpu as pltpu
from jax.sharding import PartitionSpec as P

BLOCK = 128
GROUP = 64
NT = 8
DRAG = 0.5
STEP = 0.5
DIAG = 6.0
VMEM_LIMIT = 24 * 1024 * 1024

F32 = jnp.float32
BF16 = jnp.bfloat16
I32 = jnp.int32

vmem = pl.BlockSpec(memory_space=pltpu.VMEM)
hbm = pl.BlockSpec(memory_space=pltpu.HBM)


class Sizes:
    def __init__(self, layers, radial, parcels):
        self.layers = layers
        self.quarters = radial // BLOCK
        self.blocks = layers * self.quarters
        self.tiles = parcels // BLOCK
        self.groups = parcels // GROUP
        self.gas = 0
        self.pres = 3 * self.blocks
        self.motion = self.pres + self.blocks
        self.size = self.motion + 6 * self.tiles
        self.offset = self.size + self.tiles
        self.meta = self.offset + self.tiles
        self.column = self.meta + 8
        self.rows = self.column + self.groups


def split2(x):
    high = x.astype(BF16)
    return high, (x - high.astype(F32)).astype(BF16)


def dot(a, b):
    return jnp.dot(a, b, preferred_element_type=F32)


def dot_nt(a, b):
    return lax.dot_general(a, b, (((1,), (1,)), ((), ())), preferred_element_type=F32)


def iota(shape, dim):
    return lax.broadcasted_iota(I32, shape, dim)


def block_row(sz, b):
    local = b % sz.blocks
    return b - local + (local % sz.quarters) * sz.layers + local // sz.quarters


def pack_kernel(
    sz, n_rad, motion_hbm, size_hbm, block_hbm, offset_hbm, gas_hbm, pres_hbm, radial_hbm, counts_hbm, cols_hbm,
    kinds_hbm, axial_hbm,
    out, aux,
    motion, size, block, offset, gas, pres, radial, counts, cols, kinds, axial, sem,
):
    small = (
        (counts_hbm, counts), (block_hbm, block), (radial_hbm, radial), (axial_hbm, axial), (cols_hbm, cols),
        (kinds_hbm, kinds), (offset_hbm, offset), (size_hbm, size),
    )
    large = ((motion_hbm, motion), (pres_hbm, pres), *((gas_hbm.at[c], gas.at[c]) for c in range(3)))
    copies = [pltpu.make_async_copy(src, dst, sem.at[i]) for i, (src, dst) in enumerate(small + large)]
    for copy in copies:
        copy.start()
    out[pl.ds(sz.meta, 8), :] = jnp.full((8, BLOCK), -1.0, F32)
    layers = sz.layers
    for copy in copies[: len(small)]:
        copy.wait()
    out[pl.ds(sz.size, sz.tiles), :] = size[...]
    out[pl.ds(sz.offset, sz.tiles), :] = offset[...].astype(F32)
    numbers = block_row(sz, block[...]).astype(F32)
    out[pl.ds(sz.meta, 1), pl.ds(0, sz.groups)] = numbers
    numbers = jnp.concatenate([numbers, jnp.zeros((1, BLOCK - sz.groups), F32)], axis=1)
    out[pl.ds(sz.column, sz.groups), :] = jnp.transpose(jnp.broadcast_to(numbers, (BLOCK, BLOCK)))[: sz.groups]
    width = radial.shape[1]
    lane = iota((1, width), 1)
    for slot in range(2):
        kept = jnp.where(lane < counts[0, 2 + slot], radial[slot : slot + 1, :], -1)
        out[pl.ds(sz.meta + 1 + slot, 1), pl.ds(0, width)] = kept.astype(F32)
    index = kinds[...] * (n_rad * sz.blocks) + block_row(sz, cols[...])
    index = jnp.concatenate([index, index], axis=1).astype(F32)
    index = jnp.concatenate([index, jnp.zeros((BLOCK - index.shape[0], BLOCK), F32)], axis=0)
    aux[...] = jnp.transpose(index)[: sz.blocks].astype(I32)
    lane = iota((1, axial.shape[1]), 1)
    kept = [jnp.where(lane < counts[0, slot], axial[slot : slot + 1, :], -1) for slot in range(2)]
    out[pl.ds(sz.meta + 3, 1), :] = jnp.concatenate(kept, axis=1).astype(F32)
    motion_copy, pres_copy, *gas_copies = copies[len(small) :]
    motion_copy.wait()
    for i in range(sz.tiles):
        out[pl.ds(sz.motion + i, 6, stride=sz.tiles), :] = motion[:, i * BLOCK : (i + 1) * BLOCK]
    pres_copy.wait()
    for q in range(sz.quarters):
        out[pl.ds(sz.pres + q * layers, layers), :] = pres[:, q * BLOCK : (q + 1) * BLOCK]
    for c in range(3):
        gas_copies[c].wait()
        for q in range(sz.quarters):
            out[pl.ds(sz.gas + c * sz.blocks + q * layers, layers), :] = gas[c, :, q * BLOCK : (q + 1) * BLOCK]


def take_lanes(x, idx):
    return jnp.take_along_axis(x, idx, axis=1, mode="promise_in_bounds")


def pick(sz, state, idx):
    shape = (sz.tiles, BLOCK)
    idx = jnp.broadcast_to(idx, shape)
    lane = idx & (BLOCK - 1)
    here = (idx >> 7) == iota(shape, 0)
    return [jnp.sum(jnp.where(here, take_lanes(s, lane), 0.0), axis=0, keepdims=True) for s in state]


def slab_rows(sz, n_rad, G, first):
    return jnp.concatenate([G[d, pl.ds(first, sz.tiles), :] for d in range(n_rad)], axis=0)


def state_of(sz, T, state, d):
    first = pl.multiple_of(d * sz.tiles, sz.tiles)
    return [state[pl.ds(c * T + first, sz.tiles), :] for c in range(7)]


def cross(r, n_rad):
    return r + 1 - 2 * (r % 2) if n_rad % 2 == 0 else r


def move_kernel(sz, n_rad, G, state, far, near, found_gas):
    r = lax.axis_index("rad")
    layers, tiles, blocks, groups = sz.layers, sz.tiles, sz.blocks, sz.groups
    slab_blocks = n_rad * blocks
    T = n_rad * tiles

    column = jnp.concatenate([G[d, pl.ds(sz.column, groups), :] for d in range(n_rad)], axis=0).astype(I32)
    lanes = iota((n_rad * groups, BLOCK), 1)
    chooser = jnp.concatenate(
        [(column == lanes + first).astype(F32).astype(BF16) for first in range(0, slab_blocks, BLOCK)], axis=1
    )
    gas_slab = jnp.concatenate(
        [
            jnp.concatenate([G[d, pl.ds(sz.gas + c * blocks, blocks), :] for d in range(n_rad)], axis=0)
            for c in range(3)
        ],
        axis=1,
    )
    high, low = split2(gas_slab)
    found = dot(jnp.concatenate([chooser, chooser], axis=1), jnp.concatenate([high, low], axis=0))
    for c in range(3):
        found_gas[c] = found[:, c * BLOCK : (c + 1) * BLOCK]

    rows = functools.partial(slab_rows, sz, n_rad, G)
    size = rows(sz.size)
    offset = rows(sz.offset).astype(I32)
    factor = jnp.exp(-DRAG / (size * size))
    even = iota((T, BLOCK), 1) < GROUP
    for c in range(3):
        u_even = take_lanes(found_gas[c, pl.ds(0, T, stride=2), :], offset)
        u_odd = take_lanes(found_gas[c, pl.ds(1, T, stride=2), :], offset)
        u = jnp.where(even, u_even, u_odd)
        v = rows(sz.motion + (3 + c) * tiles)
        new = u + (v - u) * factor
        state[pl.ds(c * T, T), :] = rows(sz.motion + c * tiles) + STEP * new
        state[pl.ds((3 + c) * T, T), :] = new
    state[pl.ds(6 * T, T), :] = size

    for message, sent in ((far, cross(r, n_rad)), (near, r)):
        payload = pick(sz, state_of(sz, T, state, sent), G[sent, pl.ds(sz.meta + 3, 1), :].astype(I32))
        for c in range(7):
            message[c : c + 1, :] = payload[c]
        message[7:8, :] = jnp.zeros((1, BLOCK), F32)
        for q in range(sz.quarters):
            first = sz.pres + q * layers
            message[8 + q : 9 + q, :] = G[sent, pl.ds(first + layers - 1, 1), :]
            message[12 + q : 13 + q, :] = G[sent, pl.ds(first, 1), :]


def rest_kernel(
    sz, n_rad, G, aux, table, state,
    motion_hbm, arr_hbm, gas_hbm, liquid_hbm, image,
    deps, spread, coup, motion_out, arr_rad, gas_out, liquid, sem,
):
    r = lax.axis_index("rad")
    sends = [
        pltpu.make_async_copy(src, dst, sem.at[i])
        for i, (src, dst) in enumerate(
            (
                (motion_out, motion_hbm), (arr_rad, arr_hbm), *((gas_out.at[c], gas_hbm.at[c]) for c in range(3)),
                (liquid, liquid_hbm),
            )
        )
    ]
    layers, tiles, blocks, groups = sz.layers, sz.tiles, sz.blocks, sz.groups
    slab_blocks = n_rad * blocks
    T = n_rad * tiles
    block_rows = [G[d, pl.ds(sz.meta, 1), :] for d in range(n_rad)]

    rows = functools.partial(slab_rows, sz, n_rad, G)
    size = rows(sz.size)
    mass = size * size * size
    dep = [-mass * (state[pl.ds((3 + c) * T, T), :] - rows(sz.motion + (3 + c) * tiles)) for c in range(3)] + [mass]
    even = iota((T, BLOCK), 1) < GROUP

    for c in range(4):
        high = dep[c].astype(BF16).astype(F32)
        low = dep[c] - high
        for piece, part in enumerate((high, low)):
            deps[pl.ds((piece * 8 + c) * T, T), :] = jnp.where(even, part, 0.0)
            deps[pl.ds((piece * 8 + 4 + c) * T, T), :] = jnp.where(even, 0.0, part)
    cell = iota((BLOCK, BLOCK), 0).astype(F32).astype(BF16)
    one, none = jnp.ones((BLOCK, BLOCK), BF16), jnp.zeros((BLOCK, BLOCK), BF16)
    blank = jnp.zeros((16, BLOCK), BF16)
    for d in range(n_rad):
        for i in range(0, tiles, 2):
            onehot, lhs = [], []
            for t in (i, i + 1):
                off = jnp.broadcast_to(G[d, pl.ds(sz.offset + t, 1), :], (16, BLOCK)).astype(BF16)
                onehot.append(jnp.where(cell == jnp.concatenate([off] * (BLOCK // 16), axis=0), one, none))
                lhs.append(deps[pl.ds(d * tiles + t, 16, stride=T), :].astype(BF16))
            lhs = jnp.concatenate(
                [jnp.concatenate([lhs[0], blank], axis=1), jnp.concatenate([blank, lhs[1]], axis=1)], axis=0
            )
            res = dot_nt(lhs, jnp.concatenate(onehot, axis=1))
            for k in range(2):
                t = d * tiles + i + k
                both = res[16 * k : 16 * k + 8] + res[16 * k + 8 : 16 * k + 16]
                spread[pl.ds(2 * t, 4, stride=2 * T), :] = both[:4]
                spread[pl.ds(2 * t + 1, 4, stride=2 * T), :] = both[4:]
    own = iota((blocks, groups), 0) + r * blocks
    adder = jnp.concatenate(
        [(own == b[:, :groups].astype(I32)).astype(F32) for b in block_rows] * 2, axis=1
    ).astype(BF16)
    for c in range(4):
        high, low = split2(spread[pl.ds(c * 2 * T, 2 * T), :])
        total = dot(adder, jnp.concatenate([high, low], axis=0))
        for q in range(sz.quarters):
            part = total[q * layers : (q + 1) * layers]
            at = slice(q * BLOCK, (q + 1) * BLOCK)
            if c < 3:
                gas_out[c, :, at] = G[r, pl.ds(sz.gas + c * blocks + q * layers, layers), :] + part
            else:
                liquid[:, at] = part
    for send in sends[2:]:
        send.start()

    pres = jnp.concatenate([G[d, pl.ds(sz.pres, blocks), :] for d in range(n_rad)], axis=0)
    index = [
        jnp.broadcast_to(aux[:, k : k + 1], (blocks, BLOCK)).astype(jnp.int16) for k in range(4)
    ]
    one, none = jnp.ones((blocks, BLOCK), BF16), jnp.zeros((blocks, BLOCK), BF16)
    lanes = iota((blocks, BLOCK), 1)
    counts = []
    for t in range(NT):
        row = []
        for first in range(0, slab_blocks, BLOCK):
            aim = (lanes + (t * slab_blocks + first)).astype(jnp.int16)
            count = jnp.where(aim == index[0], one, none)
            for k in range(1, 4):
                count = count + jnp.where(aim == index[k], one, none)
            row.append(count)
        counts.append(jnp.concatenate(row, axis=1))
    grouped = dot(jnp.concatenate(counts, axis=0), jnp.concatenate(split2(pres), axis=1))
    grouped = grouped[:, :BLOCK] + grouped[:, BLOCK:]
    mine = pl.multiple_of(r * tiles, tiles)
    for i in range(tiles):
        motion_out[:, i * BLOCK : (i + 1) * BLOCK] = state[pl.ds(mine + i, 6, stride=T), :]
    sends[0].start()
    width = arr_rad.shape[2]
    for slot, exists, other in ((0, r > 0, jnp.maximum(r - 1, 0)), (1, r < n_rad - 1, jnp.minimum(r + 1, n_rad - 1))):
        idx = G[other, pl.ds(sz.meta + 1 + slot, 1), :].astype(I32)
        idx = jnp.where(exists, idx, -1)
        got = pick(sz, state_of(sz, T, state, other), idx)
        for c in range(7):
            arr_rad[c, slot : slot + 1, :] = got[c][:, :width]
    sends[1].start()

    grouped = jnp.concatenate([grouped[t * blocks : (t + 1) * blocks] for t in range(NT)], axis=1)
    matrices = jnp.concatenate([table[t] for t in range(NT)], axis=1)
    sums = dot_nt(jnp.concatenate(split2(grouped), axis=0), jnp.concatenate(split2(matrices), axis=0))
    coup[...] = sums[:blocks, :BLOCK] + sums[:blocks, BLOCK:] + sums[blocks:, :BLOCK]
    layer = iota((layers, BLOCK), 0)
    for q in range(sz.quarters):
        p = G[r, pl.ds(sz.pres + q * layers, layers), :]
        below = jnp.where(layer == 0, 0.0, pltpu.roll(p, 1, 0))
        above = jnp.where(layer == layers - 1, 0.0, pltpu.roll(p, layers - 1, 0))
        image[:, q * BLOCK : (q + 1) * BLOCK] = (
            DIAG * p - above - below + coup[pl.ds(q, layers, stride=sz.quarters), :]
        )
    for send in sends:
        send.wait()


def finish_kernel(sz, n_ax, got_b, got_a, image, arr_ax, pressure_image):
    a = lax.axis_index("ax")
    even = a % 2 == 0
    low = jnp.where(a > 0, jnp.where(even, got_b[...], got_a[...]), 0.0)
    up = jnp.where(a < n_ax - 1, jnp.where(even, got_a[...], got_b[...]), 0.0)
    half = arr_ax.shape[2]
    arr_ax[:, 0, :] = low[0:7, 0:half]
    arr_ax[:, 1, :] = up[0:7, half : 2 * half]
    pressure_image[...] = image[...]
    last = sz.layers - 1
    for q in range(sz.quarters):
        at = slice(q * BLOCK, (q + 1) * BLOCK)
        pressure_image[0:1, at] = image[0:1, at] - low[8 + q : 9 + q, :]
        pressure_image[last : last + 1, at] = image[last : last + 1, at] - up[12 + q : 13 + q, :]


def on_device(
    parcel_motion,
    parcel_size,
    parcel_block,
    parcel_offset,
    gas_velocity,
    pressure,
    block_cols,
    block_kinds,
    block_table,
    send_axial,
    send_radial,
    send_counts,
):
    n_ax, n_rad = lax.axis_size("ax"), lax.axis_size("rad")
    layers, radial = pressure.shape
    parcels = parcel_size.shape[0]
    sz = Sizes(layers, radial, parcels)
    T = n_rad * sz.tiles
    cap_ax, cap_rad = send_axial.shape[-1], send_radial.shape[-1]
    params = pltpu.CompilerParams(vmem_limit_bytes=VMEM_LIMIT)
    counts = send_counts.reshape(1, 4)
    size2 = parcel_size.reshape(sz.tiles, BLOCK)
    offset2 = parcel_offset.reshape(sz.tiles, BLOCK)

    packed, aux = pl.pallas_call(
        functools.partial(pack_kernel, sz, n_rad),
        out_shape=[
            jax.ShapeDtypeStruct((sz.rows, BLOCK), F32),
            jax.ShapeDtypeStruct((sz.blocks, BLOCK), I32),
        ],
        in_specs=[hbm] * 11,
        out_specs=[vmem] * 2,
        scratch_shapes=[
            pltpu.VMEM(parcel_motion.shape, F32),
            pltpu.VMEM(size2.shape, F32),
            pltpu.VMEM((1, sz.groups), I32),
            pltpu.VMEM(offset2.shape, I32),
            pltpu.VMEM(gas_velocity.shape, F32),
            pltpu.VMEM(pressure.shape, F32),
            pltpu.VMEM((2, cap_rad), I32),
            pltpu.SMEM((1, 4), I32),
            pltpu.VMEM((4, sz.blocks), I32),
            pltpu.VMEM((4, sz.blocks), I32),
            pltpu.VMEM((2, cap_ax), I32),
            pltpu.SemaphoreType.DMA((13,)),
        ],
        compiler_params=params,
        name="pack",
    )(
        *(
            pltpu.with_memory_space_constraint(x, pltpu.HBM)
            for x in (
                parcel_motion, size2, parcel_block.reshape(1, sz.groups), offset2, gas_velocity, pressure,
                send_radial.reshape(2, cap_rad), counts, block_cols[0].T, block_kinds[0].T,
                send_axial.reshape(2, cap_ax),
            )
        )
    )
    gathered = lax.all_gather(packed, "rad", axis=0)

    state, far, near = pl.pallas_call(
        functools.partial(move_kernel, sz, n_rad),
        out_shape=[
            jax.ShapeDtypeStruct((7 * T, BLOCK), F32),
            jax.ShapeDtypeStruct((16, BLOCK), F32),
            jax.ShapeDtypeStruct((16, BLOCK), F32),
        ],
        in_specs=[vmem],
        out_specs=[vmem] * 3,
        scratch_shapes=[pltpu.VMEM((3, n_rad * sz.groups, BLOCK), F32)],
        compiler_params=params,
        cost_estimate=pl.CostEstimate(flops=4_000_000_000, bytes_accessed=1_000_000, transcendentals=0),
        name="move",
    )(gathered)

    def exchange(message, first, partner):
        to = list(range(n_ax * n_rad))
        for low in range(first, n_ax - 1, 2):
            for r in range(n_rad):
                i, j = low * n_rad + r, (low + 1) * n_rad + partner(r)
                to[i], to[j] = j, i
        alone = [i for i in range(n_ax * n_rad) if to[i] == i]
        for i, j in zip(alone[0::2], alone[1::2]):
            to[i], to[j] = j, i
        return lax.ppermute(message, ("ax", "rad"), list(enumerate(to)))

    got_b = exchange(far, 1, lambda r: cross(r, n_rad))
    got_a = exchange(near, 0, lambda r: r)

    motion_out, arr_rad, gas_out, liquid, image = pl.pallas_call(
        functools.partial(rest_kernel, sz, n_rad),
        out_shape=[
            jax.ShapeDtypeStruct((6, parcels), F32),
            jax.ShapeDtypeStruct((7, 2, cap_rad), F32),
            jax.ShapeDtypeStruct(gas_velocity.shape, F32),
            jax.ShapeDtypeStruct(pressure.shape, F32),
            jax.ShapeDtypeStruct(pressure.shape, F32),
        ],
        in_specs=[vmem] * 4,
        out_specs=[hbm] * 4 + [vmem],
        scratch_shapes=[
            pltpu.VMEM((16 * T, BLOCK), F32),
            pltpu.VMEM((4 * 2 * T, BLOCK), F32),
            pltpu.VMEM((sz.blocks, BLOCK), F32),
            pltpu.VMEM((6, parcels), F32),
            pltpu.VMEM((7, 2, cap_rad), F32),
            pltpu.VMEM(gas_velocity.shape, F32),
            pltpu.VMEM(pressure.shape, F32),
            pltpu.SemaphoreType.DMA((6,)),
        ],
        compiler_params=params,
        cost_estimate=pl.CostEstimate(flops=2_000_000_000, bytes_accessed=2_000_000, transcendentals=0),
        name="rest",
    )(gathered, aux, block_table, state)

    arr_ax, pressure_image = pl.pallas_call(
        functools.partial(finish_kernel, sz, n_ax),
        out_shape=[
            jax.ShapeDtypeStruct((7, 2, cap_ax), F32),
            jax.ShapeDtypeStruct(pressure.shape, F32),
        ],
        in_specs=[vmem] * 3,
        out_specs=[vmem] * 2,
        compiler_params=params,
        name="finish",
    )(got_b, got_a, image)

    arrivals_axial = arr_ax.transpose(1, 0, 2)[None, None]
    arrivals_radial = arr_rad.transpose(1, 0, 2)[None, None]
    return (motion_out, arrivals_axial, arrivals_radial, gas_out, liquid, pressure_image)


def solution(mesh):
    return jax.shard_map(
        on_device,
        mesh=mesh,
        in_specs=(
            P(None, ("ax", "rad")),
            P(("ax", "rad")),
            P(("ax", "rad")),
            P(("ax", "rad")),
            P(None, "ax", "rad"),
            P("ax", "rad"),
            P("ax", "rad", None),
            P("ax", "rad", None),
            P(),
            P("ax", "rad", None, None),
            P("ax", "rad", None, None),
            P("ax", "rad", None),
        ),
        out_specs=(
            P(None, ("ax", "rad")),
            P("ax", "rad", None, None, None),
            P("ax", "rad", None, None, None),
            P(None, "ax", "rad"),
            P("ax", "rad"),
            P("ax", "rad"),
        ),
        check_vma=False,
    )
```

```python
import functools

import jax
import jax.numpy as jnp
from jax import lax
from jax.experimental import pallas as pl
from jax.experimental.pallas import tpu as pltpu
from jax.sharding import PartitionSpec as P

BLOCK = 128
GROUP = 64
NT = 8
DRAG = 0.5
STEP = 0.5
DIAG = 6.0
VMEM_LIMIT = 24 * 1024 * 1024

F32 = jnp.float32
BF16 = jnp.bfloat16
I32 = jnp.int32

vmem = pl.BlockSpec(memory_space=pltpu.VMEM)
hbm = pl.BlockSpec(memory_space=pltpu.HBM)


class Sizes:
    def __init__(self, layers, radial, parcels):
        self.layers = layers
        self.quarters = radial // BLOCK
        self.blocks = layers * self.quarters
        self.tiles = parcels // BLOCK
        self.groups = parcels // GROUP
        self.gas = 0
        self.pres = 3 * self.blocks
        self.motion = self.pres + self.blocks
        self.size = self.motion + 6 * self.tiles
        self.offset = self.size + self.tiles
        self.meta = self.offset + self.tiles
        self.column = self.meta + 8
        self.rows = self.column + self.groups


def split2(x):
    high = x.astype(BF16)
    return high, (x - high.astype(F32)).astype(BF16)


def dot(a, b):
    return jnp.dot(a, b, preferred_element_type=F32)


def dot_nt(a, b):
    return lax.dot_general(a, b, (((1,), (1,)), ((), ())), preferred_element_type=F32)


def iota(shape, dim):
    return lax.broadcasted_iota(I32, shape, dim)


def block_row(sz, b):
    local = b % sz.blocks
    return b - local + (local % sz.quarters) * sz.layers + local // sz.quarters


def pack_kernel(
    sz, n_rad, motion_hbm, size_hbm, block_hbm, offset_hbm, gas_hbm, pres_hbm, radial_hbm, counts_hbm, cols_hbm,
    kinds_hbm, axial_hbm,
    out, aux,
    motion, size, block, offset, gas, pres, radial, counts, cols, kinds, axial, sem,
):
    small = (
        (counts_hbm, counts), (block_hbm, block), (radial_hbm, radial), (axial_hbm, axial), (cols_hbm, cols),
        (kinds_hbm, kinds), (offset_hbm, offset), (size_hbm, size),
    )
    large = ((motion_hbm, motion), (pres_hbm, pres), *((gas_hbm.at[c], gas.at[c]) for c in range(3)))
    copies = [pltpu.make_async_copy(src, dst, sem.at[i]) for i, (src, dst) in enumerate(small + large)]
    for copy in copies:
        copy.start()
    out[pl.ds(sz.meta, 8), :] = jnp.full((8, BLOCK), -1.0, F32)
    layers = sz.layers
    for copy in copies[: len(small)]:
        copy.wait()
    out[pl.ds(sz.size, sz.tiles), :] = size[...]
    out[pl.ds(sz.offset, sz.tiles), :] = offset[...].astype(F32)
    numbers = block_row(sz, block[...]).astype(F32)
    out[pl.ds(sz.meta, 1), pl.ds(0, sz.groups)] = numbers
    numbers = jnp.concatenate([numbers, jnp.zeros((1, BLOCK - sz.groups), F32)], axis=1)
    out[pl.ds(sz.column, sz.groups), :] = jnp.transpose(jnp.broadcast_to(numbers, (BLOCK, BLOCK)))[: sz.groups]
    width = radial.shape[1]
    lane = iota((1, width), 1)
    for slot in range(2):
        kept = jnp.where(lane < counts[0, 2 + slot], radial[slot : slot + 1, :], -1)
        out[pl.ds(sz.meta + 1 + slot, 1), pl.ds(0, width)] = kept.astype(F32)
    index = kinds[...] * (n_rad * sz.blocks) + block_row(sz, cols[...])
    index = jnp.concatenate([index, index], axis=1).astype(F32)
    index = jnp.concatenate([index, jnp.zeros((BLOCK - index.shape[0], BLOCK), F32)], axis=0)
    aux[...] = jnp.transpose(index)[: sz.blocks].astype(I32)
    lane = iota((1, axial.shape[1]), 1)
    kept = [jnp.where(lane < counts[0, slot], axial[slot : slot + 1, :], -1) for slot in range(2)]
    out[pl.ds(sz.meta + 3, 1), :] = jnp.concatenate(kept, axis=1).astype(F32)
    motion_copy, pres_copy, *gas_copies = copies[len(small) :]
    motion_copy.wait()
    for i in range(sz.tiles):
        out[pl.ds(sz.motion + i, 6, stride=sz.tiles), :] = motion[:, i * BLOCK : (i + 1) * BLOCK]
    pres_copy.wait()
    for q in range(sz.quarters):
        out[pl.ds(sz.pres + q * layers, layers), :] = pres[:, q * BLOCK : (q + 1) * BLOCK]
    for c in range(3):
        gas_copies[c].wait()
        for q in range(sz.quarters):
            out[pl.ds(sz.gas + c * sz.blocks + q * layers, layers), :] = gas[c, :, q * BLOCK : (q + 1) * BLOCK]


def take_lanes(x, idx):
    return jnp.take_along_axis(x, idx, axis=1, mode="promise_in_bounds")


def pick(sz, state, idx):
    shape = (sz.tiles, BLOCK)
    idx = jnp.broadcast_to(idx, shape)
    lane = idx & (BLOCK - 1)
    here = (idx >> 7) == iota(shape, 0)
    return [jnp.sum(jnp.where(here, take_lanes(s, lane), 0.0), axis=0, keepdims=True) for s in state]


def slab_rows(sz, n_rad, G, first):
    return jnp.concatenate([G[d, pl.ds(first, sz.tiles), :] for d in range(n_rad)], axis=0)


def state_of(sz, T, state, d):
    first = pl.multiple_of(d * sz.tiles, sz.tiles)
    return [state[pl.ds(c * T + first, sz.tiles), :] for c in range(7)]


def cross(r, n_rad):
    return r + 1 - 2 * (r % 2) if n_rad % 2 == 0 else r


def move_kernel(sz, n_rad, G, state, message, near):
    sent = cross(lax.axis_index("rad"), n_rad)
    layers, tiles, blocks, groups = sz.layers, sz.tiles, sz.blocks, sz.groups
    slab_blocks = n_rad * blocks
    T = n_rad * tiles

    column = jnp.concatenate([G[d, pl.ds(sz.column, groups), :] for d in range(n_rad)], axis=0).astype(I32)
    lanes = iota((n_rad * groups, BLOCK), 1)
    chooser = jnp.concatenate(
        [(column == lanes + first).astype(F32).astype(BF16) for first in range(0, slab_blocks, BLOCK)], axis=1
    )
    gas_slab = jnp.concatenate(
        [
            jnp.concatenate([G[d, pl.ds(sz.gas + c * blocks, blocks), :] for d in range(n_rad)], axis=0)
            for c in range(3)
        ],
        axis=1,
    )
    high, low = split2(gas_slab)
    found = dot(jnp.concatenate([chooser, chooser], axis=1), jnp.concatenate([high, low], axis=0))
    for c in range(3):
        near[c] = found[:, c * BLOCK : (c + 1) * BLOCK]

    rows = functools.partial(slab_rows, sz, n_rad, G)
    size = rows(sz.size)
    offset = rows(sz.offset).astype(I32)
    factor = jnp.exp(-DRAG / (size * size))
    even = iota((T, BLOCK), 1) < GROUP
    for c in range(3):
        u_even = take_lanes(near[c, pl.ds(0, T, stride=2), :], offset)
        u_odd = take_lanes(near[c, pl.ds(1, T, stride=2), :], offset)
        u = jnp.where(even, u_even, u_odd)
        v = rows(sz.motion + (3 + c) * tiles)
        new = u + (v - u) * factor
        state[pl.ds(c * T, T), :] = rows(sz.motion + c * tiles) + STEP * new
        state[pl.ds((3 + c) * T, T), :] = new
    state[pl.ds(6 * T, T), :] = size

    payload = pick(sz, state_of(sz, T, state, sent), G[sent, pl.ds(sz.meta + 3, 1), :].astype(I32))
    for c in range(7):
        message[c : c + 1, :] = payload[c]
    message[7:8, :] = jnp.zeros((1, BLOCK), F32)
    for q in range(sz.quarters):
        first = sz.pres + q * layers
        message[8 + q : 9 + q, :] = G[sent, pl.ds(first + layers - 1, 1), :]
        message[12 + q : 13 + q, :] = G[sent, pl.ds(first, 1), :]


def rest_kernel(
    sz, n_rad, G, aux, table, state,
    motion_hbm, arr_hbm, gas_hbm, liquid_hbm, image,
    deps, spread, coup, motion_out, arr_rad, gas_out, liquid, sem,
):
    r = lax.axis_index("rad")
    sends = [
        pltpu.make_async_copy(src, dst, sem.at[i])
        for i, (src, dst) in enumerate(
            (
                (motion_out, motion_hbm), (arr_rad, arr_hbm), *((gas_out.at[c], gas_hbm.at[c]) for c in range(3)),
                (liquid, liquid_hbm),
            )
        )
    ]
    layers, tiles, blocks, groups = sz.layers, sz.tiles, sz.blocks, sz.groups
    slab_blocks = n_rad * blocks
    T = n_rad * tiles
    block_rows = [G[d, pl.ds(sz.meta, 1), :] for d in range(n_rad)]

    rows = functools.partial(slab_rows, sz, n_rad, G)
    size = rows(sz.size)
    mass = size * size * size
    dep = [-mass * (state[pl.ds((3 + c) * T, T), :] - rows(sz.motion + (3 + c) * tiles)) for c in range(3)] + [mass]
    even = iota((T, BLOCK), 1) < GROUP

    for c in range(4):
        high = dep[c].astype(BF16).astype(F32)
        low = dep[c] - high
        for piece, part in enumerate((high, low)):
            deps[pl.ds((piece * 8 + c) * T, T), :] = jnp.where(even, part, 0.0)
            deps[pl.ds((piece * 8 + 4 + c) * T, T), :] = jnp.where(even, 0.0, part)
    cell = iota((BLOCK, BLOCK), 0).astype(F32).astype(BF16)
    one, none = jnp.ones((BLOCK, BLOCK), BF16), jnp.zeros((BLOCK, BLOCK), BF16)
    blank = jnp.zeros((16, BLOCK), BF16)
    for d in range(n_rad):
        for i in range(0, tiles, 2):
            onehot, lhs = [], []
            for t in (i, i + 1):
                off = jnp.broadcast_to(G[d, pl.ds(sz.offset + t, 1), :], (16, BLOCK)).astype(BF16)
                onehot.append(jnp.where(cell == jnp.concatenate([off] * (BLOCK // 16), axis=0), one, none))
                lhs.append(deps[pl.ds(d * tiles + t, 16, stride=T), :].astype(BF16))
            lhs = jnp.concatenate(
                [jnp.concatenate([lhs[0], blank], axis=1), jnp.concatenate([blank, lhs[1]], axis=1)], axis=0
            )
            res = dot_nt(lhs, jnp.concatenate(onehot, axis=1))
            for k in range(2):
                t = d * tiles + i + k
                both = res[16 * k : 16 * k + 8] + res[16 * k + 8 : 16 * k + 16]
                spread[pl.ds(2 * t, 4, stride=2 * T), :] = both[:4]
                spread[pl.ds(2 * t + 1, 4, stride=2 * T), :] = both[4:]
    own = iota((blocks, groups), 0) + r * blocks
    adder = jnp.concatenate(
        [(own == b[:, :groups].astype(I32)).astype(F32) for b in block_rows] * 2, axis=1
    ).astype(BF16)
    for c in range(4):
        high, low = split2(spread[pl.ds(c * 2 * T, 2 * T), :])
        total = dot(adder, jnp.concatenate([high, low], axis=0))
        for q in range(sz.quarters):
            part = total[q * layers : (q + 1) * layers]
            at = slice(q * BLOCK, (q + 1) * BLOCK)
            if c < 3:
                gas_out[c, :, at] = G[r, pl.ds(sz.gas + c * blocks + q * layers, layers), :] + part
            else:
                liquid[:, at] = part
    mine = pl.multiple_of(r * tiles, tiles)
    for i in range(tiles):
        motion_out[:, i * BLOCK : (i + 1) * BLOCK] = state[pl.ds(mine + i, 6, stride=T), :]
    width = arr_rad.shape[2]
    for slot, exists, other in ((0, r > 0, jnp.maximum(r - 1, 0)), (1, r < n_rad - 1, jnp.minimum(r + 1, n_rad - 1))):
        idx = G[other, pl.ds(sz.meta + 1 + slot, 1), :].astype(I32)
        idx = jnp.where(exists, idx, -1)
        got = pick(sz, state_of(sz, T, state, other), idx)
        for c in range(7):
            arr_rad[c, slot : slot + 1, :] = got[c][:, :width]
    for send in sends:
        send.start()

    pres = jnp.concatenate([G[d, pl.ds(sz.pres, blocks), :] for d in range(n_rad)], axis=0)
    index = [
        jnp.broadcast_to(aux[:, k : k + 1], (blocks, BLOCK)).astype(jnp.int16) for k in range(4)
    ]
    one, none = jnp.ones((blocks, BLOCK), BF16), jnp.zeros((blocks, BLOCK), BF16)
    lanes = iota((blocks, BLOCK), 1)
    counts = []
    for t in range(NT):
        row = []
        for first in range(0, slab_blocks, BLOCK):
            aim = (lanes + (t * slab_blocks + first)).astype(jnp.int16)
            count = jnp.where(aim == index[0], one, none)
            for k in range(1, 4):
                count = count + jnp.where(aim == index[k], one, none)
            row.append(count)
        counts.append(jnp.concatenate(row, axis=1))
    grouped = dot(jnp.concatenate(counts, axis=0), jnp.concatenate(split2(pres), axis=1))
    grouped = grouped[:, :BLOCK] + grouped[:, BLOCK:]

    grouped = jnp.concatenate([grouped[t * blocks : (t + 1) * blocks] for t in range(NT)], axis=1)
    matrices = jnp.concatenate([table[t] for t in range(NT)], axis=1)
    sums = dot_nt(jnp.concatenate(split2(grouped), axis=0), jnp.concatenate(split2(matrices), axis=0))
    coup[...] = sums[:blocks, :BLOCK] + sums[:blocks, BLOCK:] + sums[blocks:, :BLOCK]
    layer = iota((layers, BLOCK), 0)
    for q in range(sz.quarters):
        p = G[r, pl.ds(sz.pres + q * layers, layers), :]
        below = jnp.where(layer == 0, 0.0, pltpu.roll(p, 1, 0))
        above = jnp.where(layer == layers - 1, 0.0, pltpu.roll(p, layers - 1, 0))
        image[:, q * BLOCK : (q + 1) * BLOCK] = (
            DIAG * p - above - below + coup[pl.ds(q, layers, stride=sz.quarters), :]
        )
    for send in sends:
        send.wait()


def finish_kernel(sz, n_ax, got_a, got_b, image, arr_ax, pressure_image):
    a = lax.axis_index("ax")
    even = a % 2 == 0
    low = jnp.where(a > 0, jnp.where(even, got_b[...], got_a[...]), 0.0)
    up = jnp.where(a < n_ax - 1, jnp.where(even, got_a[...], got_b[...]), 0.0)
    half = arr_ax.shape[2]
    arr_ax[:, 0, :] = low[0:7, 0:half]
    arr_ax[:, 1, :] = up[0:7, half : 2 * half]
    pressure_image[...] = image[...]
    last = sz.layers - 1
    for q in range(sz.quarters):
        at = slice(q * BLOCK, (q + 1) * BLOCK)
        pressure_image[0:1, at] = image[0:1, at] - low[8 + q : 9 + q, :]
        pressure_image[last : last + 1, at] = image[last : last + 1, at] - up[12 + q : 13 + q, :]


def on_device(
    parcel_motion,
    parcel_size,
    parcel_block,
    parcel_offset,
    gas_velocity,
    pressure,
    block_cols,
    block_kinds,
    block_table,
    send_axial,
    send_radial,
    send_counts,
):
    n_ax, n_rad = lax.axis_size("ax"), lax.axis_size("rad")
    layers, radial = pressure.shape
    parcels = parcel_size.shape[0]
    sz = Sizes(layers, radial, parcels)
    T = n_rad * sz.tiles
    cap_ax, cap_rad = send_axial.shape[-1], send_radial.shape[-1]
    params = pltpu.CompilerParams(vmem_limit_bytes=VMEM_LIMIT)
    counts = send_counts.reshape(1, 4)
    size2 = parcel_size.reshape(sz.tiles, BLOCK)
    offset2 = parcel_offset.reshape(sz.tiles, BLOCK)

    packed, aux = pl.pallas_call(
        functools.partial(pack_kernel, sz, n_rad),
        out_shape=[
            jax.ShapeDtypeStruct((sz.rows, BLOCK), F32),
            jax.ShapeDtypeStruct((sz.blocks, BLOCK), I32),
        ],
        in_specs=[hbm] * 11,
        out_specs=[vmem] * 2,
        scratch_shapes=[
            pltpu.VMEM(parcel_motion.shape, F32),
            pltpu.VMEM(size2.shape, F32),
            pltpu.VMEM((1, sz.groups), I32),
            pltpu.VMEM(offset2.shape, I32),
            pltpu.VMEM(gas_velocity.shape, F32),
            pltpu.VMEM(pressure.shape, F32),
            pltpu.VMEM((2, cap_rad), I32),
            pltpu.SMEM((1, 4), I32),
            pltpu.VMEM((4, sz.blocks), I32),
            pltpu.VMEM((4, sz.blocks), I32),
            pltpu.VMEM((2, cap_ax), I32),
            pltpu.SemaphoreType.DMA((13,)),
        ],
        compiler_params=params,
        name="pack",
    )(
        *(
            pltpu.with_memory_space_constraint(x, pltpu.HBM)
            for x in (
                parcel_motion, size2, parcel_block.reshape(1, sz.groups), offset2, gas_velocity, pressure,
                send_radial.reshape(2, cap_rad), counts, block_cols[0].T, block_kinds[0].T,
                send_axial.reshape(2, cap_ax),
            )
        )
    )
    gathered = lax.all_gather(packed, "rad", axis=0)

    state, message = pl.pallas_call(
        functools.partial(move_kernel, sz, n_rad),
        out_shape=[
            jax.ShapeDtypeStruct((7 * T, BLOCK), F32),
            jax.ShapeDtypeStruct((16, BLOCK), F32),
        ],
        in_specs=[vmem],
        out_specs=[vmem] * 2,
        scratch_shapes=[pltpu.VMEM((3, n_rad * sz.groups, BLOCK), F32)],
        compiler_params=params,
        cost_estimate=pl.CostEstimate(flops=4_000_000_000, bytes_accessed=1_000_000, transcendentals=0),
        name="move",
    )(gathered)

    def exchange(first):
        to = list(range(n_ax * n_rad))
        for low in range(first, n_ax - 1, 2):
            for r in range(n_rad):
                i, j = low * n_rad + r, (low + 1) * n_rad + cross(r, n_rad)
                to[i], to[j] = j, i
        alone = [i for i in range(n_ax * n_rad) if to[i] == i]
        for i, j in zip(alone[0::2], alone[1::2]):
            to[i], to[j] = j, i
        return lax.ppermute(message, ("ax", "rad"), list(enumerate(to)))

    got_b = exchange(1)
    got_a = exchange(0)

    motion_out, arr_rad, gas_out, liquid, image = pl.pallas_call(
        functools.partial(rest_kernel, sz, n_rad),
        out_shape=[
            jax.ShapeDtypeStruct((6, parcels), F32),
            jax.ShapeDtypeStruct((7, 2, cap_rad), F32),
            jax.ShapeDtypeStruct(gas_velocity.shape, F32),
            jax.ShapeDtypeStruct(pressure.shape, F32),
            jax.ShapeDtypeStruct(pressure.shape, F32),
        ],
        in_specs=[vmem] * 4,
        out_specs=[hbm] * 4 + [vmem],
        scratch_shapes=[
            pltpu.VMEM((16 * T, BLOCK), F32),
            pltpu.VMEM((4 * 2 * T, BLOCK), F32),
            pltpu.VMEM((sz.blocks, BLOCK), F32),
            pltpu.VMEM((6, parcels), F32),
            pltpu.VMEM((7, 2, cap_rad), F32),
            pltpu.VMEM(gas_velocity.shape, F32),
            pltpu.VMEM(pressure.shape, F32),
            pltpu.SemaphoreType.DMA((6,)),
        ],
        compiler_params=params,
        cost_estimate=pl.CostEstimate(flops=2_000_000_000, bytes_accessed=2_000_000, transcendentals=0),
        name="rest",
    )(gathered, aux, block_table, state)

    arr_ax, pressure_image = pl.pallas_call(
        functools.partial(finish_kernel, sz, n_ax),
        out_shape=[
            jax.ShapeDtypeStruct((7, 2, cap_ax), F32),
            jax.ShapeDtypeStruct(pressure.shape, F32),
        ],
        in_specs=[vmem] * 3,
        out_specs=[vmem] * 2,
        compiler_params=params,
        name="finish",
    )(got_a, got_b, image)

    arrivals_axial = arr_ax.transpose(1, 0, 2)[None, None]
    arrivals_radial = arr_rad.transpose(1, 0, 2)[None, None]
    return (motion_out, arrivals_axial, arrivals_radial, gas_out, liquid, pressure_image)


def solution(mesh):
    return jax.shard_map(
        on_device,
        mesh=mesh,
        in_specs=(
            P(None, ("ax", "rad")),
            P(("ax", "rad")),
            P(("ax", "rad")),
            P(("ax", "rad")),
            P(None, "ax", "rad"),
            P("ax", "rad"),
            P("ax", "rad", None),
            P("ax", "rad", None),
            P(),
            P("ax", "rad", None, None),
            P("ax", "rad", None, None),
            P("ax", "rad", None),
        ),
        out_specs=(
            P(None, ("ax", "rad")),
            P("ax", "rad", None, None, None),
            P("ax", "rad", None, None, None),
            P(None, "ax", "rad"),
            P("ax", "rad"),
            P("ax", "rad"),
        ),
        check_vma=False,
    )
```
